32 devices in a mesh: dp: 2 (over x), row: 4 (over z), col: 4 (over y, core).
Axes of the slice: x: 2, y: 2, z: 4, core: 2. Of those that a mesh axis runs over, the one named last changes fastest.
Arguments:
- hidden_in: bfloat16 [8192, 2048], P(('dp', 'col'), 'row'), may hold values from -144 to 144
- w_query: bfloat16 [2048, 2048], P('row', 'col'), may hold values from -0.125 to 0.125
- w_key: bfloat16 [2048, 2048], P('row', 'col'), may hold values from -0.125 to 0.125
- w_value: bfloat16 [2048, 2048], P('row', 'col'), may hold values from -0.125 to 0.125
- w_out: bfloat16 [2048, 2048], P('col', 'row'), may hold values from -2 to 2
- w_gate: bfloat16 [2048, 8192], P('row', 'col'), may hold values from -0.125 to 0.125
- w_up: bfloat16 [2048, 8192], P('row', 'col'), may hold values from -0.125 to 0.125
- w_down: bfloat16 [8192, 2048], P('col', 'row'), may hold values from -0.0625 to 0.0625
- norm_attn: float32 [2048], P('row'), may hold values from 0.1 to 1.9
- norm_ffn: float32 [2048], P('row'), may hold values from 0.1 to 1.9
- grad_out: bfloat16 [8192, 2048], P(('dp', 'col'), 'row'), may hold values from -6 to 6
Outputs:
- layer_out: bfloat16 [8192, 2048], P(('dp', 'col'), 'row')
- grad_in: bfloat16 [8192, 2048], P(('dp', 'col'), 'row')
- grad_query: float32 [2048, 2048], P('row', 'col')
- grad_key: float32 [2048, 2048], P('row', 'col')
- grad_value: float32 [2048, 2048], P('row', 'col')
- grad_attn_out: float32 [2048, 2048], P('col', 'row')
- grad_gate: float32 [2048, 8192], P('row', 'col')
- grad_up: float32 [2048, 8192], P('row', 'col')
- grad_down: float32 [8192, 2048], P('col', 'row')
- grad_norm_attn: float32 [2048], P('row')
- grad_norm_ffn: float32 [2048], P('row')
The draws below stay inside these ranges and needn't reach their ends.
All inputs are finite; a program needn't handle non-finite values.
Results may differ from the reference program's by a relative error of at most 0.014.
Values may be sent and summed in bfloat16 or wider, within the bound.
A program may use at most 448 MiB of HBM per device.

```python
import math
import jax
import jax.numpy as jnp
from jax import lax

D = 2048
HEADS = 32
HEAD_DIM = 64
FF = 8192
SEQ = 1024
TOKENS = 8192


def draw_hidden_in(key, part):
    key = jax.random.fold_in(key, 11)
    first = jax.random.fold_in(key, 0)
    second = jax.random.fold_in(key, 1)
    third = jax.random.fold_in(key, 2)
    fifth = jax.random.fold_in(key, 4)
    row_scale = jnp.exp(jax.random.uniform(first, (TOKENS, 1), jnp.float32, math.log(0.3), math.log(3.0)))
    drawn_scale = jnp.exp(jax.random.uniform(second, (1, D), jnp.float32, math.log(0.3), math.log(3.0)))
    ranks = jax.random.permutation(fifth, D)
    outlier_count = max(2, D // 512)
    col_scale = jnp.where((ranks < outlier_count)[None, :], 12.0, drawn_scale)
    base = jax.random.normal(third, (TOKENS, D), jnp.float32)
    base = jnp.clip(base, -4.0, 4.0)
    return (base * row_scale * col_scale).astype(jnp.bfloat16)


def level_of(stream_key, extent, pieces, low, largest):
    loudness = 1.0
    for position, blocks in pieces:
        heights = jax.random.uniform(jax.random.fold_in(jax.random.fold_in(stream_key, 6), position), (blocks,), jnp.float32, low / len(pieces), largest / len(pieces))
        loudness = loudness * jnp.repeat(jnp.exp(heights), extent[position] // blocks).reshape((-1,) + (1,) * (len(extent) - 1 - position))
    return loudness


def scatter_about(rng, shape, deviation, bound, shards=(), kind=jnp.bfloat16):
    values = deviation * jax.random.normal(rng, shape, jnp.float32)
    if shards:
        values = values * level_of(rng, shape, shards, -0.22, 0.18)
    return jnp.clip(values, -bound, bound).astype(kind)


def setup_inputs(seed: int = 0) -> dict:
    streams_of = jax.random.split(jax.random.key(seed), 12)
    hidden_in = draw_hidden_in(jax.random.fold_in(streams_of[11], 71), 0)
    w_query = scatter_about(streams_of[1], (D, D), D ** -0.5, 0.125, ((0, 4), (1, 4)))
    w_key = scatter_about(streams_of[2], (D, D), D ** -0.5, 0.125, ((0, 4), (1, 4)))
    w_value = scatter_about(streams_of[3], (D, D), D ** -0.5, 0.125, ((0, 4), (1, 4)))
    w_out = scatter_about(streams_of[4], (D, D), (max(1, D // 256)) ** -0.5, 2.0, ((0, 4), (1, 4)))
    w_gate = scatter_about(streams_of[5], (D, FF), D ** -0.5, 0.125, ((0, 4), (1, 4)))
    w_up = scatter_about(streams_of[6], (D, FF), D ** -0.5, 0.125, ((0, 4), (1, 4)))
    w_down = scatter_about(streams_of[7], (FF, D), FF ** -0.5, 0.0625, ((0, 4), (1, 4)))
    norm_attn = jnp.clip(1.0 + 0.18 * jax.random.normal(streams_of[8], (D,), jnp.float32), 0.1, 1.9)
    norm_ffn = jnp.clip(1.0 + 0.18 * jax.random.normal(streams_of[9], (D,), jnp.float32), 0.1, 1.9)
    grad_out = scatter_about(streams_of[10], (TOKENS, D), 1.0, 6.0, ((0, 8), (1, 4)))
    return {"hidden_in": hidden_in, "w_query": w_query, "w_key": w_key, "w_value": w_value, "w_out": w_out, "w_gate": w_gate, "w_up": w_up, "w_down": w_down, "norm_attn": norm_attn, "norm_ffn": norm_ffn, "grad_out": grad_out}


@jax.custom_vjp
def low(v):
    return lax.optimization_barrier(v.astype(jnp.bfloat16)).astype(jnp.float32)

@jax.custom_vjp
def low_back(v):
    return v

def low_keep(v):
    return (low(v), None)

def low_pass(kept, grad):
    return (grad,)

def back_keep(v):
    return (v, None)

def back_low(kept, grad):
    return (low(grad),)
low.defvjp(low_keep, low_pass)
low_back.defvjp(back_keep, back_low)
EPSILON = 1e-05
THETA = 130000.0

def matmul(left, right):
    return jnp.dot(left, right, precision=lax.Precision.HIGHEST, preferred_element_type=jnp.float32)

def rms_scale(values, gain):
    return values * lax.rsqrt(lax.optimization_barrier(jnp.mean(values * values, axis=-1, keepdims=True)) + EPSILON) * gain

def rotate_heads(values):
    count = values.shape[0]
    heads = values.reshape(count, HEADS, HEAD_DIM)
    half = HEAD_DIM // 2
    freq = THETA ** (-(jnp.arange(half, dtype=jnp.float32) * 2.0 / HEAD_DIM))
    places = (jnp.arange(count, dtype=jnp.int32) % SEQ).astype(jnp.float32)
    angle = places[:, None] * freq[None, :]
    cosine = jnp.concatenate([jnp.cos(angle), jnp.cos(angle)], 1)[:, None, :]
    sine = jnp.concatenate([jnp.sin(angle), jnp.sin(angle)], 1)[:, None, :]
    turned = jnp.concatenate([-heads[..., half:], heads[..., :half]], -1)
    return (heads * cosine + turned * sine).reshape(count, D)

def one_sequence(inputs):
    query, keys, values = inputs
    query_heads = query.reshape(SEQ, HEADS, HEAD_DIM)
    key_heads = keys.reshape(SEQ, HEADS, HEAD_DIM)
    value_heads = values.reshape(SEQ, HEADS, HEAD_DIM)
    scores = jnp.einsum('qhd,khd->hqk', query_heads, key_heads, precision=lax.Precision.HIGHEST) * HEAD_DIM ** (-0.5)
    scores = low_back(scores)
    allowed = jnp.arange(SEQ)[:, None] >= jnp.arange(SEQ)[None, :]
    probs = jax.nn.softmax(jnp.where(allowed[None], scores, -jnp.inf), axis=-1)
    mixed = jnp.einsum('hqk,khd->qhd', low(probs), value_heads, precision=lax.Precision.HIGHEST)
    return mixed.reshape(SEQ, D)

def forward(inputs, w_query, w_key, w_value, w_out, w_gate, w_up, w_down, norm_attn, norm_ffn):
    normed_one = low(rms_scale(inputs, norm_attn))
    query = low(rotate_heads(low_back(matmul(normed_one, w_query))))
    keys = low(rotate_heads(low_back(matmul(normed_one, w_key))))
    values = low(low_back(matmul(normed_one, w_value)))
    count = TOKENS // SEQ
    mixed = lax.map(jax.checkpoint(one_sequence), (query.reshape(count, SEQ, D), keys.reshape(count, SEQ, D), values.reshape(count, SEQ, D)))
    mixed = low(low_back(mixed.reshape(TOKENS, D)))
    middle = inputs + low_back(matmul(mixed, w_out))
    normed_two = low(rms_scale(middle, norm_ffn))
    gate = low_back(matmul(normed_two, w_gate))
    upward = low_back(matmul(normed_two, w_up))
    activated = low(jax.nn.silu(gate) * upward)
    return middle + low_back(matmul(activated, w_down))

def reference(hidden_in, w_query, w_key, w_value, w_out, w_gate, w_up, w_down, norm_attn, norm_ffn, grad_out):
    floats = [a.astype(jnp.float32) for a in (hidden_in, w_query, w_key, w_value, w_out, w_gate, w_up, w_down, norm_attn, norm_ffn)]
    result, pullback = jax.vjp(forward, *floats)
    grads = pullback(grad_out.astype(jnp.float32))
    return (result.astype(jnp.bfloat16), grads[0].astype(jnp.bfloat16), grads[1], grads[2], grads[3], grads[4], grads[5], grads[6], grads[7], grads[8], grads[9])
```

```python
import jax
import jax.numpy as jnp
from jax import lax
from jax.sharding import PartitionSpec as P

HEAD_DIM = 64
EPSILON = 1e-05
THETA = 130000.0
GROUP = ("dp", "col")
LOW = jnp.bfloat16


def dot(left, right):
    return jnp.dot(left, right, preferred_element_type=jnp.float32)


def inner_rows(left, right):
    return lax.dot_general(
        left, right, (((0,), (0,)), ((), ())), preferred_element_type=jnp.float32
    )


def inner_cols(left, right):
    return lax.dot_general(
        left, right, (((1,), (1,)), ((), ())), preferred_element_type=jnp.float32
    )


def seat_pairs():
    rows, cols = lax.axis_size("row"), lax.axis_size("col")
    per = cols // rows
    return [
        (r * cols + c, (c // per) * cols + (c % per) * rows + r)
        for r in range(rows)
        for c in range(cols)
    ]


def to_group(block):
    whole = lax.all_to_all(block, "row", split_axis=0, concat_axis=1, tiled=True)
    return lax.ppermute(whole, ("row", "col"), seat_pairs())


def from_group(block):
    back = lax.ppermute(block, ("row", "col"), [(b, a) for a, b in seat_pairs()])
    return lax.all_to_all(back, "row", split_axis=1, concat_axis=0, tiled=True)


def group_gather(shard):
    return lax.all_gather(shard, GROUP, axis=0, tiled=True)


def group_scatter(partial):
    return lax.psum_scatter(
        partial.astype(LOW), GROUP, scatter_dimension=0, tiled=True
    ).astype(jnp.float32)


def my_part(block, axis):
    size = block.shape[axis] // lax.axis_size("dp")
    return lax.dynamic_slice_in_dim(block, lax.axis_index("dp") * size, size, axis)


def gather_tall(*blocks):
    mine = jnp.concatenate([my_part(b, 1) for b in blocks], 1)
    return lax.all_gather(mine, "row", axis=0, tiled=True)


def gather_wide(block):
    return lax.all_gather(my_part(block, 0), "row", axis=1, tiled=True)


def scatter_tall(grad, count):
    mine = lax.psum_scatter(grad.astype(LOW), "row", scatter_dimension=0, tiled=True)
    parts = lax.all_gather(mine, "dp", axis=0)
    width = mine.shape[1] // count
    return [
        jnp.concatenate(
            [parts[d, :, i * width : (i + 1) * width] for d in range(parts.shape[0])], 1
        ).astype(jnp.float32)
        for i in range(count)
    ]


def scatter_wide(grad):
    mine = lax.psum_scatter(grad.astype(LOW), "row", scatter_dimension=1, tiled=True)
    return lax.all_gather(mine, "dp", axis=0, tiled=True).astype(jnp.float32)


def rms_scale(values):
    return lax.rsqrt(jnp.mean(values * values, axis=1, keepdims=True) + EPSILON)


def norm_back(values, scale, weighted):
    inner = jnp.mean(weighted * values, axis=1, keepdims=True)
    return scale * weighted - values * (scale * scale * scale * inner)


def rotation_tables(length):
    half = HEAD_DIM // 2
    freq = THETA ** (-(jnp.arange(half, dtype=jnp.float32) * 2.0 / HEAD_DIM))
    angle = jnp.arange(length, dtype=jnp.float32)[:, None] * freq[None, :]
    cosine = jnp.concatenate([jnp.cos(angle), jnp.cos(angle)], 1)[None, :, None, :]
    sine = jnp.concatenate([jnp.sin(angle), jnp.sin(angle)], 1)[None, :, None, :]
    return (cosine, sine)


def turn(values, cosine, sine):
    half = values.shape[-1] // 2
    turned = jnp.concatenate([-values[..., half:], values[..., :half]], -1)
    return values * cosine + turned * sine


def turn_back(grads, cosine, sine):
    half = grads.shape[-1] // 2
    moved = grads * sine
    return grads * cosine + jnp.concatenate([moved[..., half:], -moved[..., :half]], -1)


def masked_scores(query, keys):
    scores = jnp.einsum(
        "sqhd,skhd->shqk", query, keys, preferred_element_type=jnp.float32
    ) * HEAD_DIM ** (-0.5)
    length = query.shape[1]
    allowed = jnp.arange(length)[:, None] >= jnp.arange(length)[None, :]
    return jnp.where(allowed[None, None], scores, -jnp.inf)


def attend(query, keys, values):
    scores = masked_scores(query, keys)
    highest = jnp.max(scores, axis=-1, keepdims=True)
    expo = jnp.exp(scores - highest)
    total = jnp.sum(expo, axis=-1, keepdims=True)
    low_probs = (expo / total).astype(LOW)
    mixed = jnp.einsum(
        "shqk,skhd->sqhd", low_probs, values, preferred_element_type=jnp.float32
    ).astype(LOW)
    return mixed, highest + jnp.log(total)


def attend_back(query, keys, values, grad_mixed, logsum):
    scale = HEAD_DIM ** (-0.5)
    probs = jnp.exp(masked_scores(query, keys) - logsum)
    low_probs = probs.astype(LOW)
    dprobs = jnp.einsum("sqhd,skhd->shqk", grad_mixed, values, preferred_element_type=jnp.float32)
    grad_values = jnp.einsum(
        "shqk,sqhd->skhd", low_probs, grad_mixed, preferred_element_type=jnp.float32
    )
    low_scores = (probs * (dprobs - jnp.sum(probs * dprobs, axis=-1, keepdims=True))).astype(LOW)
    grad_query = (
        jnp.einsum("shqk,skhd->sqhd", low_scores, keys, preferred_element_type=jnp.float32) * scale
    )
    grad_keys = (
        jnp.einsum("shqk,sqhd->skhd", low_scores, query, preferred_element_type=jnp.float32) * scale
    )
    return grad_query, grad_keys, grad_values


def body(
    hidden_in, w_query, w_key, w_value, w_out, w_gate, w_up, w_down, norm_attn, norm_ffn, grad_out
):
    gain_attn = lax.all_gather(norm_attn, "row", axis=0, tiled=True)
    gain_ffn = lax.all_gather(norm_ffn, "row", axis=0, tiled=True)
    w_attn = gather_tall(w_query, w_key, w_value)
    w_proj = gather_wide(w_out)
    w_ffn = gather_tall(w_gate, w_up)
    w_back = gather_wide(w_down)

    inputs = to_group(hidden_in).astype(jnp.float32)
    grad_here = to_group(grad_out)
    scale_one = rms_scale(inputs)
    normed_one = group_gather((inputs * scale_one * gain_attn).astype(LOW))
    grad_wide = group_gather(grad_here)

    tokens = normed_one.shape[0]
    columns = w_attn.shape[1] // 3
    length = tokens // lax.axis_size("dp")
    shape = (tokens // length, length, columns // HEAD_DIM, HEAD_DIM)
    projected = dot(normed_one, w_attn)
    cosine, sine = rotation_tables(length)
    query = turn(projected[:, :columns].reshape(shape), cosine, sine).astype(LOW)
    keys = turn(projected[:, columns : 2 * columns].reshape(shape), cosine, sine).astype(LOW)
    values = projected[:, 2 * columns :].reshape(shape).astype(LOW)
    mixed, logsum = attend(query, keys, values)
    mixed = mixed.reshape(tokens, columns)
    middle = inputs + group_scatter(dot(mixed, w_proj))
    scale_two = rms_scale(middle)
    normed_two = group_gather((middle * scale_two * gain_ffn).astype(LOW))

    units = w_ffn.shape[1] // 2
    lifted = dot(normed_two, w_ffn)
    gate, upward = lifted[:, :units], lifted[:, units:]
    sigmoid_gate = jax.nn.sigmoid(gate)
    activated = (gate * sigmoid_gate * upward).astype(LOW)
    layer_out = from_group((middle + group_scatter(dot(activated, w_back))).astype(LOW))

    grad_activated = inner_cols(grad_wide, w_back)
    slope = sigmoid_gate * (1.0 + gate * (1.0 - sigmoid_gate))
    grad_lifted = jnp.concatenate(
        [grad_activated * upward * slope, grad_activated * gate * sigmoid_gate], 1
    ).astype(LOW)
    grad_normed_two = group_scatter(inner_cols(grad_lifted, w_ffn))
    grad_down = scatter_wide(inner_rows(activated, grad_wide))
    grad_gate, grad_up = scatter_tall(inner_rows(normed_two, grad_lifted), 2)
    gain_two = jnp.sum(grad_normed_two * middle * scale_two, axis=0)
    grad_middle = grad_here.astype(jnp.float32) + norm_back(
        middle, scale_two, grad_normed_two * gain_ffn
    )
    grad_branch = group_gather(grad_middle.astype(LOW))
    grad_mixed = inner_cols(grad_branch, w_proj).astype(LOW).reshape(shape)
    grad_attn_out = scatter_wide(inner_rows(mixed, grad_branch))
    grad_query, grad_keys, grad_values = attend_back(query, keys, values, grad_mixed, logsum)
    grad_projected = jnp.concatenate(
        [
            turn_back(grad_query, cosine, sine).reshape(tokens, columns),
            turn_back(grad_keys, cosine, sine).reshape(tokens, columns),
            grad_values.reshape(tokens, columns),
        ],
        1,
    ).astype(LOW)
    grad_normed_one = group_scatter(inner_cols(grad_projected, w_attn))
    grad_wq, grad_wk, grad_wv = scatter_tall(inner_rows(normed_one, grad_projected), 3)
    gain_one = jnp.sum(grad_normed_one * inputs * scale_one, axis=0)
    grad_in = from_group(
        (grad_middle + norm_back(inputs, scale_one, grad_normed_one * gain_attn)).astype(LOW)
    )
    gains = lax.psum(jnp.stack([gain_one, gain_two]), ("dp", "row", "col"))
    width = norm_attn.shape[0]
    gains = lax.dynamic_slice_in_dim(gains, lax.axis_index("row") * width, width, 1)
    return (
        layer_out,
        grad_in,
        grad_wq,
        grad_wk,
        grad_wv,
        grad_attn_out,
        grad_gate,
        grad_up,
        grad_down,
        gains[0],
        gains[1],
    )


def solution(mesh):
    tokens = P(("dp", "col"), "row")
    tall = P("row", "col")
    wide = P("col", "row")
    gain = P("row")
    return jax.shard_map(
        body,
        mesh=mesh,
        in_specs=(tokens, tall, tall, tall, wide, tall, tall, wide, gain, gain, tokens),
        out_specs=(tokens, tokens, tall, tall, tall, wide, tall, tall, wide, gain, gain),
        check_vma=False,
    )
```

```python
import functools

import jax
import jax.numpy as jnp
from jax import lax
from jax.experimental import pallas as pl
from jax.experimental.pallas import tpu as pltpu
from jax.sharding import PartitionSpec as P

HEAD_DIM = 64
EPSILON = 1e-05
THETA = 130000.0
GROUP = ("dp", "col")
LOW = jnp.bfloat16


def dot(left, right):
    return jnp.dot(left, right, preferred_element_type=jnp.float32)


def inner_rows(left, right):
    return lax.dot_general(
        left, right, (((0,), (0,)), ((), ())), preferred_element_type=jnp.float32
    )


def inner_cols(left, right):
    return lax.dot_general(
        left, right, (((1,), (1,)), ((), ())), preferred_element_type=jnp.float32
    )


def seat_pairs():
    rows, cols = lax.axis_size("row"), lax.axis_size("col")
    per = cols // rows
    return [
        (r * cols + c, (c // per) * cols + (c % per) * rows + r)
        for r in range(rows)
        for c in range(cols)
    ]


def to_group(block):
    whole = lax.all_to_all(block, "row", split_axis=0, concat_axis=1, tiled=True)
    return lax.ppermute(whole, ("row", "col"), seat_pairs())


def from_group(block):
    back = lax.ppermute(block, ("row", "col"), [(b, a) for a, b in seat_pairs()])
    return lax.all_to_all(back, "row", split_axis=1, concat_axis=0, tiled=True)


def group_gather(shard):
    return lax.all_gather(shard, GROUP, axis=0, tiled=True)


def group_scatter(partial):
    return lax.psum_scatter(
        partial.astype(LOW), GROUP, scatter_dimension=0, tiled=True
    ).astype(jnp.float32)


def my_part(block, axis):
    size = block.shape[axis] // lax.axis_size("dp")
    return lax.dynamic_slice_in_dim(block, lax.axis_index("dp") * size, size, axis)


def gather_tall(*blocks):
    mine = jnp.concatenate([my_part(b, 1) for b in blocks], 1)
    return lax.all_gather(mine, "row", axis=0, tiled=True)


def gather_wide(block):
    return lax.all_gather(my_part(block, 0), "row", axis=1, tiled=True)


def after(*values):
    return lax.optimization_barrier(values)


def dp_parts(mine):
    parts = lax.axis_size("dp")
    if parts != 2:
        return list(lax.all_gather(mine, "dp", axis=0))
    other = lax.ppermute(mine, "dp", [(0, 1), (1, 0)])
    lower = lax.axis_index("dp") == 0
    return [jnp.where(lower, mine, other), jnp.where(lower, other, mine)]


def row_sum(part, axis):
    return lax.psum_scatter(part, "row", scatter_dimension=axis, tiled=True)


def join_tall(mine, count):
    parts = dp_parts(mine)
    width = mine.shape[1] // count
    return [
        jnp.concatenate([p[:, i * width : (i + 1) * width] for p in parts], 1).astype(jnp.float32)
        for i in range(count)
    ]


def join_wide(mine):
    return jnp.concatenate(dp_parts(mine), 0).astype(jnp.float32)


def rms_scale(values):
    return lax.rsqrt(jnp.mean(values * values, axis=1, keepdims=True) + EPSILON)


def norm_back(values, scale, weighted):
    inner = jnp.mean(weighted * values, axis=1, keepdims=True)
    return scale * weighted - values * (scale * scale * scale * inner)


def rotation_tables(length):
    half = HEAD_DIM // 2
    freq = THETA ** (-(jnp.arange(half, dtype=jnp.float32) * 2.0 / HEAD_DIM))
    angle = jnp.arange(length, dtype=jnp.float32)[:, None] * freq[None, :]
    cosine = jnp.concatenate([jnp.cos(angle), jnp.cos(angle)], 1)[None, :, None, :]
    sine = jnp.concatenate([jnp.sin(angle), jnp.sin(angle)], 1)[None, :, None, :]
    return (cosine, sine)


def turn(values, cosine, sine):
    half = values.shape[-1] // 2
    turned = jnp.concatenate([-values[..., half:], values[..., :half]], -1)
    return values * cosine + turned * sine


def turn_back(grads, cosine, sine):
    half = grads.shape[-1] // 2
    moved = grads * sine
    return grads * cosine + jnp.concatenate([moved[..., half:], -moved[..., :half]], -1)


def masked_scores(query, keys):
    scores = jnp.einsum(
        "sqhd,skhd->shqk", query, keys, preferred_element_type=jnp.float32
    ) * HEAD_DIM ** (-0.5)
    length = query.shape[1]
    allowed = jnp.arange(length)[:, None] >= jnp.arange(length)[None, :]
    return jnp.where(allowed[None, None], scores, -jnp.inf)


def attend(query, keys, values):
    scores = masked_scores(query, keys)
    highest = jnp.max(scores, axis=-1, keepdims=True)
    expo = jnp.exp(scores - highest)
    total = jnp.sum(expo, axis=-1, keepdims=True)
    low_probs = (expo / total).astype(LOW)
    mixed = jnp.einsum(
        "shqk,skhd->sqhd", low_probs, values, preferred_element_type=jnp.float32
    ).astype(LOW)
    return mixed, highest + jnp.log(total)


def attend_back(query, keys, values, grad_mixed, logsum):
    scale = HEAD_DIM ** (-0.5)
    probs = jnp.exp(masked_scores(query, keys) - logsum)
    low_probs = probs.astype(LOW)
    dprobs = jnp.einsum("sqhd,skhd->shqk", grad_mixed, values, preferred_element_type=jnp.float32)
    grad_values = jnp.einsum(
        "shqk,sqhd->skhd", low_probs, grad_mixed, preferred_element_type=jnp.float32
    )
    low_scores = (probs * (dprobs - jnp.sum(probs * dprobs, axis=-1, keepdims=True))).astype(LOW)
    grad_query = (
        jnp.einsum("shqk,skhd->sqhd", low_scores, keys, preferred_element_type=jnp.float32) * scale
    )
    grad_keys = (
        jnp.einsum("shqk,sqhd->skhd", low_scores, query, preferred_element_type=jnp.float32) * scale
    )
    return grad_query, grad_keys, grad_values


MESH = pl.DeviceIdType.MESH
STEP = 16
VMEM_LIMIT = 56 * 1024 * 1024


class Wires:
    def __init__(self, send, recv):
        self.send, self.recv, self.used, self.sent = send, recv, 0, []

    def slots(self, count):
        first = self.used
        self.used += count
        return first

    def copy(self, source, target, slot, device, landing=None):
        return pltpu.make_async_remote_copy(
            src_ref=source,
            dst_ref=target,
            send_sem=self.send.at[slot],
            recv_sem=self.recv.at[slot if landing is None else landing],
            device_id=device,
            device_id_type=MESH,
        )

    def start(self, source, target, slot, device):
        copy = self.copy(source, target, slot, device)
        copy.start()
        self.sent.append(copy)
        return copy

    def finish(self):
        for copy in self.sent:
            copy.wait_send()


def here():
    x, r, c = lax.axis_index("dp"), lax.axis_index("row"), lax.axis_index("col")
    mate = (x, r, c + 1 - 2 * lax.rem(c, 2))
    beside = (1 - x, r, c)
    above = (x, r, lax.rem(c + 2, 4))
    return (x, r, c), mate, beside, above


def seat_of(x, r, c, rows, cols, piece):
    per = cols // rows
    return (x, lax.div(c, per), lax.rem(c, per) * rows + piece)


def home_of(x, r, c, rows, cols, source):
    per = cols // rows
    return (x, source, r * per + lax.div(c, rows))


def greet(devices, count):
    barrier = pltpu.get_barrier_semaphore()
    for device, remote in devices:
        if remote is None:
            pl.semaphore_signal(barrier, inc=1, device_id=device, device_id_type=MESH)
        else:

            @pl.when(remote)
            def _():
                pl.semaphore_signal(barrier, inc=1, device_id=device, device_id_type=MESH)

    pl.semaphore_wait(barrier, count)


def product_into(target, left, right, turned):
    width = target.shape[1]
    tile = min(512, width)

    @pl.loop(0, width // tile)
    def _(i):
        at = pl.ds(pl.multiple_of(i * tile, tile), tile)
        if turned:
            value = inner_cols(left[...], right[at, :])
        else:
            value = dot(left[...], right[:, at])
        target[:, at] = value.astype(LOW)


def plane_kernel(rows, cols, entry, leave, mid, n_small, n_out, spread, totals, turned, *refs):
    refs = list(refs)
    big = refs.pop(0)
    weights = refs.pop(0) if entry == "sum" else None
    small = [refs.pop(0) for _ in range(n_small)]
    main = refs.pop(0)
    outs = [refs.pop(0) for _ in range(n_out)]
    shard, send, recv, local = (refs.pop(0) for _ in range(4))
    if totals:
        total, inbox, line_inbox = (refs.pop() for _ in range(3))
    wires = Wires(send, recv)
    me, mate, beside, above = here()
    x, r, c = me
    count, width = shard.shape
    half = count // 2
    low_half, high_half = pl.ds(0, half), pl.ds(half, half)
    block = width // rows
    seats = [seat_of(x, r, c, rows, cols, p) for p in range(rows)]
    homes = [home_of(x, r, c, rows, cols, s) for s in range(rows)]

    def away(device):
        return jnp.logical_not(jnp.logical_and(device[1] == r, device[2] == c))

    greeted = []
    expected = 0
    stays = (lax.div(c, cols // rows) == r) & (lax.rem(c, cols // rows) * rows + lax.rem(c, rows) == c)
    kept = jnp.where(stays, 1, 0).astype(jnp.int32)
    if entry == "seats":
        greeted += [(h, away(h)) for h in homes]
        expected = expected + rows - kept
    if leave == "homes":
        greeted += [(s, away(s)) for s in seats]
        expected = expected + rows - kept
    if spread or totals:
        others = [(x, lax.rem(r + k, rows), c) for k in range(1, rows)]
        greeted += [(o, None) for o in others]
        expected = expected + rows - 1
    greeted += [(mate, None), (beside, None), (above, None)]
    if entry == "sum":
        fetch = pltpu.make_async_copy(weights, refs[1], local.at[8])
        fetch.start()
        for i, (tx, tc) in enumerate(
            (t, d)
            for t, u in ((1 - x, above[2]), (1 - x, c), (x, above[2]), (x, c))
            for d in (u + 1 - 2 * lax.rem(u, 2), u)
        ):
            pltpu.make_async_copy(big.at[tx * cols + tc], refs[0].at[i], local.at[i]).start()
    greet(greeted, expected + 3)

    if spread:
        gains, landing = small[0], refs.pop()
        first = wires.slots(rows - 1)
        for k, other in enumerate(others):
            wires.start(gains, landing.at[r], first + k, other)

    if entry == "seats":
        (seated,) = refs
        first = wires.slots(rows)
        mine = pl.ds(pl.multiple_of(r * block, block), block)
        for p, seat in enumerate(seats):
            piece = big.at[pl.ds(p * count, count)]
            there = wires.copy(piece, seated.at[:, mine], first + p, seat, first + r)
            stay = pltpu.make_async_copy(piece, seated.at[:, mine], local.at[0])
            pl.when(away(seat))(there.start)
            pl.when(jnp.logical_not(away(seat)))(stay.start)
        for s, home in enumerate(homes):
            part = seated.at[:, pl.ds(s * block, block)]
            arrived = wires.copy(part, part, first + s, home)
            stay = pltpu.make_async_copy(part, part, local.at[0])
            pl.when(away(home))(arrived.wait_recv)
            pl.when(jnp.logical_not(away(home)))(stay.wait)
        for p, seat in enumerate(seats):
            piece = big.at[pl.ds(p * count, count)]
            pl.when(away(seat))(wires.copy(piece, seated.at[:, mine], first + p, seat).wait_send)

        def value(at):
            return seated[at, :].astype(jnp.float32)

    else:
        factors, held_weights, given, own, mated, beside_pass, above_pass, beside_in, above_in = refs
        corner = (1 - x, r, above[2])
        targets = [corner, beside, above, me]
        first = wires.slots(4)
        handed = []
        order = []
        for tx, _, tc in targets:
            order += [tx * cols + tc + 1 - 2 * lax.rem(tc, 2), tx * cols + tc]
        loads = [
            pltpu.make_async_copy(big.at[spot], factors.at[i], local.at[i])
            for i, spot in enumerate(order)
        ]
        fetch.wait()

        def supply(k):
            loads[2 * k].wait()
            product_into(given.at[k], factors.at[2 * k], held_weights, turned)
            handed.append(wires.start(given.at[k], mated.at[k], first + k, mate))
            loads[2 * k + 1].wait()
            product_into(own.at[k], factors.at[2 * k + 1], held_weights, turned)

        def add(target, k, more, start, size):
            @pl.loop(0, size // STEP)
            def _(i):
                at = pl.ds(pl.multiple_of(start + i * STEP, STEP), STEP)
                target[k, at, :] = (
                    target[k, at, :].astype(jnp.float32) + more(at).astype(jnp.float32)
                ).astype(LOW)

        def merge(k):
            handed[k].wait_recv()
            add(own, k, lambda at: mated[k, at, :], 0, count)

        supply(0)
        supply(1)
        merge(0)
        slot = wires.slots(6)
        pass_beside = wires.start(own.at[0, low_half], beside_pass, slot, beside)
        pass_above = wires.start(own.at[0, high_half], above_pass, slot + 1, above)
        supply(2)
        merge(1)
        beside_low = wires.start(own.at[1, low_half], beside_in.at[low_half], slot + 2, beside)
        supply(3)
        merge(2)
        above_high = wires.start(own.at[2, high_half], above_in.at[high_half], slot + 3, above)
        pass_beside.wait_recv()
        add(own, 2, lambda at: beside_pass[at, :], 0, half)
        above_low = wires.start(own.at[2, low_half], above_in.at[low_half], slot + 4, above)
        pass_above.wait_recv()

        @pl.loop(0, half // STEP)
        def _(i):
            at = pl.ds(pl.multiple_of(half + i * STEP, STEP), STEP)
            to = pl.ds(pl.multiple_of(i * STEP, STEP), STEP)
            own[1, at, :] = (
                own[1, at, :].astype(jnp.float32) + above_pass[to, :].astype(jnp.float32)
            ).astype(LOW)

        beside_high = wires.start(own.at[1, high_half], beside_in.at[high_half], slot + 5, beside)
        handed[3].wait_recv()
        beside_low.wait_recv()
        above_high.wait_recv()
        above_low.wait_recv()
        beside_high.wait_recv()

        def value(at):
            near = own[3, at, :].astype(jnp.float32) + mated[3, at, :].astype(jnp.float32)
            return near + (beside_in[at, :].astype(jnp.float32) + above_in[at, :].astype(jnp.float32))

    if spread:
        for k in range(rows - 1):
            wires.sent[k].wait_recv()
        landing[r] = gains[...]
        for s in range(rows):
            outs[0][:, s * block : (s + 1) * block] = landing[s]

    mid.start(outs)

    @pl.loop(0, count // STEP)
    def _(i):
        at = pl.ds(pl.multiple_of(i * STEP, STEP), STEP)
        shard[at, :] = mid.rows(at, value(at), small, outs).astype(LOW)

    if leave == "gather":
        spot = x * cols + c
        keep = pltpu.make_async_copy(shard, main.at[spot], local.at[0])
        keep.start()
        beside_spot, above_spot = beside[0] * cols + c, x * cols + above[2]
        corner_spot = beside[0] * cols + above[2]
        slot = wires.slots(10)
        to_mate = [wires.start(shard, main.at[spot], slot, mate)]
        beside_low = wires.start(shard.at[low_half], main.at[spot, low_half], slot + 1, beside)
        above_high = wires.start(shard.at[high_half], main.at[spot, high_half], slot + 2, above)
        beside_high = wires.start(shard.at[high_half], main.at[spot, high_half], slot + 3, beside)
        above_low = wires.start(shard.at[low_half], main.at[spot, low_half], slot + 4, above)

        beside_low.wait_recv()
        part = main.at[beside_spot, low_half]
        corner_low = wires.start(part, part, slot + 5, above)
        above_high.wait_recv()
        part = main.at[above_spot, high_half]
        corner_high = wires.start(part, part, slot + 6, beside)
        beside_high.wait_recv()
        to_mate.append(wires.start(main.at[beside_spot], main.at[beside_spot], slot + 7, mate))
        above_low.wait_recv()
        to_mate.append(wires.start(main.at[above_spot], main.at[above_spot], slot + 8, mate))
        corner_low.wait_recv()
        corner_high.wait_recv()
        to_mate.append(wires.start(main.at[corner_spot], main.at[corner_spot], slot + 9, mate))
        for copy in to_mate:
            copy.wait_recv()
        keep.wait()
    else:
        first = wires.slots(rows)
        place = lax.rem(c, rows)
        mine = pl.ds(pl.multiple_of(place * count, count), count)
        for s, home in enumerate(homes):
            part = shard.at[:, pl.ds(s * block, block)]
            there = wires.copy(part, main.at[mine], first + s, home, first + place)
            stay = pltpu.make_async_copy(part, main.at[mine], local.at[0])
            pl.when(away(home))(there.start)
            pl.when(jnp.logical_not(away(home)))(stay.start)
        if totals:
            gain_sums(wires, me, (mate, beside, above), others, rows, small[-1], outs, total, inbox, line_inbox)
        for p, seat in enumerate(seats):
            part = main.at[pl.ds(p * count, count)]
            pl.when(away(seat))(wires.copy(part, part, first + p, seat).wait_recv)
            pl.when(jnp.logical_not(away(seat)))(pltpu.make_async_copy(part, part, local.at[0]).wait)
        for s, home in enumerate(homes):
            part = shard.at[:, pl.ds(s * block, block)]
            pl.when(away(home))(wires.copy(part, main.at[mine], first + s, home).wait_send)
    wires.finish()


def gain_sums(wires, me, partners, others, rows, gain_two, outs, total, inbox, line_inbox):
    x, r, c = me
    block = total.shape[1] // rows
    total[0:1, :] = jnp.sum(outs[1][...], axis=0, keepdims=True)
    total[1:2, :] = jnp.sum(gain_two[...], axis=0, keepdims=True)
    total[2:, :] = jnp.zeros_like(total[2:, :])
    first = wires.slots(len(partners))
    for k, partner in enumerate(partners):
        copy = wires.copy(total, inbox.at[k], first + k, partner)
        copy.start()
        copy.wait()
        total[...] += inbox[k]
    first = wires.slots(len(others))
    copies = []
    for k, (_, row, _) in enumerate(others):
        part = total.at[:, pl.ds(pl.multiple_of(row * block, block), block)]
        copies.append(wires.start(part, line_inbox.at[r], first + k, others[k]))
    line_inbox[r] = total[:, pl.ds(pl.multiple_of(r * block, block), block)]
    for copy in copies:
        copy.wait_recv()
    outs[0][...] = sum(line_inbox[k] for k in range(rows))


def plane_call(
    entry, leave, mid, big, small, outs, collective_id, weights=None, turned=False, spread=False, totals=False
):
    rows, cols, parts = lax.axis_size("row"), lax.axis_size("col"), lax.axis_size("dp")
    if entry == "seats":
        count, width = big.shape[0] // rows, big.shape[1] * rows
    else:
        count, width = big.shape[0] // (parts * cols), weights.shape[0 if turned else 1]
        big = big.reshape(parts * cols, count, big.shape[1])
    gathered = leave == "gather"
    shape = (parts * cols, count, width) if gathered else (rows * count, width // rows)
    vmem = pl.BlockSpec(memory_space=pltpu.VMEM)
    tile = pltpu.VMEM((count, width), LOW)
    scratch = [tile, pltpu.SemaphoreType.DMA((32,)), pltpu.SemaphoreType.DMA((32,)), pltpu.SemaphoreType.DMA((9,))]
    if entry == "seats":
        scratch += [tile]
    else:
        whole, part = pltpu.VMEM((4, count, width), LOW), pltpu.VMEM((count // 2, width), LOW)
        scratch += [pltpu.VMEM(big.shape, LOW), pltpu.VMEM(weights.shape, LOW)]
        scratch += [whole, whole, whole, part, part, tile, tile]
    if spread:
        scratch += [pltpu.VMEM((rows,) + small[0].shape, jnp.float32)]
    if totals:
        scratch += [
            pltpu.VMEM((rows, 8, width // rows), jnp.float32),
            pltpu.VMEM((3, 8, width), jnp.float32),
            pltpu.VMEM((8, width), jnp.float32),
        ]
    operands = [big] if weights is None else [big, weights]
    main, *small_outs = pl.pallas_call(
        functools.partial(
            plane_kernel, rows, cols, entry, leave, mid, len(small), len(outs), spread, totals, turned
        ),
        out_shape=[jax.ShapeDtypeStruct(shape, LOW)] + list(outs),
        in_specs=[pl.BlockSpec(memory_space=pl.ANY)] * len(operands) + [vmem] * len(small),
        out_specs=[pl.BlockSpec(memory_space=pl.ANY)] + [vmem] * len(outs),
        scratch_shapes=scratch,
        compiler_params=pltpu.CompilerParams(
            collective_id=collective_id, has_side_effects=True, vmem_limit_bytes=VMEM_LIMIT
        ),
        cost_estimate=pl.CostEstimate(flops=0, bytes_accessed=20_000_000, transcendentals=0),
    )(*operands, *small)
    if gathered:
        main = main.reshape(parts * cols * count, width)
    return [main, *small_outs]


def fold(values):
    return values.reshape(values.shape[0] // 8, 8, values.shape[1]).sum(0)


class Mid:
    @staticmethod
    def start(outs):
        pass


class FirstNorm(Mid):
    @staticmethod
    def rows(at, value, small, outs):
        outs[1][at, :] = value.astype(LOW)
        return value * rms_scale(value) * outs[0][0:1, :]


class Pass(Mid):
    @staticmethod
    def rows(at, value, small, outs):
        outs[0][at, :] = value.astype(LOW)
        return value


class SecondNorm(Mid):
    @staticmethod
    def rows(at, value, small, outs):
        held, gains = small
        middle = held[at, :].astype(jnp.float32) + value
        outs[0][at, :] = middle
        return middle * rms_scale(middle) * gains[1:2, :]


class Add(Mid):
    @staticmethod
    def rows(at, value, small, outs):
        return small[0][at, :] + value


class BackSecond(Mid):
    @staticmethod
    def start(outs):
        outs[1][...] = jnp.zeros_like(outs[1])

    @staticmethod
    def rows(at, value, small, outs):
        middle, grad_out, gains = small
        middle = middle[at, :]
        scale = rms_scale(middle)
        outs[1][...] += fold(value * middle * scale)
        grad = grad_out[at, :].astype(jnp.float32) + norm_back(
            middle, scale, value * gains[1:2, :]
        )
        outs[0][at, :] = grad
        return grad


class BackFirst(Mid):
    @staticmethod
    def start(outs):
        outs[1][...] = jnp.zeros_like(outs[1])

    @staticmethod
    def rows(at, value, small, outs):
        held, grad_middle, gains = small[:3]
        inputs = held[at, :].astype(jnp.float32)
        scale = rms_scale(inputs)
        outs[1][...] += fold(value * inputs * scale)
        return grad_middle[at, :] + norm_back(inputs, scale, value * gains[0:1, :])


def plain_call(
    entry, leave, mid, big, small, outs, collective_id, weights=None, turned=False, spread=False, totals=False
):
    refs = [Holder(a) for a in small]
    given = [Holder(jnp.zeros(o.shape, o.dtype)) for o in outs]
    if spread:
        given[0].value = lax.all_gather(small[0], "row", axis=1, tiled=True)
    if entry == "seats":
        value = to_group(big).astype(jnp.float32)
    else:
        value = group_scatter((inner_cols if turned else dot)(big, weights))
    mid.start(given)
    shard = mid.rows(slice(None), value, refs, given).astype(LOW)
    main = group_gather(shard) if leave == "gather" else from_group(shard)
    if totals:
        sums = jnp.stack([given[1].value.sum(0), small[-1].sum(0)])
        sums = jnp.pad(lax.psum(sums, ("dp", "row", "col")), ((0, 6), (0, 0)))
        part = outs[0].shape[1]
        given[0].value = lax.dynamic_slice_in_dim(sums, lax.axis_index("row") * part, part, 1)
    return [main] + [g.value for g in given]


class Holder:
    def __init__(self, value):
        self.value, self.dtype, self.shape = value, value.dtype, value.shape

    def __getitem__(self, at):
        return self.value[at]

    def __setitem__(self, at, value):
        self.value = self.value.at[at].set(value)


def swap_halves(values, first):
    lanes = values.shape[1]
    half = HEAD_DIM // 2
    return jnp.where(first, pltpu.roll(values, lanes - half, 1), pltpu.roll(values, half, 1))


def attend_kernel(query, key, value, cosine, sine, mixed, q_out, k_out, v_out, logsum):
    length, lanes = query.shape
    block = min(256, length)
    lane = lax.broadcasted_iota(jnp.int32, (length, lanes), 1)
    first = lax.rem(lane, HEAD_DIM) < HEAD_DIM // 2
    cos, sin = cosine[...], sine[...]

    def rotate(values):
        return (values * cos + swap_halves(values, first) * sin).astype(LOW)

    q_out[...] = rotate(query[...])
    k_out[...] = rotate(key[...])
    low_values = value[...].astype(LOW)
    v_out[...] = low_values
    v_turned = low_values.astype(jnp.float32).T.astype(LOW)
    head = lax.broadcasted_iota(jnp.int32, (block, lanes), 1) // HEAD_DIM
    keep = lax.broadcasted_iota(jnp.int32, (block, block), 0) <= lax.broadcasted_iota(
        jnp.int32, (block, block), 1
    )
    for j in range(length // block):
        at = slice(j * block, (j + 1) * block)
        q_block = q_out[at, :].astype(jnp.float32) * HEAD_DIM ** (-0.5)
        parts = []
        for h in range(lanes // HEAD_DIM):
            q_head = jnp.where(head == h, q_block, 0.0).astype(LOW)
            near = jnp.where(keep, inner_cols(k_out[at, :], q_head), -jnp.inf)
            highest = jnp.max(near, axis=0, keepdims=True)
            if j:
                far = inner_cols(k_out[: j * block, :], q_head)
                highest = jnp.maximum(highest, jnp.max(far, axis=0, keepdims=True))
                far = jnp.exp(far - highest)
            near = jnp.exp(near - highest)
            total = jnp.sum(near, axis=0, keepdims=True)
            if j:
                total = total + jnp.sum(far, axis=0, keepdims=True)
            logsum[0, 0, h : h + 1, at] = highest + jnp.log(total)
            share = 1.0 / total
            out = dot(v_turned[:, at], (near * share).astype(LOW))
            if j:
                out = out + dot(v_turned[:, : j * block], (far * share).astype(LOW))
            parts.append(out[h * HEAD_DIM : (h + 1) * HEAD_DIM])
        mixed[at, :] = jnp.concatenate(parts, 0).T.astype(LOW)


def attend_back_kernel(
    query, key, value, grad, logsum, cosine, sine, q_out, k_out, v_out, k_sum, v_sum
):
    length, lanes = query.shape
    block = min(256, length)
    k_sum[...] = jnp.zeros_like(k_sum)
    v_sum[...] = jnp.zeros_like(v_sum)
    k_turned = key[...].astype(jnp.float32).T.astype(LOW)
    head = lax.broadcasted_iota(jnp.int32, (block, lanes), 1) // HEAD_DIM
    keep = lax.broadcasted_iota(jnp.int32, (block, block), 0) <= lax.broadcasted_iota(
        jnp.int32, (block, block), 1
    )
    scale = HEAD_DIM ** (-0.5)

    def rotate_back(values, at):
        rows = values.shape[0]
        lane = lax.broadcasted_iota(jnp.int32, (rows, lanes), 1)
        first = lax.rem(lane, HEAD_DIM) < HEAD_DIM // 2
        return (values * cosine[at, :] - swap_halves(values, first) * sine[at, :]).astype(LOW)

    for j in range(length // block):
        at = slice(j * block, (j + 1) * block)
        before = slice(0, j * block)
        q_block = query[at, :].astype(jnp.float32) * scale
        g_block = grad[at, :].astype(jnp.float32)
        parts = []
        for h in range(lanes // HEAD_DIM):
            q_head = jnp.where(head == h, q_block, 0.0).astype(LOW)
            g_head = jnp.where(head == h, g_block, 0.0).astype(LOW)
            level = logsum[0, 0, h : h + 1, at]
            near = jnp.exp(jnp.where(keep, inner_cols(key[at, :], q_head), -jnp.inf) - level)
            d_near = inner_cols(value[at, :], g_head)
            inner = jnp.sum(near * d_near, axis=0, keepdims=True)
            if j:
                far = jnp.exp(inner_cols(key[before, :], q_head) - level)
                d_far = inner_cols(value[before, :], g_head)
                inner = inner + jnp.sum(far * d_far, axis=0, keepdims=True)
                v_sum[before, :] += dot(far.astype(LOW), g_head)
                s_far = (far * (d_far - inner)).astype(LOW)
                k_sum[before, :] += dot(s_far, q_head)
            v_sum[at, :] += dot(near.astype(LOW), g_head)
            s_near = (near * (d_near - inner)).astype(LOW)
            k_sum[at, :] += dot(s_near, q_head)
            out = dot(k_turned[:, at], s_near)
            if j:
                out = out + dot(k_turned[:, before], s_far)
            parts.append(out[h * HEAD_DIM : (h + 1) * HEAD_DIM])
        q_out[at, :] = rotate_back(jnp.concatenate(parts, 0).T * scale, at)
    k_out[...] = rotate_back(k_sum[...], slice(None))
    v_out[...] = v_sum[...].astype(LOW)


def pair_tables(length):
    half = HEAD_DIM // 2
    freq = THETA ** (-(jnp.arange(half, dtype=jnp.float32) * 2.0 / HEAD_DIM))
    angle = jnp.arange(length, dtype=jnp.float32)[:, None] * freq[None, :]
    cosine, sine = jnp.cos(angle), jnp.sin(angle)
    return jnp.tile(cosine, (1, 4)), jnp.tile(jnp.concatenate([-sine, sine], 1), (1, 2))


def attend_pairs(projected, sequences):
    tokens, columns = projected.shape[0], projected.shape[1] // 3
    length, lanes = tokens // sequences, 2 * HEAD_DIM
    pairs = columns // lanes
    cosine, sine = pair_tables(length)

    def spec(offset):
        return pl.BlockSpec((length, lanes), lambda s, h: (s, offset + h))

    table = pl.BlockSpec((length, lanes), lambda s, h: (0, 0))
    level = pl.BlockSpec((1, 1, 2, length), lambda s, h: (s, h, 0, 0))
    shape = jax.ShapeDtypeStruct((tokens, columns), LOW)
    return pl.pallas_call(
        attend_kernel,
        grid=(sequences, pairs),
        in_specs=[spec(0), spec(pairs), spec(2 * pairs), table, table],
        out_specs=[spec(0)] * 4 + [level],
        out_shape=[shape] * 4 + [jax.ShapeDtypeStruct((sequences, pairs, 2, length), jnp.float32)],
        compiler_params=pltpu.CompilerParams(vmem_limit_bytes=VMEM_LIMIT),
        cost_estimate=pl.CostEstimate(
            flops=8 * tokens * length * columns, bytes_accessed=100_000_000, transcendentals=0
        ),
    )(projected, projected, projected, cosine, sine)


def attend_pairs_back(query, keys, values, grad_mixed, logsum, sequences):
    tokens, columns = query.shape
    length, lanes = tokens // sequences, 2 * HEAD_DIM
    pairs = columns // lanes
    cosine, sine = pair_tables(length)
    spec = pl.BlockSpec((length, lanes), lambda s, h: (s, h))
    table = pl.BlockSpec((length, lanes), lambda s, h: (0, 0))
    level = pl.BlockSpec((1, 1, 2, length), lambda s, h: (s, h, 0, 0))
    shape = jax.ShapeDtypeStruct((tokens, columns), LOW)
    return pl.pallas_call(
        attend_back_kernel,
        grid=(sequences, pairs),
        in_specs=[spec] * 4 + [level, table, table],
        out_specs=[spec] * 3,
        out_shape=[shape] * 3,
        scratch_shapes=[pltpu.VMEM((length, lanes), jnp.float32)] * 2,
        compiler_params=pltpu.CompilerParams(vmem_limit_bytes=VMEM_LIMIT),
        cost_estimate=pl.CostEstimate(
            flops=20 * tokens * length * columns, bytes_accessed=160_000_000, transcendentals=0
        ),
    )(query, keys, values, grad_mixed, logsum, cosine, sine)


def attend_plain(projected, sequences):
    tokens, columns = projected.shape[0], projected.shape[1] // 3
    length = tokens // sequences
    shape = (sequences, length, columns // HEAD_DIM, HEAD_DIM)
    cosine, sine = rotation_tables(length)
    query = turn(projected[:, :columns].reshape(shape), cosine, sine).astype(LOW)
    keys = turn(projected[:, columns : 2 * columns].reshape(shape), cosine, sine).astype(LOW)
    values = projected[:, 2 * columns :].reshape(shape).astype(LOW)
    mixed, logsum = attend(query, keys, values)
    flat = (tokens, columns)
    return mixed.reshape(flat), query.reshape(flat), keys.reshape(flat), values.reshape(flat), logsum


def attend_plain_back(query, keys, values, grad_mixed, logsum, sequences):
    tokens, columns = query.shape
    length = tokens // sequences
    shape = (sequences, length, columns // HEAD_DIM, HEAD_DIM)
    cosine, sine = rotation_tables(length)
    grad_query, grad_keys, grad_values = attend_back(
        *(a.reshape(shape) for a in (query, keys, values, grad_mixed)), logsum
    )
    return [
        g.reshape(tokens, columns).astype(LOW)
        for g in (turn_back(grad_query, cosine, sine), turn_back(grad_keys, cosine, sine), grad_values)
    ]


def body(
    hidden_in, w_query, w_key, w_value, w_out, w_gate, w_up, w_down, norm_attn, norm_ffn, grad_out
):
    rows, cols, parts = lax.axis_size("row"), lax.axis_size("col"), lax.axis_size("dp")
    plane = plane_call if (cols, parts) == (4, 2) and cols % rows == 0 else plain_call
    count, width = hidden_in.shape[0] // rows, hidden_in.shape[1] * rows
    low_rows = jax.ShapeDtypeStruct((count, width), LOW)
    full_rows = jax.ShapeDtypeStruct((count, width), jnp.float32)
    gain_rows = jax.ShapeDtypeStruct((8, width), jnp.float32)

    w_attn = gather_tall(w_query, w_key, w_value)
    w_proj = gather_wide(w_out)
    w_ffn = gather_tall(w_gate, w_up)
    w_back = gather_wide(w_down)

    local_gains = jnp.pad(jnp.stack([norm_attn, norm_ffn]), ((0, 6), (0, 0)))
    normed_one, gains, held = plane(
        "seats", "gather", FirstNorm, hidden_in, [local_gains], [gain_rows, low_rows], 1, spread=True
    )
    projected = dot(normed_one, w_attn)
    columns = w_attn.shape[1] // 3
    paired = columns % (2 * HEAD_DIM) == 0
    mixed, query, keys, values, logsum = (attend_pairs if paired else attend_plain)(projected, parts)
    normed_two, middle = plane(
        "sum", "gather", SecondNorm, mixed, [held, gains], [full_rows], 2, w_proj
    )
    grad_out, middle = after(grad_out, middle)
    grad_wide, grad_here = plane("seats", "gather", Pass, grad_out, [], [low_rows], 3)

    units = w_ffn.shape[1] // 2
    lifted = dot(normed_two, w_ffn)
    gate, upward = lifted[:, :units], lifted[:, units:]
    sigmoid_gate = jax.nn.sigmoid(gate)
    activated = (gate * sigmoid_gate * upward).astype(LOW)

    part_down, w_back = after(inner_rows(activated, grad_wide).astype(LOW), w_back)
    grad_activated = inner_cols(grad_wide, w_back)
    slope = sigmoid_gate * (1.0 + gate * (1.0 - sigmoid_gate))
    grad_lifted = jnp.concatenate(
        [grad_activated * upward * slope, grad_activated * gate * sigmoid_gate], 1
    ).astype(LOW)
    part_ffn, grad_lifted = after(inner_rows(normed_two, grad_lifted).astype(LOW), grad_lifted)
    mine_down, part_ffn, grad_lifted = after(row_sum(part_down, 1), part_ffn, grad_lifted)
    mine_ffn = row_sum(part_ffn, 0)
    grad_branch, grad_middle, gain_two = plane(
        "sum",
        "gather",
        BackSecond,
        grad_lifted,
        [middle, grad_here, gains],
        [full_rows, gain_rows],
        4,
        w_ffn,
        True,
    )
    grad_mixed = inner_cols(grad_branch, w_proj).astype(LOW)
    part_out, grad_mixed = after(inner_rows(mixed, grad_branch).astype(LOW), grad_mixed)
    grad_projected = jnp.concatenate(
        (attend_pairs_back if paired else attend_plain_back)(
            query, keys, values, grad_mixed, logsum, parts
        ),
        1,
    )
    part_attn, grad_projected = after(
        inner_rows(normed_one, grad_projected).astype(LOW), grad_projected
    )
    grad_projected, activated = after(grad_projected, activated)
    grad_in, gain_grads, _ = plane(
        "sum",
        "homes",
        BackFirst,
        grad_projected,
        [held, grad_middle, gains, gain_two],
        [jax.ShapeDtypeStruct((8, norm_attn.shape[0]), jnp.float32), gain_rows],
        6,
        w_attn,
        True,
        totals=True,
    )
    mine_ffn, part_out, activated, grad_in = after(mine_ffn, part_out, activated, grad_in)
    mine_out = row_sum(part_out, 1)
    mine_out, part_attn = after(mine_out, part_attn)
    mine_attn = row_sum(part_attn, 0)
    (layer_out,) = plane("sum", "homes", Add, activated, [middle], [], 5, w_back)
    grad_down, grad_attn_out = join_wide(mine_down), join_wide(mine_out)
    grad_gate, grad_up = join_tall(mine_ffn, 2)
    grad_wq, grad_wk, grad_wv = join_tall(mine_attn, 3)
    return (
        layer_out,
        grad_in,
        grad_wq,
        grad_wk,
        grad_wv,
        grad_attn_out,
        grad_gate,
        grad_up,
        grad_down,
        gain_grads[0],
        gain_grads[1],
    )


def solution(mesh):
    tokens = P(("dp", "col"), "row")
    tall = P("row", "col")
    wide = P("col", "row")
    gain = P("row")
    return jax.shard_map(
        body,
        mesh=mesh,
        in_specs=(tokens, tall, tall, tall, wide, tall, tall, wide, gain, gain, tokens),
        out_specs=(tokens, tokens, tall, tall, tall, wide, tall, tall, wide, gain, gain),
        check_vma=False,
    )
```

```python
import functools

import jax
import jax.numpy as jnp
from jax import lax
from jax.experimental import pallas as pl
from jax.experimental.pallas import tpu as pltpu
from jax.sharding import PartitionSpec as P

HEAD_DIM = 64
EPSILON = 1e-05
THETA = 130000.0
GROUP = ("dp", "col")
LOW = jnp.bfloat16


def dot(left, right):
    return jnp.dot(left, right, preferred_element_type=jnp.float32)


def inner_rows(left, right):
    return lax.dot_general(
        left, right, (((0,), (0,)), ((), ())), preferred_element_type=jnp.float32
    )


def inner_cols(left, right):
    return lax.dot_general(
        left, right, (((1,), (1,)), ((), ())), preferred_element_type=jnp.float32
    )


def seat_pairs():
    rows, cols = lax.axis_size("row"), lax.axis_size("col")
    per = cols // rows
    return [
        (r * cols + c, (c // per) * cols + (c % per) * rows + r)
        for r in range(rows)
        for c in range(cols)
    ]


def to_group(block):
    whole = lax.all_to_all(block, "row", split_axis=0, concat_axis=1, tiled=True)
    return lax.ppermute(whole, ("row", "col"), seat_pairs())


def from_group(block):
    back = lax.ppermute(block, ("row", "col"), [(b, a) for a, b in seat_pairs()])
    return lax.all_to_all(back, "row", split_axis=1, concat_axis=0, tiled=True)


def group_gather(shard):
    return lax.all_gather(shard, GROUP, axis=0, tiled=True)


def group_scatter(partial):
    return lax.psum_scatter(
        partial.astype(LOW), GROUP, scatter_dimension=0, tiled=True
    ).astype(jnp.float32)


def my_part(block, axis):
    size = block.shape[axis] // lax.axis_size("dp")
    return lax.dynamic_slice_in_dim(block, lax.axis_index("dp") * size, size, axis)


def halves(block):
    middle = block.shape[1] // 2
    return [block[:, :middle], block[:, middle:]]


def pair_units(gate, upward):
    (g, h), (u, v) = halves(gate), halves(upward)
    return jnp.concatenate([g, u, h, v], 1)


def stack(block):
    units = block.shape[0]
    return jnp.concatenate([block[:, i : i + units] for i in range(0, block.shape[1], units)], 0)


def unstack(blocks, units):
    return jnp.concatenate([blocks[i : i + units] for i in range(0, blocks.shape[0], units)], 1)


def after(*values):
    return lax.optimization_barrier(values)


def dp_other(mine):
    if lax.axis_size("dp") == 2:
        return lax.ppermute(mine, "dp", [(0, 1), (1, 0)])
    return lax.all_gather(mine, "dp", axis=0)


def dp_parts(mine, other):
    if lax.axis_size("dp") != 2:
        return list(other)
    lower = lax.axis_index("dp") == 0
    return [jnp.where(lower, mine, other), jnp.where(lower, other, mine)]


def row_sum(part, axis):
    return lax.psum_scatter(part, "row", scatter_dimension=axis, tiled=True)


def join_tall(mine, other, pieces):
    parts = dp_parts(mine, other)
    width = mine.shape[1] // sum(map(len, pieces))
    return [
        jnp.concatenate(
            [p[:, i * width : (i + 1) * width] for p in parts for i in piece], 1
        ).astype(jnp.float32)
        for piece in pieces
    ]


def join_wide(mine, other):
    return jnp.concatenate(dp_parts(mine, other), 0).astype(jnp.float32)


def rms_scale(values):
    return lax.rsqrt(jnp.mean(values * values, axis=1, keepdims=True) + EPSILON)


def norm_back(values, scale, weighted):
    inner = jnp.mean(weighted * values, axis=1, keepdims=True)
    return scale * weighted - values * (scale * scale * scale * inner)


def rotation_tables(length):
    half = HEAD_DIM // 2
    freq = THETA ** (-(jnp.arange(half, dtype=jnp.float32) * 2.0 / HEAD_DIM))
    angle = jnp.arange(length, dtype=jnp.float32)[:, None] * freq[None, :]
    cosine = jnp.concatenate([jnp.cos(angle), jnp.cos(angle)], 1)[None, :, None, :]
    sine = jnp.concatenate([jnp.sin(angle), jnp.sin(angle)], 1)[None, :, None, :]
    return (cosine, sine)


def turn(values, cosine, sine):
    half = values.shape[-1] // 2
    turned = jnp.concatenate([-values[..., half:], values[..., :half]], -1)
    return values * cosine + turned * sine


def turn_back(grads, cosine, sine):
    half = grads.shape[-1] // 2
    moved = grads * sine
    return grads * cosine + jnp.concatenate([moved[..., half:], -moved[..., :half]], -1)


def masked_scores(query, keys):
    scores = jnp.einsum(
        "sqhd,skhd->shqk", query, keys, preferred_element_type=jnp.float32
    ) * HEAD_DIM ** (-0.5)
    length = query.shape[1]
    allowed = jnp.arange(length)[:, None] >= jnp.arange(length)[None, :]
    return jnp.where(allowed[None, None], scores, -jnp.inf)


def attend(query, keys, values):
    scores = masked_scores(query, keys)
    highest = jnp.max(scores, axis=-1, keepdims=True)
    expo = jnp.exp(scores - highest)
    total = jnp.sum(expo, axis=-1, keepdims=True)
    low_probs = (expo / total).astype(LOW)
    mixed = jnp.einsum(
        "shqk,skhd->sqhd", low_probs, values, preferred_element_type=jnp.float32
    ).astype(LOW)
    return mixed, highest + jnp.log(total)


def attend_back(query, keys, values, grad_mixed, logsum):
    scale = HEAD_DIM ** (-0.5)
    probs = jnp.exp(masked_scores(query, keys) - logsum)
    low_probs = probs.astype(LOW)
    dprobs = jnp.einsum("sqhd,skhd->shqk", grad_mixed, values, preferred_element_type=jnp.float32)
    grad_values = jnp.einsum(
        "shqk,sqhd->skhd", low_probs, grad_mixed, preferred_element_type=jnp.float32
    )
    low_scores = (probs * (dprobs - jnp.sum(probs * dprobs, axis=-1, keepdims=True))).astype(LOW)
    grad_query = (
        jnp.einsum("shqk,skhd->sqhd", low_scores, keys, preferred_element_type=jnp.float32) * scale
    )
    grad_keys = (
        jnp.einsum("shqk,sqhd->skhd", low_scores, query, preferred_element_type=jnp.float32) * scale
    )
    return grad_query, grad_keys, grad_values


MESH = pl.DeviceIdType.MESH
STEP = 16
VMEM_LIMIT = 56 * 1024 * 1024


class Wires:
    def __init__(self, send, recv):
        self.send, self.recv, self.used, self.sent = send, recv, 0, []

    def slots(self, count):
        first = self.used
        self.used += count
        return first

    def copy(self, source, target, slot, device, landing=None):
        return pltpu.make_async_remote_copy(
            src_ref=source,
            dst_ref=target,
            send_sem=self.send.at[slot],
            recv_sem=self.recv.at[slot if landing is None else landing],
            device_id=device,
            device_id_type=MESH,
        )

    def start(self, source, target, slot, device):
        copy = self.copy(source, target, slot, device)
        copy.start()
        self.sent.append(copy)
        return copy

    def finish(self):
        for copy in self.sent:
            copy.wait_send()


def here():
    x, r, c = lax.axis_index("dp"), lax.axis_index("row"), lax.axis_index("col")
    mate = (x, r, c + 1 - 2 * lax.rem(c, 2))
    beside = (1 - x, r, c)
    above = (x, r, lax.rem(c + 2, 4))
    return (x, r, c), mate, beside, above


def seat_of(x, r, c, rows, cols, piece):
    per = cols // rows
    return (x, lax.div(c, per), lax.rem(c, per) * rows + piece)


def home_of(x, r, c, rows, cols, source):
    per = cols // rows
    return (x, source, r * per + lax.div(c, rows))


def greet(devices, count):
    barrier = pltpu.get_barrier_semaphore()
    for device, remote in devices:
        if remote is None:
            pl.semaphore_signal(barrier, inc=1, device_id=device, device_id_type=MESH)
        else:

            @pl.when(remote)
            def _():
                pl.semaphore_signal(barrier, inc=1, device_id=device, device_id_type=MESH)

    pl.semaphore_wait(barrier, count)


COLUMNS = 1024


def weight_block(source, held, i, form, depth, size):
    if form == "turned":
        at = pl.ds(pl.multiple_of(i * size, size), size)
        return source.at[at, :depth], held.at[at, :]
    return (
        source.at[pl.ds(pl.multiple_of(i * depth, depth), depth), source.shape[1] - size :],
        held.at[:, pl.ds(pl.multiple_of(i * size, size), size)],
    )


def product_into(target, left, held, form, arrive=None):
    width = target.shape[1]
    size = min(COLUMNS, width)

    @pl.loop(0, width // size)
    def _(i):
        if arrive is not None:
            arrive(i, size)
        at = pl.ds(pl.multiple_of(i * size, size), size)
        if form == "turned":
            value = inner_cols(left[...], held[at, :])
        else:
            value = dot(left[...], held[:, at])
        target[:, at] = value.astype(LOW)


class PlaneGather:
    def __init__(self, wires, shard, main, sems, cols):
        (x, _, c), self.mate, self.beside, self.above = here()
        self.wires, self.shard, self.main, self.sems = wires, shard, main, sems
        half = shard.shape[0] // 2
        self.halves = [pl.ds(0, half), pl.ds(half, half)]
        self.spot = x * cols + c
        self.beside_spot, self.above_spot = self.beside[0] * cols + c, x * cols + self.above[2]
        self.corner_spot = self.beside[0] * cols + self.above[2]
        self.kept, self.to_mate, self.from_beside, self.from_above = [], [], [], []

    def start(self, i):
        part, target = self.shard.at[self.halves[i]], self.main.at[self.spot, self.halves[i]]
        self.kept.append(pltpu.make_async_copy(part, target, self.sems.at[i]))
        self.kept[-1].start()
        slot = self.wires.slots(3)
        self.from_beside.append(self.wires.start(part, target, slot, self.beside))
        self.from_above.append(self.wires.start(part, target, slot + 1, self.above))
        self.to_mate.append(self.wires.start(part, target, slot + 2, self.mate))

    def finish(self):
        slot = self.wires.slots(5)
        start, main = self.wires.start, self.main
        self.from_beside[0].wait_recv()
        part = main.at[self.beside_spot, self.halves[0]]
        corner_low = start(part, part, slot, self.above)
        self.from_above[0].wait_recv()
        self.from_above[1].wait_recv()
        part = main.at[self.above_spot, self.halves[1]]
        corner_high = start(part, part, slot + 1, self.beside)
        part = main.at[self.above_spot]
        self.to_mate.append(start(part, part, slot + 2, self.mate))
        self.from_beside[1].wait_recv()
        part = main.at[self.beside_spot]
        self.to_mate.append(start(part, part, slot + 3, self.mate))
        corner_low.wait_recv()
        corner_high.wait_recv()
        part = main.at[self.corner_spot]
        self.to_mate.append(start(part, part, slot + 4, self.mate))
        for copy in self.to_mate:
            copy.wait_recv()
        for copy in self.kept:
            copy.wait()


class Homing:
    def __init__(self, wires, shard, main, sem, rows, cols):
        x, r, c = here()[0]
        self.wires, self.shard, self.main, self.sem, self.rows = wires, shard, main, sem, rows
        self.seats = [seat_of(x, r, c, rows, cols, p) for p in range(rows)]
        self.homes = [home_of(x, r, c, rows, cols, s) for s in range(rows)]
        self.me, self.place = (x, r, c), lax.rem(c, rows)
        self.count, self.block = shard.shape[0], shard.shape[1] // rows

    def away(self, device):
        return jnp.logical_not(jnp.logical_and(device[1] == self.me[1], device[2] == self.me[2]))

    def sends(self):
        mine = pl.ds(pl.multiple_of(self.place * self.count, self.count), self.count)
        for s, home in enumerate(self.homes):
            part = self.shard.at[:, pl.ds(s * self.block, self.block)]
            there = self.wires.copy(part, self.main.at[mine], self.slot + s, home, self.slot + self.place)
            yield self.away(home), there, part, self.main.at[mine]

    def start(self):
        self.slot = self.wires.slots(self.rows)
        for remote, there, part, target in self.sends():
            pl.when(remote)(there.start)
            pl.when(jnp.logical_not(remote))(pltpu.make_async_copy(part, target, self.sem).start)

    def finish(self):
        for p, seat in enumerate(self.seats):
            part = self.main.at[pl.ds(p * self.count, self.count)]
            remote = self.away(seat)
            pl.when(remote)(self.wires.copy(part, part, self.slot + p, seat).wait_recv)
            pl.when(jnp.logical_not(remote))(pltpu.make_async_copy(part, part, self.sem).wait)
        for remote, there, _, _ in self.sends():
            pl.when(remote)(there.wait_send)


def plane_kernel(rows, cols, entry, leave, mid, counts, beside_work, totals, form, *refs):
    n_small, n_out, n_swap, n_extra, n_made, n_ship = counts
    refs = list(refs)
    big = refs.pop(0)
    weights = refs.pop(0)
    small = [refs.pop(0) for _ in range(n_small)]
    mine_parts = [refs.pop(0) for _ in range(n_swap)]
    extra = [refs.pop(0) for _ in range(n_extra)]
    leaving = [refs.pop(0) for _ in range(n_ship)]
    main = refs.pop(0)
    outs = [refs.pop(0) for _ in range(n_out)]
    other_parts = [refs.pop(0) for _ in range(n_swap)]
    made = [refs.pop(0) for _ in range(n_made)]
    landing = [refs.pop(0) for _ in range(n_ship)]
    shard, send, recv, local = (refs.pop(0) for _ in range(4))
    if totals:
        total, inbox, line_inbox = (refs.pop() for _ in range(3))
    wires = Wires(send, recv)
    me, mate, beside, above = here()
    x, r, c = me
    count, width = shard.shape
    half = count // 2
    low_half, high_half = pl.ds(0, half), pl.ds(half, half)
    homing = None
    if leave == "homes":
        homing = Homing(wires, shard, main, local.at[20], rows, cols)
    elif n_ship:
        homing = Homing(wires, leaving[0], landing[0], local.at[22], rows, cols)
    if leave == "gather":
        gather = PlaneGather(wires, shard, main, local.at[pl.ds(20, 2)], cols)
    greeted = []
    expected = 0
    if homing is not None:
        stays = (lax.div(c, cols // rows) == r) & (lax.rem(c, cols // rows) * rows + lax.rem(c, rows) == c)
        greeted += [(s, homing.away(s)) for s in homing.seats]
        expected = expected + rows - jnp.where(stays, 1, 0).astype(jnp.int32)
    if totals:
        others = [(x, lax.rem(r + k, rows), c) for k in range(1, rows)]
        greeted += [(o, None) for o in others]
        expected = expected + rows - 1
    greeted += [(mate, None), (beside, None), (above, None)]
    if entry == "sum":
        depth = big.shape[2]
        block_width = min(COLUMNS, width) if form == "turned" else width * depth // weights.shape[0]

        def fetch(i):
            ends = weight_block(weights, refs[1], i, form, depth, block_width)
            return pltpu.make_async_copy(*ends, local.at[4 + i])

        def arrive(i, size):
            for k in range(size // block_width):
                fetch(i * (size // block_width) + k).wait()

        @pl.loop(0, width // block_width)
        def _(i):
            fetch(i).start()

        chips = [(1 - x, above[2]), (1 - x, c), (x, above[2]), (x, c)]
        loads = [
            pltpu.make_async_copy(big.at[(tx * cols + tc) // 2], refs[0].at[k], local.at[k])
            for k, (tx, tc) in enumerate(chips)
        ]
        for load in loads:
            load.start()
    greet(greeted, expected + 3)
    if n_ship:
        homing.start()

    if entry == "sum":
        factors, held_weights, both, mated, beside_pass, above_pass, beside_in, above_in = refs
        first = wires.slots(4)
        handed = []
        core = lax.rem(c, 2)
        own_start = pl.multiple_of(core * count, count)
        given_rows = pl.ds(pl.multiple_of((1 - core) * count, count), count)

        def own_rows(start, size):
            return pl.ds(pl.multiple_of(own_start + start, size), size)

        def supply(k, arrive=None):
            loads[k].wait()
            product_into(both.at[k], factors.at[k], held_weights, form, arrive)
            handed.append(wires.start(both.at[k, given_rows], mated.at[k], first + k, mate))

        def add(k, more, start, size):
            @pl.loop(0, size // STEP)
            def _(i):
                at = own_rows(start + i * STEP, STEP)
                to = pl.ds(pl.multiple_of(start + i * STEP, STEP), STEP)
                both[k, at, :] = (
                    both[k, at, :].astype(jnp.float32) + more(to).astype(jnp.float32)
                ).astype(LOW)

        def merge(k):
            handed[k].wait_recv()
            add(k, lambda at: mated[k, at, :], 0, count)

        own_low, own_high = own_rows(0, half), own_rows(half, half)
        slot = wires.slots(6)
        supply(0, arrive)
        handed[0].wait_recv()
        add(0, lambda at: mated[0, at, :], 0, half)
        pass_beside = wires.start(both.at[0, own_low], beside_pass, slot, beside)
        add(0, lambda at: mated[0, at, :], half, half)
        pass_above = wires.start(both.at[0, own_high], above_pass, slot + 1, above)
        supply(1)
        merge(1)
        beside_low = wires.start(both.at[1, own_low], beside_in.at[low_half], slot + 2, beside)
        supply(2)
        merge(2)
        pass_beside.wait_recv()
        add(2, lambda at: beside_pass[at, :], 0, half)
        above_low = wires.start(both.at[2, own_low], above_in.at[low_half], slot + 3, above)
        above_high = wires.start(both.at[2, own_high], above_in.at[high_half], slot + 4, above)
        supply(3)
        if beside_work is not None:
            beside_work(0, held_weights, extra, made)
        pass_above.wait_recv()
        add(1, lambda at: above_pass[pl.ds(pl.multiple_of(at.start - half, STEP), STEP), :], half, half)
        beside_high = wires.start(both.at[1, own_high], beside_in.at[high_half], slot + 5, beside)
        slot = wires.slots(n_swap)
        swaps = [
            wires.start(source, target, slot + i, beside)
            for i, (source, target) in enumerate(zip(mine_parts, other_parts))
        ]
        if beside_work is not None:
            beside_work(1, held_weights, extra, made)
        handed[3].wait_recv()

        def value(at):
            near = both[3, own_rows(at.start, STEP), :].astype(jnp.float32)
            near = near + mated[3, at, :].astype(jnp.float32)
            return near + (beside_in[at, :].astype(jnp.float32) + above_in[at, :].astype(jnp.float32))

    mid.start(outs)
    for k in range(2):
        if entry == "sum":
            (beside_low, beside_high)[k].wait_recv()
            (above_low, above_high)[k].wait_recv()

        @pl.loop(k * (half // STEP), (k + 1) * (half // STEP))
        def _(i):
            at = pl.ds(pl.multiple_of(i * STEP, STEP), STEP)
            shard[at, :] = mid.rows(at, value(at), small, outs).astype(LOW)

        if leave == "gather":
            gather.start(k)

    if leave == "gather":
        gather.finish()
    elif leave == "homes":
        homing.start()
    else:
        keep = pltpu.make_async_copy(shard, main, local.at[20])
        keep.start()
    if beside_work is not None:
        beside_work(2, None, extra, made)
    if leave == "stay":
        keep.wait()
    if totals:
        gain_sums(wires, me, (mate, beside, above), others, rows, small[-1], outs, total, inbox, line_inbox)
    if homing is not None:
        homing.finish()
    if n_swap:
        for copy in swaps:
            copy.wait_recv()
    wires.finish()


def enter_kernel(
    rows, cols, hidden_in, grad_out, gains_in, normed, grads, held, grad_here, gains,
    shard, seated, grad_seated, hidden_relay, grad_relay, landing, send, recv, local,
):
    wires = Wires(send, recv)
    me, mate, beside, above = here()
    x, r, c = me
    count, width = seated.shape
    block = width // rows
    side = 2 * lax.div(c, 2)
    far = 2 - side
    ways = [(x, c, side), (x, c, side + 1), (x, above[2], side), (x, above[2], side + 1)]
    via = side + lax.rem(r, 2)
    sources = [(x, s, via) for s in range(rows)]
    others = [(x, lax.rem(r + k, rows), c) for k in range(1, rows)]

    def away(device):
        return jnp.logical_not(jnp.logical_and(device[1] == r, device[2] == c))

    kept = jnp.where(lax.rem(c, 2) == lax.rem(r, 2), 1, 0).astype(jnp.int32)
    greeted = [(s, away(s)) for s in sources] + [(o, None) for o in others]
    greeted += [(above, None), (mate, None), (beside, None)]
    greet(greeted, 2 * rows + 2 - kept)

    mine = pl.ds(pl.multiple_of(r * block, block), block)
    slot = wires.slots(rows - 1)
    spread = [wires.start(gains_in, landing.at[r], slot + k, other) for k, other in enumerate(others)]

    class Seating:
        def __init__(self, source, target, relay, sem):
            self.source, self.target, self.relay, self.sem = source, target, relay, sem
            self.slot, self.hop = wires.slots(rows), wires.slots(1)

        def pieces(self):
            near = pl.multiple_of(side * count, count)
            return [
                self.source.at[pl.ds(near, count)],
                self.source.at[pl.ds(near + count, count)],
                self.relay.at[pl.ds(0, count)],
                self.relay.at[pl.ds(count, count)],
            ]

        def cross(self):
            across = self.source.at[pl.ds(pl.multiple_of(far * count, count), 2 * count)]
            self.crossing = wires.start(across, self.relay, self.hop, above)

        def go(self, which):
            for i in which:
                piece, seat = self.pieces()[i], ways[i]
                there = wires.copy(piece, self.target.at[:, mine], self.slot + i, seat, self.slot + r)
                stay = pltpu.make_async_copy(piece, self.target.at[:, mine], self.sem)
                pl.when(away(seat))(there.start)
                pl.when(jnp.logical_not(away(seat)))(stay.start)

        def arrive(self):
            for s, source in enumerate(sources):
                part = self.target.at[:, pl.ds(s * block, block)]
                arrived = wires.copy(part, part, self.slot + s, source)
                stay = pltpu.make_async_copy(part, part, self.sem)
                pl.when(away(source))(arrived.wait_recv)
                pl.when(jnp.logical_not(away(source)))(stay.wait)

        def sent(self):
            for i, piece in enumerate(self.pieces()):
                there = wires.copy(piece, self.target.at[:, mine], self.slot + i, ways[i])
                pl.when(away(ways[i]))(there.wait_send)

    hidden = Seating(hidden_in, seated, hidden_relay, local.at[0])
    grad = Seating(grad_out, grad_seated, grad_relay, local.at[1])
    hidden.cross()
    hidden.go((0, 1))
    grad.cross()
    hidden.crossing.wait_recv()
    hidden.go((2, 3))
    for copy in spread:
        copy.wait_recv()
    landing[r] = gains_in[...]
    for s in range(rows):
        gains[:, s * block : (s + 1) * block] = landing[s]
    hidden.arrive()
    grad.go((0, 1))
    grad.crossing.wait_recv()
    grad.go((2, 3))
    keep = pltpu.make_async_copy(seated, held, local.at[2])
    keep.start()

    gather = PlaneGather(wires, shard, normed, local.at[pl.ds(4, 2)], cols)
    for k in range(2):

        @pl.loop(k * (count // STEP // 2), (k + 1) * (count // STEP // 2))
        def _(i):
            at = pl.ds(pl.multiple_of(i * STEP, STEP), STEP)
            value = seated[at, :].astype(jnp.float32)
            shard[at, :] = (value * rms_scale(value) * gains[0:1, :]).astype(LOW)

        gather.start(k)
    gather.finish()
    grad.arrive()
    keep_grad = pltpu.make_async_copy(grad_seated, grad_here, local.at[3])
    keep_grad.start()
    gather = PlaneGather(wires, grad_seated, grads, local.at[pl.ds(6, 2)], cols)
    gather.start(0)
    gather.start(1)
    gather.finish()
    hidden.sent()
    grad.sent()
    keep.wait()
    keep_grad.wait()
    wires.finish()


def enter_call(hidden_in, grad_out, gains, collective_id):
    rows, cols, parts = lax.axis_size("row"), lax.axis_size("col"), lax.axis_size("dp")
    count, width = hidden_in.shape[0] // rows, hidden_in.shape[1] * rows
    block = width // rows
    vmem = pl.BlockSpec(memory_space=pltpu.VMEM)
    hbm = pl.BlockSpec(memory_space=pl.ANY)
    shape = jax.ShapeDtypeStruct((count, width), LOW)
    tile = pltpu.VMEM((count, width), LOW)
    relay = pltpu.VMEM((2 * count, block), LOW)
    whole = jax.ShapeDtypeStruct((parts * cols, count, width), LOW)
    normed, grads, held, grad_here, gains = pl.pallas_call(
        functools.partial(enter_kernel, rows, cols),
        out_shape=[whole, whole, shape, shape, jax.ShapeDtypeStruct((8, width), jnp.float32)],
        in_specs=[hbm, hbm, vmem],
        out_specs=[hbm, hbm, hbm, hbm, vmem],
        scratch_shapes=[tile, tile, tile, relay, relay, pltpu.VMEM((rows, 8, block), jnp.float32)]
        + [pltpu.SemaphoreType.DMA((48,))] * 2
        + [pltpu.SemaphoreType.DMA((8,))],
        compiler_params=pltpu.CompilerParams(
            collective_id=collective_id, has_side_effects=True, vmem_limit_bytes=VMEM_LIMIT
        ),
        cost_estimate=pl.CostEstimate(flops=0, bytes_accessed=20_000_000, transcendentals=0),
    )(hidden_in, grad_out, gains)
    flat = (parts * cols * count, width)
    return normed.reshape(flat), grads.reshape(flat), held, grad_here, gains


def enter_plain(hidden_in, grad_out, gains, collective_id):
    gains = lax.all_gather(gains, "row", axis=1, tiled=True)
    held = to_group(hidden_in)
    value = held.astype(jnp.float32)
    normed = group_gather((value * rms_scale(value) * gains[0:1]).astype(LOW))
    grad_here = to_group(grad_out)
    return normed, group_gather(grad_here), held, grad_here, gains


def gain_sums(wires, me, partners, others, rows, gain_two, outs, total, inbox, line_inbox):
    x, r, c = me
    block = total.shape[1] // rows
    total[0:1, :] = jnp.sum(outs[1][...], axis=0, keepdims=True)
    total[1:2, :] = jnp.sum(gain_two[...], axis=0, keepdims=True)
    total[2:, :] = jnp.zeros_like(total[2:, :])
    first = wires.slots(len(partners))
    for k, partner in enumerate(partners):
        copy = wires.copy(total, inbox.at[k], first + k, partner)
        copy.start()
        copy.wait()
        total[...] += inbox[k]
    first = wires.slots(len(others))
    copies = []
    for k, (_, row, _) in enumerate(others):
        part = total.at[:, pl.ds(pl.multiple_of(row * block, block), block)]
        copies.append(wires.start(part, line_inbox.at[r], first + k, others[k]))
    line_inbox[r] = total[:, pl.ds(pl.multiple_of(r * block, block), block)]
    for copy in copies:
        copy.wait_recv()
    outs[0][...] = sum(line_inbox[k] for k in range(rows))


def plane_call(
    entry, leave, mid, big, small, outs, collective_id, weights=None, form=None, totals=False, swap=(),
    beside_work=None, extra=(), made=(), ship=(),
):
    rows, cols, parts = lax.axis_size("row"), lax.axis_size("col"), lax.axis_size("dp")
    count, width = big.shape[0] // (parts * cols), small[0].shape[1]
    depth = big.shape[1]
    big = big.reshape(parts * cols // 2, 2 * count, depth)
    gathered = leave == "gather"
    shape = {"gather": (parts * cols, count, width), "homes": (rows * count, width // rows), "stay": (count, width)}[leave]
    landed = [jax.ShapeDtypeStruct((rows * a.shape[0], a.shape[1] // rows), a.dtype) for a in ship]
    plain = len(swap) + len(made) + len(ship)
    vmem = pl.BlockSpec(memory_space=pltpu.VMEM)
    hbm = pl.BlockSpec(memory_space=pl.ANY)
    tile = pltpu.VMEM((count, width), LOW)
    whole, part = pltpu.VMEM((4, count, width), LOW), pltpu.VMEM((count // 2, width), LOW)
    scratch = [tile, pltpu.SemaphoreType.DMA((40,)), pltpu.SemaphoreType.DMA((40,)), pltpu.SemaphoreType.DMA((24,))]
    scratch += [
        pltpu.VMEM(big.shape, LOW),
        pltpu.VMEM((width, depth) if form == "turned" else (depth, width), LOW),
        pltpu.VMEM((4, 2 * count, width), LOW),
    ]
    scratch += [whole, part, part, tile, tile]
    if totals:
        scratch += [
            pltpu.VMEM((rows, 8, width // rows), jnp.float32),
            pltpu.VMEM((3, 8, width), jnp.float32),
            pltpu.VMEM((8, width), jnp.float32),
        ]
    counts = (len(small), len(outs), len(swap), len(extra), len(made), len(ship))
    main, *others = pl.pallas_call(
        functools.partial(plane_kernel, rows, cols, entry, leave, mid, counts, beside_work, totals, form),
        out_shape=[jax.ShapeDtypeStruct(shape, LOW)]
        + list(outs)
        + [jax.ShapeDtypeStruct(m.shape, m.dtype) for m in (*swap, *made, *landed)],
        in_specs=[hbm, hbm] + [vmem] * len(small) + [hbm] * (len(swap) + len(extra) + len(ship)),
        out_specs=[hbm] + [vmem] * len(outs) + [hbm] * plain,
        scratch_shapes=scratch,
        compiler_params=pltpu.CompilerParams(
            collective_id=collective_id, has_side_effects=True, vmem_limit_bytes=VMEM_LIMIT
        ),
        cost_estimate=pl.CostEstimate(flops=0, bytes_accessed=20_000_000, transcendentals=0),
    )(big, weights, *small, *swap, *extra, *ship)
    if gathered:
        main = main.reshape(parts * cols * count, width)
    return [main, *others]


def fold(values):
    return values.reshape(values.shape[0] // 8, 8, values.shape[1]).sum(0)


class Mid:
    @staticmethod
    def start(outs):
        pass


class SecondNorm(Mid):
    @staticmethod
    def rows(at, value, small, outs):
        held, gains = small
        middle = held[at, :].astype(jnp.float32) + value
        outs[0][at, :] = middle
        return middle * rms_scale(middle) * gains[1:2, :]


class Add(Mid):
    @staticmethod
    def rows(at, value, small, outs):
        return small[0][at, :] + value


class BackSecond(Mid):
    @staticmethod
    def start(outs):
        outs[1][...] = jnp.zeros_like(outs[1])

    @staticmethod
    def rows(at, value, small, outs):
        middle, grad_out, gains = small
        middle = middle[at, :]
        scale = rms_scale(middle)
        outs[1][...] += fold(value * middle * scale)
        grad = grad_out[at, :].astype(jnp.float32) + norm_back(
            middle, scale, value * gains[1:2, :]
        )
        outs[0][at, :] = grad
        return grad


class BackFirst(Mid):
    @staticmethod
    def start(outs):
        outs[1][...] = jnp.zeros_like(outs[1])

    @staticmethod
    def rows(at, value, small, outs):
        held, grad_middle, gains = small[:3]
        inputs = held[at, :].astype(jnp.float32)
        scale = rms_scale(inputs)
        outs[1][...] += fold(value * inputs * scale)
        return grad_middle[at, :] + norm_back(inputs, scale, value * gains[0:1, :])


def plain_call(
    entry, leave, mid, big, small, outs, collective_id, weights=None, form=None, totals=False, swap=(),
    beside_work=None, extra=(), made=(), ship=(),
):
    refs = [Holder(a) for a in small]
    given = [Holder(jnp.zeros(o.shape, o.dtype)) for o in outs]
    depth, width = big.shape[1], small[0].shape[1]
    if form == "turned":
        product = inner_cols(big, weights[:, :depth])
    else:
        block = width * depth // weights.shape[0]
        whole = unstack(weights[:, weights.shape[1] - block :], depth)
        product = dot(big, whole)
    mid.start(given)
    shard = mid.rows(slice(None), group_scatter(product), refs, given).astype(LOW)
    main = {"gather": group_gather, "homes": from_group, "stay": lambda a: a}[leave](shard)
    if totals:
        sums = jnp.stack([given[1].value.sum(0), small[-1].sum(0)])
        sums = jnp.pad(lax.psum(sums, ("dp", "row", "col")), ((0, 6), (0, 0)))
        part = outs[0].shape[1]
        given[0].value = lax.dynamic_slice_in_dim(sums, lax.axis_index("row") * part, part, 1)
    others = [dp_other(m) for m in swap]
    if beside_work is not None:
        grads, slope_up, gated, tokens = extra
        lifted = lift_back_plain(grads, whole, slope_up, gated)
        others += [lifted, inner_rows(tokens, lifted).astype(LOW)]
    return [main] + [g.value for g in given] + others + [from_group(a) for a in ship]


class Holder:
    def __init__(self, value):
        self.value, self.dtype, self.shape = value, value.dtype, value.shape

    def __getitem__(self, at):
        return self.value[at]

    def __setitem__(self, at, value):
        self.value = self.value.at[at].set(value)


def swap_halves(values, first):
    lanes = values.shape[1]
    half = HEAD_DIM // 2
    return jnp.where(first, pltpu.roll(values, lanes - half, 1), pltpu.roll(values, half, 1))


def attend_kernel(query, key, value, cosine, sine, mixed, q_out, k_out, v_out, logsum):
    length, lanes = query.shape
    block = min(256, length)
    lane = lax.broadcasted_iota(jnp.int32, (length, lanes), 1)
    first = lax.rem(lane, HEAD_DIM) < HEAD_DIM // 2
    cos, sin = cosine[...], sine[...]

    def rotate(values):
        return (values * cos + swap_halves(values, first) * sin).astype(LOW)

    q_out[...] = rotate(query[...])
    k_out[...] = rotate(key[...])
    low_values = value[...].astype(LOW)
    v_out[...] = low_values
    v_turned = low_values.astype(jnp.float32).T.astype(LOW)
    head = lax.broadcasted_iota(jnp.int32, (block, lanes), 1) // HEAD_DIM
    keep = lax.broadcasted_iota(jnp.int32, (block, block), 0) <= lax.broadcasted_iota(
        jnp.int32, (block, block), 1
    )
    for j in range(length // block):
        at = slice(j * block, (j + 1) * block)
        q_block = q_out[at, :].astype(jnp.float32) * HEAD_DIM ** (-0.5)
        parts = []
        for h in range(lanes // HEAD_DIM):
            q_head = jnp.where(head == h, q_block, 0.0).astype(LOW)
            near = jnp.where(keep, inner_cols(k_out[at, :], q_head), -jnp.inf)
            highest = jnp.max(near, axis=0, keepdims=True)
            if j:
                far = inner_cols(k_out[: j * block, :], q_head)
                highest = jnp.maximum(highest, jnp.max(far, axis=0, keepdims=True))
                far = jnp.exp(far - highest)
            near = jnp.exp(near - highest)
            total = jnp.sum(near, axis=0, keepdims=True)
            if j:
                total = total + jnp.sum(far, axis=0, keepdims=True)
            logsum[0, 0, h : h + 1, at] = highest + jnp.log(total)
            share = 1.0 / total
            out = dot(v_turned[:, at], (near * share).astype(LOW))
            if j:
                out = out + dot(v_turned[:, : j * block], (far * share).astype(LOW))
            parts.append(out[h * HEAD_DIM : (h + 1) * HEAD_DIM])
        mixed[at, :] = jnp.concatenate(parts, 0).T.astype(LOW)


def attend_back_kernel(n_swap, query, key, value, grad, logsum, cosine, sine, *refs):
    mine_parts, refs = refs[:n_swap], refs[n_swap:]
    made, refs = refs[0], refs[1:]
    other_parts, refs = refs[:n_swap], refs[n_swap:]
    (k_sum, v_sum, q_out, k_out, v_out, out_sems), refs = refs[:6], refs[6:]
    length, lanes = query.shape
    if n_swap:
        beside = here()[2]
        wires = Wires(*refs)
        swaps = [
            wires.copy(source, target, i, beside)
            for i, (source, target) in enumerate(zip(mine_parts, other_parts))
        ]
        here_first = (pl.program_id(0) == 0) & (pl.program_id(1) == 0)
        here_last = (pl.program_id(0) == pl.num_programs(0) - 1) & (
            pl.program_id(1) == pl.num_programs(1) - 1
        )

        @pl.when(here_first)
        def _():
            greet([(beside, None)], 1)
            for copy in swaps:
                copy.start()

    block = min(256, length)
    k_sum[...] = jnp.zeros_like(k_sum)
    v_sum[...] = jnp.zeros_like(v_sum)
    k_turned = key[...].astype(jnp.float32).T.astype(LOW)
    head = lax.broadcasted_iota(jnp.int32, (block, lanes), 1) // HEAD_DIM
    keep = lax.broadcasted_iota(jnp.int32, (block, block), 0) <= lax.broadcasted_iota(
        jnp.int32, (block, block), 1
    )
    scale = HEAD_DIM ** (-0.5)

    def rotate_back(values, at):
        rows = values.shape[0]
        lane = lax.broadcasted_iota(jnp.int32, (rows, lanes), 1)
        first = lax.rem(lane, HEAD_DIM) < HEAD_DIM // 2
        return (values * cosine[at, :] - swap_halves(values, first) * sine[at, :]).astype(LOW)

    for j in range(length // block):
        at = slice(j * block, (j + 1) * block)
        before = slice(0, j * block)
        q_block = query[at, :].astype(jnp.float32) * scale
        g_block = grad[at, :].astype(jnp.float32)
        parts = []
        for h in range(lanes // HEAD_DIM):
            q_head = jnp.where(head == h, q_block, 0.0).astype(LOW)
            g_head = jnp.where(head == h, g_block, 0.0).astype(LOW)
            level = logsum[0, 0, h : h + 1, at]
            near = jnp.exp(jnp.where(keep, inner_cols(key[at, :], q_head), -jnp.inf) - level)
            d_near = inner_cols(value[at, :], g_head)
            inner = jnp.sum(near * d_near, axis=0, keepdims=True)
            if j:
                far = jnp.exp(inner_cols(key[before, :], q_head) - level)
                d_far = inner_cols(value[before, :], g_head)
                inner = inner + jnp.sum(far * d_far, axis=0, keepdims=True)
                v_sum[before, :] += dot(far.astype(LOW), g_head)
                s_far = (far * (d_far - inner)).astype(LOW)
                k_sum[before, :] += dot(s_far, q_head)
            v_sum[at, :] += dot(near.astype(LOW), g_head)
            s_near = (near * (d_near - inner)).astype(LOW)
            k_sum[at, :] += dot(s_near, q_head)
            out = dot(k_turned[:, at], s_near)
            if j:
                out = out + dot(k_turned[:, before], s_far)
            parts.append(out[h * HEAD_DIM : (h + 1) * HEAD_DIM])
        q_out[at, :] = rotate_back(jnp.concatenate(parts, 0).T * scale, at)
    k_out[...] = rotate_back(k_sum[...], slice(None))
    v_out[...] = v_sum[...].astype(LOW)
    rows_at = pl.ds(pl.multiple_of(pl.program_id(0) * length, length), length)
    columns = made.shape[1] // 3
    copies = [
        pltpu.make_async_copy(
            out,
            made.at[rows_at, pl.ds(pl.multiple_of(i * columns + pl.program_id(1) * lanes, lanes), lanes)],
            out_sems.at[i],
        )
        for i, out in enumerate((q_out, k_out, v_out))
    ]
    for copy in copies:
        copy.start()
    for copy in copies:
        copy.wait()
    if n_swap:

        @pl.when(here_last)
        def _():
            for copy in swaps:
                copy.wait()


def pair_tables(length):
    half = HEAD_DIM // 2
    freq = THETA ** (-(jnp.arange(half, dtype=jnp.float32) * 2.0 / HEAD_DIM))
    angle = jnp.arange(length, dtype=jnp.float32)[:, None] * freq[None, :]
    cosine, sine = jnp.cos(angle), jnp.sin(angle)
    return jnp.tile(cosine, (1, 4)), jnp.tile(jnp.concatenate([-sine, sine], 1), (1, 2))


def attend_pairs(projected, sequences):
    tokens, columns = projected.shape[0], projected.shape[1] // 3
    length, lanes = tokens // sequences, 2 * HEAD_DIM
    pairs = columns // lanes
    cosine, sine = pair_tables(length)

    def spec(offset):
        return pl.BlockSpec((length, lanes), lambda s, h: (s, offset + h))

    table = pl.BlockSpec((length, lanes), lambda s, h: (0, 0))
    level = pl.BlockSpec((1, 1, 2, length), lambda s, h: (s, h, 0, 0))
    shape = jax.ShapeDtypeStruct((tokens, columns), LOW)
    return pl.pallas_call(
        attend_kernel,
        grid=(sequences, pairs),
        in_specs=[spec(0), spec(pairs), spec(2 * pairs), table, table],
        out_specs=[spec(0)] * 4 + [level],
        out_shape=[shape] * 4 + [jax.ShapeDtypeStruct((sequences, pairs, 2, length), jnp.float32)],
        compiler_params=pltpu.CompilerParams(vmem_limit_bytes=VMEM_LIMIT),
        cost_estimate=pl.CostEstimate(
            flops=8 * tokens * length * columns, bytes_accessed=100_000_000, transcendentals=0
        ),
    )(projected, projected, projected, cosine, sine)


def attend_pairs_back(query, keys, values, grad_mixed, logsum, sequences, swap, collective_id):
    tokens, columns = query.shape
    length, lanes = tokens // sequences, 2 * HEAD_DIM
    pairs = columns // lanes
    cosine, sine = pair_tables(length)
    spec = pl.BlockSpec((length, lanes), lambda s, h: (s, h))
    table = pl.BlockSpec((length, lanes), lambda s, h: (0, 0))
    level = pl.BlockSpec((1, 1, 2, length), lambda s, h: (s, h, 0, 0))
    hbm = pl.BlockSpec(memory_space=pl.ANY)
    return pl.pallas_call(
        functools.partial(attend_back_kernel, len(swap)),
        grid=(sequences, pairs),
        in_specs=[spec] * 4 + [level, table, table] + [hbm] * len(swap),
        out_specs=[hbm] * (1 + len(swap)),
        out_shape=[jax.ShapeDtypeStruct((tokens, 3 * columns), LOW)] + [jax.ShapeDtypeStruct(m.shape, m.dtype) for m in swap],
        scratch_shapes=[pltpu.VMEM((length, lanes), jnp.float32)] * 2
        + [pltpu.VMEM((length, lanes), LOW)] * 3
        + [pltpu.SemaphoreType.DMA((4,))] * 3,
        compiler_params=pltpu.CompilerParams(
            collective_id=collective_id, has_side_effects=True, vmem_limit_bytes=VMEM_LIMIT
        ),
        cost_estimate=pl.CostEstimate(
            flops=20 * tokens * length * columns, bytes_accessed=60_000_000, transcendentals=0
        ),
    )(query, keys, values, grad_mixed, logsum, cosine, sine, *swap)


def lift_kernel(tokens, weights, activated, slope_up, gated):
    rows, width = activated.shape
    step = min(256, rows)
    for i in range(rows // step):
        at = slice(i * step, (i + 1) * step)
        left = tokens[at, :]
        gate, upward = dot(left, weights[:, :width]), dot(left, weights[:, width:])
        sigmoid = 1.0 / (1.0 + jnp.exp(-gate))
        passed = gate * sigmoid
        activated[at, :] = (passed * upward).astype(LOW)
        gated[at, :] = passed.astype(LOW)
        slope_up[at, :] = (upward * (sigmoid + passed * (1.0 - sigmoid))).astype(LOW)


def lift(tokens, weights):
    count, width = tokens.shape
    units = weights.shape[1] // 2
    tile, rows = units // 2, min(512, count)
    out = pl.BlockSpec((rows, tile), lambda j, i: (i, j))
    shape = jax.ShapeDtypeStruct((count, units), LOW)
    return pl.pallas_call(
        lift_kernel,
        grid=(2, count // rows),
        in_specs=[
            pl.BlockSpec((rows, width), lambda j, i: (i, 0)),
            pl.BlockSpec((width, 2 * tile), lambda j, i: (0, j)),
        ],
        out_specs=[out] * 3,
        out_shape=[shape] * 3,
        compiler_params=pltpu.CompilerParams(vmem_limit_bytes=VMEM_LIMIT),
        cost_estimate=pl.CostEstimate(
            flops=4 * count * width * units, bytes_accessed=30_000_000, transcendentals=0
        ),
    )(tokens, weights)


def lift_back_rows(weights, grads, slope_up, gated, lifted):
    units = slope_up.shape[1]
    tile = units // 2
    for j in range(2):
        here_units = slice(j * tile, (j + 1) * tile)
        grad = inner_cols(grads[...], weights[here_units, :])
        start = 2 * j * tile
        lifted[:, start : start + tile] = (grad * slope_up[:, here_units].astype(jnp.float32)).astype(LOW)
        lifted[:, start + tile : start + 2 * tile] = (
            grad * gated[:, here_units].astype(jnp.float32)
        ).astype(LOW)


def lift_back_work(stage, weights, extra, made):
    grads, slope_up, gated, tokens = extra
    lifted, grad_weights = made
    count, units = slope_up.shape
    width = tokens.shape[1]
    if stage < 2:
        rows = count // 4
        first = stage * (count // 2)
        at = pl.ds(first, count // 2)
        pltpu.emit_pipeline(
            functools.partial(lift_back_rows, weights),
            grid=(2,),
            in_specs=[
                pl.BlockSpec((rows, width), lambda i: (i, 0)),
                pl.BlockSpec((rows, units), lambda i: (i, 0)),
                pl.BlockSpec((rows, units), lambda i: (i, 0)),
            ],
            out_specs=[pl.BlockSpec((rows, 2 * units), lambda i: (i, 0))],
        )(grads.at[at], slope_up.at[at], gated.at[at], lifted.at[at])

    def inner(left, right, out):
        out[...] = inner_rows(left[...], right[...]).astype(LOW)

    if stage > 0:
        part, tile = width // 2, units // 2
        mine = pl.ds((stage - 1) * part, part)
        pltpu.emit_pipeline(
            inner,
            grid=(4,),
            in_specs=[
                pl.BlockSpec((count, part), lambda j: (0, 0)),
                pl.BlockSpec((count, tile), lambda j: (0, j)),
            ],
            out_specs=[pl.BlockSpec((part, tile), lambda j: (0, j))],
        )(tokens.at[:, mine], lifted, grad_weights.at[mine])


def lift_back_plain(grads, weights, slope_up, gated):
    grad = inner_cols(grads, weights)
    up, through = (grad * f.astype(jnp.float32) for f in (slope_up, gated))
    return pair_units(up, through).astype(LOW)


def attend_plain(projected, sequences):
    tokens, columns = projected.shape[0], projected.shape[1] // 3
    length = tokens // sequences
    shape = (sequences, length, columns // HEAD_DIM, HEAD_DIM)
    cosine, sine = rotation_tables(length)
    query = turn(projected[:, :columns].reshape(shape), cosine, sine).astype(LOW)
    keys = turn(projected[:, columns : 2 * columns].reshape(shape), cosine, sine).astype(LOW)
    values = projected[:, 2 * columns :].reshape(shape).astype(LOW)
    mixed, logsum = attend(query, keys, values)
    flat = (tokens, columns)
    return mixed.reshape(flat), query.reshape(flat), keys.reshape(flat), values.reshape(flat), logsum


def attend_plain_back(query, keys, values, grad_mixed, logsum, sequences, swap, collective_id):
    tokens, columns = query.shape
    length = tokens // sequences
    shape = (sequences, length, columns // HEAD_DIM, HEAD_DIM)
    cosine, sine = rotation_tables(length)
    grad_query, grad_keys, grad_values = attend_back(
        *(a.reshape(shape) for a in (query, keys, values, grad_mixed)), logsum
    )
    grads = (turn_back(grad_query, cosine, sine), turn_back(grad_keys, cosine, sine), grad_values)
    grads = jnp.concatenate([g.reshape(tokens, columns).astype(LOW) for g in grads], 1)
    return [grads] + [dp_other(m) for m in swap]


def body(
    hidden_in, w_query, w_key, w_value, w_out, w_gate, w_up, w_down, norm_attn, norm_ffn, grad_out
):
    rows, cols, parts = lax.axis_size("row"), lax.axis_size("col"), lax.axis_size("dp")
    own_kernels = (parts, rows, cols) == (2, 4, 4)
    plane, enter = (plane_call, enter_call) if own_kernels else (plain_call, enter_plain)
    count, width = hidden_in.shape[0] // rows, hidden_in.shape[1] * rows
    full_rows = jax.ShapeDtypeStruct((count, width), jnp.float32)
    gain_rows = jax.ShapeDtypeStruct((8, width), jnp.float32)

    local_gains = jnp.pad(jnp.stack([norm_attn, norm_ffn]), ((0, 6), (0, 0)))
    own_attn = [my_part(w, 1) for w in (w_query, w_key, w_value)] + [stack(my_part(w_out, 0))]
    w_attn = lax.all_gather(jnp.concatenate(own_attn, 1), "row", axis=0, tiled=True)
    normed_one, grad_wide, held, grad_here, gains = enter(hidden_in, grad_out, local_gains, 1)
    own_ffn = pair_units(my_part(w_gate, 1), my_part(w_up, 1))
    w_ffn = lax.all_gather(own_ffn, "row", axis=0, tiled=True)
    w_back = lax.all_gather(my_part(w_down, 0), "row", axis=0, tiled=True)

    columns = w_attn.shape[1] // 4
    projected = dot(normed_one, w_attn[:, : 3 * columns])
    paired = columns % (2 * HEAD_DIM) == 0
    mixed, query, keys, values, logsum = (attend_pairs if paired else attend_plain)(projected, parts)
    normed_two, middle = plane(
        "sum", "gather", SecondNorm, mixed, [held, gains], [full_rows], 2, w_attn, "stacked"
    )

    activated, slope_up, gated = lift(normed_two, w_ffn)
    part_down, w_back = after(inner_rows(activated, grad_wide).astype(LOW), w_back)
    mine_down = row_sum(part_down, 1)
    low = functools.partial(jax.ShapeDtypeStruct, dtype=LOW)
    out_rows, grad_lifted, part_ffn = plane(
        "sum",
        "stay",
        Add,
        activated,
        [middle],
        [],
        3,
        w_back,
        "stacked",
        beside_work=lift_back_work,
        extra=[grad_wide, slope_up, gated, normed_two],
        made=[low((normed_two.shape[0], w_ffn.shape[1])), low((width, w_ffn.shape[1]))],
    )
    mine_ffn = row_sum(part_ffn, 0)
    grad_branch, grad_middle, gain_two, layer_out = plane(
        "sum",
        "gather",
        BackSecond,
        grad_lifted,
        [middle, grad_here, gains],
        [full_rows, gain_rows],
        4,
        w_ffn,
        "turned",
        ship=[out_rows],
    )
    grad_branch, mine_down = after(grad_branch, mine_down)
    w_proj = unstack(w_attn[:, 3 * columns :], columns)
    grad_mixed = inner_cols(grad_branch, w_proj).astype(LOW)
    part_out, grad_mixed = after(inner_rows(grad_branch, mixed).astype(LOW), grad_mixed)
    grad_projected, other_down = (attend_pairs_back if paired else attend_plain_back)(
        query, keys, values, grad_mixed, logsum, parts, [mine_down], 5
    )
    part_attn, grad_projected = after(
        inner_rows(normed_one, grad_projected).astype(LOW), grad_projected
    )
    part_attn, grad_projected = after(jnp.concatenate([part_attn, part_out], 1), grad_projected)
    mine_attn = row_sum(part_attn, 0)
    grad_in, gain_grads, _, other_ffn = plane(
        "sum",
        "homes",
        BackFirst,
        grad_projected,
        [held, grad_middle, gains, gain_two],
        [jax.ShapeDtypeStruct((8, norm_attn.shape[0]), jnp.float32), gain_rows],
        6,
        w_attn,
        "turned",
        totals=True,
        swap=[mine_ffn],
    )
    grad_in, other_down = after(grad_in, other_down)
    other_attn = dp_other(mine_attn)
    grad_down = join_wide(mine_down, other_down)
    grad_gate, grad_up = join_tall(mine_ffn, other_ffn, [(0, 2), (1, 3)])
    grad_wq, grad_wk, grad_wv, grad_attn_out = join_tall(
        mine_attn, other_attn, [(0,), (1,), (2,), (3,)]
    )
    grad_attn_out = grad_attn_out.T
    return (
        layer_out,
        grad_in,
        grad_wq,
        grad_wk,
        grad_wv,
        grad_attn_out,
        grad_gate,
        grad_up,
        grad_down,
        gain_grads[0],
        gain_grads[1],
    )


def solution(mesh):
    tokens = P(("dp", "col"), "row")
    tall = P("row", "col")
    wide = P("col", "row")
    gain = P("row")
    return jax.shard_map(
        body,
        mesh=mesh,
        in_specs=(tokens, tall, tall, tall, wide, tall, tall, wide, gain, gain, tokens),
        out_specs=(tokens, tokens, tall, tall, tall, wide, tall, tall, wide, gain, gain),
        check_vma=False,
    )
```

```python
import functools

import jax
import jax.numpy as jnp
from jax import lax
from jax.experimental import pallas as pl
from jax.experimental.pallas import tpu as pltpu
from jax.sharding import PartitionSpec as P

HEAD_DIM = 64
EPSILON = 1e-05
THETA = 130000.0
GROUP = ("dp", "col")
LOW = jnp.bfloat16


def dot(left, right):
    return jnp.dot(left, right, preferred_element_type=jnp.float32)


def inner_rows(left, right):
    return lax.dot_general(
        left, right, (((0,), (0,)), ((), ())), preferred_element_type=jnp.float32
    )


def inner_cols(left, right):
    return lax.dot_general(
        left, right, (((1,), (1,)), ((), ())), preferred_element_type=jnp.float32
    )


def seat_pairs():
    rows, cols = lax.axis_size("row"), lax.axis_size("col")
    per = cols // rows
    return [
        (r * cols + c, (c // per) * cols + (c % per) * rows + r)
        for r in range(rows)
        for c in range(cols)
    ]


def to_group(block):
    whole = lax.all_to_all(block, "row", split_axis=0, concat_axis=1, tiled=True)
    return lax.ppermute(whole, ("row", "col"), seat_pairs())


def from_group(block):
    back = lax.ppermute(block, ("row", "col"), [(b, a) for a, b in seat_pairs()])
    return lax.all_to_all(back, "row", split_axis=1, concat_axis=0, tiled=True)


def group_gather(shard):
    return lax.all_gather(shard, GROUP, axis=0, tiled=True)


def group_scatter(partial):
    return lax.psum_scatter(
        partial.astype(LOW), GROUP, scatter_dimension=0, tiled=True
    ).astype(jnp.float32)


def my_part(block, axis):
    size = block.shape[axis] // lax.axis_size("dp")
    return lax.dynamic_slice_in_dim(block, lax.axis_index("dp") * size, size, axis)


def halves(block):
    middle = block.shape[1] // 2
    return [block[:, :middle], block[:, middle:]]


def pair_units(gate, upward):
    (g, h), (u, v) = halves(gate), halves(upward)
    return jnp.concatenate([g, u, h, v], 1)


def stack(block):
    units = block.shape[0]
    return jnp.concatenate([block[:, i : i + units] for i in range(0, block.shape[1], units)], 0)


def unstack(blocks, units):
    return jnp.concatenate([blocks[i : i + units] for i in range(0, blocks.shape[0], units)], 1)


def after(*values):
    return lax.optimization_barrier(values)


def dp_other(mine):
    if lax.axis_size("dp") == 2:
        return lax.ppermute(mine, "dp", [(0, 1), (1, 0)])
    return lax.all_gather(mine, "dp", axis=0)


def dp_parts(mine, other):
    if lax.axis_size("dp") != 2:
        return list(other)
    lower = lax.axis_index("dp") == 0
    return [jnp.where(lower, mine, other), jnp.where(lower, other, mine)]


def row_sum(part, axis):
    return lax.psum_scatter(part, "row", scatter_dimension=axis, tiled=True)


def join_tall(mine, other, pieces):
    parts = dp_parts(mine, other)
    width = mine.shape[1] // sum(map(len, pieces))
    return [
        jnp.concatenate(
            [p[:, i * width : (i + 1) * width] for p in parts for i in piece], 1
        ).astype(jnp.float32)
        for piece in pieces
    ]


def join_wide(mine, other):
    return jnp.concatenate(dp_parts(mine, other), 0).astype(jnp.float32)


def rms_scale(values):
    return lax.rsqrt(jnp.mean(values * values, axis=1, keepdims=True) + EPSILON)


def norm_back(values, scale, weighted):
    inner = jnp.mean(weighted * values, axis=1, keepdims=True)
    return scale * weighted - values * (scale * scale * scale * inner)


def rotation_tables(length):
    half = HEAD_DIM // 2
    freq = THETA ** (-(jnp.arange(half, dtype=jnp.float32) * 2.0 / HEAD_DIM))
    angle = jnp.arange(length, dtype=jnp.float32)[:, None] * freq[None, :]
    cosine = jnp.concatenate([jnp.cos(angle), jnp.cos(angle)], 1)[None, :, None, :]
    sine = jnp.concatenate([jnp.sin(angle), jnp.sin(angle)], 1)[None, :, None, :]
    return (cosine, sine)


def turn(values, cosine, sine):
    half = values.shape[-1] // 2
    turned = jnp.concatenate([-values[..., half:], values[..., :half]], -1)
    return values * cosine + turned * sine


def turn_back(grads, cosine, sine):
    half = grads.shape[-1] // 2
    moved = grads * sine
    return grads * cosine + jnp.concatenate([moved[..., half:], -moved[..., :half]], -1)


def masked_scores(query, keys):
    scores = jnp.einsum(
        "sqhd,skhd->shqk", query, keys, preferred_element_type=jnp.float32
    ) * HEAD_DIM ** (-0.5)
    length = query.shape[1]
    allowed = jnp.arange(length)[:, None] >= jnp.arange(length)[None, :]
    return jnp.where(allowed[None, None], scores, -jnp.inf)


def attend(query, keys, values):
    scores = masked_scores(query, keys)
    highest = jnp.max(scores, axis=-1, keepdims=True)
    expo = jnp.exp(scores - highest)
    total = jnp.sum(expo, axis=-1, keepdims=True)
    low_probs = (expo / total).astype(LOW)
    mixed = jnp.einsum(
        "shqk,skhd->sqhd", low_probs, values, preferred_element_type=jnp.float32
    ).astype(LOW)
    return mixed, highest + jnp.log(total)


def attend_back(query, keys, values, grad_mixed, logsum):
    scale = HEAD_DIM ** (-0.5)
    probs = jnp.exp(masked_scores(query, keys) - logsum)
    low_probs = probs.astype(LOW)
    dprobs = jnp.einsum("sqhd,skhd->shqk", grad_mixed, values, preferred_element_type=jnp.float32)
    grad_values = jnp.einsum(
        "shqk,sqhd->skhd", low_probs, grad_mixed, preferred_element_type=jnp.float32
    )
    low_scores = (probs * (dprobs - jnp.sum(probs * dprobs, axis=-1, keepdims=True))).astype(LOW)
    grad_query = (
        jnp.einsum("shqk,skhd->sqhd", low_scores, keys, preferred_element_type=jnp.float32) * scale
    )
    grad_keys = (
        jnp.einsum("shqk,sqhd->skhd", low_scores, query, preferred_element_type=jnp.float32) * scale
    )
    return grad_query, grad_keys, grad_values


MESH = pl.DeviceIdType.MESH
STEP = 16
VMEM_LIMIT = 56 * 1024 * 1024


class Wires:
    def __init__(self, send, recv):
        self.send, self.recv, self.used, self.sent = send, recv, 0, []

    def slots(self, count):
        first = self.used
        self.used += count
        return first

    def copy(self, source, target, slot, device, landing=None):
        return pltpu.make_async_remote_copy(
            src_ref=source,
            dst_ref=target,
            send_sem=self.send.at[slot],
            recv_sem=self.recv.at[slot if landing is None else landing],
            device_id=device,
            device_id_type=MESH,
        )

    def start(self, source, target, slot, device):
        copy = self.copy(source, target, slot, device)
        copy.start()
        self.sent.append(copy)
        return copy

    def finish(self):
        for copy in self.sent:
            copy.wait_send()


def here():
    x, r, c = lax.axis_index("dp"), lax.axis_index("row"), lax.axis_index("col")
    mate = (x, r, c + 1 - 2 * lax.rem(c, 2))
    beside = (1 - x, r, c)
    above = (x, r, lax.rem(c + 2, 4))
    return (x, r, c), mate, beside, above


def seat_of(x, r, c, rows, cols, piece):
    per = cols // rows
    return (x, lax.div(c, per), lax.rem(c, per) * rows + piece)


def home_of(x, r, c, rows, cols, source):
    per = cols // rows
    return (x, source, r * per + lax.div(c, rows))


def greet(devices, count):
    barrier = pltpu.get_barrier_semaphore()
    for device, remote in devices:
        if remote is None:
            pl.semaphore_signal(barrier, inc=1, device_id=device, device_id_type=MESH)
        else:

            @pl.when(remote)
            def _():
                pl.semaphore_signal(barrier, inc=1, device_id=device, device_id_type=MESH)

    pl.semaphore_wait(barrier, count)


COLUMNS = 1024
SWAPS = (2, 4)


def weight_block(source, held, i, form, depth, size):
    if form == "turned":
        at = pl.ds(pl.multiple_of(i * size, size), size)
        return source.at[at, :depth], held.at[at, :]
    return (
        source.at[pl.ds(pl.multiple_of(i * depth, depth), depth), source.shape[1] - size :],
        held.at[:, pl.ds(pl.multiple_of(i * size, size), size)],
    )


def product_into(target, left, held, form, arrive=None):
    width = target.shape[1]
    size = min(COLUMNS, width)

    @pl.loop(0, width // size)
    def _(i):
        if arrive is not None:
            arrive(i, size)
        at = pl.ds(pl.multiple_of(i * size, size), size)
        if form == "turned":
            value = inner_cols(left[...], held[at, :])
        else:
            value = dot(left[...], held[:, at])
        target[:, at] = value.astype(LOW)


class PlaneGather:
    def __init__(self, wires, shard, main, sems, cols):
        (x, _, c), self.mate, self.beside, self.above = here()
        self.wires, self.shard, self.main, self.sems = wires, shard, main, sems
        half = shard.shape[0] // 2
        self.halves = [pl.ds(0, half), pl.ds(half, half)]
        self.spot = x * cols + c
        self.beside_spot, self.above_spot = self.beside[0] * cols + c, x * cols + self.above[2]
        self.corner_spot = self.beside[0] * cols + self.above[2]
        self.kept, self.to_mate, self.from_beside, self.from_above = [], [], [], []

    def start(self, i):
        part, target = self.shard.at[self.halves[i]], self.main.at[self.spot, self.halves[i]]
        self.kept.append(pltpu.make_async_copy(part, target, self.sems.at[i]))
        self.kept[-1].start()
        slot = self.wires.slots(3)
        self.from_beside.append(self.wires.start(part, target, slot, self.beside))
        self.from_above.append(self.wires.start(part, target, slot + 1, self.above))
        self.to_mate.append(self.wires.start(part, target, slot + 2, self.mate))

    def finish(self):
        slot = self.wires.slots(5)
        start, main = self.wires.start, self.main
        self.from_beside[0].wait_recv()
        part = main.at[self.beside_spot, self.halves[0]]
        corner_low = start(part, part, slot, self.above)
        self.from_above[0].wait_recv()
        self.from_above[1].wait_recv()
        part = main.at[self.above_spot, self.halves[1]]
        corner_high = start(part, part, slot + 1, self.beside)
        part = main.at[self.above_spot]
        self.to_mate.append(start(part, part, slot + 2, self.mate))
        self.from_beside[1].wait_recv()
        part = main.at[self.beside_spot]
        self.to_mate.append(start(part, part, slot + 3, self.mate))
        corner_low.wait_recv()
        corner_high.wait_recv()
        part = main.at[self.corner_spot]
        self.to_mate.append(start(part, part, slot + 4, self.mate))
        for copy in self.to_mate:
            copy.wait_recv()
        for copy in self.kept:
            copy.wait()


class Homing:
    def __init__(self, wires, shard, main, sem, rows, cols):
        x, r, c = here()[0]
        self.wires, self.shard, self.main, self.sem, self.rows = wires, shard, main, sem, rows
        self.seats = [seat_of(x, r, c, rows, cols, p) for p in range(rows)]
        self.homes = [home_of(x, r, c, rows, cols, s) for s in range(rows)]
        self.me, self.place = (x, r, c), lax.rem(c, rows)
        self.count, self.block = shard.shape[0], shard.shape[1] // rows

    def away(self, device):
        return jnp.logical_not(jnp.logical_and(device[1] == self.me[1], device[2] == self.me[2]))

    def sends(self):
        mine = pl.ds(pl.multiple_of(self.place * self.count, self.count), self.count)
        for s, home in enumerate(self.homes):
            part = self.shard.at[:, pl.ds(s * self.block, self.block)]
            there = self.wires.copy(part, self.main.at[mine], self.slot + s, home, self.slot + self.place)
            yield self.away(home), there, part, self.main.at[mine]

    def start(self):
        self.slot = self.wires.slots(self.rows)
        for remote, there, part, target in self.sends():
            pl.when(remote)(there.start)
            pl.when(jnp.logical_not(remote))(pltpu.make_async_copy(part, target, self.sem).start)

    def finish(self):
        for p, seat in enumerate(self.seats):
            part = self.main.at[pl.ds(p * self.count, self.count)]
            remote = self.away(seat)
            pl.when(remote)(self.wires.copy(part, part, self.slot + p, seat).wait_recv)
            pl.when(jnp.logical_not(remote))(pltpu.make_async_copy(part, part, self.sem).wait)
        for remote, there, _, _ in self.sends():
            pl.when(remote)(there.wait_send)


class LineSum:
    def __init__(self, wires, part, axis, columns, out, scratch, sems, rows):
        x, r, c = here()[0]
        self.wires, self.out, self.axis, self.rows, self.x, self.r = wires, out, axis, rows, x, r
        self.boxes, self.own, self.other = scratch[:2], scratch[2], scratch[3]
        self.devices = [(x, lax.rem(r + 1, rows), c), (x, lax.rem(r + rows - 1, rows), c)]
        self.beside = (1 - x, r, c)
        self.slot = wires.slots(2 * (rows - 1) + 1)
        size = part.shape[axis] // rows
        blocks = [pl.ds(k * size, size) for k in range(rows)]
        self.loads = [
            pltpu.make_async_copy(
                part.at[at, columns] if axis == 0 else part.at[:, at], self.own.at[k], sems.at[k]
            )
            for k, at in enumerate(blocks)
        ]
        for load in self.loads:
            load.start()

    def greeted(self):
        return [(self.devices[0], self.r < self.rows - 1), (self.devices[1], self.r > 0)]

    def blocks(self, step):
        return [lax.rem(2 * self.rows - step + self.r, self.rows), lax.rem(self.rows + self.r + step, self.rows)]

    def copies(self, step):
        return [
            self.wires.copy(self.own.at[s], box.at[step - 1], self.slot + 2 * (step - 1) + i, device)
            for i, (s, box, device) in enumerate(zip(self.blocks(step), self.boxes, self.devices))
        ]

    def sends(self, step):
        r, rows = self.r, self.rows
        return [(r < step) & (r < rows - 1), (r > rows - 1 - step) & (r > 0)]

    def arrivals(self, step):
        r, rows = self.r, self.rows
        return [(r > 0) & (r <= step), (r < rows - 1) & (r >= rows - 1 - step)]

    def chunk(self):
        rows, width = self.other.shape
        return min(rows, STEP * max(1, 2048 // width))

    def gain(self, step, blocks):
        copies, size = self.copies(step), self.chunk()
        for there, copy, s, box in zip(self.arrivals(step), copies, blocks, self.boxes):

            @pl.when(there)
            def _():
                copy.wait_recv()

                @pl.loop(0, self.other.shape[0] // size)
                def _(i):
                    at = pl.ds(pl.multiple_of(i * size, size), size)
                    total = self.own[s, at, :].astype(jnp.float32)
                    self.own[s, at, :] = (total + box[step - 1, at, :].astype(jnp.float32)).astype(LOW)

    def advance(self, step):
        if step == 1:
            for load in self.loads:
                load.wait()
        else:
            self.gain(step - 1, self.blocks(step))
        for there, copy in zip(self.sends(step), self.copies(step)):
            pl.when(there)(copy.start)

    def complete(self):
        self.gain(self.rows - 1, [self.r, self.r])

    def end(self):
        self.share = self.wires.start(self.own.at[self.r], self.other, self.slot + 2 * self.rows - 2, self.beside)
        self.write(lambda at: self.own[self.r, at, :], self.x)

    def finish(self):
        self.share.wait_recv()
        self.write(lambda at: self.other[at, :], 1 - self.x)
        for step in range(1, self.rows):
            for there, copy in zip(self.sends(step), self.copies(step)):
                pl.when(there)(copy.wait_send)

    def write(self, share, place):
        rows, width = self.other.shape
        size = self.chunk()

        @pl.loop(0, rows // size)
        def _(k):
            at = pl.multiple_of(k * size, size)
            value = share(pl.ds(at, size)).astype(jnp.float32)
            if self.axis == 0:
                self.out[pl.ds(at, size), pl.ds(pl.multiple_of(place * width, width), width)] = value
            else:
                self.out[pl.ds(pl.multiple_of(place * rows + at, size), size), :] = value


def plane_kernel(rows, cols, entry, leave, mid, counts, beside_work, line_axes, totals, form, *refs):
    n_small, n_out, n_swap, n_extra, n_made, n_ship, n_lines = counts
    refs = list(refs)
    big = refs.pop(0)
    weights = refs.pop(0)
    small = [refs.pop(0) for _ in range(n_small)]
    mine_parts = [refs.pop(0) for _ in range(n_swap)]
    extra = [refs.pop(0) for _ in range(n_extra)]
    leaving = [refs.pop(0) for _ in range(n_ship)]
    line_parts = [refs.pop(0) for _ in line_axes]
    main = refs.pop(0)
    outs = [refs.pop(0) for _ in range(n_out)]
    other_parts = [refs.pop(0) for _ in range(n_swap)]
    made = [refs.pop(0) for _ in range(n_made)]
    landing = [refs.pop(0) for _ in range(n_ship)]
    line_outs = [refs.pop(0) for _ in range(sum(n_lines))]
    shard, send, recv, local = (refs.pop(0) for _ in range(4))
    if totals:
        total, inbox, line_inbox = (refs.pop() for _ in range(3))
    line_scratch = [[refs.pop(8) for _ in range(4)] for _ in line_outs]
    wires = Wires(send, recv)
    me, mate, beside, above = here()
    x, r, c = me
    count, width = shard.shape
    half = count // 2
    low_half, high_half = pl.ds(0, half), pl.ds(half, half)
    homing = None
    if leave == "homes":
        homing = Homing(wires, shard, main, local.at[20], rows, cols)
    elif n_ship:
        homing = Homing(wires, leaving[0], landing[0], local.at[22], rows, cols)
    if leave == "gather":
        gather = PlaneGather(wires, shard, main, local.at[pl.ds(20, 2)], cols)
    greeted = []
    expected = 0
    if homing is not None:
        stays = (lax.div(c, cols // rows) == r) & (lax.rem(c, cols // rows) * rows + lax.rem(c, rows) == c)
        greeted += [(s, homing.away(s)) for s in homing.seats]
        expected = expected + rows - jnp.where(stays, 1, 0).astype(jnp.int32)
    lines = []
    for part, axis, pieces in zip(line_parts, line_axes, n_lines):
        for k in range(pieces):
            i, size = len(lines), part.shape[1] // pieces
            sems = local.at[pl.ds(24 + rows * i, rows)]
            columns = slice(k * size, (k + 1) * size)
            lines.append(LineSum(wires, part, axis, columns, line_outs[i], line_scratch[i], sems, rows))
    for line in lines[:1]:
        greeted += line.greeted()
        expected = expected + sum(jnp.where(there, 1, 0).astype(jnp.int32) for _, there in line.greeted())
    if totals:
        others = [(x, lax.rem(r + k, rows), c) for k in range(1, rows)]
        greeted += [(o, None) for o in others]
        expected = expected + rows - 1
    greeted += [(mate, None), (beside, None), (above, None)]
    swaps = []

    def send_swaps(first, last):
        for source, target in zip(mine_parts, other_parts):
            size = source.shape[0] // 4
            if first == last:
                return
            part = pl.ds(first * size, (last - first) * size)
            swaps.append(wires.start(source.at[part], target.at[part], wires.slots(1), beside))

    if entry == "sum":
        depth = big.shape[2]
        block_width = min(COLUMNS, width) if form == "turned" else width * depth // weights.shape[0]

        def fetch(i):
            ends = weight_block(weights, refs[1], i, form, depth, block_width)
            return pltpu.make_async_copy(*ends, local.at[4 + i])

        def arrive(i, size):
            for k in range(size // block_width):
                fetch(i * (size // block_width) + k).wait()

        @pl.loop(0, width // block_width)
        def _(i):
            fetch(i).start()

        chips = [(1 - x, above[2]), (1 - x, c), (x, above[2]), (x, c)]
        loads = [
            pltpu.make_async_copy(big.at[(tx * cols + tc) // 2], refs[0].at[k], local.at[k])
            for k, (tx, tc) in enumerate(chips)
        ]
        for load in loads:
            load.start()
    greet(greeted, expected + 3)
    if n_ship:
        homing.start()
    for line in lines:
        line.advance(1)

    if entry == "sum":
        factors, held_weights, both, mated, beside_pass, above_pass, beside_in, above_in = refs
        first = wires.slots(4)
        handed = []
        core = lax.rem(c, 2)
        own_start = pl.multiple_of(core * count, count)
        given_rows = pl.ds(pl.multiple_of((1 - core) * count, count), count)

        def own_rows(start, size):
            return pl.ds(pl.multiple_of(own_start + start, size), size)

        def supply(k, arrive=None):
            loads[k].wait()
            product_into(both.at[k], factors.at[k], held_weights, form, arrive)
            handed.append(wires.start(both.at[k, given_rows], mated.at[k], first + k, mate))

        def add(k, more, start, size):
            @pl.loop(0, size // STEP)
            def _(i):
                at = own_rows(start + i * STEP, STEP)
                to = pl.ds(pl.multiple_of(start + i * STEP, STEP), STEP)
                both[k, at, :] = (
                    both[k, at, :].astype(jnp.float32) + more(to).astype(jnp.float32)
                ).astype(LOW)

        def merge(k):
            handed[k].wait_recv()
            add(k, lambda at: mated[k, at, :], 0, count)

        own_low, own_high = own_rows(0, half), own_rows(half, half)
        if lines:
            send_swaps(0, SWAPS[0])
            slot = wires.slots(6)
            supply(0, arrive)
            handed[0].wait_recv()
            passes = []
            for k, rows_out in enumerate((own_low, own_high)):
                add(0, lambda at: mated[0, at, :], k * half, half)
                to = above_pass.at[pl.ds(k * half, half)]
                passes.append(wires.start(both.at[0, rows_out], to, slot + k, above))
            supply(1)
            merge(1)
            supply(2)
            merge(2)
            above_low = wires.start(both.at[2, own_low], above_in.at[low_half], slot + 2, above)
            above_high = wires.start(both.at[2, own_high], above_in.at[high_half], slot + 3, above)
            supply(3)
            passes[0].wait_recv()
            add(1, lambda at: above_pass[at, :], 0, half)
            beside_low = wires.start(both.at[1, own_low], beside_in.at[low_half], slot + 4, beside)
            for line in lines:
                line.advance(2)
            passes[1].wait_recv()
            add(1, lambda at: above_pass[at, :], half, half)
            beside_high = wires.start(both.at[1, own_high], beside_in.at[high_half], slot + 5, beside)
            send_swaps(SWAPS[0], SWAPS[1])
            groups = [lines[: len(lines) // 2], lines[len(lines) // 2 :]]
            for line in groups[0]:
                line.advance(3)
        else:
            slot = wires.slots(6)
            supply(0, arrive)
            handed[0].wait_recv()
            add(0, lambda at: mated[0, at, :], 0, half)
            pass_beside = wires.start(both.at[0, own_low], beside_pass, slot, beside)
            add(0, lambda at: mated[0, at, :], half, half)
            pass_above = wires.start(both.at[0, own_high], above_pass, slot + 1, above)
            supply(1)
            merge(1)
            beside_low = wires.start(both.at[1, own_low], beside_in.at[low_half], slot + 2, beside)
            supply(2)
            merge(2)
            pass_beside.wait_recv()
            add(2, lambda at: beside_pass[at, :], 0, half)
            above_low = wires.start(both.at[2, own_low], above_in.at[low_half], slot + 3, above)
            above_high = wires.start(both.at[2, own_high], above_in.at[high_half], slot + 4, above)
            supply(3)
            if beside_work is not None:
                beside_work(0, held_weights, extra, made)
            pass_above.wait_recv()
            add(1, lambda at: above_pass[pl.ds(pl.multiple_of(at.start - half, STEP), STEP), :], half, half)
            beside_high = wires.start(both.at[1, own_high], beside_in.at[high_half], slot + 5, beside)
        if beside_work is not None:
            beside_work(1, held_weights, extra, made)
        handed[3].wait_recv()

        def value(at):
            near = both[3, own_rows(at.start, STEP), :].astype(jnp.float32)
            near = near + mated[3, at, :].astype(jnp.float32)
            return near + (beside_in[at, :].astype(jnp.float32) + above_in[at, :].astype(jnp.float32))

    mid.start(outs)
    for k in range(2):
        if entry == "sum":
            (beside_low, beside_high)[k].wait_recv()
            (above_low, above_high)[k].wait_recv()

        @pl.loop(k * (half // STEP), (k + 1) * (half // STEP))
        def _(i):
            at = pl.ds(pl.multiple_of(i * STEP, STEP), STEP)
            shard[at, :] = mid.rows(at, value(at), small, outs).astype(LOW)

        if leave == "gather":
            gather.start(k)

    if leave == "gather":
        gather.finish()
    elif leave == "homes":
        if not lines:
            homing.start()
    else:
        keep = pltpu.make_async_copy(shard, main, local.at[20])
        keep.start()
    if beside_work is not None:
        beside_work(2, None, extra, made)
    if leave == "stay":
        keep.wait()
    if not lines:
        send_swaps(0, 4)
    if totals and not lines:
        gain_sums(wires, me, (mate, beside, above), others, rows, small[-1], outs, total, inbox, line_inbox)
    for k, group in enumerate(groups if lines else ()):
        for line in group:
            line.complete()
        if k == 0:
            for line in groups[1]:
                line.advance(rows - 1)
            gain_sums(wires, me, (mate, beside, above), others, rows, small[-1], outs, total, inbox, line_inbox)
        else:
            homing.start()
        for line in group:
            line.end()
        if k == 1:
            send_swaps(SWAPS[1], 4)
    if homing is not None:
        homing.finish()
    for line in lines:
        line.finish()
    if n_swap:
        for copy in swaps:
            copy.wait_recv()
    wires.finish()


def enter_kernel(
    rows, cols, hidden_in, grad_out, gains_in, normed, grads, held, grad_here, gains,
    shard, seated, grad_seated, hidden_relay, grad_relay, landing, send, recv, local,
):
    wires = Wires(send, recv)
    me, mate, beside, above = here()
    x, r, c = me
    count, width = seated.shape
    block = width // rows
    side = 2 * lax.div(c, 2)
    far = 2 - side
    ways = [(x, c, side), (x, c, side + 1), (x, above[2], side), (x, above[2], side + 1)]
    via = side + lax.rem(r, 2)
    sources = [(x, s, via) for s in range(rows)]
    others = [(x, lax.rem(r + k, rows), c) for k in range(1, rows)]

    def away(device):
        return jnp.logical_not(jnp.logical_and(device[1] == r, device[2] == c))

    kept = jnp.where(lax.rem(c, 2) == lax.rem(r, 2), 1, 0).astype(jnp.int32)
    greeted = [(s, away(s)) for s in sources] + [(o, None) for o in others]
    greeted += [(above, None), (mate, None), (beside, None)]
    greet(greeted, 2 * rows + 2 - kept)

    mine = pl.ds(pl.multiple_of(r * block, block), block)
    slot = wires.slots(rows - 1)
    spread = [wires.start(gains_in, landing.at[r], slot + k, other) for k, other in enumerate(others)]

    class Seating:
        def __init__(self, source, target, relay, sem):
            self.source, self.target, self.relay, self.sem = source, target, relay, sem
            self.slot, self.hop = wires.slots(rows), wires.slots(1)

        def pieces(self):
            near = pl.multiple_of(side * count, count)
            return [
                self.source.at[pl.ds(near, count)],
                self.source.at[pl.ds(near + count, count)],
                self.relay.at[pl.ds(0, count)],
                self.relay.at[pl.ds(count, count)],
            ]

        def cross(self):
            across = self.source.at[pl.ds(pl.multiple_of(far * count, count), 2 * count)]
            self.crossing = wires.start(across, self.relay, self.hop, above)

        def go(self, which):
            for i in which:
                piece, seat = self.pieces()[i], ways[i]
                there = wires.copy(piece, self.target.at[:, mine], self.slot + i, seat, self.slot + r)
                stay = pltpu.make_async_copy(piece, self.target.at[:, mine], self.sem)
                pl.when(away(seat))(there.start)
                pl.when(jnp.logical_not(away(seat)))(stay.start)

        def arrive(self):
            for s, source in enumerate(sources):
                part = self.target.at[:, pl.ds(s * block, block)]
                arrived = wires.copy(part, part, self.slot + s, source)
                stay = pltpu.make_async_copy(part, part, self.sem)
                pl.when(away(source))(arrived.wait_recv)
                pl.when(jnp.logical_not(away(source)))(stay.wait)

        def sent(self):
            for i, piece in enumerate(self.pieces()):
                there = wires.copy(piece, self.target.at[:, mine], self.slot + i, ways[i])
                pl.when(away(ways[i]))(there.wait_send)

    hidden = Seating(hidden_in, seated, hidden_relay, local.at[0])
    grad = Seating(grad_out, grad_seated, grad_relay, local.at[1])
    hidden.cross()
    hidden.go((0, 1))
    grad.cross()
    hidden.crossing.wait_recv()
    hidden.go((2, 3))
    for copy in spread:
        copy.wait_recv()
    landing[r] = gains_in[...]
    for s in range(rows):
        gains[:, s * block : (s + 1) * block] = landing[s]
    hidden.arrive()
    grad.go((0, 1))
    grad.crossing.wait_recv()
    grad.go((2, 3))
    keep = pltpu.make_async_copy(seated, held, local.at[2])
    keep.start()

    gather = PlaneGather(wires, shard, normed, local.at[pl.ds(4, 2)], cols)
    for k in range(2):

        @pl.loop(k * (count // STEP // 2), (k + 1) * (count // STEP // 2))
        def _(i):
            at = pl.ds(pl.multiple_of(i * STEP, STEP), STEP)
            value = seated[at, :].astype(jnp.float32)
            shard[at, :] = (value * rms_scale(value) * gains[0:1, :]).astype(LOW)

        gather.start(k)
    gather.finish()
    grad.arrive()
    keep_grad = pltpu.make_async_copy(grad_seated, grad_here, local.at[3])
    keep_grad.start()
    gather = PlaneGather(wires, grad_seated, grads, local.at[pl.ds(6, 2)], cols)
    gather.start(0)
    gather.start(1)
    gather.finish()
    hidden.sent()
    grad.sent()
    keep.wait()
    keep_grad.wait()
    wires.finish()


def enter_call(hidden_in, grad_out, gains, collective_id):
    rows, cols, parts = lax.axis_size("row"), lax.axis_size("col"), lax.axis_size("dp")
    count, width = hidden_in.shape[0] // rows, hidden_in.shape[1] * rows
    block = width // rows
    vmem = pl.BlockSpec(memory_space=pltpu.VMEM)
    hbm = pl.BlockSpec(memory_space=pl.ANY)
    shape = jax.ShapeDtypeStruct((count, width), LOW)
    tile = pltpu.VMEM((count, width), LOW)
    relay = pltpu.VMEM((2 * count, block), LOW)
    whole = jax.ShapeDtypeStruct((parts * cols, count, width), LOW)
    normed, grads, held, grad_here, gains = pl.pallas_call(
        functools.partial(enter_kernel, rows, cols),
        out_shape=[whole, whole, shape, shape, jax.ShapeDtypeStruct((8, width), jnp.float32)],
        in_specs=[hbm, hbm, vmem],
        out_specs=[hbm, hbm, hbm, hbm, vmem],
        scratch_shapes=[tile, tile, tile, relay, relay, pltpu.VMEM((rows, 8, block), jnp.float32)]
        + [pltpu.SemaphoreType.DMA((48,))] * 2
        + [pltpu.SemaphoreType.DMA((8,))],
        compiler_params=pltpu.CompilerParams(
            collective_id=collective_id, has_side_effects=True, vmem_limit_bytes=VMEM_LIMIT
        ),
        cost_estimate=pl.CostEstimate(flops=0, bytes_accessed=20_000_000, transcendentals=0),
    )(hidden_in, grad_out, gains)
    flat = (parts * cols * count, width)
    return normed.reshape(flat), grads.reshape(flat), held, grad_here, gains


def enter_plain(hidden_in, grad_out, gains, collective_id):
    gains = lax.all_gather(gains, "row", axis=1, tiled=True)
    held = to_group(hidden_in)
    value = held.astype(jnp.float32)
    normed = group_gather((value * rms_scale(value) * gains[0:1]).astype(LOW))
    grad_here = to_group(grad_out)
    return normed, group_gather(grad_here), held, grad_here, gains


def gain_sums(wires, me, partners, others, rows, gain_two, outs, total, inbox, line_inbox):
    x, r, c = me
    block = total.shape[1] // rows
    total[0:1, :] = jnp.sum(outs[1][...], axis=0, keepdims=True)
    total[1:2, :] = jnp.sum(gain_two[...], axis=0, keepdims=True)
    total[2:, :] = jnp.zeros_like(total[2:, :])
    first = wires.slots(len(partners))
    for k, partner in enumerate(partners):
        copy = wires.copy(total, inbox.at[k], first + k, partner)
        copy.start()
        copy.wait()
        total[...] += inbox[k]
    first = wires.slots(len(others))
    copies = []
    for k, (_, row, _) in enumerate(others):
        part = total.at[:, pl.ds(pl.multiple_of(row * block, block), block)]
        copies.append(wires.start(part, line_inbox.at[r], first + k, others[k]))
    line_inbox[r] = total[:, pl.ds(pl.multiple_of(r * block, block), block)]
    for copy in copies:
        copy.wait_recv()
    outs[0][...] = sum(line_inbox[k] for k in range(rows))


def plane_call(
    entry, leave, mid, big, small, outs, collective_id, weights=None, form=None, totals=False, swap=(),
    beside_work=None, extra=(), made=(), ship=(), line=(), line_axes=(), line_pieces=(),
):
    rows, cols, parts = lax.axis_size("row"), lax.axis_size("col"), lax.axis_size("dp")
    count, width = big.shape[0] // (parts * cols), small[0].shape[1]
    depth = big.shape[1]
    big = big.reshape(parts * cols // 2, 2 * count, depth)
    gathered = leave == "gather"
    shape = {"gather": (parts * cols, count, width), "homes": (rows * count, width // rows), "stay": (count, width)}[leave]
    landed = [jax.ShapeDtypeStruct((rows * a.shape[0], a.shape[1] // rows), a.dtype) for a in ship]
    plain = len(swap) + len(made) + len(ship)
    vmem = pl.BlockSpec(memory_space=pltpu.VMEM)
    hbm = pl.BlockSpec(memory_space=pl.ANY)
    tile = pltpu.VMEM((count, width), LOW)
    whole, part = pltpu.VMEM((4, count, width), LOW), pltpu.VMEM((count // 2, width), LOW)
    scratch = [tile, pltpu.SemaphoreType.DMA((64,)), pltpu.SemaphoreType.DMA((64,)), pltpu.SemaphoreType.DMA((40,))]
    scratch += [
        pltpu.VMEM(big.shape, LOW),
        pltpu.VMEM((width, depth) if form == "turned" else (depth, width), LOW),
        pltpu.VMEM((4, 2 * count, width), LOW),
    ]
    scratch += [whole, part, tile if line else part, tile, tile]
    line_outs = []
    for array, axis, pieces in zip(line, line_axes, line_pieces):
        block = [n // rows if i == axis else n for i, n in enumerate(array.shape)]
        block[1] //= pieces
        scratch += ([pltpu.VMEM((n, *block), LOW) for n in (rows - 1, rows - 1, rows)] + [pltpu.VMEM(tuple(block), LOW)]) * pieces
        block[1 - axis] *= parts
        line_outs += [jax.ShapeDtypeStruct(tuple(block), jnp.float32)] * pieces
    if totals:
        scratch += [
            pltpu.VMEM((rows, 8, width // rows), jnp.float32),
            pltpu.VMEM((3, 8, width), jnp.float32),
            pltpu.VMEM((8, width), jnp.float32),
        ]
    counts = (len(small), len(outs), len(swap), len(extra), len(made), len(ship), tuple(line_pieces))
    main, *others = pl.pallas_call(
        functools.partial(plane_kernel, rows, cols, entry, leave, mid, counts, beside_work, line_axes, totals, form),
        out_shape=[jax.ShapeDtypeStruct(shape, LOW)]
        + list(outs)
        + [jax.ShapeDtypeStruct(m.shape, m.dtype) for m in (*swap, *made, *landed, *line_outs)],
        in_specs=[hbm, hbm] + [vmem] * len(small) + [hbm] * (len(swap) + len(extra) + len(ship) + len(line)),
        out_specs=[hbm] + [vmem] * len(outs) + [hbm] * plain + [vmem] * len(line_outs),
        scratch_shapes=scratch,
        compiler_params=pltpu.CompilerParams(
            collective_id=collective_id, has_side_effects=True, vmem_limit_bytes=VMEM_LIMIT
        ),
        cost_estimate=pl.CostEstimate(flops=0, bytes_accessed=20_000_000, transcendentals=0),
    )(big, weights, *small, *swap, *extra, *ship, *line)
    if gathered:
        main = main.reshape(parts * cols * count, width)
    return [main, *others]


def fold(values):
    return values.reshape(values.shape[0] // 8, 8, values.shape[1]).sum(0)


class Mid:
    @staticmethod
    def start(outs):
        pass


class SecondNorm(Mid):
    @staticmethod
    def rows(at, value, small, outs):
        held, gains = small
        middle = held[at, :].astype(jnp.float32) + value
        outs[0][at, :] = middle
        return middle * rms_scale(middle) * gains[1:2, :]


class Add(Mid):
    @staticmethod
    def rows(at, value, small, outs):
        return small[0][at, :] + value


class BackSecond(Mid):
    @staticmethod
    def start(outs):
        outs[1][...] = jnp.zeros_like(outs[1])

    @staticmethod
    def rows(at, value, small, outs):
        middle, grad_out, gains = small
        middle = middle[at, :]
        scale = rms_scale(middle)
        outs[1][...] += fold(value * middle * scale)
        grad = grad_out[at, :].astype(jnp.float32) + norm_back(
            middle, scale, value * gains[1:2, :]
        )
        outs[0][at, :] = grad
        return grad


class BackFirst(Mid):
    @staticmethod
    def start(outs):
        outs[1][...] = jnp.zeros_like(outs[1])

    @staticmethod
    def rows(at, value, small, outs):
        held, grad_middle, gains = small[:3]
        inputs = held[at, :].astype(jnp.float32)
        scale = rms_scale(inputs)
        outs[1][...] += fold(value * inputs * scale)
        return grad_middle[at, :] + norm_back(inputs, scale, value * gains[0:1, :])


def plain_call(
    entry, leave, mid, big, small, outs, collective_id, weights=None, form=None, totals=False, swap=(),
    beside_work=None, extra=(), made=(), ship=(), line=(), line_axes=(), line_pieces=(),
):
    refs = [Holder(a) for a in small]
    given = [Holder(jnp.zeros(o.shape, o.dtype)) for o in outs]
    depth, width = big.shape[1], small[0].shape[1]
    if form == "turned":
        product = inner_cols(big, weights[:, :depth])
    else:
        block = width * depth // weights.shape[0]
        whole = unstack(weights[:, weights.shape[1] - block :], depth)
        product = dot(big, whole)
    mid.start(given)
    shard = mid.rows(slice(None), group_scatter(product), refs, given).astype(LOW)
    main = {"gather": group_gather, "homes": from_group, "stay": lambda a: a}[leave](shard)
    if totals:
        sums = jnp.stack([given[1].value.sum(0), small[-1].sum(0)])
        sums = jnp.pad(lax.psum(sums, ("dp", "row", "col")), ((0, 6), (0, 0)))
        part = outs[0].shape[1]
        given[0].value = lax.dynamic_slice_in_dim(sums, lax.axis_index("row") * part, part, 1)
    others = [dp_other(m) for m in swap]
    if beside_work is not None:
        grads, slope_up, gated, tokens = extra
        lifted = lift_back_plain(grads, whole, slope_up, gated)
        others += [lifted, inner_rows(tokens, lifted).astype(LOW)]
    others += [from_group(a) for a in ship]
    for array, axis, pieces in zip(line, line_axes, line_pieces):
        mine = row_sum(array, axis)
        other = dp_other(mine)
        others += join_tall(mine, other, [(i,) for i in range(pieces)]) if axis == 0 else [join_wide(mine, other)]
    return [main] + [g.value for g in given] + others


class Holder:
    def __init__(self, value):
        self.value, self.dtype, self.shape = value, value.dtype, value.shape

    def __getitem__(self, at):
        return self.value[at]

    def __setitem__(self, at, value):
        self.value = self.value.at[at].set(value)


def swap_halves(values, first):
    lanes = values.shape[1]
    half = HEAD_DIM // 2
    return jnp.where(first, pltpu.roll(values, lanes - half, 1), pltpu.roll(values, half, 1))


def attend_kernel(query, key, value, cosine, sine, mixed, q_out, k_out, v_out, logsum):
    length, lanes = query.shape
    block = min(256, length)
    lane = lax.broadcasted_iota(jnp.int32, (length, lanes), 1)
    first = lax.rem(lane, HEAD_DIM) < HEAD_DIM // 2
    cos, sin = cosine[...], sine[...]

    def rotate(values):
        return (values * cos + swap_halves(values, first) * sin).astype(LOW)

    q_out[...] = rotate(query[...])
    k_out[...] = rotate(key[...])
    low_values = value[...].astype(LOW)
    v_out[...] = low_values
    v_turned = low_values.astype(jnp.float32).T.astype(LOW)
    head = lax.broadcasted_iota(jnp.int32, (block, lanes), 1) // HEAD_DIM
    keep = lax.broadcasted_iota(jnp.int32, (block, block), 0) <= lax.broadcasted_iota(
        jnp.int32, (block, block), 1
    )
    for j in range(length // block):
        at = slice(j * block, (j + 1) * block)
        q_block = q_out[at, :].astype(jnp.float32) * HEAD_DIM ** (-0.5)
        parts = []
        for h in range(lanes // HEAD_DIM):
            q_head = jnp.where(head == h, q_block, 0.0).astype(LOW)
            near = jnp.where(keep, inner_cols(k_out[at, :], q_head), -jnp.inf)
            highest = jnp.max(near, axis=0, keepdims=True)
            if j:
                far = inner_cols(k_out[: j * block, :], q_head)
                highest = jnp.maximum(highest, jnp.max(far, axis=0, keepdims=True))
                far = jnp.exp(far - highest)
            near = jnp.exp(near - highest)
            total = jnp.sum(near, axis=0, keepdims=True)
            if j:
                total = total + jnp.sum(far, axis=0, keepdims=True)
            logsum[0, 0, h : h + 1, at] = highest + jnp.log(total)
            share = 1.0 / total
            out = dot(v_turned[:, at], (near * share).astype(LOW))
            if j:
                out = out + dot(v_turned[:, : j * block], (far * share).astype(LOW))
            parts.append(out[h * HEAD_DIM : (h + 1) * HEAD_DIM])
        mixed[at, :] = jnp.concatenate(parts, 0).T.astype(LOW)


def attend_back_kernel(n_swap, query, key, value, grad, logsum, cosine, sine, *refs):
    mine_parts, refs = refs[:n_swap], refs[n_swap:]
    made, refs = refs[0], refs[1:]
    other_parts, refs = refs[:n_swap], refs[n_swap:]
    (k_sum, v_sum, q_out, k_out, v_out, out_sems), refs = refs[:6], refs[6:]
    length, lanes = query.shape
    if n_swap:
        beside = here()[2]
        wires = Wires(*refs)
        swaps = [
            wires.copy(source, target, i, beside)
            for i, (source, target) in enumerate(zip(mine_parts, other_parts))
        ]
        here_first = (pl.program_id(0) == 0) & (pl.program_id(1) == 0)
        here_last = (pl.program_id(0) == pl.num_programs(0) - 1) & (
            pl.program_id(1) == pl.num_programs(1) - 1
        )

        @pl.when(here_first)
        def _():
            greet([(beside, None)], 1)
            for copy in swaps:
                copy.start()

    block = min(256, length)
    k_sum[...] = jnp.zeros_like(k_sum)
    v_sum[...] = jnp.zeros_like(v_sum)
    k_turned = key[...].astype(jnp.float32).T.astype(LOW)
    head = lax.broadcasted_iota(jnp.int32, (block, lanes), 1) // HEAD_DIM
    keep = lax.broadcasted_iota(jnp.int32, (block, block), 0) <= lax.broadcasted_iota(
        jnp.int32, (block, block), 1
    )
    scale = HEAD_DIM ** (-0.5)

    def rotate_back(values, at):
        rows = values.shape[0]
        lane = lax.broadcasted_iota(jnp.int32, (rows, lanes), 1)
        first = lax.rem(lane, HEAD_DIM) < HEAD_DIM // 2
        return (values * cosine[at, :] - swap_halves(values, first) * sine[at, :]).astype(LOW)

    for j in range(length // block):
        at = slice(j * block, (j + 1) * block)
        before = slice(0, j * block)
        q_block = query[at, :].astype(jnp.float32) * scale
        g_block = grad[at, :].astype(jnp.float32)
        parts = []
        for h in range(lanes // HEAD_DIM):
            q_head = jnp.where(head == h, q_block, 0.0).astype(LOW)
            g_head = jnp.where(head == h, g_block, 0.0).astype(LOW)
            level = logsum[0, 0, h : h + 1, at]
            near = jnp.exp(jnp.where(keep, inner_cols(key[at, :], q_head), -jnp.inf) - level)
            d_near = inner_cols(value[at, :], g_head)
            inner = jnp.sum(near * d_near, axis=0, keepdims=True)
            if j:
                far = jnp.exp(inner_cols(key[before, :], q_head) - level)
                d_far = inner_cols(value[before, :], g_head)
                inner = inner + jnp.sum(far * d_far, axis=0, keepdims=True)
                v_sum[before, :] += dot(far.astype(LOW), g_head)
                s_far = (far * (d_far - inner)).astype(LOW)
                k_sum[before, :] += dot(s_far, q_head)
            v_sum[at, :] += dot(near.astype(LOW), g_head)
            s_near = (near * (d_near - inner)).astype(LOW)
            k_sum[at, :] += dot(s_near, q_head)
            out = dot(k_turned[:, at], s_near)
            if j:
                out = out + dot(k_turned[:, before], s_far)
            parts.append(out[h * HEAD_DIM : (h + 1) * HEAD_DIM])
        q_out[at, :] = rotate_back(jnp.concatenate(parts, 0).T * scale, at)
    k_out[...] = rotate_back(k_sum[...], slice(None))
    v_out[...] = v_sum[...].astype(LOW)
    rows_at = pl.ds(pl.multiple_of(pl.program_id(0) * length, length), length)
    columns = made.shape[1] // 3
    copies = [
        pltpu.make_async_copy(
            out,
            made.at[rows_at, pl.ds(pl.multiple_of(i * columns + pl.program_id(1) * lanes, lanes), lanes)],
            out_sems.at[i],
        )
        for i, out in enumerate((q_out, k_out, v_out))
    ]
    for copy in copies:
        copy.start()
    for copy in copies:
        copy.wait()
    if n_swap:

        @pl.when(here_last)
        def _():
            for copy in swaps:
                copy.wait()


def pair_tables(length):
    half = HEAD_DIM // 2
    freq = THETA ** (-(jnp.arange(half, dtype=jnp.float32) * 2.0 / HEAD_DIM))
    angle = jnp.arange(length, dtype=jnp.float32)[:, None] * freq[None, :]
    cosine, sine = jnp.cos(angle), jnp.sin(angle)
    return jnp.tile(cosine, (1, 4)), jnp.tile(jnp.concatenate([-sine, sine], 1), (1, 2))


def attend_pairs(projected, sequences):
    tokens, columns = projected.shape[0], projected.shape[1] // 3
    length, lanes = tokens // sequences, 2 * HEAD_DIM
    pairs = columns // lanes
    cosine, sine = pair_tables(length)

    def spec(offset):
        return pl.BlockSpec((length, lanes), lambda s, h: (s, offset + h))

    table = pl.BlockSpec((length, lanes), lambda s, h: (0, 0))
    level = pl.BlockSpec((1, 1, 2, length), lambda s, h: (s, h, 0, 0))
    shape = jax.ShapeDtypeStruct((tokens, columns), LOW)
    return pl.pallas_call(
        attend_kernel,
        grid=(sequences, pairs),
        in_specs=[spec(0), spec(pairs), spec(2 * pairs), table, table],
        out_specs=[spec(0)] * 4 + [level],
        out_shape=[shape] * 4 + [jax.ShapeDtypeStruct((sequences, pairs, 2, length), jnp.float32)],
        compiler_params=pltpu.CompilerParams(vmem_limit_bytes=VMEM_LIMIT),
        cost_estimate=pl.CostEstimate(
            flops=8 * tokens * length * columns, bytes_accessed=100_000_000, transcendentals=0
        ),
    )(projected, projected, projected, cosine, sine)


def attend_pairs_back(query, keys, values, grad_mixed, logsum, sequences, swap, collective_id):
    tokens, columns = query.shape
    length, lanes = tokens // sequences, 2 * HEAD_DIM
    pairs = columns // lanes
    cosine, sine = pair_tables(length)
    spec = pl.BlockSpec((length, lanes), lambda s, h: (s, h))
    table = pl.BlockSpec((length, lanes), lambda s, h: (0, 0))
    level = pl.BlockSpec((1, 1, 2, length), lambda s, h: (s, h, 0, 0))
    hbm = pl.BlockSpec(memory_space=pl.ANY)
    return pl.pallas_call(
        functools.partial(attend_back_kernel, len(swap)),
        grid=(sequences, pairs),
        in_specs=[spec] * 4 + [level, table, table] + [hbm] * len(swap),
        out_specs=[hbm] * (1 + len(swap)),
        out_shape=[jax.ShapeDtypeStruct((tokens, 3 * columns), LOW)] + [jax.ShapeDtypeStruct(m.shape, m.dtype) for m in swap],
        scratch_shapes=[pltpu.VMEM((length, lanes), jnp.float32)] * 2
        + [pltpu.VMEM((length, lanes), LOW)] * 3
        + [pltpu.SemaphoreType.DMA((4,))] * 3,
        compiler_params=pltpu.CompilerParams(
            collective_id=collective_id, has_side_effects=True, vmem_limit_bytes=VMEM_LIMIT
        ),
        cost_estimate=pl.CostEstimate(
            flops=20 * tokens * length * columns, bytes_accessed=60_000_000, transcendentals=0
        ),
    )(query, keys, values, grad_mixed, logsum, cosine, sine, *swap)


def lift_kernel(tokens, weights, activated, slope_up, gated):
    rows, width = activated.shape
    step = min(256, rows)
    for i in range(rows // step):
        at = slice(i * step, (i + 1) * step)
        left = tokens[at, :]
        gate, upward = dot(left, weights[:, :width]), dot(left, weights[:, width:])
        sigmoid = 1.0 / (1.0 + jnp.exp(-gate))
        passed = gate * sigmoid
        activated[at, :] = (passed * upward).astype(LOW)
        gated[at, :] = passed.astype(LOW)
        slope_up[at, :] = (upward * (sigmoid + passed * (1.0 - sigmoid))).astype(LOW)


def lift(tokens, weights):
    count, width = tokens.shape
    units = weights.shape[1] // 2
    tile, rows = units // 2, min(512, count)
    out = pl.BlockSpec((rows, tile), lambda j, i: (i, j))
    shape = jax.ShapeDtypeStruct((count, units), LOW)
    return pl.pallas_call(
        lift_kernel,
        grid=(2, count // rows),
        in_specs=[
            pl.BlockSpec((rows, width), lambda j, i: (i, 0)),
            pl.BlockSpec((width, 2 * tile), lambda j, i: (0, j)),
        ],
        out_specs=[out] * 3,
        out_shape=[shape] * 3,
        compiler_params=pltpu.CompilerParams(vmem_limit_bytes=VMEM_LIMIT),
        cost_estimate=pl.CostEstimate(
            flops=4 * count * width * units, bytes_accessed=30_000_000, transcendentals=0
        ),
    )(tokens, weights)


def lift_back_rows(weights, grads, slope_up, gated, lifted):
    units = slope_up.shape[1]
    tile = units // 2
    for j in range(2):
        here_units = slice(j * tile, (j + 1) * tile)
        grad = inner_cols(grads[...], weights[here_units, :])
        start = 2 * j * tile
        lifted[:, start : start + tile] = (grad * slope_up[:, here_units].astype(jnp.float32)).astype(LOW)
        lifted[:, start + tile : start + 2 * tile] = (
            grad * gated[:, here_units].astype(jnp.float32)
        ).astype(LOW)


def lift_back_work(stage, weights, extra, made):
    grads, slope_up, gated, tokens = extra
    lifted, grad_weights = made
    count, units = slope_up.shape
    width = tokens.shape[1]
    if stage < 2:
        rows = count // 4
        first = stage * (count // 2)
        at = pl.ds(first, count // 2)
        pltpu.emit_pipeline(
            functools.partial(lift_back_rows, weights),
            grid=(2,),
            in_specs=[
                pl.BlockSpec((rows, width), lambda i: (i, 0)),
                pl.BlockSpec((rows, units), lambda i: (i, 0)),
                pl.BlockSpec((rows, units), lambda i: (i, 0)),
            ],
            out_specs=[pl.BlockSpec((rows, 2 * units), lambda i: (i, 0))],
        )(grads.at[at], slope_up.at[at], gated.at[at], lifted.at[at])

    def inner(left, right, out):
        out[...] = inner_rows(left[...], right[...]).astype(LOW)

    if stage > 0:
        part, tile = width // 2, units // 2
        part_units = pl.ds((stage - 1) * units, units)
        pltpu.emit_pipeline(
            inner,
            grid=(2, 2),
            in_specs=[
                pl.BlockSpec((count, part), lambda i, j: (0, i)),
                pl.BlockSpec((count, tile), lambda i, j: (0, j)),
            ],
            out_specs=[pl.BlockSpec((part, tile), lambda i, j: (i, j))],
        )(tokens, lifted.at[:, part_units], grad_weights.at[:, part_units])


def lift_back_plain(grads, weights, slope_up, gated):
    grad = inner_cols(grads, weights)
    up, through = (grad * f.astype(jnp.float32) for f in (slope_up, gated))
    return pair_units(up, through).astype(LOW)


def attend_plain(projected, sequences):
    tokens, columns = projected.shape[0], projected.shape[1] // 3
    length = tokens // sequences
    shape = (sequences, length, columns // HEAD_DIM, HEAD_DIM)
    cosine, sine = rotation_tables(length)
    query = turn(projected[:, :columns].reshape(shape), cosine, sine).astype(LOW)
    keys = turn(projected[:, columns : 2 * columns].reshape(shape), cosine, sine).astype(LOW)
    values = projected[:, 2 * columns :].reshape(shape).astype(LOW)
    mixed, logsum = attend(query, keys, values)
    flat = (tokens, columns)
    return mixed.reshape(flat), query.reshape(flat), keys.reshape(flat), values.reshape(flat), logsum


def attend_plain_back(query, keys, values, grad_mixed, logsum, sequences, swap, collective_id):
    tokens, columns = query.shape
    length = tokens // sequences
    shape = (sequences, length, columns // HEAD_DIM, HEAD_DIM)
    cosine, sine = rotation_tables(length)
    grad_query, grad_keys, grad_values = attend_back(
        *(a.reshape(shape) for a in (query, keys, values, grad_mixed)), logsum
    )
    grads = (turn_back(grad_query, cosine, sine), turn_back(grad_keys, cosine, sine), grad_values)
    grads = jnp.concatenate([g.reshape(tokens, columns).astype(LOW) for g in grads], 1)
    return [grads] + [dp_other(m) for m in swap]


def body(
    hidden_in, w_query, w_key, w_value, w_out, w_gate, w_up, w_down, norm_attn, norm_ffn, grad_out
):
    rows, cols, parts = lax.axis_size("row"), lax.axis_size("col"), lax.axis_size("dp")
    own_kernels = (parts, rows, cols) == (2, 4, 4)
    plane, enter = (plane_call, enter_call) if own_kernels else (plain_call, enter_plain)
    count, width = hidden_in.shape[0] // rows, hidden_in.shape[1] * rows
    full_rows = jax.ShapeDtypeStruct((count, width), jnp.float32)
    gain_rows = jax.ShapeDtypeStruct((8, width), jnp.float32)

    local_gains = jnp.pad(jnp.stack([norm_attn, norm_ffn]), ((0, 6), (0, 0)))
    own_attn = [my_part(w, 1) for w in (w_query, w_key, w_value)] + [stack(my_part(w_out, 0))]
    w_attn = lax.all_gather(jnp.concatenate(own_attn, 1), "row", axis=0, tiled=True)
    normed_one, grad_wide, held, grad_here, gains = enter(hidden_in, grad_out, local_gains, 1)
    own_ffn = pair_units(my_part(w_gate, 1), my_part(w_up, 1))
    w_ffn = lax.all_gather(own_ffn, "row", axis=0, tiled=True)
    w_back = lax.all_gather(my_part(w_down, 0), "row", axis=0, tiled=True)

    columns = w_attn.shape[1] // 4
    projected = dot(normed_one, w_attn[:, : 3 * columns])
    paired = columns % (2 * HEAD_DIM) == 0
    mixed, query, keys, values, logsum = (attend_pairs if paired else attend_plain)(projected, parts)
    normed_two, middle = plane(
        "sum", "gather", SecondNorm, mixed, [held, gains], [full_rows], 2, w_attn, "stacked"
    )

    w_proj, w_ffn = after(unstack(w_attn[:, 3 * columns :], columns), w_ffn)
    activated, slope_up, gated = lift(normed_two, w_ffn)
    part_down, w_back = after(inner_rows(activated, grad_wide).astype(LOW), w_back)
    mine_down = row_sum(part_down, 1)
    low = functools.partial(jax.ShapeDtypeStruct, dtype=LOW)
    out_rows, grad_lifted, part_ffn = plane(
        "sum",
        "stay",
        Add,
        activated,
        [middle],
        [],
        3,
        w_back,
        "stacked",
        beside_work=lift_back_work,
        extra=[grad_wide, slope_up, gated, normed_two],
        made=[low((normed_two.shape[0], w_ffn.shape[1])), low((width, w_ffn.shape[1]))],
    )
    mine_ffn = row_sum(part_ffn, 0)
    grad_branch, grad_middle, gain_two, layer_out = plane(
        "sum",
        "gather",
        BackSecond,
        grad_lifted,
        [middle, grad_here, gains],
        [full_rows, gain_rows],
        4,
        w_ffn,
        "turned",
        ship=[out_rows],
    )
    grad_branch, mine_down = after(grad_branch, mine_down)
    grad_mixed = inner_cols(grad_branch, w_proj).astype(LOW)
    part_out, grad_mixed = after(inner_rows(mixed, grad_branch).astype(LOW), grad_mixed)
    grad_projected, other_down = (attend_pairs_back if paired else attend_plain_back)(
        query, keys, values, grad_mixed, logsum, parts, [mine_down], 5
    )
    part_attn = inner_rows(normed_one, grad_projected).astype(LOW)
    grad_in, gain_grads, _, other_ffn, grad_wq, grad_wk, grad_wv, grad_attn_out = plane(
        "sum",
        "homes",
        BackFirst,
        grad_projected,
        [held, grad_middle, gains, gain_two],
        [jax.ShapeDtypeStruct((8, norm_attn.shape[0]), jnp.float32), gain_rows],
        6,
        w_attn,
        "turned",
        totals=True,
        swap=[mine_ffn],
        line=[part_attn, part_out],
        line_axes=(0, 1),
        line_pieces=(3, 1),
    )
    grad_down = join_wide(mine_down, other_down)
    grad_gate, grad_up = join_tall(mine_ffn, other_ffn, [(0, 2), (1, 3)])
    return (
        layer_out,
        grad_in,
        grad_wq,
        grad_wk,
        grad_wv,
        grad_attn_out,
        grad_gate,
        grad_up,
        grad_down,
        gain_grads[0],
        gain_grads[1],
    )


def solution(mesh):
    tokens = P(("dp", "col"), "row")
    tall = P("row", "col")
    wide = P("col", "row")
    gain = P("row")
    return jax.shard_map(
        body,
        mesh=mesh,
        in_specs=(tokens, tall, tall, tall, wide, tall, tall, wide, gain, gain, tokens),
        out_specs=(tokens, tokens, tall, tall, tall, wide, tall, tall, wide, gain, gain),
        check_vma=False,
    )
```

```python
import functools

import jax
import jax.numpy as jnp
from jax import lax
from jax.experimental import pallas as pl
from jax.experimental.pallas import tpu as pltpu
from jax.sharding import PartitionSpec as P

HEAD_DIM = 64
EPSILON = 1e-05
THETA = 130000.0
GROUP = ("dp", "col")
LOW = jnp.bfloat16


def dot(left, right):
    return jnp.dot(left, right, preferred_element_type=jnp.float32)


def inner_rows(left, right):
    return lax.dot_general(
        left, right, (((0,), (0,)), ((), ())), preferred_element_type=jnp.float32
    )


def inner_cols(left, right):
    return lax.dot_general(
        left, right, (((1,), (1,)), ((), ())), preferred_element_type=jnp.float32
    )


def seat_pairs():
    rows, cols = lax.axis_size("row"), lax.axis_size("col")
    per = cols // rows
    return [
        (r * cols + c, (c // per) * cols + (c % per) * rows + r)
        for r in range(rows)
        for c in range(cols)
    ]


def to_group(block):
    whole = lax.all_to_all(block, "row", split_axis=0, concat_axis=1, tiled=True)
    return lax.ppermute(whole, ("row", "col"), seat_pairs())


def from_group(block):
    back = lax.ppermute(block, ("row", "col"), [(b, a) for a, b in seat_pairs()])
    return lax.all_to_all(back, "row", split_axis=1, concat_axis=0, tiled=True)


def group_gather(shard):
    return lax.all_gather(shard, GROUP, axis=0, tiled=True)


def group_scatter(partial):
    return lax.psum_scatter(
        partial.astype(LOW), GROUP, scatter_dimension=0, tiled=True
    ).astype(jnp.float32)


def my_part(block, axis):
    size = block.shape[axis] // lax.axis_size("dp")
    return lax.dynamic_slice_in_dim(block, lax.axis_index("dp") * size, size, axis)


def halves(block):
    middle = block.shape[1] // 2
    return [block[:, :middle], block[:, middle:]]


def pair_units(gate, upward):
    (g, h), (u, v) = halves(gate), halves(upward)
    return jnp.concatenate([g, u, h, v], 1)


def stack(block):
    units = block.shape[0]
    return jnp.concatenate([block[:, i : i + units] for i in range(0, block.shape[1], units)], 0)


def unstack(blocks, units):
    return jnp.concatenate([blocks[i : i + units] for i in range(0, blocks.shape[0], units)], 1)


def after(*values):
    return lax.optimization_barrier(values)


def pass_on(block, way, first):
    rows = lax.axis_size("row")
    pairs = [(i, i + 1) for i in range(first, rows - 1)]
    if way < 0:
        pairs = [(rows - 1 - i, rows - 1 - j) for i, j in pairs]
    return lax.ppermute(block, "row", pairs)


def dp_other(mine):
    if lax.axis_size("dp") == 2:
        return lax.ppermute(mine, "dp", [(0, 1), (1, 0)])
    return lax.all_gather(mine, "dp", axis=0)


def dp_parts(mine, other):
    if lax.axis_size("dp") != 2:
        return list(other)
    lower = lax.axis_index("dp") == 0
    return [jnp.where(lower, mine, other), jnp.where(lower, other, mine)]


def row_sum(part, axis):
    return lax.psum_scatter(part, "row", scatter_dimension=axis, tiled=True)


def join_tall(mine, other, pieces):
    width = mine.shape[1] // sum(map(len, pieces))
    cuts = [slice(i * width, (i + 1) * width) for i in range(mine.shape[1] // width)]
    cut = [dp_parts(mine[:, at], other[..., at]) for at in cuts]
    return [
        jnp.concatenate([cut[i][d] for d in range(len(cut[0])) for i in piece], 1).astype(jnp.float32)
        for piece in pieces
    ]


def join_wide(mine, other):
    return jnp.concatenate(dp_parts(mine, other), 0).astype(jnp.float32)


def rms_scale(values):
    return lax.rsqrt(jnp.mean(values * values, axis=1, keepdims=True) + EPSILON)


def norm_back(values, scale, weighted):
    inner = jnp.mean(weighted * values, axis=1, keepdims=True)
    return scale * weighted - values * (scale * scale * scale * inner)


def rotation_tables(length):
    half = HEAD_DIM // 2
    freq = THETA ** (-(jnp.arange(half, dtype=jnp.float32) * 2.0 / HEAD_DIM))
    angle = jnp.arange(length, dtype=jnp.float32)[:, None] * freq[None, :]
    cosine = jnp.concatenate([jnp.cos(angle), jnp.cos(angle)], 1)[None, :, None, :]
    sine = jnp.concatenate([jnp.sin(angle), jnp.sin(angle)], 1)[None, :, None, :]
    return (cosine, sine)


def turn(values, cosine, sine):
    half = values.shape[-1] // 2
    turned = jnp.concatenate([-values[..., half:], values[..., :half]], -1)
    return values * cosine + turned * sine


def turn_back(grads, cosine, sine):
    half = grads.shape[-1] // 2
    moved = grads * sine
    return grads * cosine + jnp.concatenate([moved[..., half:], -moved[..., :half]], -1)


def masked_scores(query, keys):
    scores = jnp.einsum(
        "sqhd,skhd->shqk", query, keys, preferred_element_type=jnp.float32
    ) * HEAD_DIM ** (-0.5)
    length = query.shape[1]
    allowed = jnp.arange(length)[:, None] >= jnp.arange(length)[None, :]
    return jnp.where(allowed[None, None], scores, -jnp.inf)


def attend(query, keys, values):
    scores = masked_scores(query, keys)
    highest = jnp.max(scores, axis=-1, keepdims=True)
    expo = jnp.exp(scores - highest)
    total = jnp.sum(expo, axis=-1, keepdims=True)
    low_probs = (expo / total).astype(LOW)
    mixed = jnp.einsum(
        "shqk,skhd->sqhd", low_probs, values, preferred_element_type=jnp.float32
    ).astype(LOW)
    return mixed, highest + jnp.log(total)


def attend_back(query, keys, values, grad_mixed, logsum):
    scale = HEAD_DIM ** (-0.5)
    probs = jnp.exp(masked_scores(query, keys) - logsum)
    low_probs = probs.astype(LOW)
    dprobs = jnp.einsum("sqhd,skhd->shqk", grad_mixed, values, preferred_element_type=jnp.float32)
    grad_values = jnp.einsum(
        "shqk,sqhd->skhd", low_probs, grad_mixed, preferred_element_type=jnp.float32
    )
    low_scores = (probs * (dprobs - jnp.sum(probs * dprobs, axis=-1, keepdims=True))).astype(LOW)
    grad_query = (
        jnp.einsum("shqk,skhd->sqhd", low_scores, keys, preferred_element_type=jnp.float32) * scale
    )
    grad_keys = (
        jnp.einsum("shqk,sqhd->skhd", low_scores, query, preferred_element_type=jnp.float32) * scale
    )
    return grad_query, grad_keys, grad_values


MESH = pl.DeviceIdType.MESH
STEP = 16
VMEM_LIMIT = 56 * 1024 * 1024


class Wires:
    def __init__(self, send, recv):
        self.send, self.recv, self.used, self.sent = send, recv, 0, []

    def slots(self, count):
        first = self.used
        self.used += count
        return first

    def copy(self, source, target, slot, device, landing=None):
        return pltpu.make_async_remote_copy(
            src_ref=source,
            dst_ref=target,
            send_sem=self.send.at[slot],
            recv_sem=self.recv.at[slot if landing is None else landing],
            device_id=device,
            device_id_type=MESH,
        )

    def start(self, source, target, slot, device):
        copy = self.copy(source, target, slot, device)
        copy.start()
        self.sent.append(copy)
        return copy

    def finish(self):
        for copy in self.sent:
            copy.wait_send()


def here():
    x, r, c = lax.axis_index("dp"), lax.axis_index("row"), lax.axis_index("col")
    mate = (x, r, c + 1 - 2 * lax.rem(c, 2))
    beside = (1 - x, r, c)
    above = (x, r, lax.rem(c + 2, 4))
    return (x, r, c), mate, beside, above


def seat_of(x, r, c, rows, cols, piece):
    per = cols // rows
    return (x, lax.div(c, per), lax.rem(c, per) * rows + piece)


def home_of(x, r, c, rows, cols, source):
    per = cols // rows
    return (x, source, r * per + lax.div(c, rows))


def greet(devices, count):
    barrier = pltpu.get_barrier_semaphore()
    for device, remote in devices:
        if remote is None:
            pl.semaphore_signal(barrier, inc=1, device_id=device, device_id_type=MESH)
        else:

            @pl.when(remote)
            def _():
                pl.semaphore_signal(barrier, inc=1, device_id=device, device_id_type=MESH)

    pl.semaphore_wait(barrier, count)


COLUMNS = 1024
SWAPS = (2, 4)
DISTANCES = (0, -1, -2, -3, 1, 2, 3)


def weight_block(source, held, i, form, depth, size):
    if form == "turned":
        at = pl.ds(pl.multiple_of(i * size, size), size)
        return source.at[at, :depth], held.at[at, :]
    return (
        source.at[pl.ds(pl.multiple_of(i * depth, depth), depth), source.shape[1] - size :],
        held.at[:, pl.ds(pl.multiple_of(i * size, size), size)],
    )


def product_into(target, left, held, form, arrive=None):
    width = target.shape[1]
    size = min(COLUMNS, width)

    @pl.loop(0, width // size)
    def _(i):
        if arrive is not None:
            arrive(i, size)
        at = pl.ds(pl.multiple_of(i * size, size), size)
        if form == "turned":
            value = inner_cols(left[...], held[at, :])
        else:
            value = dot(left[...], held[:, at])
        target[:, at] = value.astype(LOW)


class PlaneGather:
    def __init__(self, wires, shard, main, sems, cols):
        (x, _, c), self.mate, self.beside, self.above = here()
        self.wires, self.shard, self.main, self.sems = wires, shard, main, sems
        half = shard.shape[0] // 2
        self.halves = [pl.ds(0, half), pl.ds(half, half)]
        self.spot = x * cols + c
        self.beside_spot, self.above_spot = self.beside[0] * cols + c, x * cols + self.above[2]
        self.corner_spot = self.beside[0] * cols + self.above[2]
        self.kept, self.to_mate, self.from_beside, self.from_above = [], [], [], []

    def start(self, i):
        part, target = self.shard.at[self.halves[i]], self.main.at[self.spot, self.halves[i]]
        self.kept.append(pltpu.make_async_copy(part, target, self.sems.at[i]))
        self.kept[-1].start()
        slot = self.wires.slots(3)
        self.from_beside.append(self.wires.start(part, target, slot, self.beside))
        self.from_above.append(self.wires.start(part, target, slot + 1, self.above))
        self.to_mate.append(self.wires.start(part, target, slot + 2, self.mate))

    def finish(self):
        slot = self.wires.slots(5)
        start, main = self.wires.start, self.main
        self.from_beside[0].wait_recv()
        part = main.at[self.beside_spot, self.halves[0]]
        corner_low = start(part, part, slot, self.above)
        self.from_above[0].wait_recv()
        self.from_above[1].wait_recv()
        part = main.at[self.above_spot, self.halves[1]]
        corner_high = start(part, part, slot + 1, self.beside)
        part = main.at[self.above_spot]
        self.to_mate.append(start(part, part, slot + 2, self.mate))
        self.from_beside[1].wait_recv()
        part = main.at[self.beside_spot]
        self.to_mate.append(start(part, part, slot + 3, self.mate))
        corner_low.wait_recv()
        corner_high.wait_recv()
        part = main.at[self.corner_spot]
        self.to_mate.append(start(part, part, slot + 4, self.mate))
        for copy in self.to_mate:
            copy.wait_recv()
        for copy in self.kept:
            copy.wait()


class Homing:
    def __init__(self, wires, shard, main, sem, rows, cols):
        x, r, c = here()[0]
        self.wires, self.shard, self.main, self.sem, self.rows = wires, shard, main, sem, rows
        self.seats = [seat_of(x, r, c, rows, cols, p) for p in range(rows)]
        self.homes = [home_of(x, r, c, rows, cols, s) for s in range(rows)]
        self.me, self.place = (x, r, c), lax.rem(c, rows)
        self.count, self.block = shard.shape[0], shard.shape[1] // rows

    def away(self, device):
        return jnp.logical_not(jnp.logical_and(device[1] == self.me[1], device[2] == self.me[2]))

    def sends(self):
        mine = pl.ds(pl.multiple_of(self.place * self.count, self.count), self.count)
        for s, home in enumerate(self.homes):
            part = self.shard.at[:, pl.ds(s * self.block, self.block)]
            there = self.wires.copy(part, self.main.at[mine], self.slot + s, home, self.slot + self.place)
            yield self.away(home), there, part, self.main.at[mine]

    def start(self):
        self.slot = self.wires.slots(self.rows)
        for remote, there, part, target in self.sends():
            pl.when(remote)(there.start)
            pl.when(jnp.logical_not(remote))(pltpu.make_async_copy(part, target, self.sem).start)

    def finish(self):
        for p, seat in enumerate(self.seats):
            part = self.main.at[pl.ds(p * self.count, self.count)]
            remote = self.away(seat)
            pl.when(remote)(self.wires.copy(part, part, self.slot + p, seat).wait_recv)
            pl.when(jnp.logical_not(remote))(pltpu.make_async_copy(part, part, self.sem).wait)
        for remote, there, _, _ in self.sends():
            pl.when(remote)(there.wait_send)


class LineSum:
    def __init__(self, wires, part, axis, columns, out, scratch, sems, rows):
        x, r, c = here()[0]
        self.wires, self.out, self.axis, self.rows, self.x, self.r = wires, out, axis, rows, x, r
        self.boxes, self.own, self.other = scratch[:2], scratch[2], scratch[3]
        self.devices = [(x, lax.rem(r + 1, rows), c), (x, lax.rem(r + rows - 1, rows), c)]
        self.beside = (1 - x, r, c)
        self.slot = wires.slots(2 * (rows - 1) + 1)
        size = part.shape[axis] // rows
        blocks = [pl.ds(k * size, size) for k in range(rows)]
        self.loads = [
            pltpu.make_async_copy(
                part.at[at, columns] if axis == 0 else part.at[:, at], self.own.at[k], sems.at[k]
            )
            for k, at in enumerate(blocks)
        ]
        for load in self.loads:
            load.start()

    def greeted(self):
        return [(self.devices[0], self.r < self.rows - 1), (self.devices[1], self.r > 0)]

    def blocks(self, step):
        return [lax.rem(2 * self.rows - step + self.r, self.rows), lax.rem(self.rows + self.r + step, self.rows)]

    def copies(self, step):
        return [
            self.wires.copy(self.own.at[s], box.at[step - 1], self.slot + 2 * (step - 1) + i, device)
            for i, (s, box, device) in enumerate(zip(self.blocks(step), self.boxes, self.devices))
        ]

    def sends(self, step):
        r, rows = self.r, self.rows
        return [(r < step) & (r < rows - 1), (r > rows - 1 - step) & (r > 0)]

    def arrivals(self, step):
        r, rows = self.r, self.rows
        return [(r > 0) & (r <= step), (r < rows - 1) & (r >= rows - 1 - step)]

    def chunk(self):
        rows, width = self.other.shape
        return min(rows, STEP * max(1, 2048 // width))

    def gain(self, step, blocks):
        copies, size = self.copies(step), self.chunk()
        for there, copy, s, box in zip(self.arrivals(step), copies, blocks, self.boxes):

            @pl.when(there)
            def _():
                copy.wait_recv()

                @pl.loop(0, self.other.shape[0] // size)
                def _(i):
                    at = pl.ds(pl.multiple_of(i * size, size), size)
                    total = self.own[s, at, :].astype(jnp.float32)
                    self.own[s, at, :] = (total + box[step - 1, at, :].astype(jnp.float32)).astype(LOW)

    def advance(self, step):
        if step == 1:
            for load in self.loads:
                load.wait()
        else:
            self.gain(step - 1, self.blocks(step))
        for there, copy in zip(self.sends(step), self.copies(step)):
            pl.when(there)(copy.start)

    def complete(self):
        self.gain(self.rows - 1, [self.r, self.r])

    def end(self):
        self.share = self.wires.start(self.own.at[self.r], self.other, self.slot + 2 * self.rows - 2, self.beside)
        self.write(lambda at: self.own[self.r, at, :], self.x)

    def finish(self):
        self.share.wait_recv()
        self.write(lambda at: self.other[at, :], 1 - self.x)
        for step in range(1, self.rows):
            for there, copy in zip(self.sends(step), self.copies(step)):
                pl.when(there)(copy.wait_send)

    def write(self, share, place):
        rows, width = self.other.shape
        size = self.chunk()

        @pl.loop(0, rows // size)
        def _(k):
            at = pl.multiple_of(k * size, size)
            value = share(pl.ds(at, size)).astype(jnp.float32)
            if self.axis == 0:
                self.out[pl.ds(at, size), pl.ds(pl.multiple_of(place * width, width), width)] = value
            else:
                self.out[pl.ds(pl.multiple_of(place * rows + at, size), size), :] = value


def plane_kernel(rows, cols, entry, leave, mid, counts, beside_work, line_axes, totals, form, *refs):
    n_blocks, n_small, n_out, n_swap, n_extra, n_made, n_ship, n_lines = counts
    refs = list(refs)
    big = refs.pop(0)
    blocks = [refs.pop(0) for _ in range(n_blocks)]
    weights = blocks[0]
    small = [refs.pop(0) for _ in range(n_small)]
    mine_parts = [refs.pop(0) for _ in range(n_swap)]
    extra = [refs.pop(0) for _ in range(n_extra)]
    leaving = [refs.pop(0) for _ in range(n_ship)]
    line_parts = [refs.pop(0) for _ in line_axes]
    main = refs.pop(0)
    outs = [refs.pop(0) for _ in range(n_out)]
    other_parts = [refs.pop(0) for _ in range(n_swap)]
    made = [refs.pop(0) for _ in range(n_made)]
    landing = [refs.pop(0) for _ in range(n_ship)]
    line_outs = [refs.pop(0) for _ in range(sum(n_lines))]
    shard, send, recv, local = (refs.pop(0) for _ in range(4))
    if totals:
        total, inbox, line_inbox = (refs.pop() for _ in range(3))
    line_scratch = [[refs.pop(8) for _ in range(4)] for _ in line_outs]
    wires = Wires(send, recv)
    me, mate, beside, above = here()
    x, r, c = me
    count, width = shard.shape
    half = count // 2
    low_half, high_half = pl.ds(0, half), pl.ds(half, half)
    homing = None
    if leave == "homes":
        homing = Homing(wires, shard, main, local.at[20], rows, cols)
    elif n_ship:
        homing = Homing(wires, leaving[0], landing[0], local.at[22], rows, cols)
    if leave == "gather":
        gather = PlaneGather(wires, shard, main, local.at[pl.ds(20, 2)], cols)
    greeted = []
    expected = 0
    if homing is not None:
        stays = (lax.div(c, cols // rows) == r) & (lax.rem(c, cols // rows) * rows + lax.rem(c, rows) == c)
        greeted += [(s, homing.away(s)) for s in homing.seats]
        expected = expected + rows - jnp.where(stays, 1, 0).astype(jnp.int32)
    lines = []
    for part, axis, pieces in zip(line_parts, line_axes, n_lines):
        for k in range(pieces):
            i, size = len(lines), part.shape[1] // pieces
            sems = local.at[pl.ds(24 + rows * i, rows)]
            columns = slice(k * size, (k + 1) * size)
            lines.append(LineSum(wires, part, axis, columns, line_outs[i], line_scratch[i], sems, rows))
    for line in lines[:1]:
        greeted += line.greeted()
        expected = expected + sum(jnp.where(there, 1, 0).astype(jnp.int32) for _, there in line.greeted())
    if totals:
        others = [(x, lax.rem(r + k, rows), c) for k in range(1, rows)]
        greeted += [(o, None) for o in others]
        expected = expected + rows - 1
    greeted += [(mate, None), (beside, None), (above, None)]
    swaps = []

    def send_swaps(first, last):
        for source, target in zip(mine_parts, other_parts):
            size = source.shape[0] // 4
            if first == last:
                return
            part = pl.ds(first * size, (last - first) * size)
            swaps.append(wires.start(source.at[part], target.at[part], wires.slots(1), beside))

    if entry == "sum":
        depth = big.shape[2]
        if form == "blocks":
            block_width = weights.shape[1]
        else:
            block_width = min(COLUMNS, width) if form == "turned" else width * depth // weights.shape[0]

        def fetch(i, source=weights):
            if form == "blocks":
                ends = source, refs[1].at[:, pl.ds(pl.multiple_of(i * block_width, block_width), block_width)]
            else:
                ends = weight_block(source, refs[1], i, form, depth, block_width)
            return pltpu.make_async_copy(*ends, local.at[4 + i])

        def arrive(i, size):
            for k in range(size // block_width):
                fetch(i * (size // block_width) + k).wait()

        @pl.loop(0, width // block_width)
        def _(i):
            if form == "blocks":
                for distance, block in zip(DISTANCES, blocks):
                    pl.when(i == r + distance)(fetch(i, block).start)
            else:
                fetch(i).start()

        chips = [(1 - x, above[2]), (1 - x, c), (x, above[2]), (x, c)]
        loads = [
            pltpu.make_async_copy(big.at[(tx * cols + tc) // 2], refs[0].at[k], local.at[k])
            for k, (tx, tc) in enumerate(chips)
        ]
        for load in loads:
            load.start()
    greet(greeted, expected + 3)
    if n_ship:
        homing.start()
    for line in lines:
        line.advance(1)

    if entry == "sum":
        factors, held_weights, both, mated, beside_pass, above_pass, beside_in, above_in = refs
        first = wires.slots(4)
        handed = []
        core = lax.rem(c, 2)
        own_start = pl.multiple_of(core * count, count)
        given_rows = pl.ds(pl.multiple_of((1 - core) * count, count), count)

        def own_rows(start, size):
            return pl.ds(pl.multiple_of(own_start + start, size), size)

        def supply(k, arrive=None):
            loads[k].wait()
            product_into(both.at[k], factors.at[k], held_weights, form, arrive)
            handed.append(wires.start(both.at[k, given_rows], mated.at[k], first + k, mate))

        def add(k, more, start, size):
            @pl.loop(0, size // STEP)
            def _(i):
                at = own_rows(start + i * STEP, STEP)
                to = pl.ds(pl.multiple_of(start + i * STEP, STEP), STEP)
                both[k, at, :] = (
                    both[k, at, :].astype(jnp.float32) + more(to).astype(jnp.float32)
                ).astype(LOW)

        def merge(k):
            handed[k].wait_recv()
            add(k, lambda at: mated[k, at, :], 0, count)

        own_low, own_high = own_rows(0, half), own_rows(half, half)
        if lines:
            send_swaps(0, SWAPS[0])
            slot = wires.slots(6)
            supply(0, arrive)
            handed[0].wait_recv()
            passes = []
            for k, rows_out in enumerate((own_low, own_high)):
                add(0, lambda at: mated[0, at, :], k * half, half)
                to = above_pass.at[pl.ds(k * half, half)]
                passes.append(wires.start(both.at[0, rows_out], to, slot + k, above))
            supply(1)
            merge(1)
            supply(2)
            merge(2)
            above_low = wires.start(both.at[2, own_low], above_in.at[low_half], slot + 2, above)
            above_high = wires.start(both.at[2, own_high], above_in.at[high_half], slot + 3, above)
            supply(3)
            passes[0].wait_recv()
            add(1, lambda at: above_pass[at, :], 0, half)
            beside_low = wires.start(both.at[1, own_low], beside_in.at[low_half], slot + 4, beside)
            for line in lines:
                line.advance(2)
            passes[1].wait_recv()
            add(1, lambda at: above_pass[at, :], half, half)
            beside_high = wires.start(both.at[1, own_high], beside_in.at[high_half], slot + 5, beside)
            send_swaps(SWAPS[0], SWAPS[1])
            groups = [lines[: len(lines) // 2], lines[len(lines) // 2 :]]
            for line in groups[0]:
                line.advance(3)
        else:
            slot = wires.slots(6)
            supply(0, arrive)
            handed[0].wait_recv()
            add(0, lambda at: mated[0, at, :], 0, half)
            pass_beside = wires.start(both.at[0, own_low], beside_pass, slot, beside)
            add(0, lambda at: mated[0, at, :], half, half)
            pass_above = wires.start(both.at[0, own_high], above_pass, slot + 1, above)
            supply(1)
            merge(1)
            beside_low = wires.start(both.at[1, own_low], beside_in.at[low_half], slot + 2, beside)
            supply(2)
            merge(2)
            pass_beside.wait_recv()
            add(2, lambda at: beside_pass[at, :], 0, half)
            above_low = wires.start(both.at[2, own_low], above_in.at[low_half], slot + 3, above)
            above_high = wires.start(both.at[2, own_high], above_in.at[high_half], slot + 4, above)
            supply(3)
            if beside_work is not None:
                beside_work(0, held_weights, extra, made)
            pass_above.wait_recv()
            add(1, lambda at: above_pass[pl.ds(pl.multiple_of(at.start - half, STEP), STEP), :], half, half)
            beside_high = wires.start(both.at[1, own_high], beside_in.at[high_half], slot + 5, beside)
        if beside_work is not None:
            beside_work(1, held_weights, extra, made)
        handed[3].wait_recv()

        def value(at):
            near = both[3, own_rows(at.start, STEP), :].astype(jnp.float32)
            near = near + mated[3, at, :].astype(jnp.float32)
            return near + (beside_in[at, :].astype(jnp.float32) + above_in[at, :].astype(jnp.float32))

    mid.start(outs)
    for k in range(2):
        if entry == "sum":
            (beside_low, beside_high)[k].wait_recv()
            (above_low, above_high)[k].wait_recv()

        @pl.loop(k * (half // STEP), (k + 1) * (half // STEP))
        def _(i):
            at = pl.ds(pl.multiple_of(i * STEP, STEP), STEP)
            shard[at, :] = mid.rows(at, value(at), small, outs).astype(LOW)

        if leave == "gather":
            gather.start(k)

    if leave == "gather":
        gather.finish()
    elif leave == "homes":
        if not lines:
            homing.start()
    else:
        keep = pltpu.make_async_copy(shard, main, local.at[20])
        keep.start()
    if beside_work is not None:
        beside_work(2, None, extra, made)
    if leave == "stay":
        keep.wait()
    if not lines:
        send_swaps(0, 4)
    if totals and not lines:
        gain_sums(wires, me, (mate, beside, above), others, rows, small[-1], outs, total, inbox, line_inbox)
    for k, group in enumerate(groups if lines else ()):
        for line in group:
            line.complete()
        if k == 0:
            for line in groups[1]:
                line.advance(rows - 1)
            gain_sums(wires, me, (mate, beside, above), others, rows, small[-1], outs, total, inbox, line_inbox)
        else:
            homing.start()
        for line in group:
            line.end()
        if k == 1:
            send_swaps(SWAPS[1], 4)
    for line in lines:
        line.finish()
    if homing is not None:
        homing.finish()
    if n_swap:
        for copy in swaps:
            copy.wait_recv()
    wires.finish()


def enter_kernel(
    rows, cols, hidden_in, grad_out, gains_in, normed, grads, held, grad_here, gains,
    shard, seated, grad_seated, hidden_relay, grad_relay, landing, send, recv, local,
):
    wires = Wires(send, recv)
    me, mate, beside, above = here()
    x, r, c = me
    count, width = seated.shape
    block = width // rows
    side = 2 * lax.div(c, 2)
    far = 2 - side
    ways = [(x, c, side), (x, c, side + 1), (x, above[2], side), (x, above[2], side + 1)]
    via = side + lax.rem(r, 2)
    sources = [(x, s, via) for s in range(rows)]
    others = [(x, lax.rem(r + k, rows), c) for k in range(1, rows)]

    def away(device):
        return jnp.logical_not(jnp.logical_and(device[1] == r, device[2] == c))

    kept = jnp.where(lax.rem(c, 2) == lax.rem(r, 2), 1, 0).astype(jnp.int32)
    greeted = [(s, away(s)) for s in sources] + [(o, None) for o in others]
    greeted += [(above, None), (mate, None), (beside, None)]
    greet(greeted, 2 * rows + 2 - kept)

    mine = pl.ds(pl.multiple_of(r * block, block), block)
    slot = wires.slots(rows - 1)
    spread = [wires.start(gains_in, landing.at[r], slot + k, other) for k, other in enumerate(others)]

    class Seating:
        def __init__(self, source, target, relay, sem):
            self.source, self.target, self.relay, self.sem = source, target, relay, sem
            self.slot, self.hop = wires.slots(rows), wires.slots(1)

        def pieces(self):
            near = pl.multiple_of(side * count, count)
            return [
                self.source.at[pl.ds(near, count)],
                self.source.at[pl.ds(near + count, count)],
                self.relay.at[pl.ds(0, count)],
                self.relay.at[pl.ds(count, count)],
            ]

        def cross(self):
            across = self.source.at[pl.ds(pl.multiple_of(far * count, count), 2 * count)]
            self.crossing = wires.start(across, self.relay, self.hop, above)

        def go(self, which):
            for i in which:
                piece, seat = self.pieces()[i], ways[i]
                there = wires.copy(piece, self.target.at[:, mine], self.slot + i, seat, self.slot + r)
                stay = pltpu.make_async_copy(piece, self.target.at[:, mine], self.sem)
                pl.when(away(seat))(there.start)
                pl.when(jnp.logical_not(away(seat)))(stay.start)

        def arrive(self):
            for s, source in enumerate(sources):
                part = self.target.at[:, pl.ds(s * block, block)]
                arrived = wires.copy(part, part, self.slot + s, source)
                stay = pltpu.make_async_copy(part, part, self.sem)
                pl.when(away(source))(arrived.wait_recv)
                pl.when(jnp.logical_not(away(source)))(stay.wait)

        def sent(self):
            for i, piece in enumerate(self.pieces()):
                there = wires.copy(piece, self.target.at[:, mine], self.slot + i, ways[i])
                pl.when(away(ways[i]))(there.wait_send)

    hidden = Seating(hidden_in, seated, hidden_relay, local.at[0])
    grad = Seating(grad_out, grad_seated, grad_relay, local.at[1])
    hidden.cross()
    hidden.go((0, 1))
    grad.cross()
    hidden.crossing.wait_recv()
    hidden.go((2, 3))
    for copy in spread:
        copy.wait_recv()
    landing[r] = gains_in[...]
    for s in range(rows):
        gains[:, s * block : (s + 1) * block] = landing[s]
    hidden.arrive()
    grad.go((0, 1))
    grad.crossing.wait_recv()
    grad.go((2, 3))
    keep = pltpu.make_async_copy(seated, held, local.at[2])
    keep.start()

    gather = PlaneGather(wires, shard, normed, local.at[pl.ds(4, 2)], cols)
    for k in range(2):

        @pl.loop(k * (count // STEP // 2), (k + 1) * (count // STEP // 2))
        def _(i):
            at = pl.ds(pl.multiple_of(i * STEP, STEP), STEP)
            value = seated[at, :].astype(jnp.float32)
            shard[at, :] = (value * rms_scale(value) * gains[0:1, :]).astype(LOW)

        gather.start(k)
    gather.finish()
    grad.arrive()
    keep_grad = pltpu.make_async_copy(grad_seated, grad_here, local.at[3])
    keep_grad.start()
    gather = PlaneGather(wires, grad_seated, grads, local.at[pl.ds(6, 2)], cols)
    gather.start(0)
    gather.start(1)
    gather.finish()
    hidden.sent()
    grad.sent()
    keep.wait()
    keep_grad.wait()
    wires.finish()


def enter_call(hidden_in, grad_out, gains, collective_id):
    rows, cols, parts = lax.axis_size("row"), lax.axis_size("col"), lax.axis_size("dp")
    count, width = hidden_in.shape[0] // rows, hidden_in.shape[1] * rows
    block = width // rows
    vmem = pl.BlockSpec(memory_space=pltpu.VMEM)
    hbm = pl.BlockSpec(memory_space=pl.ANY)
    shape = jax.ShapeDtypeStruct((count, width), LOW)
    tile = pltpu.VMEM((count, width), LOW)
    relay = pltpu.VMEM((2 * count, block), LOW)
    whole = jax.ShapeDtypeStruct((parts * cols, count, width), LOW)
    normed, grads, held, grad_here, gains = pl.pallas_call(
        functools.partial(enter_kernel, rows, cols),
        out_shape=[whole, whole, shape, shape, jax.ShapeDtypeStruct((8, width), jnp.float32)],
        in_specs=[hbm, hbm, vmem],
        out_specs=[hbm, hbm, hbm, hbm, vmem],
        scratch_shapes=[tile, tile, tile, relay, relay, pltpu.VMEM((rows, 8, block), jnp.float32)]
        + [pltpu.SemaphoreType.DMA((48,))] * 2
        + [pltpu.SemaphoreType.DMA((8,))],
        compiler_params=pltpu.CompilerParams(
            collective_id=collective_id, has_side_effects=True, vmem_limit_bytes=VMEM_LIMIT
        ),
        cost_estimate=pl.CostEstimate(flops=0, bytes_accessed=20_000_000, transcendentals=0),
    )(hidden_in, grad_out, gains)
    flat = (parts * cols * count, width)
    return normed.reshape(flat), grads.reshape(flat), held, grad_here, gains


def enter_plain(hidden_in, grad_out, gains, collective_id):
    gains = lax.all_gather(gains, "row", axis=1, tiled=True)
    held = to_group(hidden_in)
    value = held.astype(jnp.float32)
    normed = group_gather((value * rms_scale(value) * gains[0:1]).astype(LOW))
    grad_here = to_group(grad_out)
    return normed, group_gather(grad_here), held, grad_here, gains


def gain_sums(wires, me, partners, others, rows, gain_two, outs, total, inbox, line_inbox):
    x, r, c = me
    block = total.shape[1] // rows
    total[0:1, :] = jnp.sum(outs[1][...], axis=0, keepdims=True)
    total[1:2, :] = jnp.sum(gain_two[...], axis=0, keepdims=True)
    total[2:, :] = jnp.zeros_like(total[2:, :])
    first = wires.slots(len(partners))
    for k, partner in enumerate(partners):
        copy = wires.copy(total, inbox.at[k], first + k, partner)
        copy.start()
        copy.wait()
        total[...] += inbox[k]
    first = wires.slots(len(others))
    copies = []
    for k, (_, row, _) in enumerate(others):
        part = total.at[:, pl.ds(pl.multiple_of(row * block, block), block)]
        copies.append(wires.start(part, line_inbox.at[r], first + k, others[k]))
    line_inbox[r] = total[:, pl.ds(pl.multiple_of(r * block, block), block)]
    for copy in copies:
        copy.wait_recv()
    outs[0][...] = sum(line_inbox[k] for k in range(rows))


def plane_call(
    entry, leave, mid, big, small, outs, collective_id, weights=None, form=None, totals=False, swap=(),
    beside_work=None, extra=(), made=(), ship=(), line=(), line_axes=(), line_pieces=(),
):
    rows, cols, parts = lax.axis_size("row"), lax.axis_size("col"), lax.axis_size("dp")
    count, width = big.shape[0] // (parts * cols), small[0].shape[1]
    depth = big.shape[1]
    big = big.reshape(parts * cols // 2, 2 * count, depth)
    gathered = leave == "gather"
    shape = {"gather": (parts * cols, count, width), "homes": (rows * count, width // rows), "stay": (count, width)}[leave]
    landed = [jax.ShapeDtypeStruct((rows * a.shape[0], a.shape[1] // rows), a.dtype) for a in ship]
    plain = len(swap) + len(made) + len(ship)
    vmem = pl.BlockSpec(memory_space=pltpu.VMEM)
    hbm = pl.BlockSpec(memory_space=pl.ANY)
    tile = pltpu.VMEM((count, width), LOW)
    whole, part = pltpu.VMEM((4, count, width), LOW), pltpu.VMEM((count // 2, width), LOW)
    scratch = [tile, pltpu.SemaphoreType.DMA((64,)), pltpu.SemaphoreType.DMA((64,)), pltpu.SemaphoreType.DMA((40,))]
    scratch += [
        pltpu.VMEM(big.shape, LOW),
        pltpu.VMEM((width, depth) if form == "turned" else (depth, width), LOW),
        pltpu.VMEM((4, 2 * count, width), LOW),
    ]
    scratch += [whole, part, tile if line else part, tile, tile]
    line_outs = []
    for array, axis, pieces in zip(line, line_axes, line_pieces):
        block = [n // rows if i == axis else n for i, n in enumerate(array.shape)]
        block[1] //= pieces
        scratch += ([pltpu.VMEM((n, *block), LOW) for n in (rows - 1, rows - 1, rows)] + [pltpu.VMEM(tuple(block), LOW)]) * pieces
        block[1 - axis] *= parts
        line_outs += [jax.ShapeDtypeStruct(tuple(block), jnp.float32)] * pieces
    if totals:
        scratch += [
            pltpu.VMEM((rows, 8, width // rows), jnp.float32),
            pltpu.VMEM((3, 8, width), jnp.float32),
            pltpu.VMEM((8, width), jnp.float32),
        ]
    blocks = weights if form == "blocks" else [weights]
    counts = (len(blocks), len(small), len(outs), len(swap), len(extra), len(made), len(ship), tuple(line_pieces))
    main, *others = pl.pallas_call(
        functools.partial(plane_kernel, rows, cols, entry, leave, mid, counts, beside_work, line_axes, totals, form),
        out_shape=[jax.ShapeDtypeStruct(shape, LOW)]
        + list(outs)
        + [jax.ShapeDtypeStruct(m.shape, m.dtype) for m in (*swap, *made, *landed, *line_outs)],
        in_specs=[hbm] * (1 + len(blocks)) + [vmem] * len(small) + [hbm] * (len(swap) + len(extra) + len(ship) + len(line)),
        out_specs=[hbm] + [vmem] * len(outs) + [hbm] * plain + [vmem] * len(line_outs),
        scratch_shapes=scratch,
        compiler_params=pltpu.CompilerParams(
            collective_id=collective_id, has_side_effects=True, vmem_limit_bytes=VMEM_LIMIT
        ),
        cost_estimate=pl.CostEstimate(flops=0, bytes_accessed=20_000_000, transcendentals=0),
    )(big, *blocks, *small, *swap, *extra, *ship, *line)
    if gathered:
        main = main.reshape(parts * cols * count, width)
    return [main, *others]


def fold(values):
    return values.reshape(values.shape[0] // 8, 8, values.shape[1]).sum(0)


class Mid:
    @staticmethod
    def start(outs):
        pass


class SecondNorm(Mid):
    @staticmethod
    def rows(at, value, small, outs):
        held, gains = small
        middle = held[at, :].astype(jnp.float32) + value
        outs[0][at, :] = middle
        return middle * rms_scale(middle) * gains[1:2, :]


class Add(Mid):
    @staticmethod
    def rows(at, value, small, outs):
        return small[0][at, :] + value


class BackSecond(Mid):
    @staticmethod
    def start(outs):
        outs[1][...] = jnp.zeros_like(outs[1])

    @staticmethod
    def rows(at, value, small, outs):
        middle, grad_out, gains = small
        middle = middle[at, :]
        scale = rms_scale(middle)
        outs[1][...] += fold(value * middle * scale)
        grad = grad_out[at, :].astype(jnp.float32) + norm_back(
            middle, scale, value * gains[1:2, :]
        )
        outs[0][at, :] = grad
        return grad


class BackFirst(Mid):
    @staticmethod
    def start(outs):
        outs[1][...] = jnp.zeros_like(outs[1])

    @staticmethod
    def rows(at, value, small, outs):
        held, grad_middle, gains = small[:3]
        inputs = held[at, :].astype(jnp.float32)
        scale = rms_scale(inputs)
        outs[1][...] += fold(value * inputs * scale)
        return grad_middle[at, :] + norm_back(inputs, scale, value * gains[0:1, :])


def plain_call(
    entry, leave, mid, big, small, outs, collective_id, weights=None, form=None, totals=False, swap=(),
    beside_work=None, extra=(), made=(), ship=(), line=(), line_axes=(), line_pieces=(),
):
    refs = [Holder(a) for a in small]
    given = [Holder(jnp.zeros(o.shape, o.dtype)) for o in outs]
    depth, width = big.shape[1], small[0].shape[1]
    if form == "turned":
        product = inner_cols(big, weights[:, :depth])
    else:
        block = width * depth // weights.shape[0]
        whole = unstack(weights[:, weights.shape[1] - block :], depth)
        product = dot(big, whole)
    mid.start(given)
    shard = mid.rows(slice(None), group_scatter(product), refs, given).astype(LOW)
    main = {"gather": group_gather, "homes": from_group, "stay": lambda a: a}[leave](shard)
    if totals:
        sums = jnp.stack([given[1].value.sum(0), small[-1].sum(0)])
        sums = jnp.pad(lax.psum(sums, ("dp", "row", "col")), ((0, 6), (0, 0)))
        part = outs[0].shape[1]
        given[0].value = lax.dynamic_slice_in_dim(sums, lax.axis_index("row") * part, part, 1)
    others = [dp_other(m) for m in swap]
    if beside_work is not None:
        grads, slope_up, gated, tokens = extra
        lifted = lift_back_plain(grads, whole, slope_up, gated)
        others += [lifted, inner_rows(tokens, lifted).astype(LOW)]
    others += [from_group(a) for a in ship]
    for array, axis, pieces in zip(line, line_axes, line_pieces):
        mine = row_sum(array, axis)
        other = dp_other(mine)
        others += join_tall(mine, other, [(i,) for i in range(pieces)]) if axis == 0 else [join_wide(mine, other)]
    return [main] + [g.value for g in given] + others


class Holder:
    def __init__(self, value):
        self.value, self.dtype, self.shape = value, value.dtype, value.shape

    def __getitem__(self, at):
        return self.value[at]

    def __setitem__(self, at, value):
        self.value = self.value.at[at].set(value)


def swap_halves(values, first):
    lanes = values.shape[1]
    half = HEAD_DIM // 2
    return jnp.where(first, pltpu.roll(values, lanes - half, 1), pltpu.roll(values, half, 1))


def attend_kernel(query, key, value, cosine, sine, mixed, q_out, k_out, v_out, logsum):
    length, lanes = query.shape
    block = min(256, length)
    lane = lax.broadcasted_iota(jnp.int32, (length, lanes), 1)
    first = lax.rem(lane, HEAD_DIM) < HEAD_DIM // 2
    cos, sin = cosine[...], sine[...]

    def rotate(values):
        return (values * cos + swap_halves(values, first) * sin).astype(LOW)

    q_out[...] = rotate(query[...])
    k_out[...] = rotate(key[...])
    low_values = value[...].astype(LOW)
    v_out[...] = low_values
    v_turned = low_values.astype(jnp.float32).T.astype(LOW)
    head = lax.broadcasted_iota(jnp.int32, (block, lanes), 1) // HEAD_DIM
    keep = lax.broadcasted_iota(jnp.int32, (block, block), 0) <= lax.broadcasted_iota(
        jnp.int32, (block, block), 1
    )
    for j in range(length // block):
        at = slice(j * block, (j + 1) * block)
        q_block = q_out[at, :].astype(jnp.float32) * HEAD_DIM ** (-0.5)
        parts = []
        for h in range(lanes // HEAD_DIM):
            q_head = jnp.where(head == h, q_block, 0.0).astype(LOW)
            near = jnp.where(keep, inner_cols(k_out[at, :], q_head), -jnp.inf)
            highest = jnp.max(near, axis=0, keepdims=True)
            if j:
                far = inner_cols(k_out[: j * block, :], q_head)
                highest = jnp.maximum(highest, jnp.max(far, axis=0, keepdims=True))
                far = jnp.exp(far - highest)
            near = jnp.exp(near - highest)
            total = jnp.sum(near, axis=0, keepdims=True)
            if j:
                total = total + jnp.sum(far, axis=0, keepdims=True)
            logsum[0, 0, h : h + 1, at] = highest + jnp.log(total)
            share = 1.0 / total
            out = dot(v_turned[:, at], (near * share).astype(LOW))
            if j:
                out = out + dot(v_turned[:, : j * block], (far * share).astype(LOW))
            parts.append(out[h * HEAD_DIM : (h + 1) * HEAD_DIM])
        mixed[at, :] = jnp.concatenate(parts, 0).T.astype(LOW)


def attend_back_kernel(n_swap, query, key, value, grad, logsum, cosine, sine, *refs):
    mine_parts, refs = refs[:n_swap], refs[n_swap:]
    made, refs = refs[0], refs[1:]
    other_parts, refs = refs[:n_swap], refs[n_swap:]
    (k_sum, v_sum, q_out, k_out, v_out, out_sems), refs = refs[:6], refs[6:]
    length, lanes = query.shape
    if n_swap:
        beside = here()[2]
        wires = Wires(*refs)
        swaps = [
            wires.copy(source, target, i, beside)
            for i, (source, target) in enumerate(zip(mine_parts, other_parts))
        ]
        here_first = (pl.program_id(0) == 0) & (pl.program_id(1) == 0)
        here_last = (pl.program_id(0) == pl.num_programs(0) - 1) & (
            pl.program_id(1) == pl.num_programs(1) - 1
        )

        @pl.when(here_first)
        def _():
            greet([(beside, None)], 1)
            for copy in swaps:
                copy.start()

    block = min(256, length)
    k_sum[...] = jnp.zeros_like(k_sum)
    v_sum[...] = jnp.zeros_like(v_sum)
    k_turned = key[...].astype(jnp.float32).T.astype(LOW)
    head = lax.broadcasted_iota(jnp.int32, (block, lanes), 1) // HEAD_DIM
    keep = lax.broadcasted_iota(jnp.int32, (block, block), 0) <= lax.broadcasted_iota(
        jnp.int32, (block, block), 1
    )
    scale = HEAD_DIM ** (-0.5)

    def rotate_back(values, at):
        rows = values.shape[0]
        lane = lax.broadcasted_iota(jnp.int32, (rows, lanes), 1)
        first = lax.rem(lane, HEAD_DIM) < HEAD_DIM // 2
        return (values * cosine[at, :] - swap_halves(values, first) * sine[at, :]).astype(LOW)

    for j in range(length // block):
        at = slice(j * block, (j + 1) * block)
        before = slice(0, j * block)
        q_block = query[at, :].astype(jnp.float32) * scale
        g_block = grad[at, :].astype(jnp.float32)
        parts = []
        for h in range(lanes // HEAD_DIM):
            q_head = jnp.where(head == h, q_block, 0.0).astype(LOW)
            g_head = jnp.where(head == h, g_block, 0.0).astype(LOW)
            level = logsum[0, 0, h : h + 1, at]
            near = jnp.exp(jnp.where(keep, inner_cols(key[at, :], q_head), -jnp.inf) - level)
            d_near = inner_cols(value[at, :], g_head)
            inner = jnp.sum(near * d_near, axis=0, keepdims=True)
            if j:
                far = jnp.exp(inner_cols(key[before, :], q_head) - level)
                d_far = inner_cols(value[before, :], g_head)
                inner = inner + jnp.sum(far * d_far, axis=0, keepdims=True)
                v_sum[before, :] += dot(far.astype(LOW), g_head)
                s_far = (far * (d_far - inner)).astype(LOW)
                k_sum[before, :] += dot(s_far, q_head)
            v_sum[at, :] += dot(near.astype(LOW), g_head)
            s_near = (near * (d_near - inner)).astype(LOW)
            k_sum[at, :] += dot(s_near, q_head)
            out = dot(k_turned[:, at], s_near)
            if j:
                out = out + dot(k_turned[:, before], s_far)
            parts.append(out[h * HEAD_DIM : (h + 1) * HEAD_DIM])
        q_out[at, :] = rotate_back(jnp.concatenate(parts, 0).T * scale, at)
    k_out[...] = rotate_back(k_sum[...], slice(None))
    v_out[...] = v_sum[...].astype(LOW)
    rows_at = pl.ds(pl.multiple_of(pl.program_id(0) * length, length), length)
    columns = made.shape[1] // 3
    copies = [
        pltpu.make_async_copy(
            out,
            made.at[rows_at, pl.ds(pl.multiple_of(i * columns + pl.program_id(1) * lanes, lanes), lanes)],
            out_sems.at[i],
        )
        for i, out in enumerate((q_out, k_out, v_out))
    ]
    for copy in copies:
        copy.start()
    for copy in copies:
        copy.wait()
    if n_swap:

        @pl.when(here_last)
        def _():
            for copy in swaps:
                copy.wait()


def pair_tables(length):
    half = HEAD_DIM // 2
    freq = THETA ** (-(jnp.arange(half, dtype=jnp.float32) * 2.0 / HEAD_DIM))
    angle = jnp.arange(length, dtype=jnp.float32)[:, None] * freq[None, :]
    cosine, sine = jnp.cos(angle), jnp.sin(angle)
    return jnp.tile(cosine, (1, 4)), jnp.tile(jnp.concatenate([-sine, sine], 1), (1, 2))


def attend_pairs(projected, sequences):
    tokens, columns = projected.shape[0], projected.shape[1] // 3
    length, lanes = tokens // sequences, 2 * HEAD_DIM
    pairs = columns // lanes
    cosine, sine = pair_tables(length)

    def spec(offset):
        return pl.BlockSpec((length, lanes), lambda s, h: (s, offset + h))

    table = pl.BlockSpec((length, lanes), lambda s, h: (0, 0))
    level = pl.BlockSpec((1, 1, 2, length), lambda s, h: (s, h, 0, 0))
    shape = jax.ShapeDtypeStruct((tokens, columns), LOW)
    return pl.pallas_call(
        attend_kernel,
        grid=(sequences, pairs),
        in_specs=[spec(0), spec(pairs), spec(2 * pairs), table, table],
        out_specs=[spec(0)] * 4 + [level],
        out_shape=[shape] * 4 + [jax.ShapeDtypeStruct((sequences, pairs, 2, length), jnp.float32)],
        compiler_params=pltpu.CompilerParams(vmem_limit_bytes=VMEM_LIMIT),
        cost_estimate=pl.CostEstimate(
            flops=8 * tokens * length * columns, bytes_accessed=100_000_000, transcendentals=0
        ),
    )(projected, projected, projected, cosine, sine)


def attend_pairs_back(query, keys, values, grad_mixed, logsum, sequences, swap, collective_id):
    tokens, columns = query.shape
    length, lanes = tokens // sequences, 2 * HEAD_DIM
    pairs = columns // lanes
    cosine, sine = pair_tables(length)
    spec = pl.BlockSpec((length, lanes), lambda s, h: (s, h))
    table = pl.BlockSpec((length, lanes), lambda s, h: (0, 0))
    level = pl.BlockSpec((1, 1, 2, length), lambda s, h: (s, h, 0, 0))
    hbm = pl.BlockSpec(memory_space=pl.ANY)
    return pl.pallas_call(
        functools.partial(attend_back_kernel, len(swap)),
        grid=(sequences, pairs),
        in_specs=[spec] * 4 + [level, table, table] + [hbm] * len(swap),
        out_specs=[hbm] * (1 + len(swap)),
        out_shape=[jax.ShapeDtypeStruct((tokens, 3 * columns), LOW)] + [jax.ShapeDtypeStruct(m.shape, m.dtype) for m in swap],
        scratch_shapes=[pltpu.VMEM((length, lanes), jnp.float32)] * 2
        + [pltpu.VMEM((length, lanes), LOW)] * 3
        + [pltpu.SemaphoreType.DMA((4,))] * 3,
        compiler_params=pltpu.CompilerParams(
            collective_id=collective_id, has_side_effects=True, vmem_limit_bytes=VMEM_LIMIT
        ),
        cost_estimate=pl.CostEstimate(
            flops=20 * tokens * length * columns, bytes_accessed=60_000_000, transcendentals=0
        ),
    )(query, keys, values, grad_mixed, logsum, cosine, sine, *swap)


def lift_kernel(tokens, weights, *refs):
    activated, slope_up, gated = refs[-3:]
    rows, width = activated.shape
    step = min(256, rows)
    for i in range(rows // step):
        at = slice(i * step, (i + 1) * step)
        left = tokens[at, :]
        gate, upward = dot(left, weights[:, :width]), dot(left, weights[:, width:])
        sigmoid = 1.0 / (1.0 + jnp.exp(-gate))
        passed = gate * sigmoid
        activated[at, :] = (passed * upward).astype(LOW)
        gated[at, :] = passed.astype(LOW)
        slope_up[at, :] = (upward * (sigmoid + passed * (1.0 - sigmoid))).astype(LOW)


def lift(tokens, weights, part, begun=()):
    count, width = tokens.shape
    units = weights.shape[1] // 2
    tile, rows = units // 2, min(512, count)
    out = pl.BlockSpec((rows, tile), lambda i: (i, part))
    shape = jax.ShapeDtypeStruct((count, units), LOW)
    return pl.pallas_call(
        lift_kernel,
        grid=(count // rows,),
        in_specs=[
            pl.BlockSpec((rows, width), lambda i: (i, 0)),
            pl.BlockSpec((width, 2 * tile), lambda i: (0, part)),
        ]
        + [pl.BlockSpec(memory_space=pl.ANY)] * len(begun),
        out_specs=[out] * 3,
        out_shape=[shape] * 3,
        input_output_aliases={2 + k: k for k in range(len(begun))},
        compiler_params=pltpu.CompilerParams(vmem_limit_bytes=VMEM_LIMIT),
        cost_estimate=pl.CostEstimate(
            flops=2 * count * width * units, bytes_accessed=20_000_000, transcendentals=0
        ),
    )(tokens, weights, *begun)


def lift_back_rows(weights, grads, slope_up, gated, lifted):
    units = slope_up.shape[1]
    tile = units // 2
    for j in range(2):
        here_units = slice(j * tile, (j + 1) * tile)
        grad = inner_cols(grads[...], weights[here_units, :])
        start = 2 * j * tile
        lifted[:, start : start + tile] = (grad * slope_up[:, here_units].astype(jnp.float32)).astype(LOW)
        lifted[:, start + tile : start + 2 * tile] = (
            grad * gated[:, here_units].astype(jnp.float32)
        ).astype(LOW)


def lift_back_work(stage, weights, extra, made):
    grads, slope_up, gated, tokens = extra
    lifted, grad_weights = made
    count, units = slope_up.shape
    width = tokens.shape[1]
    if stage < 2:
        rows = count // 4
        first = stage * (count // 2)
        at = pl.ds(first, count // 2)
        pltpu.emit_pipeline(
            functools.partial(lift_back_rows, weights),
            grid=(2,),
            in_specs=[
                pl.BlockSpec((rows, width), lambda i: (i, 0)),
                pl.BlockSpec((rows, units), lambda i: (i, 0)),
                pl.BlockSpec((rows, units), lambda i: (i, 0)),
            ],
            out_specs=[pl.BlockSpec((rows, 2 * units), lambda i: (i, 0))],
        )(grads.at[at], slope_up.at[at], gated.at[at], lifted.at[at])

    def inner(left, right, out):
        out[...] = inner_rows(left[...], right[...]).astype(LOW)

    if stage > 0:
        part, tile = width // 2, units // 2
        part_units = pl.ds((stage - 1) * units, units)
        pltpu.emit_pipeline(
            inner,
            grid=(2, 2),
            in_specs=[
                pl.BlockSpec((count, part), lambda i, j: (0, i)),
                pl.BlockSpec((count, tile), lambda i, j: (0, j)),
            ],
            out_specs=[pl.BlockSpec((part, tile), lambda i, j: (i, j))],
        )(tokens, lifted.at[:, part_units], grad_weights.at[:, part_units])


def lift_back_plain(grads, weights, slope_up, gated):
    grad = inner_cols(grads, weights)
    up, through = (grad * f.astype(jnp.float32) for f in (slope_up, gated))
    return pair_units(up, through).astype(LOW)


def attend_plain(projected, sequences):
    tokens, columns = projected.shape[0], projected.shape[1] // 3
    length = tokens // sequences
    shape = (sequences, length, columns // HEAD_DIM, HEAD_DIM)
    cosine, sine = rotation_tables(length)
    query = turn(projected[:, :columns].reshape(shape), cosine, sine).astype(LOW)
    keys = turn(projected[:, columns : 2 * columns].reshape(shape), cosine, sine).astype(LOW)
    values = projected[:, 2 * columns :].reshape(shape).astype(LOW)
    mixed, logsum = attend(query, keys, values)
    flat = (tokens, columns)
    return mixed.reshape(flat), query.reshape(flat), keys.reshape(flat), values.reshape(flat), logsum


def attend_plain_back(query, keys, values, grad_mixed, logsum, sequences, swap, collective_id):
    tokens, columns = query.shape
    length = tokens // sequences
    shape = (sequences, length, columns // HEAD_DIM, HEAD_DIM)
    cosine, sine = rotation_tables(length)
    grad_query, grad_keys, grad_values = attend_back(
        *(a.reshape(shape) for a in (query, keys, values, grad_mixed)), logsum
    )
    grads = (turn_back(grad_query, cosine, sine), turn_back(grad_keys, cosine, sine), grad_values)
    grads = jnp.concatenate([g.reshape(tokens, columns).astype(LOW) for g in grads], 1)
    return [grads] + [dp_other(m) for m in swap]


def body(
    hidden_in, w_query, w_key, w_value, w_out, w_gate, w_up, w_down, norm_attn, norm_ffn, grad_out
):
    rows, cols, parts = lax.axis_size("row"), lax.axis_size("col"), lax.axis_size("dp")
    own_kernels = (parts, rows, cols) == (2, 4, 4)
    plane, enter = (plane_call, enter_call) if own_kernels else (plain_call, enter_plain)
    count, width = hidden_in.shape[0] // rows, hidden_in.shape[1] * rows
    full_rows = jax.ShapeDtypeStruct((count, width), jnp.float32)
    gain_rows = jax.ShapeDtypeStruct((8, width), jnp.float32)

    local_gains = jnp.pad(jnp.stack([norm_attn, norm_ffn]), ((0, 6), (0, 0)))
    own_attn = [my_part(w, 1) for w in (w_query, w_key, w_value)] + [stack(my_part(w_out, 0))]
    w_attn = lax.all_gather(jnp.concatenate(own_attn, 1), "row", axis=0, tiled=True)
    normed_one, grad_wide, held, grad_here, gains = enter(hidden_in, grad_out, local_gains, 1)
    own_ffn = pair_units(my_part(w_gate, 1), my_part(w_up, 1))
    w_ffn = lax.all_gather(own_ffn, "row", axis=0, tiled=True)
    own_back, normed_one = after(my_part(w_down, 0), normed_one)
    if own_kernels:
        ahead, back = [pass_on(own_back, 1, 0)], [pass_on(own_back, -1, 0)]
    else:
        w_back = lax.all_gather(own_back, "row", axis=0, tiled=True)

    columns = w_attn.shape[1] // 4
    projected = dot(normed_one, w_attn[:, : 3 * columns])
    paired = columns % (2 * HEAD_DIM) == 0
    mixed, query, keys, values, logsum = (attend_pairs if paired else attend_plain)(projected, parts)
    normed_two, middle = plane(
        "sum", "gather", SecondNorm, mixed, [held, gains], [full_rows], 2, w_attn, "stacked"
    )

    if own_kernels:
        ahead[0], back[0], normed_two = after(ahead[0], back[0], normed_two)
        ahead.append(pass_on(ahead[0], 1, 1))
        back.append(pass_on(back[0], -1, 1))
    w_proj, w_ffn = after(unstack(w_attn[:, 3 * columns :], columns), w_ffn)
    begun = lift(normed_two, w_ffn, 0)
    if own_kernels:
        ahead[1], back[1], *begun = after(ahead[1], back[1], *begun)
        ahead.append(pass_on(ahead[1], 1, 2))
        back.append(pass_on(back[1], -1, 2))
        w_back = [own_back, *ahead, *back]
    activated, slope_up, gated = lift(normed_two, w_ffn, 1, begun)
    part_down = inner_rows(activated, grad_wide).astype(LOW)
    part_down, w_back = after(part_down, w_back)
    mine_down = row_sum(part_down, 1)
    low = functools.partial(jax.ShapeDtypeStruct, dtype=LOW)
    out_rows, grad_lifted, part_ffn = plane(
        "sum",
        "stay",
        Add,
        activated,
        [middle],
        [],
        3,
        w_back,
        "blocks" if own_kernels else "stacked",
        beside_work=lift_back_work,
        extra=[grad_wide, slope_up, gated, normed_two],
        made=[low((normed_two.shape[0], w_ffn.shape[1])), low((width, w_ffn.shape[1]))],
    )
    mine_ffn = row_sum(part_ffn, 0)
    grad_branch, grad_middle, gain_two, layer_out = plane(
        "sum",
        "gather",
        BackSecond,
        grad_lifted,
        [middle, grad_here, gains],
        [full_rows, gain_rows],
        4,
        w_ffn,
        "turned",
        ship=[out_rows],
    )
    grad_branch, mine_down = after(grad_branch, mine_down)
    grad_mixed = inner_cols(grad_branch, w_proj).astype(LOW)
    part_out, grad_mixed = after(inner_rows(mixed, grad_branch).astype(LOW), grad_mixed)
    grad_projected, other_down = (attend_pairs_back if paired else attend_plain_back)(
        query, keys, values, grad_mixed, logsum, parts, [mine_down], 5
    )
    part_attn = inner_rows(normed_one, grad_projected).astype(LOW)
    grad_in, gain_grads, _, other_ffn, grad_wq, grad_wk, grad_wv, grad_attn_out = plane(
        "sum",
        "homes",
        BackFirst,
        grad_projected,
        [held, grad_middle, gains, gain_two],
        [jax.ShapeDtypeStruct((8, norm_attn.shape[0]), jnp.float32), gain_rows],
        6,
        w_attn,
        "turned",
        totals=True,
        swap=[mine_ffn],
        line=[part_attn, part_out],
        line_axes=(0, 1),
        line_pieces=(3, 1),
    )
    grad_down = join_wide(mine_down, other_down)
    grad_gate, grad_up = join_tall(mine_ffn, other_ffn, [(0, 2), (1, 3)])
    return (
        layer_out,
        grad_in,
        grad_wq,
        grad_wk,
        grad_wv,
        grad_attn_out,
        grad_gate,
        grad_up,
        grad_down,
        gain_grads[0],
        gain_grads[1],
    )


def solution(mesh):
    tokens = P(("dp", "col"), "row")
    tall = P("row", "col")
    wide = P("col", "row")
    gain = P("row")
    return jax.shard_map(
        body,
        mesh=mesh,
        in_specs=(tokens, tall, tall, tall, wide, tall, tall, wide, gain, gain, tokens),
        out_specs=(tokens, tokens, tall, tall, tall, wide, tall, tall, wide, gain, gain),
        check_vma=False,
    )
```

```python
import functools

import jax
import jax.numpy as jnp
from jax import lax
from jax.experimental import pallas as pl
from jax.experimental.pallas import tpu as pltpu
from jax.sharding import PartitionSpec as P

HEAD_DIM = 64
EPSILON = 1e-05
THETA = 130000.0
GROUP = ("dp", "col")
LOW = jnp.bfloat16


def dot(left, right):
    return jnp.dot(left, right, preferred_element_type=jnp.float32)


def inner_rows(left, right):
    return lax.dot_general(
        left, right, (((0,), (0,)), ((), ())), preferred_element_type=jnp.float32
    )


def inner_cols(left, right):
    return lax.dot_general(
        left, right, (((1,), (1,)), ((), ())), preferred_element_type=jnp.float32
    )


def seat_pairs():
    rows, cols = lax.axis_size("row"), lax.axis_size("col")
    per = cols // rows
    return [
        (r * cols + c, (c // per) * cols + (c % per) * rows + r)
        for r in range(rows)
        for c in range(cols)
    ]


def to_group(block):
    whole = lax.all_to_all(block, "row", split_axis=0, concat_axis=1, tiled=True)
    return lax.ppermute(whole, ("row", "col"), seat_pairs())


def from_group(block):
    back = lax.ppermute(block, ("row", "col"), [(b, a) for a, b in seat_pairs()])
    return lax.all_to_all(back, "row", split_axis=1, concat_axis=0, tiled=True)


def group_gather(shard):
    return lax.all_gather(shard, GROUP, axis=0, tiled=True)


def group_scatter(partial):
    return lax.psum_scatter(
        partial.astype(LOW), GROUP, scatter_dimension=0, tiled=True
    ).astype(jnp.float32)


def my_part(block, axis):
    size = block.shape[axis] // lax.axis_size("dp")
    return lax.dynamic_slice_in_dim(block, lax.axis_index("dp") * size, size, axis)


def halves(block):
    middle = block.shape[1] // 2
    return [block[:, :middle], block[:, middle:]]


def pair_units(gate, upward):
    (g, h), (u, v) = halves(gate), halves(upward)
    return jnp.concatenate([g, u, h, v], 1)


def stack(block):
    units = block.shape[0]
    return jnp.concatenate([block[:, i : i + units] for i in range(0, block.shape[1], units)], 0)


def unstack(blocks, units):
    return jnp.concatenate([blocks[i : i + units] for i in range(0, blocks.shape[0], units)], 1)


def after(*values):
    return lax.optimization_barrier(values)


def pass_on(block, way, first):
    rows = lax.axis_size("row")
    pairs = [(i, i + 1) for i in range(first, rows - 1)]
    if way < 0:
        pairs = [(rows - 1 - i, rows - 1 - j) for i, j in pairs]
    return lax.ppermute(block, "row", pairs)


def dp_other(mine):
    if lax.axis_size("dp") == 2:
        return lax.ppermute(mine, "dp", [(0, 1), (1, 0)])
    return lax.all_gather(mine, "dp", axis=0)


def dp_parts(mine, other):
    if lax.axis_size("dp") != 2:
        return list(other)
    lower = lax.axis_index("dp") == 0
    return [jnp.where(lower, mine, other), jnp.where(lower, other, mine)]


def row_sum(part, axis):
    return lax.psum_scatter(part, "row", scatter_dimension=axis, tiled=True)


def join_tall(mine, other, pieces):
    width = mine.shape[1] // sum(map(len, pieces))
    cuts = [slice(i * width, (i + 1) * width) for i in range(mine.shape[1] // width)]
    cut = [dp_parts(mine[:, at], other[..., at]) for at in cuts]
    return [
        jnp.concatenate([cut[i][d] for d in range(len(cut[0])) for i in piece], 1).astype(jnp.float32)
        for piece in pieces
    ]


def join_wide(mine, other):
    return jnp.concatenate(dp_parts(mine, other), 0).astype(jnp.float32)


def rms_scale(values):
    return lax.rsqrt(jnp.mean(values * values, axis=1, keepdims=True) + EPSILON)


def norm_back(values, scale, weighted):
    inner = jnp.mean(weighted * values, axis=1, keepdims=True)
    return scale * weighted - values * (scale * scale * scale * inner)


def rotation_tables(length):
    half = HEAD_DIM // 2
    freq = THETA ** (-(jnp.arange(half, dtype=jnp.float32) * 2.0 / HEAD_DIM))
    angle = jnp.arange(length, dtype=jnp.float32)[:, None] * freq[None, :]
    cosine = jnp.concatenate([jnp.cos(angle), jnp.cos(angle)], 1)[None, :, None, :]
    sine = jnp.concatenate([jnp.sin(angle), jnp.sin(angle)], 1)[None, :, None, :]
    return (cosine, sine)


def turn(values, cosine, sine):
    half = values.shape[-1] // 2
    turned = jnp.concatenate([-values[..., half:], values[..., :half]], -1)
    return values * cosine + turned * sine


def turn_back(grads, cosine, sine):
    half = grads.shape[-1] // 2
    moved = grads * sine
    return grads * cosine + jnp.concatenate([moved[..., half:], -moved[..., :half]], -1)


def masked_scores(query, keys):
    scores = jnp.einsum(
        "sqhd,skhd->shqk", query, keys, preferred_element_type=jnp.float32
    ) * HEAD_DIM ** (-0.5)
    length = query.shape[1]
    allowed = jnp.arange(length)[:, None] >= jnp.arange(length)[None, :]
    return jnp.where(allowed[None, None], scores, -jnp.inf)


def attend(query, keys, values):
    scores = masked_scores(query, keys)
    highest = jnp.max(scores, axis=-1, keepdims=True)
    expo = jnp.exp(scores - highest)
    total = jnp.sum(expo, axis=-1, keepdims=True)
    low_probs = (expo / total).astype(LOW)
    mixed = jnp.einsum(
        "shqk,skhd->sqhd", low_probs, values, preferred_element_type=jnp.float32
    ).astype(LOW)
    return mixed, highest + jnp.log(total)


def attend_back(query, keys, values, grad_mixed, logsum):
    scale = HEAD_DIM ** (-0.5)
    probs = jnp.exp(masked_scores(query, keys) - logsum)
    low_probs = probs.astype(LOW)
    dprobs = jnp.einsum("sqhd,skhd->shqk", grad_mixed, values, preferred_element_type=jnp.float32)
    grad_values = jnp.einsum(
        "shqk,sqhd->skhd", low_probs, grad_mixed, preferred_element_type=jnp.float32
    )
    low_scores = (probs * (dprobs - jnp.sum(probs * dprobs, axis=-1, keepdims=True))).astype(LOW)
    grad_query = (
        jnp.einsum("shqk,skhd->sqhd", low_scores, keys, preferred_element_type=jnp.float32) * scale
    )
    grad_keys = (
        jnp.einsum("shqk,sqhd->skhd", low_scores, query, preferred_element_type=jnp.float32) * scale
    )
    return grad_query, grad_keys, grad_values


MESH = pl.DeviceIdType.MESH
STEP = 16
VMEM_LIMIT = 56 * 1024 * 1024


class Wires:
    def __init__(self, send, recv):
        self.send, self.recv, self.used, self.sent = send, recv, 0, []

    def slots(self, count):
        first = self.used
        self.used += count
        return first

    def copy(self, source, target, slot, device, landing=None):
        return pltpu.make_async_remote_copy(
            src_ref=source,
            dst_ref=target,
            send_sem=self.send.at[slot],
            recv_sem=self.recv.at[slot if landing is None else landing],
            device_id=device,
            device_id_type=MESH,
        )

    def start(self, source, target, slot, device):
        copy = self.copy(source, target, slot, device)
        copy.start()
        self.sent.append(copy)
        return copy

    def finish(self):
        for copy in self.sent:
            copy.wait_send()


def here():
    x, r, c = lax.axis_index("dp"), lax.axis_index("row"), lax.axis_index("col")
    mate = (x, r, c + 1 - 2 * lax.rem(c, 2))
    beside = (1 - x, r, c)
    above = (x, r, lax.rem(c + 2, 4))
    return (x, r, c), mate, beside, above


def seat_of(x, r, c, rows, cols, piece):
    per = cols // rows
    return (x, lax.div(c, per), lax.rem(c, per) * rows + piece)


def home_of(x, r, c, rows, cols, source):
    per = cols // rows
    return (x, source, r * per + lax.div(c, rows))


def greet(devices, count):
    barrier = pltpu.get_barrier_semaphore()
    for device, remote in devices:
        if remote is None:
            pl.semaphore_signal(barrier, inc=1, device_id=device, device_id_type=MESH)
        else:

            @pl.when(remote)
            def _():
                pl.semaphore_signal(barrier, inc=1, device_id=device, device_id_type=MESH)

    pl.semaphore_wait(barrier, count)


COLUMNS = 1024
SWAPS = (2, 4)
DISTANCES = (0, -1, -2, -3, 1, 2, 3)


def weight_block(source, held, i, form, depth, size):
    if form == "turned":
        at = pl.ds(pl.multiple_of(i * size, size), size)
        return source.at[at, :depth], held.at[at, :]
    return (
        source.at[pl.ds(pl.multiple_of(i * depth, depth), depth), source.shape[1] - size :],
        held.at[:, pl.ds(pl.multiple_of(i * size, size), size)],
    )


def product_into(target, left, held, form, arrive=None):
    width = target.shape[1]
    size = min(COLUMNS, width)

    @pl.loop(0, width // size)
    def _(i):
        if arrive is not None:
            arrive(i, size)
        at = pl.ds(pl.multiple_of(i * size, size), size)
        if form == "turned":
            value = inner_cols(left[...], held[at, :])
        else:
            value = dot(left[...], held[:, at])
        target[:, at] = value.astype(LOW)


class PlaneGather:
    def __init__(self, wires, shard, main, sems, cols):
        (x, _, c), self.mate, self.beside, self.above = here()
        self.wires, self.shard, self.main, self.sems = wires, shard, main, sems
        half = shard.shape[0] // 2
        self.halves = [pl.ds(0, half), pl.ds(half, half)]
        self.spot = x * cols + c
        self.beside_spot, self.above_spot = self.beside[0] * cols + c, x * cols + self.above[2]
        self.corner_spot = self.beside[0] * cols + self.above[2]
        self.kept, self.to_mate, self.from_beside, self.from_above = [], [], [], []

    def start(self, i):
        part, target = self.shard.at[self.halves[i]], self.main.at[self.spot, self.halves[i]]
        self.kept.append(pltpu.make_async_copy(part, target, self.sems.at[i]))
        self.kept[-1].start()
        slot = self.wires.slots(3)
        self.from_beside.append(self.wires.start(part, target, slot, self.beside))
        self.from_above.append(self.wires.start(part, target, slot + 1, self.above))
        self.to_mate.append(self.wires.start(part, target, slot + 2, self.mate))

    def finish(self):
        slot = self.wires.slots(5)
        start, main = self.wires.start, self.main
        self.from_beside[0].wait_recv()
        part = main.at[self.beside_spot, self.halves[0]]
        corner_low = start(part, part, slot, self.above)
        self.from_above[0].wait_recv()
        self.from_above[1].wait_recv()
        part = main.at[self.above_spot, self.halves[1]]
        corner_high = start(part, part, slot + 1, self.beside)
        part = main.at[self.above_spot]
        self.to_mate.append(start(part, part, slot + 2, self.mate))
        self.from_beside[1].wait_recv()
        part = main.at[self.beside_spot]
        self.to_mate.append(start(part, part, slot + 3, self.mate))
        corner_low.wait_recv()
        corner_high.wait_recv()
        part = main.at[self.corner_spot]
        self.to_mate.append(start(part, part, slot + 4, self.mate))
        for copy in self.to_mate:
            copy.wait_recv()
        for copy in self.kept:
            copy.wait()


class Homing:
    def __init__(self, wires, shard, main, sem, rows, cols):
        x, r, c = here()[0]
        self.wires, self.shard, self.main, self.sem, self.rows = wires, shard, main, sem, rows
        self.seats = [seat_of(x, r, c, rows, cols, p) for p in range(rows)]
        self.homes = [home_of(x, r, c, rows, cols, s) for s in range(rows)]
        self.me, self.place = (x, r, c), lax.rem(c, rows)
        self.count, self.block = shard.shape[0], shard.shape[1] // rows

    def away(self, device):
        return jnp.logical_not(jnp.logical_and(device[1] == self.me[1], device[2] == self.me[2]))

    def sends(self):
        mine = pl.ds(pl.multiple_of(self.place * self.count, self.count), self.count)
        for s, home in enumerate(self.homes):
            part = self.shard.at[:, pl.ds(s * self.block, self.block)]
            there = self.wires.copy(part, self.main.at[mine], self.slot + s, home, self.slot + self.place)
            yield self.away(home), there, part, self.main.at[mine]

    def start(self):
        self.slot = self.wires.slots(self.rows)
        for remote, there, part, target in self.sends():
            pl.when(remote)(there.start)
            pl.when(jnp.logical_not(remote))(pltpu.make_async_copy(part, target, self.sem).start)

    def finish(self):
        for p, seat in enumerate(self.seats):
            part = self.main.at[pl.ds(p * self.count, self.count)]
            remote = self.away(seat)
            pl.when(remote)(self.wires.copy(part, part, self.slot + p, seat).wait_recv)
            pl.when(jnp.logical_not(remote))(pltpu.make_async_copy(part, part, self.sem).wait)
        for remote, there, _, _ in self.sends():
            pl.when(remote)(there.wait_send)


class LineSum:
    def __init__(self, wires, part, axis, columns, out, scratch, sems, rows):
        x, r, c = here()[0]
        self.wires, self.out, self.axis, self.rows, self.x, self.r = wires, out, axis, rows, x, r
        self.boxes, self.own, self.other = scratch[:2], scratch[2], scratch[3]
        self.devices = [(x, lax.rem(r + 1, rows), c), (x, lax.rem(r + rows - 1, rows), c)]
        self.beside = (1 - x, r, c)
        self.slot = wires.slots(2 * (rows - 1) + 1)
        size = part.shape[axis] // rows
        blocks = [pl.ds(k * size, size) for k in range(rows)]
        self.loads = [
            pltpu.make_async_copy(
                part.at[at, columns] if axis == 0 else part.at[:, at], self.own.at[k], sems.at[k]
            )
            for k, at in enumerate(blocks)
        ]
        for load in self.loads:
            load.start()

    def greeted(self):
        return [(self.devices[0], self.r < self.rows - 1), (self.devices[1], self.r > 0)]

    def blocks(self, step):
        return [lax.rem(2 * self.rows - step + self.r, self.rows), lax.rem(self.rows + self.r + step, self.rows)]

    def copies(self, step):
        return [
            self.wires.copy(self.own.at[s], box.at[step - 1], self.slot + 2 * (step - 1) + i, device)
            for i, (s, box, device) in enumerate(zip(self.blocks(step), self.boxes, self.devices))
        ]

    def sends(self, step):
        r, rows = self.r, self.rows
        return [(r < step) & (r < rows - 1), (r > rows - 1 - step) & (r > 0)]

    def arrivals(self, step):
        r, rows = self.r, self.rows
        return [(r > 0) & (r <= step), (r < rows - 1) & (r >= rows - 1 - step)]

    def chunk(self):
        rows, width = self.other.shape
        return min(rows, STEP * max(1, 2048 // width))

    def gain(self, step, blocks):
        copies, size = self.copies(step), self.chunk()
        for there, copy, s, box in zip(self.arrivals(step), copies, blocks, self.boxes):

            @pl.when(there)
            def _():
                copy.wait_recv()

                @pl.loop(0, self.other.shape[0] // size)
                def _(i):
                    at = pl.ds(pl.multiple_of(i * size, size), size)
                    total = self.own[s, at, :].astype(jnp.float32)
                    self.own[s, at, :] = (total + box[step - 1, at, :].astype(jnp.float32)).astype(LOW)

    def advance(self, step):
        if step == 1:
            for load in self.loads:
                load.wait()
        else:
            self.gain(step - 1, self.blocks(step))
        for there, copy in zip(self.sends(step), self.copies(step)):
            pl.when(there)(copy.start)

    def complete(self):
        self.gain(self.rows - 1, [self.r, self.r])

    def end(self):
        self.share = self.wires.start(self.own.at[self.r], self.other, self.slot + 2 * self.rows - 2, self.beside)
        self.write(lambda at: self.own[self.r, at, :], self.x)

    def finish(self):
        self.share.wait_recv()
        self.write(lambda at: self.other[at, :], 1 - self.x)
        for step in range(1, self.rows):
            for there, copy in zip(self.sends(step), self.copies(step)):
                pl.when(there)(copy.wait_send)

    def write(self, share, place):
        rows, width = self.other.shape
        size = self.chunk()

        @pl.loop(0, rows // size)
        def _(k):
            at = pl.multiple_of(k * size, size)
            value = share(pl.ds(at, size)).astype(jnp.float32)
            if self.axis == 0:
                self.out[pl.ds(at, size), pl.ds(pl.multiple_of(place * width, width), width)] = value
            else:
                self.out[pl.ds(pl.multiple_of(place * rows + at, size), size), :] = value


def plane_kernel(rows, cols, entry, leave, mid, counts, beside_work, line_axes, totals, form, *refs):
    n_blocks, n_small, n_out, n_swap, n_extra, n_made, n_ship, n_lines = counts
    refs = list(refs)
    big = refs.pop(0)
    blocks = [refs.pop(0) for _ in range(n_blocks)]
    weights = blocks[0]
    small = [refs.pop(0) for _ in range(n_small)]
    mine_parts = [refs.pop(0) for _ in range(n_swap)]
    extra = [refs.pop(0) for _ in range(n_extra)]
    leaving = [refs.pop(0) for _ in range(n_ship)]
    line_parts = [refs.pop(0) for _ in line_axes]
    main = refs.pop(0)
    outs = [refs.pop(0) for _ in range(n_out)]
    other_parts = [refs.pop(0) for _ in range(n_swap)]
    made = [refs.pop(0) for _ in range(n_made)]
    landing = [refs.pop(0) for _ in range(n_ship)]
    line_outs = [refs.pop(0) for _ in range(sum(n_lines))]
    shard, send, recv, local = (refs.pop(0) for _ in range(4))
    if totals:
        total, inbox, line_inbox = (refs.pop() for _ in range(3))
    line_scratch = [[refs.pop(8) for _ in range(4)] for _ in line_outs]
    wires = Wires(send, recv)
    me, mate, beside, above = here()
    x, r, c = me
    count, width = shard.shape
    half = count // 2
    low_half, high_half = pl.ds(0, half), pl.ds(half, half)
    homing = None
    if leave == "homes":
        homing = Homing(wires, shard, main, local.at[20], rows, cols)
    elif n_ship:
        homing = Homing(wires, leaving[0], landing[0], local.at[22], rows, cols)
    if leave == "gather":
        gather = PlaneGather(wires, shard, main, local.at[pl.ds(20, 2)], cols)
    greeted = []
    expected = 0
    if homing is not None:
        stays = (lax.div(c, cols // rows) == r) & (lax.rem(c, cols // rows) * rows + lax.rem(c, rows) == c)
        greeted += [(s, homing.away(s)) for s in homing.seats]
        expected = expected + rows - jnp.where(stays, 1, 0).astype(jnp.int32)
    lines = []
    for part, axis, pieces in zip(line_parts, line_axes, n_lines):
        for k in range(pieces):
            i, size = len(lines), part.shape[1] // pieces
            sems = local.at[pl.ds(24 + rows * i, rows)]
            columns = slice(k * size, (k + 1) * size)
            lines.append(LineSum(wires, part, axis, columns, line_outs[i], line_scratch[i], sems, rows))
    for line in lines[:1]:
        greeted += line.greeted()
        expected = expected + sum(jnp.where(there, 1, 0).astype(jnp.int32) for _, there in line.greeted())
    if totals:
        others = [(x, lax.rem(r + k, rows), c) for k in range(1, rows)]
        greeted += [(o, None) for o in others]
        expected = expected + rows - 1
    greeted += [(mate, None), (beside, None), (above, None)]
    swaps = []

    def send_swaps(first, last):
        for source, target in zip(mine_parts, other_parts):
            size = source.shape[0] // 4
            if first == last:
                return
            part = pl.ds(first * size, (last - first) * size)
            swaps.append(wires.start(source.at[part], target.at[part], wires.slots(1), beside))

    if entry == "sum":
        depth = big.shape[2]
        if form == "blocks":
            block_width = weights.shape[1]
        else:
            block_width = min(COLUMNS, width) if form == "turned" else width * depth // weights.shape[0]

        def fetch(i, source=weights):
            if form == "blocks":
                ends = source, refs[1].at[:, pl.ds(pl.multiple_of(i * block_width, block_width), block_width)]
            else:
                ends = weight_block(source, refs[1], i, form, depth, block_width)
            return pltpu.make_async_copy(*ends, local.at[4 + i])

        def arrive(i, size):
            for k in range(size // block_width):
                fetch(i * (size // block_width) + k).wait()

        @pl.loop(0, width // block_width)
        def _(i):
            if form == "blocks":
                for distance, block in zip(DISTANCES, blocks):
                    pl.when(i == r + distance)(fetch(i, block).start)
            else:
                fetch(i).start()

        chips = [(1 - x, above[2]), (1 - x, c), (x, above[2]), (x, c)]
        loads = [
            pltpu.make_async_copy(big.at[(tx * cols + tc) // 2], refs[0].at[k], local.at[k])
            for k, (tx, tc) in enumerate(chips)
        ]
        for load in loads:
            load.start()
    greet(greeted, expected + 3)
    if n_ship:
        homing.start()
    for line in lines:
        line.advance(1)

    if entry == "sum":
        factors, held_weights, both, mated, beside_pass, above_pass, beside_in, above_in = refs
        first = wires.slots(4)
        handed = []
        core = lax.rem(c, 2)
        own_start = pl.multiple_of(core * count, count)
        given_rows = pl.ds(pl.multiple_of((1 - core) * count, count), count)

        def own_rows(start, size):
            return pl.ds(pl.multiple_of(own_start + start, size), size)

        def supply(k, arrive=None):
            loads[k].wait()
            product_into(both.at[k], factors.at[k], held_weights, form, arrive)
            handed.append(wires.start(both.at[k, given_rows], mated.at[k], first + k, mate))

        def add(k, more, start, size):
            @pl.loop(0, size // STEP)
            def _(i):
                at = own_rows(start + i * STEP, STEP)
                to = pl.ds(pl.multiple_of(start + i * STEP, STEP), STEP)
                both[k, at, :] = (
                    both[k, at, :].astype(jnp.float32) + more(to).astype(jnp.float32)
                ).astype(LOW)

        def merge(k):
            handed[k].wait_recv()
            add(k, lambda at: mated[k, at, :], 0, count)

        own_low, own_high = own_rows(0, half), own_rows(half, half)
        if lines:
            send_swaps(0, SWAPS[0])
            slot = wires.slots(6)
            supply(0, arrive)
            handed[0].wait_recv()
            passes = []
            for k, rows_out in enumerate((own_low, own_high)):
                add(0, lambda at: mated[0, at, :], k * half, half)
                to = above_pass.at[pl.ds(k * half, half)]
                passes.append(wires.start(both.at[0, rows_out], to, slot + k, above))
            supply(1)
            merge(1)
            supply(2)
            merge(2)
            above_low = wires.start(both.at[2, own_low], above_in.at[low_half], slot + 2, above)
            above_high = wires.start(both.at[2, own_high], above_in.at[high_half], slot + 3, above)
            supply(3)
            passes[0].wait_recv()
            add(1, lambda at: above_pass[at, :], 0, half)
            beside_low = wires.start(both.at[1, own_low], beside_in.at[low_half], slot + 4, beside)
            for line in lines:
                line.advance(2)
            passes[1].wait_recv()
            add(1, lambda at: above_pass[at, :], half, half)
            beside_high = wires.start(both.at[1, own_high], beside_in.at[high_half], slot + 5, beside)
            send_swaps(SWAPS[0], SWAPS[1])
            groups = [lines[: len(lines) // 2], lines[len(lines) // 2 :]]
            for line in groups[0]:
                line.advance(3)
        else:
            slot = wires.slots(6)
            supply(0, arrive)
            handed[0].wait_recv()
            add(0, lambda at: mated[0, at, :], 0, half)
            pass_beside = wires.start(both.at[0, own_low], beside_pass, slot, beside)
            add(0, lambda at: mated[0, at, :], half, half)
            pass_above = wires.start(both.at[0, own_high], above_pass, slot + 1, above)
            supply(1)
            merge(1)
            beside_low = wires.start(both.at[1, own_low], beside_in.at[low_half], slot + 2, beside)
            supply(2)
            merge(2)
            pass_beside.wait_recv()
            add(2, lambda at: beside_pass[at, :], 0, half)
            above_low = wires.start(both.at[2, own_low], above_in.at[low_half], slot + 3, above)
            above_high = wires.start(both.at[2, own_high], above_in.at[high_half], slot + 4, above)
            supply(3)
            if beside_work is not None:
                beside_work(0, held_weights, extra, made)
            pass_above.wait_recv()
            add(1, lambda at: above_pass[pl.ds(pl.multiple_of(at.start - half, STEP), STEP), :], half, half)
            beside_high = wires.start(both.at[1, own_high], beside_in.at[high_half], slot + 5, beside)
        if beside_work is not None:
            beside_work(1, held_weights, extra, made)
        handed[3].wait_recv()

        def value(at):
            near = both[3, own_rows(at.start, STEP), :].astype(jnp.float32)
            near = near + mated[3, at, :].astype(jnp.float32)
            return near + (beside_in[at, :].astype(jnp.float32) + above_in[at, :].astype(jnp.float32))

    mid.start(outs)
    for k in range(2):
        if entry == "sum":
            (beside_low, beside_high)[k].wait_recv()
            (above_low, above_high)[k].wait_recv()

        @pl.loop(k * (half // STEP), (k + 1) * (half // STEP))
        def _(i):
            at = pl.ds(pl.multiple_of(i * STEP, STEP), STEP)
            shard[at, :] = mid.rows(at, value(at), small, outs).astype(LOW)

        if leave == "gather":
            gather.start(k)

    if leave == "gather":
        gather.finish()
    elif leave == "homes":
        if not lines:
            homing.start()
    else:
        keep = pltpu.make_async_copy(shard, main, local.at[20])
        keep.start()
    if leave == "stay":
        keep.wait()
    if not lines:
        send_swaps(0, 4)
    if totals and not lines:
        gain_sums(wires, me, (mate, beside, above), others, rows, small[-1], outs, total, inbox, line_inbox)
    for k, group in enumerate(groups if lines else ()):
        for line in group:
            line.complete()
        if k == 0:
            for line in groups[1]:
                line.advance(rows - 1)
            gain_sums(wires, me, (mate, beside, above), others, rows, small[-1], outs, total, inbox, line_inbox)
        else:
            homing.start()
        for line in group:
            line.end()
        if k == 1:
            send_swaps(SWAPS[1], 4)
    for line in lines:
        line.finish()
    if homing is not None:
        homing.finish()
    if n_swap:
        for copy in swaps:
            copy.wait_recv()
    wires.finish()


def enter_kernel(
    rows, cols, hidden_in, grad_out, gains_in, normed, grads, held, grad_here, gains,
    shard, seated, grad_seated, hidden_relay, grad_relay, landing, send, recv, local,
):
    wires = Wires(send, recv)
    me, mate, beside, above = here()
    x, r, c = me
    count, width = seated.shape
    block = width // rows
    side = 2 * lax.div(c, 2)
    far = 2 - side
    ways = [(x, c, side), (x, c, side + 1), (x, above[2], side), (x, above[2], side + 1)]
    via = side + lax.rem(r, 2)
    sources = [(x, s, via) for s in range(rows)]
    others = [(x, lax.rem(r + k, rows), c) for k in range(1, rows)]

    def away(device):
        return jnp.logical_not(jnp.logical_and(device[1] == r, device[2] == c))

    kept = jnp.where(lax.rem(c, 2) == lax.rem(r, 2), 1, 0).astype(jnp.int32)
    greeted = [(s, away(s)) for s in sources] + [(o, None) for o in others]
    greeted += [(above, None), (mate, None), (beside, None)]
    greet(greeted, 2 * rows + 2 - kept)

    mine = pl.ds(pl.multiple_of(r * block, block), block)
    slot = wires.slots(rows - 1)
    spread = [wires.start(gains_in, landing.at[r], slot + k, other) for k, other in enumerate(others)]

    class Seating:
        def __init__(self, source, target, relay, sem):
            self.source, self.target, self.relay, self.sem = source, target, relay, sem
            self.slot, self.hop = wires.slots(rows), wires.slots(1)

        def pieces(self):
            near = pl.multiple_of(side * count, count)
            return [
                self.source.at[pl.ds(near, count)],
                self.source.at[pl.ds(near + count, count)],
                self.relay.at[pl.ds(0, count)],
                self.relay.at[pl.ds(count, count)],
            ]

        def cross(self):
            across = self.source.at[pl.ds(pl.multiple_of(far * count, count), 2 * count)]
            self.crossing = wires.start(across, self.relay, self.hop, above)

        def go(self, which):
            for i in which:
                piece, seat = self.pieces()[i], ways[i]
                there = wires.copy(piece, self.target.at[:, mine], self.slot + i, seat, self.slot + r)
                stay = pltpu.make_async_copy(piece, self.target.at[:, mine], self.sem)
                pl.when(away(seat))(there.start)
                pl.when(jnp.logical_not(away(seat)))(stay.start)

        def arrive(self):
            for s, source in enumerate(sources):
                part = self.target.at[:, pl.ds(s * block, block)]
                arrived = wires.copy(part, part, self.slot + s, source)
                stay = pltpu.make_async_copy(part, part, self.sem)
                pl.when(away(source))(arrived.wait_recv)
                pl.when(jnp.logical_not(away(source)))(stay.wait)

        def sent(self):
            for i, piece in enumerate(self.pieces()):
                there = wires.copy(piece, self.target.at[:, mine], self.slot + i, ways[i])
                pl.when(away(ways[i]))(there.wait_send)

    hidden = Seating(hidden_in, seated, hidden_relay, local.at[0])
    grad = Seating(grad_out, grad_seated, grad_relay, local.at[1])
    hidden.cross()
    hidden.go((0, 1))
    grad.cross()
    hidden.crossing.wait_recv()
    hidden.go((2, 3))
    for copy in spread:
        copy.wait_recv()
    landing[r] = gains_in[...]
    for s in range(rows):
        gains[:, s * block : (s + 1) * block] = landing[s]
    hidden.arrive()
    grad.go((0, 1))
    grad.crossing.wait_recv()
    grad.go((2, 3))
    keep = pltpu.make_async_copy(seated, held, local.at[2])
    keep.start()

    gather = PlaneGather(wires, shard, normed, local.at[pl.ds(4, 2)], cols)
    for k in range(2):

        @pl.loop(k * (count // STEP // 2), (k + 1) * (count // STEP // 2))
        def _(i):
            at = pl.ds(pl.multiple_of(i * STEP, STEP), STEP)
            value = seated[at, :].astype(jnp.float32)
            shard[at, :] = (value * rms_scale(value) * gains[0:1, :]).astype(LOW)

        gather.start(k)
    gather.finish()
    grad.arrive()
    keep_grad = pltpu.make_async_copy(grad_seated, grad_here, local.at[3])
    keep_grad.start()
    gather = PlaneGather(wires, grad_seated, grads, local.at[pl.ds(6, 2)], cols)
    gather.start(0)
    gather.start(1)
    gather.finish()
    hidden.sent()
    grad.sent()
    keep.wait()
    keep_grad.wait()
    wires.finish()


def enter_call(hidden_in, grad_out, gains, collective_id):
    rows, cols, parts = lax.axis_size("row"), lax.axis_size("col"), lax.axis_size("dp")
    count, width = hidden_in.shape[0] // rows, hidden_in.shape[1] * rows
    block = width // rows
    vmem = pl.BlockSpec(memory_space=pltpu.VMEM)
    hbm = pl.BlockSpec(memory_space=pl.ANY)
    shape = jax.ShapeDtypeStruct((count, width), LOW)
    tile = pltpu.VMEM((count, width), LOW)
    relay = pltpu.VMEM((2 * count, block), LOW)
    whole = jax.ShapeDtypeStruct((parts * cols, count, width), LOW)
    normed, grads, held, grad_here, gains = pl.pallas_call(
        functools.partial(enter_kernel, rows, cols),
        out_shape=[whole, whole, shape, shape, jax.ShapeDtypeStruct((8, width), jnp.float32)],
        in_specs=[hbm, hbm, vmem],
        out_specs=[hbm, hbm, hbm, hbm, vmem],
        scratch_shapes=[tile, tile, tile, relay, relay, pltpu.VMEM((rows, 8, block), jnp.float32)]
        + [pltpu.SemaphoreType.DMA((48,))] * 2
        + [pltpu.SemaphoreType.DMA((8,))],
        compiler_params=pltpu.CompilerParams(
            collective_id=collective_id, has_side_effects=True, vmem_limit_bytes=VMEM_LIMIT
        ),
        cost_estimate=pl.CostEstimate(flops=0, bytes_accessed=20_000_000, transcendentals=0),
    )(hidden_in, grad_out, gains)
    flat = (parts * cols * count, width)
    return normed.reshape(flat), grads.reshape(flat), held, grad_here, gains


def enter_plain(hidden_in, grad_out, gains, collective_id):
    gains = lax.all_gather(gains, "row", axis=1, tiled=True)
    held = to_group(hidden_in)
    value = held.astype(jnp.float32)
    normed = group_gather((value * rms_scale(value) * gains[0:1]).astype(LOW))
    grad_here = to_group(grad_out)
    return normed, group_gather(grad_here), held, grad_here, gains


def gain_sums(wires, me, partners, others, rows, gain_two, outs, total, inbox, line_inbox):
    x, r, c = me
    block = total.shape[1] // rows
    total[0:1, :] = jnp.sum(outs[1][...], axis=0, keepdims=True)
    total[1:2, :] = jnp.sum(gain_two[...], axis=0, keepdims=True)
    total[2:, :] = jnp.zeros_like(total[2:, :])
    first = wires.slots(len(partners))
    for k, partner in enumerate(partners):
        copy = wires.copy(total, inbox.at[k], first + k, partner)
        copy.start()
        copy.wait()
        total[...] += inbox[k]
    first = wires.slots(len(others))
    copies = []
    for k, (_, row, _) in enumerate(others):
        part = total.at[:, pl.ds(pl.multiple_of(row * block, block), block)]
        copies.append(wires.start(part, line_inbox.at[r], first + k, others[k]))
    line_inbox[r] = total[:, pl.ds(pl.multiple_of(r * block, block), block)]
    for copy in copies:
        copy.wait_recv()
    outs[0][...] = sum(line_inbox[k] for k in range(rows))


def plane_call(
    entry, leave, mid, big, small, outs, collective_id, weights=None, form=None, totals=False, swap=(),
    beside_work=None, extra=(), made=(), ship=(), line=(), line_axes=(), line_pieces=(),
):
    rows, cols, parts = lax.axis_size("row"), lax.axis_size("col"), lax.axis_size("dp")
    count, width = big.shape[0] // (parts * cols), small[0].shape[1]
    depth = big.shape[1]
    big = big.reshape(parts * cols // 2, 2 * count, depth)
    gathered = leave == "gather"
    shape = {"gather": (parts * cols, count, width), "homes": (rows * count, width // rows), "stay": (count, width)}[leave]
    landed = [jax.ShapeDtypeStruct((rows * a.shape[0], a.shape[1] // rows), a.dtype) for a in ship]
    plain = len(swap) + len(made) + len(ship)
    vmem = pl.BlockSpec(memory_space=pltpu.VMEM)
    hbm = pl.BlockSpec(memory_space=pl.ANY)
    tile = pltpu.VMEM((count, width), LOW)
    whole, part = pltpu.VMEM((4, count, width), LOW), pltpu.VMEM((count // 2, width), LOW)
    scratch = [tile, pltpu.SemaphoreType.DMA((64,)), pltpu.SemaphoreType.DMA((64,)), pltpu.SemaphoreType.DMA((40,))]
    scratch += [
        pltpu.VMEM(big.shape, LOW),
        pltpu.VMEM((width, depth) if form == "turned" else (depth, width), LOW),
        pltpu.VMEM((4, 2 * count, width), LOW),
    ]
    scratch += [whole, part, tile if line else part, tile, tile]
    line_outs = []
    for array, axis, pieces in zip(line, line_axes, line_pieces):
        block = [n // rows if i == axis else n for i, n in enumerate(array.shape)]
        block[1] //= pieces
        scratch += ([pltpu.VMEM((n, *block), LOW) for n in (rows - 1, rows - 1, rows)] + [pltpu.VMEM(tuple(block), LOW)]) * pieces
        block[1 - axis] *= parts
        line_outs += [jax.ShapeDtypeStruct(tuple(block), jnp.float32)] * pieces
    if totals:
        scratch += [
            pltpu.VMEM((rows, 8, width // rows), jnp.float32),
            pltpu.VMEM((3, 8, width), jnp.float32),
            pltpu.VMEM((8, width), jnp.float32),
        ]
    blocks = weights if form == "blocks" else [weights]
    counts = (len(blocks), len(small), len(outs), len(swap), len(extra), len(made), len(ship), tuple(line_pieces))
    main, *others = pl.pallas_call(
        functools.partial(plane_kernel, rows, cols, entry, leave, mid, counts, beside_work, line_axes, totals, form),
        out_shape=[jax.ShapeDtypeStruct(shape, LOW)]
        + list(outs)
        + [jax.ShapeDtypeStruct(m.shape, m.dtype) for m in (*swap, *made, *landed, *line_outs)],
        in_specs=[hbm] * (1 + len(blocks)) + [vmem] * len(small) + [hbm] * (len(swap) + len(extra) + len(ship) + len(line)),
        out_specs=[hbm] + [vmem] * len(outs) + [hbm] * plain + [vmem] * len(line_outs),
        scratch_shapes=scratch,
        compiler_params=pltpu.CompilerParams(
            collective_id=collective_id, has_side_effects=True, vmem_limit_bytes=VMEM_LIMIT
        ),
        cost_estimate=pl.CostEstimate(flops=0, bytes_accessed=20_000_000, transcendentals=0),
    )(big, *blocks, *small, *swap, *extra, *ship, *line)
    if gathered:
        main = main.reshape(parts * cols * count, width)
    return [main, *others]


def fold(values):
    return values.reshape(values.shape[0] // 8, 8, values.shape[1]).sum(0)


class Mid:
    @staticmethod
    def start(outs):
        pass


class SecondNorm(Mid):
    @staticmethod
    def rows(at, value, small, outs):
        held, gains = small
        middle = held[at, :].astype(jnp.float32) + value
        outs[0][at, :] = middle
        return middle * rms_scale(middle) * gains[1:2, :]


class Add(Mid):
    @staticmethod
    def rows(at, value, small, outs):
        return small[0][at, :] + value


class BackSecond(Mid):
    @staticmethod
    def start(outs):
        outs[1][...] = jnp.zeros_like(outs[1])

    @staticmethod
    def rows(at, value, small, outs):
        middle, grad_out, gains = small
        middle = middle[at, :]
        scale = rms_scale(middle)
        outs[1][...] += fold(value * middle * scale)
        grad = grad_out[at, :].astype(jnp.float32) + norm_back(
            middle, scale, value * gains[1:2, :]
        )
        outs[0][at, :] = grad
        return grad


class BackFirst(Mid):
    @staticmethod
    def start(outs):
        outs[1][...] = jnp.zeros_like(outs[1])

    @staticmethod
    def rows(at, value, small, outs):
        held, grad_middle, gains = small[:3]
        inputs = held[at, :].astype(jnp.float32)
        scale = rms_scale(inputs)
        outs[1][...] += fold(value * inputs * scale)
        return grad_middle[at, :] + norm_back(inputs, scale, value * gains[0:1, :])


def plain_call(
    entry, leave, mid, big, small, outs, collective_id, weights=None, form=None, totals=False, swap=(),
    beside_work=None, extra=(), made=(), ship=(), line=(), line_axes=(), line_pieces=(),
):
    refs = [Holder(a) for a in small]
    given = [Holder(jnp.zeros(o.shape, o.dtype)) for o in outs]
    depth, width = big.shape[1], small[0].shape[1]
    if form == "turned":
        product = inner_cols(big, weights[:, :depth])
    else:
        block = width * depth // weights.shape[0]
        whole = unstack(weights[:, weights.shape[1] - block :], depth)
        product = dot(big, whole)
    mid.start(given)
    shard = mid.rows(slice(None), group_scatter(product), refs, given).astype(LOW)
    main = {"gather": group_gather, "homes": from_group, "stay": lambda a: a}[leave](shard)
    if totals:
        sums = jnp.stack([given[1].value.sum(0), small[-1].sum(0)])
        sums = jnp.pad(lax.psum(sums, ("dp", "row", "col")), ((0, 6), (0, 0)))
        part = outs[0].shape[1]
        given[0].value = lax.dynamic_slice_in_dim(sums, lax.axis_index("row") * part, part, 1)
    others = [dp_other(m) for m in swap]
    if beside_work is not None:
        grads, slope_up, gated, tokens = extra
        lifted = lift_back_plain(grads, whole, slope_up, gated)
        others += [lifted, inner_rows(tokens, lifted).astype(LOW)]
    others += [from_group(a) for a in ship]
    for array, axis, pieces in zip(line, line_axes, line_pieces):
        mine = row_sum(array, axis)
        other = dp_other(mine)
        others += join_tall(mine, other, [(i,) for i in range(pieces)]) if axis == 0 else [join_wide(mine, other)]
    return [main] + [g.value for g in given] + others


class Holder:
    def __init__(self, value):
        self.value, self.dtype, self.shape = value, value.dtype, value.shape

    def __getitem__(self, at):
        return self.value[at]

    def __setitem__(self, at, value):
        self.value = self.value.at[at].set(value)


def swap_halves(values, first):
    lanes = values.shape[1]
    half = HEAD_DIM // 2
    return jnp.where(first, pltpu.roll(values, lanes - half, 1), pltpu.roll(values, half, 1))


def attend_kernel(query, key, value, cosine, sine, mixed, q_out, k_out, v_out, logsum):
    length, lanes = query.shape
    block = min(256, length)
    lane = lax.broadcasted_iota(jnp.int32, (length, lanes), 1)
    first = lax.rem(lane, HEAD_DIM) < HEAD_DIM // 2
    cos, sin = cosine[...], sine[...]

    def rotate(values):
        return (values * cos + swap_halves(values, first) * sin).astype(LOW)

    q_out[...] = rotate(query[...])
    k_out[...] = rotate(key[...])
    low_values = value[...].astype(LOW)
    v_out[...] = low_values
    v_turned = low_values.astype(jnp.float32).T.astype(LOW)
    head = lax.broadcasted_iota(jnp.int32, (block, lanes), 1) // HEAD_DIM
    keep = lax.broadcasted_iota(jnp.int32, (block, block), 0) <= lax.broadcasted_iota(
        jnp.int32, (block, block), 1
    )
    for j in range(length // block):
        at = slice(j * block, (j + 1) * block)
        q_block = q_out[at, :].astype(jnp.float32) * HEAD_DIM ** (-0.5)
        parts = []
        for h in range(lanes // HEAD_DIM):
            q_head = jnp.where(head == h, q_block, 0.0).astype(LOW)
            near = jnp.where(keep, inner_cols(k_out[at, :], q_head), -jnp.inf)
            highest = jnp.max(near, axis=0, keepdims=True)
            if j:
                far = inner_cols(k_out[: j * block, :], q_head)
                highest = jnp.maximum(highest, jnp.max(far, axis=0, keepdims=True))
                far = jnp.exp(far - highest)
            near = jnp.exp(near - highest)
            total = jnp.sum(near, axis=0, keepdims=True)
            if j:
                total = total + jnp.sum(far, axis=0, keepdims=True)
            logsum[0, 0, h : h + 1, at] = highest + jnp.log(total)
            share = 1.0 / total
            out = dot(v_turned[:, at], (near * share).astype(LOW))
            if j:
                out = out + dot(v_turned[:, : j * block], (far * share).astype(LOW))
            parts.append(out[h * HEAD_DIM : (h + 1) * HEAD_DIM])
        mixed[at, :] = jnp.concatenate(parts, 0).T.astype(LOW)


def attend_back_kernel(n_swap, query, key, value, grad, logsum, cosine, sine, *refs):
    mine_parts, refs = refs[:n_swap], refs[n_swap:]
    made, refs = refs[0], refs[1:]
    other_parts, refs = refs[:n_swap], refs[n_swap:]
    (k_sum, v_sum, q_out, k_out, v_out, out_sems), refs = refs[:6], refs[6:]
    length, lanes = query.shape
    if n_swap:
        beside = here()[2]
        wires = Wires(*refs)
        swaps = [
            wires.copy(source, target, i, beside)
            for i, (source, target) in enumerate(zip(mine_parts, other_parts))
        ]
        here_first = (pl.program_id(0) == 0) & (pl.program_id(1) == 0)
        here_last = (pl.program_id(0) == pl.num_programs(0) - 1) & (
            pl.program_id(1) == pl.num_programs(1) - 1
        )

        @pl.when(here_first)
        def _():
            greet([(beside, None)], 1)
            for copy in swaps:
                copy.start()

    block = min(256, length)
    k_sum[...] = jnp.zeros_like(k_sum)
    v_sum[...] = jnp.zeros_like(v_sum)
    k_turned = key[...].astype(jnp.float32).T.astype(LOW)
    head = lax.broadcasted_iota(jnp.int32, (block, lanes), 1) // HEAD_DIM
    keep = lax.broadcasted_iota(jnp.int32, (block, block), 0) <= lax.broadcasted_iota(
        jnp.int32, (block, block), 1
    )
    scale = HEAD_DIM ** (-0.5)

    def rotate_back(values, at):
        rows = values.shape[0]
        lane = lax.broadcasted_iota(jnp.int32, (rows, lanes), 1)
        first = lax.rem(lane, HEAD_DIM) < HEAD_DIM // 2
        return (values * cosine[at, :] - swap_halves(values, first) * sine[at, :]).astype(LOW)

    for j in range(length // block):
        at = slice(j * block, (j + 1) * block)
        before = slice(0, j * block)
        q_block = query[at, :].astype(jnp.float32) * scale
        g_block = grad[at, :].astype(jnp.float32)
        parts = []
        for h in range(lanes // HEAD_DIM):
            q_head = jnp.where(head == h, q_block, 0.0).astype(LOW)
            g_head = jnp.where(head == h, g_block, 0.0).astype(LOW)
            level = logsum[0, 0, h : h + 1, at]
            near = jnp.exp(jnp.where(keep, inner_cols(key[at, :], q_head), -jnp.inf) - level)
            d_near = inner_cols(value[at, :], g_head)
            inner = jnp.sum(near * d_near, axis=0, keepdims=True)
            if j:
                far = jnp.exp(inner_cols(key[before, :], q_head) - level)
                d_far = inner_cols(value[before, :], g_head)
                inner = inner + jnp.sum(far * d_far, axis=0, keepdims=True)
                v_sum[before, :] += dot(far.astype(LOW), g_head)
                s_far = (far * (d_far - inner)).astype(LOW)
                k_sum[before, :] += dot(s_far, q_head)
            v_sum[at, :] += dot(near.astype(LOW), g_head)
            s_near = (near * (d_near - inner)).astype(LOW)
            k_sum[at, :] += dot(s_near, q_head)
            out = dot(k_turned[:, at], s_near)
            if j:
                out = out + dot(k_turned[:, before], s_far)
            parts.append(out[h * HEAD_DIM : (h + 1) * HEAD_DIM])
        q_out[at, :] = rotate_back(jnp.concatenate(parts, 0).T * scale, at)
    k_out[...] = rotate_back(k_sum[...], slice(None))
    v_out[...] = v_sum[...].astype(LOW)
    rows_at = pl.ds(pl.multiple_of(pl.program_id(0) * length, length), length)
    columns = made.shape[1] // 3
    copies = [
        pltpu.make_async_copy(
            out,
            made.at[rows_at, pl.ds(pl.multiple_of(i * columns + pl.program_id(1) * lanes, lanes), lanes)],
            out_sems.at[i],
        )
        for i, out in enumerate((q_out, k_out, v_out))
    ]
    for copy in copies:
        copy.start()
    for copy in copies:
        copy.wait()
    if n_swap:

        @pl.when(here_last)
        def _():
            for copy in swaps:
                copy.wait()


def pair_tables(length):
    half = HEAD_DIM // 2
    freq = THETA ** (-(jnp.arange(half, dtype=jnp.float32) * 2.0 / HEAD_DIM))
    angle = jnp.arange(length, dtype=jnp.float32)[:, None] * freq[None, :]
    cosine, sine = jnp.cos(angle), jnp.sin(angle)
    return jnp.tile(cosine, (1, 4)), jnp.tile(jnp.concatenate([-sine, sine], 1), (1, 2))


def attend_pairs(projected, sequences):
    tokens, columns = projected.shape[0], projected.shape[1] // 3
    length, lanes = tokens // sequences, 2 * HEAD_DIM
    pairs = columns // lanes
    cosine, sine = pair_tables(length)

    def spec(offset):
        return pl.BlockSpec((length, lanes), lambda s, h: (s, offset + h))

    table = pl.BlockSpec((length, lanes), lambda s, h: (0, 0))
    level = pl.BlockSpec((1, 1, 2, length), lambda s, h: (s, h, 0, 0))
    shape = jax.ShapeDtypeStruct((tokens, columns), LOW)
    return pl.pallas_call(
        attend_kernel,
        grid=(sequences, pairs),
        in_specs=[spec(0), spec(pairs), spec(2 * pairs), table, table],
        out_specs=[spec(0)] * 4 + [level],
        out_shape=[shape] * 4 + [jax.ShapeDtypeStruct((sequences, pairs, 2, length), jnp.float32)],
        compiler_params=pltpu.CompilerParams(vmem_limit_bytes=VMEM_LIMIT),
        cost_estimate=pl.CostEstimate(
            flops=8 * tokens * length * columns, bytes_accessed=100_000_000, transcendentals=0
        ),
    )(projected, projected, projected, cosine, sine)


def attend_pairs_back(query, keys, values, grad_mixed, logsum, sequences, swap, collective_id):
    tokens, columns = query.shape
    length, lanes = tokens // sequences, 2 * HEAD_DIM
    pairs = columns // lanes
    cosine, sine = pair_tables(length)
    spec = pl.BlockSpec((length, lanes), lambda s, h: (s, h))
    table = pl.BlockSpec((length, lanes), lambda s, h: (0, 0))
    level = pl.BlockSpec((1, 1, 2, length), lambda s, h: (s, h, 0, 0))
    hbm = pl.BlockSpec(memory_space=pl.ANY)
    return pl.pallas_call(
        functools.partial(attend_back_kernel, len(swap)),
        grid=(sequences, pairs),
        in_specs=[spec] * 4 + [level, table, table] + [hbm] * len(swap),
        out_specs=[hbm] * (1 + len(swap)),
        out_shape=[jax.ShapeDtypeStruct((tokens, 3 * columns), LOW)] + [jax.ShapeDtypeStruct(m.shape, m.dtype) for m in swap],
        scratch_shapes=[pltpu.VMEM((length, lanes), jnp.float32)] * 2
        + [pltpu.VMEM((length, lanes), LOW)] * 3
        + [pltpu.SemaphoreType.DMA((4,))] * 3,
        compiler_params=pltpu.CompilerParams(
            collective_id=collective_id, has_side_effects=True, vmem_limit_bytes=VMEM_LIMIT
        ),
        cost_estimate=pl.CostEstimate(
            flops=20 * tokens * length * columns, bytes_accessed=60_000_000, transcendentals=0
        ),
    )(query, keys, values, grad_mixed, logsum, cosine, sine, *swap)


def lift_kernel(tokens, weights, *refs):
    activated, slope_up, gated = refs[-3:]
    rows, width = activated.shape
    step = min(256, rows)
    for i in range(rows // step):
        at = slice(i * step, (i + 1) * step)
        left = tokens[at, :]
        both = dot(left, weights[...])
        gate, upward = both[:, :width], both[:, width:]
        sigmoid = 1.0 / (1.0 + jnp.exp(-gate))
        passed = gate * sigmoid
        activated[at, :] = (passed * upward).astype(LOW)
        gated[at, :] = passed.astype(LOW)
        slope_up[at, :] = (upward * (sigmoid + passed * (1.0 - sigmoid))).astype(LOW)


def lift(tokens, weights, part, begun=()):
    count, width = tokens.shape
    units = weights.shape[1] // 2
    tile, rows = units // 2, min(512, count)
    out = pl.BlockSpec((rows, tile), lambda i: (i, part))
    shape = jax.ShapeDtypeStruct((count, units), LOW)
    return pl.pallas_call(
        lift_kernel,
        grid=(count // rows,),
        in_specs=[
            pl.BlockSpec((rows, width), lambda i: (i, 0)),
            pl.BlockSpec((width, 2 * tile), lambda i: (0, part)),
        ]
        + [pl.BlockSpec(memory_space=pl.ANY)] * len(begun),
        out_specs=[out] * 3,
        out_shape=[shape] * 3,
        input_output_aliases={2 + k: k for k in range(len(begun))},
        compiler_params=pltpu.CompilerParams(vmem_limit_bytes=VMEM_LIMIT),
        cost_estimate=pl.CostEstimate(
            flops=2 * count * width * units, bytes_accessed=20_000_000, transcendentals=0
        ),
    )(tokens, weights, *begun)


def lift_back_rows(weights, grads, slope_up, gated, lifted):
    units = slope_up.shape[1]
    tile = units // 2
    for j in range(2):
        here_units = slice(j * tile, (j + 1) * tile)
        grad = inner_cols(grads[...], weights[here_units, :])
        start = 2 * j * tile
        lifted[:, start : start + tile] = (grad * slope_up[:, here_units].astype(jnp.float32)).astype(LOW)
        lifted[:, start + tile : start + 2 * tile] = (
            grad * gated[:, here_units].astype(jnp.float32)
        ).astype(LOW)


def lift_back_work(stage, weights, extra, made):
    grads, slope_up, gated, tokens = extra
    lifted, grad_weights = made
    count, units = slope_up.shape
    width = tokens.shape[1]
    if stage < 2:
        rows = count // 4
        first = stage * (count // 2)
        at = pl.ds(first, count // 2)
        pltpu.emit_pipeline(
            functools.partial(lift_back_rows, weights),
            grid=(2,),
            in_specs=[
                pl.BlockSpec((rows, width), lambda i: (i, 0)),
                pl.BlockSpec((rows, units), lambda i: (i, 0)),
                pl.BlockSpec((rows, units), lambda i: (i, 0)),
            ],
            out_specs=[pl.BlockSpec((rows, 2 * units), lambda i: (i, 0))],
        )(grads.at[at], slope_up.at[at], gated.at[at], lifted.at[at])

    def inner(left, right, out):
        out[...] = inner_rows(left[...], right[...]).astype(LOW)

    if stage == 1:
        part, tile = width // 2, units // 2
        pltpu.emit_pipeline(
            inner,
            grid=(2, 4),
            in_specs=[
                pl.BlockSpec((count, part), lambda i, j: (0, i)),
                pl.BlockSpec((count, tile), lambda i, j: (0, j)),
            ],
            out_specs=[pl.BlockSpec((part, tile), lambda i, j: (i, j))],
        )(tokens, lifted, grad_weights)


def lift_back_plain(grads, weights, slope_up, gated):
    grad = inner_cols(grads, weights)
    up, through = (grad * f.astype(jnp.float32) for f in (slope_up, gated))
    return pair_units(up, through).astype(LOW)


def attend_plain(projected, sequences):
    tokens, columns = projected.shape[0], projected.shape[1] // 3
    length = tokens // sequences
    shape = (sequences, length, columns // HEAD_DIM, HEAD_DIM)
    cosine, sine = rotation_tables(length)
    query = turn(projected[:, :columns].reshape(shape), cosine, sine).astype(LOW)
    keys = turn(projected[:, columns : 2 * columns].reshape(shape), cosine, sine).astype(LOW)
    values = projected[:, 2 * columns :].reshape(shape).astype(LOW)
    mixed, logsum = attend(query, keys, values)
    flat = (tokens, columns)
    return mixed.reshape(flat), query.reshape(flat), keys.reshape(flat), values.reshape(flat), logsum


def attend_plain_back(query, keys, values, grad_mixed, logsum, sequences, swap, collective_id):
    tokens, columns = query.shape
    length = tokens // sequences
    shape = (sequences, length, columns // HEAD_DIM, HEAD_DIM)
    cosine, sine = rotation_tables(length)
    grad_query, grad_keys, grad_values = attend_back(
        *(a.reshape(shape) for a in (query, keys, values, grad_mixed)), logsum
    )
    grads = (turn_back(grad_query, cosine, sine), turn_back(grad_keys, cosine, sine), grad_values)
    grads = jnp.concatenate([g.reshape(tokens, columns).astype(LOW) for g in grads], 1)
    return [grads] + [dp_other(m) for m in swap]


def body(
    hidden_in, w_query, w_key, w_value, w_out, w_gate, w_up, w_down, norm_attn, norm_ffn, grad_out
):
    rows, cols, parts = lax.axis_size("row"), lax.axis_size("col"), lax.axis_size("dp")
    own_kernels = (parts, rows, cols) == (2, 4, 4)
    plane, enter = (plane_call, enter_call) if own_kernels else (plain_call, enter_plain)
    count, width = hidden_in.shape[0] // rows, hidden_in.shape[1] * rows
    full_rows = jax.ShapeDtypeStruct((count, width), jnp.float32)
    gain_rows = jax.ShapeDtypeStruct((8, width), jnp.float32)

    local_gains = jnp.pad(jnp.stack([norm_attn, norm_ffn]), ((0, 6), (0, 0)))
    own_attn = [my_part(w, 1) for w in (w_query, w_key, w_value)] + [stack(my_part(w_out, 0))]
    w_attn = lax.all_gather(jnp.concatenate(own_attn, 1), "row", axis=0, tiled=True)
    normed_one, grad_wide, held, grad_here, gains = enter(hidden_in, grad_out, local_gains, 1)
    own_ffn = pair_units(my_part(w_gate, 1), my_part(w_up, 1))
    w_ffn = lax.all_gather(own_ffn, "row", axis=0, tiled=True)
    own_back, normed_one = after(my_part(w_down, 0), normed_one)
    if own_kernels:
        ahead, back = [pass_on(own_back, 1, 0)], [pass_on(own_back, -1, 0)]
    else:
        w_back = lax.all_gather(own_back, "row", axis=0, tiled=True)

    columns = w_attn.shape[1] // 4
    projected = dot(normed_one, w_attn[:, : 3 * columns])
    paired = columns % (2 * HEAD_DIM) == 0
    mixed, query, keys, values, logsum = (attend_pairs if paired else attend_plain)(projected, parts)
    normed_two, middle = plane(
        "sum", "gather", SecondNorm, mixed, [held, gains], [full_rows], 2, w_attn, "stacked"
    )

    if own_kernels:
        ahead[0], back[0], normed_two = after(ahead[0], back[0], normed_two)
        ahead.append(pass_on(ahead[0], 1, 1))
        back.append(pass_on(back[0], -1, 1))
    w_proj, w_ffn = after(unstack(w_attn[:, 3 * columns :], columns), w_ffn)
    begun = lift(normed_two, w_ffn, 0)
    if own_kernels:
        ahead[1], back[1], *begun = after(ahead[1], back[1], *begun)
        ahead.append(pass_on(ahead[1], 1, 2))
        back.append(pass_on(back[1], -1, 2))
        w_back = [own_back, *ahead, *back]
    activated, slope_up, gated = lift(normed_two, w_ffn, 1, begun)
    part_down = inner_rows(activated, grad_wide).astype(LOW)
    part_down, w_back = after(part_down, w_back)
    mine_down = row_sum(part_down, 1)
    low = functools.partial(jax.ShapeDtypeStruct, dtype=LOW)
    out_rows, grad_lifted, part_ffn = plane(
        "sum",
        "stay",
        Add,
        activated,
        [middle],
        [],
        3,
        w_back,
        "blocks" if own_kernels else "stacked",
        beside_work=lift_back_work,
        extra=[grad_wide, slope_up, gated, normed_two],
        made=[low((normed_two.shape[0], w_ffn.shape[1])), low((width, w_ffn.shape[1]))],
    )
    mine_ffn = row_sum(part_ffn, 0)
    grad_branch, grad_middle, gain_two, layer_out = plane(
        "sum",
        "gather",
        BackSecond,
        grad_lifted,
        [middle, grad_here, gains],
        [full_rows, gain_rows],
        4,
        w_ffn,
        "turned",
        ship=[out_rows],
    )
    grad_branch, mine_down = after(grad_branch, mine_down)
    grad_mixed = inner_cols(grad_branch, w_proj).astype(LOW)
    part_out, grad_mixed = after(inner_rows(mixed, grad_branch).astype(LOW), grad_mixed)
    grad_projected, other_down = (attend_pairs_back if paired else attend_plain_back)(
        query, keys, values, grad_mixed, logsum, parts, [mine_down], 5
    )
    part_attn = inner_rows(normed_one, grad_projected).astype(LOW)
    grad_in, gain_grads, _, other_ffn, grad_wq, grad_wk, grad_wv, grad_attn_out = plane(
        "sum",
        "homes",
        BackFirst,
        grad_projected,
        [held, grad_middle, gains, gain_two],
        [jax.ShapeDtypeStruct((8, norm_attn.shape[0]), jnp.float32), gain_rows],
        6,
        w_attn,
        "turned",
        totals=True,
        swap=[mine_ffn],
        line=[part_attn, part_out],
        line_axes=(0, 1),
        line_pieces=(3, 1),
    )
    grad_down = join_wide(mine_down, other_down)
    grad_gate, grad_up = join_tall(mine_ffn, other_ffn, [(0, 2), (1, 3)])
    return (
        layer_out,
        grad_in,
        grad_wq,
        grad_wk,
        grad_wv,
        grad_attn_out,
        grad_gate,
        grad_up,
        grad_down,
        gain_grads[0],
        gain_grads[1],
    )


def solution(mesh):
    tokens = P(("dp", "col"), "row")
    tall = P("row", "col")
    wide = P("col", "row")
    gain = P("row")
    return jax.shard_map(
        body,
        mesh=mesh,
        in_specs=(tokens, tall, tall, tall, wide, tall, tall, wide, gain, gain, tokens),
        out_specs=(tokens, tokens, tall, tall, tall, wide, tall, tall, wide, gain, gain),
        check_vma=False,
    )
```

```python
import functools

import jax
import jax.numpy as jnp
from jax import lax
from jax.experimental import pallas as pl
from jax.experimental.pallas import tpu as pltpu
from jax.sharding import PartitionSpec as P

HEAD_DIM = 64
EPSILON = 1e-05
THETA = 130000.0
GROUP = ("dp", "col")
LOW = jnp.bfloat16


def dot(left, right):
    return jnp.dot(left, right, preferred_element_type=jnp.float32)


def inner_rows(left, right):
    return lax.dot_general(
        left, right, (((0,), (0,)), ((), ())), preferred_element_type=jnp.float32
    )


def inner_cols(left, right):
    return lax.dot_general(
        left, right, (((1,), (1,)), ((), ())), preferred_element_type=jnp.float32
    )


def seat_pairs():
    rows, cols = lax.axis_size("row"), lax.axis_size("col")
    per = cols // rows
    return [
        (r * cols + c, (c // per) * cols + (c % per) * rows + r)
        for r in range(rows)
        for c in range(cols)
    ]


def to_group(block):
    whole = lax.all_to_all(block, "row", split_axis=0, concat_axis=1, tiled=True)
    return lax.ppermute(whole, ("row", "col"), seat_pairs())


def from_group(block):
    back = lax.ppermute(block, ("row", "col"), [(b, a) for a, b in seat_pairs()])
    return lax.all_to_all(back, "row", split_axis=1, concat_axis=0, tiled=True)


def group_gather(shard):
    return lax.all_gather(shard, GROUP, axis=0, tiled=True)


def group_scatter(partial):
    return lax.psum_scatter(
        partial.astype(LOW), GROUP, scatter_dimension=0, tiled=True
    ).astype(jnp.float32)


def my_part(block, axis):
    size = block.shape[axis] // lax.axis_size("dp")
    return lax.dynamic_slice_in_dim(block, lax.axis_index("dp") * size, size, axis)


def halves(block):
    middle = block.shape[1] // 2
    return [block[:, :middle], block[:, middle:]]


def pair_units(gate, upward):
    (g, h), (u, v) = halves(gate), halves(upward)
    return jnp.concatenate([g, u, h, v], 1)


def stack(block):
    units = block.shape[0]
    return jnp.concatenate([block[:, i : i + units] for i in range(0, block.shape[1], units)], 0)


def unstack(blocks, units):
    cut = blocks.reshape(-1, units, blocks.shape[1])
    return cut.transpose(1, 0, 2).reshape(units, -1)


def after(*values):
    return lax.optimization_barrier(values)


def pass_on(block, way, first):
    rows = lax.axis_size("row")
    pairs = [(i, i + 1) for i in range(first, rows - 1)]
    if way < 0:
        pairs = [(rows - 1 - i, rows - 1 - j) for i, j in pairs]
    return lax.ppermute(block, "row", pairs)


def dp_other(mine):
    if lax.axis_size("dp") == 2:
        return lax.ppermute(mine, "dp", [(0, 1), (1, 0)])
    return lax.all_gather(mine, "dp", axis=0)


def dp_parts(mine, other):
    if lax.axis_size("dp") != 2:
        return list(other)
    lower = lax.axis_index("dp") == 0
    return [jnp.where(lower, mine, other), jnp.where(lower, other, mine)]


def row_sum(part, axis):
    return lax.psum_scatter(part, "row", scatter_dimension=axis, tiled=True)


def join_tall(mine, other, pieces):
    width = mine.shape[1] // sum(map(len, pieces))
    cuts = [slice(i * width, (i + 1) * width) for i in range(mine.shape[1] // width)]
    cut = [dp_parts(mine[:, at], other[..., at]) for at in cuts]
    return [
        jnp.concatenate([cut[i][d] for d in range(len(cut[0])) for i in piece], 1).astype(jnp.float32)
        for piece in pieces
    ]


def join_wide(mine, other):
    return jnp.concatenate(dp_parts(mine, other), 0).astype(jnp.float32)


def rms_scale(values):
    return lax.rsqrt(jnp.mean(values * values, axis=1, keepdims=True) + EPSILON)


def norm_back(values, scale, weighted):
    inner = jnp.mean(weighted * values, axis=1, keepdims=True)
    return scale * weighted - values * (scale * scale * scale * inner)


def rotation_tables(length):
    half = HEAD_DIM // 2
    freq = THETA ** (-(jnp.arange(half, dtype=jnp.float32) * 2.0 / HEAD_DIM))
    angle = jnp.arange(length, dtype=jnp.float32)[:, None] * freq[None, :]
    cosine = jnp.concatenate([jnp.cos(angle), jnp.cos(angle)], 1)[None, :, None, :]
    sine = jnp.concatenate([jnp.sin(angle), jnp.sin(angle)], 1)[None, :, None, :]
    return (cosine, sine)


def turn(values, cosine, sine):
    half = values.shape[-1] // 2
    turned = jnp.concatenate([-values[..., half:], values[..., :half]], -1)
    return values * cosine + turned * sine


def turn_back(grads, cosine, sine):
    half = grads.shape[-1] // 2
    moved = grads * sine
    return grads * cosine + jnp.concatenate([moved[..., half:], -moved[..., :half]], -1)


def masked_scores(query, keys):
    scores = jnp.einsum(
        "sqhd,skhd->shqk", query, keys, preferred_element_type=jnp.float32
    ) * HEAD_DIM ** (-0.5)
    length = query.shape[1]
    allowed = jnp.arange(length)[:, None] >= jnp.arange(length)[None, :]
    return jnp.where(allowed[None, None], scores, -jnp.inf)


def attend(query, keys, values):
    scores = masked_scores(query, keys)
    highest = jnp.max(scores, axis=-1, keepdims=True)
    expo = jnp.exp(scores - highest)
    total = jnp.sum(expo, axis=-1, keepdims=True)
    low_probs = (expo / total).astype(LOW)
    mixed = jnp.einsum(
        "shqk,skhd->sqhd", low_probs, values, preferred_element_type=jnp.float32
    ).astype(LOW)
    return mixed, highest + jnp.log(total)


def attend_back(query, keys, values, grad_mixed, logsum):
    scale = HEAD_DIM ** (-0.5)
    probs = jnp.exp(masked_scores(query, keys) - logsum)
    low_probs = probs.astype(LOW)
    dprobs = jnp.einsum("sqhd,skhd->shqk", grad_mixed, values, preferred_element_type=jnp.float32)
    grad_values = jnp.einsum(
        "shqk,sqhd->skhd", low_probs, grad_mixed, preferred_element_type=jnp.float32
    )
    low_scores = (probs * (dprobs - jnp.sum(probs * dprobs, axis=-1, keepdims=True))).astype(LOW)
    grad_query = (
        jnp.einsum("shqk,skhd->sqhd", low_scores, keys, preferred_element_type=jnp.float32) * scale
    )
    grad_keys = (
        jnp.einsum("shqk,sqhd->skhd", low_scores, query, preferred_element_type=jnp.float32) * scale
    )
    return grad_query, grad_keys, grad_values


MESH = pl.DeviceIdType.MESH
STEP = 16
VMEM_LIMIT = 56 * 1024 * 1024


class Wires:
    def __init__(self, send, recv):
        self.send, self.recv, self.used, self.sent = send, recv, 0, []

    def slots(self, count):
        first = self.used
        self.used += count
        return first

    def copy(self, source, target, slot, device, landing=None):
        return pltpu.make_async_remote_copy(
            src_ref=source,
            dst_ref=target,
            send_sem=self.send.at[slot],
            recv_sem=self.recv.at[slot if landing is None else landing],
            device_id=device,
            device_id_type=MESH,
        )

    def start(self, source, target, slot, device):
        copy = self.copy(source, target, slot, device)
        copy.start()
        self.sent.append(copy)
        return copy

    def finish(self):
        for copy in self.sent:
            copy.wait_send()


def here():
    x, r, c = lax.axis_index("dp"), lax.axis_index("row"), lax.axis_index("col")
    mate = (x, r, c + 1 - 2 * lax.rem(c, 2))
    beside = (1 - x, r, c)
    above = (x, r, lax.rem(c + 2, 4))
    return (x, r, c), mate, beside, above


def seat_of(x, r, c, rows, cols, piece):
    per = cols // rows
    return (x, lax.div(c, per), lax.rem(c, per) * rows + piece)


def home_of(x, r, c, rows, cols, source):
    per = cols // rows
    return (x, source, r * per + lax.div(c, rows))


def greet(devices, count):
    barrier = pltpu.get_barrier_semaphore()
    for device, remote in devices:
        if remote is None:
            pl.semaphore_signal(barrier, inc=1, device_id=device, device_id_type=MESH)
        else:

            @pl.when(remote)
            def _():
                pl.semaphore_signal(barrier, inc=1, device_id=device, device_id_type=MESH)

    pl.semaphore_wait(barrier, count)


COLUMNS = 1024
SWAPS = (2, 4)
DISTANCES = (0, -1, -2, -3, 1, 2, 3)


def weight_block(source, held, i, form, depth, size):
    if form == "turned":
        at = pl.ds(pl.multiple_of(i * size, size), size)
        return source.at[at, :depth], held.at[at, :]
    return (
        source.at[pl.ds(pl.multiple_of(i * depth, depth), depth), source.shape[1] - size :],
        held.at[:, pl.ds(pl.multiple_of(i * size, size), size)],
    )


def product_into(target, left, held, form, arrive=None):
    width = target.shape[1]
    size = min(COLUMNS, width)

    @pl.loop(0, width // size)
    def _(i):
        if arrive is not None:
            arrive(i, size)
        at = pl.ds(pl.multiple_of(i * size, size), size)
        if form == "turned":
            value = inner_cols(left[...], held[at, :])
        else:
            value = dot(left[...], held[:, at])
        target[:, at] = value.astype(LOW)


class PlaneGather:
    def __init__(self, wires, shard, main, sems, cols):
        (x, _, c), self.mate, self.beside, self.above = here()
        self.wires, self.shard, self.main, self.sems = wires, shard, main, sems
        half = shard.shape[0] // 2
        self.halves = [pl.ds(0, half), pl.ds(half, half)]
        self.spot = x * cols + c
        self.beside_spot, self.above_spot = self.beside[0] * cols + c, x * cols + self.above[2]
        self.corner_spot = self.beside[0] * cols + self.above[2]
        self.kept, self.to_mate, self.from_beside, self.from_above = [], [], [], []

    def start(self, i):
        part, target = self.shard.at[self.halves[i]], self.main.at[self.spot, self.halves[i]]
        self.kept.append(pltpu.make_async_copy(part, target, self.sems.at[i]))
        self.kept[-1].start()
        slot = self.wires.slots(3)
        self.from_beside.append(self.wires.start(part, target, slot, self.beside))
        self.from_above.append(self.wires.start(part, target, slot + 1, self.above))
        self.to_mate.append(self.wires.start(part, target, slot + 2, self.mate))

    def finish(self):
        slot = self.wires.slots(5)
        start, main = self.wires.start, self.main
        self.from_beside[0].wait_recv()
        part = main.at[self.beside_spot, self.halves[0]]
        corner_low = start(part, part, slot, self.above)
        self.from_above[0].wait_recv()
        self.from_above[1].wait_recv()
        part = main.at[self.above_spot, self.halves[1]]
        corner_high = start(part, part, slot + 1, self.beside)
        part = main.at[self.above_spot]
        self.to_mate.append(start(part, part, slot + 2, self.mate))
        self.from_beside[1].wait_recv()
        part = main.at[self.beside_spot]
        self.to_mate.append(start(part, part, slot + 3, self.mate))
        corner_low.wait_recv()
        corner_high.wait_recv()
        part = main.at[self.corner_spot]
        self.to_mate.append(start(part, part, slot + 4, self.mate))
        for copy in self.to_mate:
            copy.wait_recv()
        for copy in self.kept:
            copy.wait()


class Homing:
    def __init__(self, wires, shard, main, sem, rows, cols):
        x, r, c = here()[0]
        self.wires, self.shard, self.main, self.sem, self.rows = wires, shard, main, sem, rows
        self.seats = [seat_of(x, r, c, rows, cols, p) for p in range(rows)]
        self.homes = [home_of(x, r, c, rows, cols, s) for s in range(rows)]
        self.me, self.place = (x, r, c), lax.rem(c, rows)
        self.count, self.block = shard.shape[0], shard.shape[1] // rows

    def away(self, device):
        return jnp.logical_not(jnp.logical_and(device[1] == self.me[1], device[2] == self.me[2]))

    def sends(self):
        mine = pl.ds(pl.multiple_of(self.place * self.count, self.count), self.count)
        for s, home in enumerate(self.homes):
            part = self.shard.at[:, pl.ds(s * self.block, self.block)]
            there = self.wires.copy(part, self.main.at[mine], self.slot + s, home, self.slot + self.place)
            yield self.away(home), there, part, self.main.at[mine]

    def start(self):
        self.slot = self.wires.slots(self.rows)
        for remote, there, part, target in self.sends():
            pl.when(remote)(there.start)
            pl.when(jnp.logical_not(remote))(pltpu.make_async_copy(part, target, self.sem).start)

    def finish(self):
        for p, seat in enumerate(self.seats):
            part = self.main.at[pl.ds(p * self.count, self.count)]
            remote = self.away(seat)
            pl.when(remote)(self.wires.copy(part, part, self.slot + p, seat).wait_recv)
            pl.when(jnp.logical_not(remote))(pltpu.make_async_copy(part, part, self.sem).wait)
        for remote, there, _, _ in self.sends():
            pl.when(remote)(there.wait_send)


class LineSum:
    def __init__(self, wires, part, axis, columns, out, scratch, sems, rows):
        x, r, c = here()[0]
        self.wires, self.out, self.axis, self.rows, self.x, self.r = wires, out, axis, rows, x, r
        self.boxes, self.own, self.other = scratch[:2], scratch[2], scratch[3]
        self.devices = [(x, lax.rem(r + 1, rows), c), (x, lax.rem(r + rows - 1, rows), c)]
        self.beside = (1 - x, r, c)
        self.slot = wires.slots(2 * (rows - 1) + 1)
        size = part.shape[axis] // rows
        blocks = [pl.ds(k * size, size) for k in range(rows)]
        self.loads = [
            pltpu.make_async_copy(
                part.at[at, columns] if axis == 0 else part.at[:, at], self.own.at[k], sems.at[k]
            )
            for k, at in enumerate(blocks)
        ]
        for load in self.loads:
            load.start()

    def greeted(self):
        return [(self.devices[0], self.r < self.rows - 1), (self.devices[1], self.r > 0)]

    def blocks(self, step):
        return [lax.rem(2 * self.rows - step + self.r, self.rows), lax.rem(self.rows + self.r + step, self.rows)]

    def copies(self, step):
        return [
            self.wires.copy(self.own.at[s], box.at[step - 1], self.slot + 2 * (step - 1) + i, device)
            for i, (s, box, device) in enumerate(zip(self.blocks(step), self.boxes, self.devices))
        ]

    def sends(self, step):
        r, rows = self.r, self.rows
        return [(r < step) & (r < rows - 1), (r > rows - 1 - step) & (r > 0)]

    def arrivals(self, step):
        r, rows = self.r, self.rows
        return [(r > 0) & (r <= step), (r < rows - 1) & (r >= rows - 1 - step)]

    def chunk(self):
        rows, width = self.other.shape
        return min(rows, STEP * max(1, 2048 // width))

    def gain(self, step, blocks):
        copies, size = self.copies(step), self.chunk()
        for there, copy, s, box in zip(self.arrivals(step), copies, blocks, self.boxes):

            @pl.when(there)
            def _():
                copy.wait_recv()

                @pl.loop(0, self.other.shape[0] // size)
                def _(i):
                    at = pl.ds(pl.multiple_of(i * size, size), size)
                    total = self.own[s, at, :].astype(jnp.float32)
                    self.own[s, at, :] = (total + box[step - 1, at, :].astype(jnp.float32)).astype(LOW)

    def advance(self, step):
        if step == 1:
            for load in self.loads:
                load.wait()
        else:
            self.gain(step - 1, self.blocks(step))
        for there, copy in zip(self.sends(step), self.copies(step)):
            pl.when(there)(copy.start)

    def complete(self):
        self.gain(self.rows - 1, [self.r, self.r])

    def end(self):
        self.share = self.wires.start(self.own.at[self.r], self.other, self.slot + 2 * self.rows - 2, self.beside)
        self.write(lambda at: self.own[self.r, at, :], self.x)

    def finish(self):
        self.share.wait_recv()
        self.write(lambda at: self.other[at, :], 1 - self.x)
        for step in range(1, self.rows):
            for there, copy in zip(self.sends(step), self.copies(step)):
                pl.when(there)(copy.wait_send)

    def write(self, share, place):
        rows, width = self.other.shape
        size = self.chunk()

        @pl.loop(0, rows // size)
        def _(k):
            at = pl.multiple_of(k * size, size)
            value = share(pl.ds(at, size)).astype(jnp.float32)
            if self.axis == 0:
                self.out[pl.ds(at, size), pl.ds(pl.multiple_of(place * width, width), width)] = value
            else:
                self.out[pl.ds(pl.multiple_of(place * rows + at, size), size), :] = value


def plane_kernel(rows, cols, entry, leave, mid, counts, beside_work, line_axes, totals, form, *refs):
    n_blocks, n_small, n_out, n_swap, n_extra, n_made, n_ship, n_lines = counts
    refs = list(refs)
    big = refs.pop(0)
    blocks = [refs.pop(0) for _ in range(n_blocks)]
    weights = blocks[0]
    small = [refs.pop(0) for _ in range(n_small)]
    mine_parts = [refs.pop(0) for _ in range(n_swap)]
    extra = [refs.pop(0) for _ in range(n_extra)]
    leaving = [refs.pop(0) for _ in range(n_ship)]
    line_parts = [refs.pop(0) for _ in line_axes]
    main = refs.pop(0)
    outs = [refs.pop(0) for _ in range(n_out)]
    other_parts = [refs.pop(0) for _ in range(n_swap)]
    made = [refs.pop(0) for _ in range(n_made)]
    landing = [refs.pop(0) for _ in range(n_ship)]
    line_outs = [refs.pop(0) for _ in range(sum(n_lines))]
    shard, send, recv, local = (refs.pop(0) for _ in range(4))
    if totals:
        total, inbox, line_inbox = (refs.pop() for _ in range(3))
    line_scratch = [[refs.pop(8) for _ in range(4)] for _ in line_outs]
    wires = Wires(send, recv)
    me, mate, beside, above = here()
    x, r, c = me
    count, width = shard.shape
    half = count // 2
    low_half, high_half = pl.ds(0, half), pl.ds(half, half)
    homing = None
    if leave == "homes":
        homing = Homing(wires, shard, main, local.at[20], rows, cols)
    elif n_ship:
        homing = Homing(wires, leaving[0], landing[0], local.at[22], rows, cols)
    if leave == "gather":
        gather = PlaneGather(wires, shard, main, local.at[pl.ds(20, 2)], cols)
    greeted = []
    expected = 0
    if homing is not None:
        stays = (lax.div(c, cols // rows) == r) & (lax.rem(c, cols // rows) * rows + lax.rem(c, rows) == c)
        greeted += [(s, homing.away(s)) for s in homing.seats]
        expected = expected + rows - jnp.where(stays, 1, 0).astype(jnp.int32)
    lines = []
    for part, axis, pieces in zip(line_parts, line_axes, n_lines):
        for k in range(pieces):
            i, size = len(lines), part.shape[1] // pieces
            sems = local.at[pl.ds(24 + rows * i, rows)]
            columns = slice(k * size, (k + 1) * size)
            lines.append(LineSum(wires, part, axis, columns, line_outs[i], line_scratch[i], sems, rows))
    for line in lines[:1]:
        greeted += line.greeted()
        expected = expected + sum(jnp.where(there, 1, 0).astype(jnp.int32) for _, there in line.greeted())
    if totals:
        others = [(x, lax.rem(r + k, rows), c) for k in range(1, rows)]
        greeted += [(o, None) for o in others]
        expected = expected + rows - 1
    greeted += [(mate, None), (beside, None), (above, None)]
    swaps = []

    def send_swaps(first, last):
        for source, target in zip(mine_parts, other_parts):
            size = source.shape[0] // 4
            if first == last:
                return
            part = pl.ds(first * size, (last - first) * size)
            swaps.append(wires.start(source.at[part], target.at[part], wires.slots(1), beside))

    if entry == "sum":
        depth = big.shape[2]
        if form == "blocks":
            block_width = weights.shape[1]
        else:
            block_width = min(COLUMNS, width) if form == "turned" else width * depth // weights.shape[0]

        def fetch(i, source=weights):
            if form == "blocks":
                ends = source, refs[1].at[:, pl.ds(pl.multiple_of(i * block_width, block_width), block_width)]
            else:
                ends = weight_block(source, refs[1], i, form, depth, block_width)
            return pltpu.make_async_copy(*ends, local.at[4 + i])

        def arrive(i, size):
            for k in range(size // block_width):
                fetch(i * (size // block_width) + k).wait()

        @pl.loop(0, width // block_width)
        def _(i):
            if form == "blocks":
                for distance, block in zip(DISTANCES, blocks):
                    pl.when(i == r + distance)(fetch(i, block).start)
            else:
                fetch(i).start()

        chips = [(1 - x, above[2]), (1 - x, c), (x, above[2]), (x, c)]
        loads = [
            pltpu.make_async_copy(big.at[(tx * cols + tc) // 2], refs[0].at[k], local.at[k])
            for k, (tx, tc) in enumerate(chips)
        ]
        for load in loads:
            load.start()
    greet(greeted, expected + 3)
    if n_ship:
        homing.start()
    for line in lines:
        line.advance(1)

    if entry == "sum":
        factors, held_weights, both, mated, beside_pass, above_pass, beside_in, above_in = refs
        first = wires.slots(4)
        handed = []
        core = lax.rem(c, 2)
        own_start = pl.multiple_of(core * count, count)
        given_rows = pl.ds(pl.multiple_of((1 - core) * count, count), count)

        def own_rows(start, size):
            return pl.ds(pl.multiple_of(own_start + start, size), size)

        def supply(k, arrive=None):
            loads[k].wait()
            product_into(both.at[k], factors.at[k], held_weights, form, arrive)
            handed.append(wires.start(both.at[k, given_rows], mated.at[k], first + k, mate))

        def add(k, more, start, size):
            @pl.loop(0, size // STEP)
            def _(i):
                at = own_rows(start + i * STEP, STEP)
                to = pl.ds(pl.multiple_of(start + i * STEP, STEP), STEP)
                both[k, at, :] = (
                    both[k, at, :].astype(jnp.float32) + more(to).astype(jnp.float32)
                ).astype(LOW)

        def merge(k):
            handed[k].wait_recv()
            add(k, lambda at: mated[k, at, :], 0, count)

        own_low, own_high = own_rows(0, half), own_rows(half, half)
        if lines:
            send_swaps(0, SWAPS[0])
            slot = wires.slots(6)
            supply(0, arrive)
            handed[0].wait_recv()
            passes = []
            for k, rows_out in enumerate((own_low, own_high)):
                add(0, lambda at: mated[0, at, :], k * half, half)
                to = above_pass.at[pl.ds(k * half, half)]
                passes.append(wires.start(both.at[0, rows_out], to, slot + k, above))
            supply(1)
            merge(1)
            supply(2)
            merge(2)
            above_low = wires.start(both.at[2, own_low], above_in.at[low_half], slot + 2, above)
            above_high = wires.start(both.at[2, own_high], above_in.at[high_half], slot + 3, above)
            supply(3)
            passes[0].wait_recv()
            add(1, lambda at: above_pass[at, :], 0, half)
            beside_low = wires.start(both.at[1, own_low], beside_in.at[low_half], slot + 4, beside)
            for line in lines:
                line.advance(2)
            passes[1].wait_recv()
            add(1, lambda at: above_pass[at, :], half, half)
            beside_high = wires.start(both.at[1, own_high], beside_in.at[high_half], slot + 5, beside)
            send_swaps(SWAPS[0], SWAPS[1])
            groups = [lines[: len(lines) // 2], lines[len(lines) // 2 :]]
            for line in groups[0]:
                line.advance(3)
        else:
            slot = wires.slots(6)
            supply(0, arrive)
            handed[0].wait_recv()
            add(0, lambda at: mated[0, at, :], 0, half)
            pass_beside = wires.start(both.at[0, own_low], beside_pass, slot, beside)
            add(0, lambda at: mated[0, at, :], half, half)
            pass_above = wires.start(both.at[0, own_high], above_pass, slot + 1, above)
            supply(1)
            merge(1)
            beside_low = wires.start(both.at[1, own_low], beside_in.at[low_half], slot + 2, beside)
            supply(2)
            merge(2)
            pass_beside.wait_recv()
            add(2, lambda at: beside_pass[at, :], 0, half)
            above_low = wires.start(both.at[2, own_low], above_in.at[low_half], slot + 3, above)
            above_high = wires.start(both.at[2, own_high], above_in.at[high_half], slot + 4, above)
            supply(3)
            if beside_work is not None:
                beside_work(0, held_weights, extra, made)
            pass_above.wait_recv()
            add(1, lambda at: above_pass[pl.ds(pl.multiple_of(at.start - half, STEP), STEP), :], half, half)
            beside_high = wires.start(both.at[1, own_high], beside_in.at[high_half], slot + 5, beside)
        if beside_work is not None:
            beside_work(1, held_weights, extra, made)
        handed[3].wait_recv()

        def value(at):
            near = both[3, own_rows(at.start, STEP), :].astype(jnp.float32)
            near = near + mated[3, at, :].astype(jnp.float32)
            return near + (beside_in[at, :].astype(jnp.float32) + above_in[at, :].astype(jnp.float32))

    mid.start(outs)
    for k in range(2):
        if entry == "sum":
            (beside_low, beside_high)[k].wait_recv()
            (above_low, above_high)[k].wait_recv()

        @pl.loop(k * (half // STEP), (k + 1) * (half // STEP))
        def _(i):
            at = pl.ds(pl.multiple_of(i * STEP, STEP), STEP)
            shard[at, :] = mid.rows(at, value(at), small, outs).astype(LOW)

        if leave == "gather":
            gather.start(k)

    if leave == "gather":
        gather.finish()
    elif leave == "homes":
        if not lines:
            homing.start()
    else:
        keep = pltpu.make_async_copy(shard, main, local.at[20])
        keep.start()
    if leave == "stay":
        keep.wait()
    if not lines:
        send_swaps(0, 4)
    if totals and not lines:
        gain_sums(wires, me, (mate, beside, above), others, rows, small[-1], outs, total, inbox, line_inbox)
    for k, group in enumerate(groups if lines else ()):
        for line in group:
            line.complete()
        if k == 0:
            for line in groups[1]:
                line.advance(rows - 1)
            gain_sums(wires, me, (mate, beside, above), others, rows, small[-1], outs, total, inbox, line_inbox)
        else:
            homing.start()
        for line in group:
            line.end()
        if k == 1:
            send_swaps(SWAPS[1], 4)
    for line in lines:
        line.finish()
    if homing is not None:
        homing.finish()
    if n_swap:
        for copy in swaps:
            copy.wait_recv()
    wires.finish()


def enter_kernel(
    rows, cols, hidden_in, grad_out, gains_in, normed, held, grad_here, gains,
    shard, seated, grad_seated, hidden_relay, grad_relay, landing, send, recv, local,
):
    wires = Wires(send, recv)
    me, mate, beside, above = here()
    x, r, c = me
    count, width = seated.shape
    block = width // rows
    side = 2 * lax.div(c, 2)
    far = 2 - side
    ways = [(x, c, side), (x, c, side + 1), (x, above[2], side), (x, above[2], side + 1)]
    via = side + lax.rem(r, 2)
    sources = [(x, s, via) for s in range(rows)]
    others = [(x, lax.rem(r + k, rows), c) for k in range(1, rows)]

    def away(device):
        return jnp.logical_not(jnp.logical_and(device[1] == r, device[2] == c))

    kept = jnp.where(lax.rem(c, 2) == lax.rem(r, 2), 1, 0).astype(jnp.int32)
    greeted = [(s, away(s)) for s in sources] + [(o, None) for o in others]
    greeted += [(above, None), (mate, None), (beside, None)]
    greet(greeted, 2 * rows + 2 - kept)

    mine = pl.ds(pl.multiple_of(r * block, block), block)
    slot = wires.slots(rows - 1)
    spread = [wires.start(gains_in, landing.at[r], slot + k, other) for k, other in enumerate(others)]

    class Seating:
        def __init__(self, source, target, relay, sem):
            self.source, self.target, self.relay, self.sem = source, target, relay, sem
            self.slot, self.hop = wires.slots(rows), wires.slots(1)

        def pieces(self):
            near = pl.multiple_of(side * count, count)
            return [
                self.source.at[pl.ds(near, count)],
                self.source.at[pl.ds(near + count, count)],
                self.relay.at[pl.ds(0, count)],
                self.relay.at[pl.ds(count, count)],
            ]

        def cross(self):
            across = self.source.at[pl.ds(pl.multiple_of(far * count, count), 2 * count)]
            self.crossing = wires.start(across, self.relay, self.hop, above)

        def go(self, which):
            for i in which:
                piece, seat = self.pieces()[i], ways[i]
                there = wires.copy(piece, self.target.at[:, mine], self.slot + i, seat, self.slot + r)
                stay = pltpu.make_async_copy(piece, self.target.at[:, mine], self.sem)
                pl.when(away(seat))(there.start)
                pl.when(jnp.logical_not(away(seat)))(stay.start)

        def arrive(self):
            for s, source in enumerate(sources):
                part = self.target.at[:, pl.ds(s * block, block)]
                arrived = wires.copy(part, part, self.slot + s, source)
                stay = pltpu.make_async_copy(part, part, self.sem)
                pl.when(away(source))(arrived.wait_recv)
                pl.when(jnp.logical_not(away(source)))(stay.wait)

        def sent(self):
            for i, piece in enumerate(self.pieces()):
                there = wires.copy(piece, self.target.at[:, mine], self.slot + i, ways[i])
                pl.when(away(ways[i]))(there.wait_send)

    hidden = Seating(hidden_in, seated, hidden_relay, local.at[0])
    grad = Seating(grad_out, grad_seated, grad_relay, local.at[1])
    hidden.cross()
    hidden.go((0, 1))
    grad.cross()
    hidden.crossing.wait_recv()
    hidden.go((2, 3))
    for copy in spread:
        copy.wait_recv()
    landing[r] = gains_in[...]
    for s in range(rows):
        gains[:, s * block : (s + 1) * block] = landing[s]
    hidden.arrive()
    keep = pltpu.make_async_copy(seated, held, local.at[2])
    keep.start()

    gather = PlaneGather(wires, shard, normed, local.at[pl.ds(4, 2)], cols)
    for k in range(2):

        @pl.loop(k * (count // STEP // 2), (k + 1) * (count // STEP // 2))
        def _(i):
            at = pl.ds(pl.multiple_of(i * STEP, STEP), STEP)
            value = seated[at, :].astype(jnp.float32)
            shard[at, :] = (value * rms_scale(value) * gains[0:1, :]).astype(LOW)

        gather.start(k)
    gather.finish()
    grad.go((0, 1))
    grad.crossing.wait_recv()
    grad.go((2, 3))
    grad.arrive()
    keep_grad = pltpu.make_async_copy(grad_seated, grad_here, local.at[3])
    keep_grad.start()
    hidden.sent()
    grad.sent()
    keep.wait()
    keep_grad.wait()
    wires.finish()


def enter_call(hidden_in, grad_out, gains, collective_id):
    rows, cols, parts = lax.axis_size("row"), lax.axis_size("col"), lax.axis_size("dp")
    count, width = hidden_in.shape[0] // rows, hidden_in.shape[1] * rows
    block = width // rows
    vmem = pl.BlockSpec(memory_space=pltpu.VMEM)
    hbm = pl.BlockSpec(memory_space=pl.ANY)
    shape = jax.ShapeDtypeStruct((count, width), LOW)
    tile = pltpu.VMEM((count, width), LOW)
    relay = pltpu.VMEM((2 * count, block), LOW)
    whole = jax.ShapeDtypeStruct((parts * cols, count, width), LOW)
    normed, held, grad_here, gains = pl.pallas_call(
        functools.partial(enter_kernel, rows, cols),
        out_shape=[whole, shape, shape, jax.ShapeDtypeStruct((8, width), jnp.float32)],
        in_specs=[hbm, hbm, vmem],
        out_specs=[hbm, hbm, hbm, vmem],
        scratch_shapes=[tile, tile, tile, relay, relay, pltpu.VMEM((rows, 8, block), jnp.float32)]
        + [pltpu.SemaphoreType.DMA((48,))] * 2
        + [pltpu.SemaphoreType.DMA((8,))],
        compiler_params=pltpu.CompilerParams(
            collective_id=collective_id, has_side_effects=True, vmem_limit_bytes=VMEM_LIMIT
        ),
        cost_estimate=pl.CostEstimate(flops=0, bytes_accessed=20_000_000, transcendentals=0),
    )(hidden_in, grad_out, gains)
    flat = (parts * cols * count, width)
    return normed.reshape(flat), held, grad_here, gains


def spread_kernel(cols, shard, main, send, recv, local):
    wires = Wires(send, recv)
    greet([(device, None) for device in here()[1:]], 3)
    gather = PlaneGather(wires, shard, main, local, cols)
    gather.start(0)
    gather.start(1)
    gather.finish()
    wires.finish()


def spread_call(shard, collective_id):
    cols, parts = lax.axis_size("col"), lax.axis_size("dp")
    hbm = pl.BlockSpec(memory_space=pl.ANY)
    main = pl.pallas_call(
        functools.partial(spread_kernel, cols),
        out_shape=jax.ShapeDtypeStruct((parts * cols, *shard.shape), LOW),
        in_specs=[pl.BlockSpec(memory_space=pltpu.VMEM)],
        out_specs=hbm,
        scratch_shapes=[pltpu.SemaphoreType.DMA((16,))] * 2 + [pltpu.SemaphoreType.DMA((2,))],
        compiler_params=pltpu.CompilerParams(
            collective_id=collective_id, has_side_effects=True, vmem_limit_bytes=VMEM_LIMIT
        ),
        cost_estimate=pl.CostEstimate(flops=0, bytes_accessed=20_000_000, transcendentals=0),
    )(shard)
    return main.reshape(-1, shard.shape[1])


def spread_plain(shard, collective_id):
    return group_gather(shard)


def enter_plain(hidden_in, grad_out, gains, collective_id):
    gains = lax.all_gather(gains, "row", axis=1, tiled=True)
    held = to_group(hidden_in)
    value = held.astype(jnp.float32)
    normed = group_gather((value * rms_scale(value) * gains[0:1]).astype(LOW))
    return normed, held, to_group(grad_out), gains


def gain_sums(wires, me, partners, others, rows, gain_two, outs, total, inbox, line_inbox):
    x, r, c = me
    block = total.shape[1] // rows
    total[0:1, :] = jnp.sum(outs[1][...], axis=0, keepdims=True)
    total[1:2, :] = jnp.sum(gain_two[...], axis=0, keepdims=True)
    total[2:, :] = jnp.zeros_like(total[2:, :])
    first = wires.slots(len(partners))
    for k, partner in enumerate(partners):
        copy = wires.copy(total, inbox.at[k], first + k, partner)
        copy.start()
        copy.wait()
        total[...] += inbox[k]
    first = wires.slots(len(others))
    copies = []
    for k, (_, row, _) in enumerate(others):
        part = total.at[:, pl.ds(pl.multiple_of(row * block, block), block)]
        copies.append(wires.start(part, line_inbox.at[r], first + k, others[k]))
    line_inbox[r] = total[:, pl.ds(pl.multiple_of(r * block, block), block)]
    for copy in copies:
        copy.wait_recv()
    outs[0][...] = sum(line_inbox[k] for k in range(rows))


def plane_call(
    entry, leave, mid, big, small, outs, collective_id, weights=None, form=None, totals=False, swap=(),
    beside_work=None, extra=(), made=(), ship=(), line=(), line_axes=(), line_pieces=(),
):
    rows, cols, parts = lax.axis_size("row"), lax.axis_size("col"), lax.axis_size("dp")
    count, width = big.shape[0] // (parts * cols), small[0].shape[1]
    depth = big.shape[1]
    big = big.reshape(parts * cols // 2, 2 * count, depth)
    gathered = leave == "gather"
    shape = {"gather": (parts * cols, count, width), "homes": (rows * count, width // rows), "stay": (count, width)}[leave]
    landed = [jax.ShapeDtypeStruct((rows * a.shape[0], a.shape[1] // rows), a.dtype) for a in ship]
    plain = len(swap) + len(made) + len(ship)
    vmem = pl.BlockSpec(memory_space=pltpu.VMEM)
    hbm = pl.BlockSpec(memory_space=pl.ANY)
    tile = pltpu.VMEM((count, width), LOW)
    whole, part = pltpu.VMEM((4, count, width), LOW), pltpu.VMEM((count // 2, width), LOW)
    scratch = [tile, pltpu.SemaphoreType.DMA((64,)), pltpu.SemaphoreType.DMA((64,)), pltpu.SemaphoreType.DMA((40,))]
    scratch += [
        pltpu.VMEM(big.shape, LOW),
        pltpu.VMEM((width, depth) if form == "turned" else (depth, width), LOW),
        pltpu.VMEM((4, 2 * count, width), LOW),
    ]
    scratch += [whole, part, tile if line else part, tile, tile]
    line_outs = []
    for array, axis, pieces in zip(line, line_axes, line_pieces):
        block = [n // rows if i == axis else n for i, n in enumerate(array.shape)]
        block[1] //= pieces
        scratch += ([pltpu.VMEM((n, *block), LOW) for n in (rows - 1, rows - 1, rows)] + [pltpu.VMEM(tuple(block), LOW)]) * pieces
        block[1 - axis] *= parts
        line_outs += [jax.ShapeDtypeStruct(tuple(block), jnp.float32)] * pieces
    if totals:
        scratch += [
            pltpu.VMEM((rows, 8, width // rows), jnp.float32),
            pltpu.VMEM((3, 8, width), jnp.float32),
            pltpu.VMEM((8, width), jnp.float32),
        ]
    blocks = weights if form == "blocks" else [weights]
    counts = (len(blocks), len(small), len(outs), len(swap), len(extra), len(made), len(ship), tuple(line_pieces))
    main, *others = pl.pallas_call(
        functools.partial(plane_kernel, rows, cols, entry, leave, mid, counts, beside_work, line_axes, totals, form),
        out_shape=[jax.ShapeDtypeStruct(shape, LOW)]
        + list(outs)
        + [jax.ShapeDtypeStruct(m.shape, m.dtype) for m in (*swap, *made, *landed, *line_outs)],
        in_specs=[hbm] * (1 + len(blocks)) + [vmem] * len(small) + [hbm] * (len(swap) + len(extra) + len(ship) + len(line)),
        out_specs=[hbm] + [vmem] * len(outs) + [hbm] * plain + [vmem] * len(line_outs),
        scratch_shapes=scratch,
        compiler_params=pltpu.CompilerParams(
            collective_id=collective_id, has_side_effects=True, vmem_limit_bytes=VMEM_LIMIT
        ),
        cost_estimate=pl.CostEstimate(flops=0, bytes_accessed=20_000_000, transcendentals=0),
    )(big, *blocks, *small, *swap, *extra, *ship, *line)
    if gathered:
        main = main.reshape(parts * cols * count, width)
    return [main, *others]


def fold(values):
    return values.reshape(values.shape[0] // 8, 8, values.shape[1]).sum(0)


class Mid:
    @staticmethod
    def start(outs):
        pass


class SecondNorm(Mid):
    @staticmethod
    def rows(at, value, small, outs):
        held, gains = small
        middle = held[at, :].astype(jnp.float32) + value
        outs[0][at, :] = middle
        return middle * rms_scale(middle) * gains[1:2, :]


class Add(Mid):
    @staticmethod
    def rows(at, value, small, outs):
        return small[0][at, :] + value


class BackSecond(Mid):
    @staticmethod
    def start(outs):
        outs[1][...] = jnp.zeros_like(outs[1])

    @staticmethod
    def rows(at, value, small, outs):
        middle, grad_out, gains = small
        middle = middle[at, :]
        scale = rms_scale(middle)
        outs[1][...] += fold(value * middle * scale)
        grad = grad_out[at, :].astype(jnp.float32) + norm_back(
            middle, scale, value * gains[1:2, :]
        )
        outs[0][at, :] = grad
        return grad


class BackFirst(Mid):
    @staticmethod
    def start(outs):
        outs[1][...] = jnp.zeros_like(outs[1])

    @staticmethod
    def rows(at, value, small, outs):
        held, grad_middle, gains = small[:3]
        inputs = held[at, :].astype(jnp.float32)
        scale = rms_scale(inputs)
        outs[1][...] += fold(value * inputs * scale)
        return grad_middle[at, :] + norm_back(inputs, scale, value * gains[0:1, :])


def plain_call(
    entry, leave, mid, big, small, outs, collective_id, weights=None, form=None, totals=False, swap=(),
    beside_work=None, extra=(), made=(), ship=(), line=(), line_axes=(), line_pieces=(),
):
    refs = [Holder(a) for a in small]
    given = [Holder(jnp.zeros(o.shape, o.dtype)) for o in outs]
    depth, width = big.shape[1], small[0].shape[1]
    if form == "turned":
        product = inner_cols(big, weights[:, :depth])
    else:
        block = width * depth // weights.shape[0]
        whole = unstack(weights[:, weights.shape[1] - block :], depth)
        product = dot(big, whole)
    mid.start(given)
    shard = mid.rows(slice(None), group_scatter(product), refs, given).astype(LOW)
    main = {"gather": group_gather, "homes": from_group, "stay": lambda a: a}[leave](shard)
    if totals:
        sums = jnp.stack([given[1].value.sum(0), small[-1].sum(0)])
        sums = jnp.pad(lax.psum(sums, ("dp", "row", "col")), ((0, 6), (0, 0)))
        part = outs[0].shape[1]
        given[0].value = lax.dynamic_slice_in_dim(sums, lax.axis_index("row") * part, part, 1)
    others = [dp_other(m) for m in swap]
    if beside_work is not None:
        grads, slope_up, gated, tokens = extra
        lifted = lift_back_plain(grads, whole, slope_up, gated)
        others += [lifted, inner_rows(tokens, lifted).astype(LOW)]
    others += [from_group(a) for a in ship]
    for array, axis, pieces in zip(line, line_axes, line_pieces):
        mine = row_sum(array, axis)
        other = dp_other(mine)
        others += join_tall(mine, other, [(i,) for i in range(pieces)]) if axis == 0 else [join_wide(mine, other)]
    return [main] + [g.value for g in given] + others


class Holder:
    def __init__(self, value):
        self.value, self.dtype, self.shape = value, value.dtype, value.shape

    def __getitem__(self, at):
        return self.value[at]

    def __setitem__(self, at, value):
        self.value = self.value.at[at].set(value)


def swap_halves(values, first):
    lanes = values.shape[1]
    half = HEAD_DIM // 2
    return jnp.where(first, pltpu.roll(values, lanes - half, 1), pltpu.roll(values, half, 1))


def attend_kernel(query, key, value, cosine, sine, mixed, q_out, k_out, v_out, logsum):
    length, lanes = query.shape
    block = min(256, length)
    lane = lax.broadcasted_iota(jnp.int32, (length, lanes), 1)
    first = lax.rem(lane, HEAD_DIM) < HEAD_DIM // 2
    cos, sin = cosine[...], sine[...]

    def rotate(values):
        return (values * cos + swap_halves(values, first) * sin).astype(LOW)

    q_out[...] = rotate(query[...])
    k_out[...] = rotate(key[...])
    low_values = value[...].astype(LOW)
    v_out[...] = low_values
    v_turned = low_values.astype(jnp.float32).T.astype(LOW)
    head = lax.broadcasted_iota(jnp.int32, (block, lanes), 1) // HEAD_DIM
    keep = lax.broadcasted_iota(jnp.int32, (block, block), 0) <= lax.broadcasted_iota(
        jnp.int32, (block, block), 1
    )
    for j in range(length // block):
        at = slice(j * block, (j + 1) * block)
        q_block = q_out[at, :].astype(jnp.float32) * HEAD_DIM ** (-0.5)
        parts = []
        for h in range(lanes // HEAD_DIM):
            q_head = jnp.where(head == h, q_block, 0.0).astype(LOW)
            near = jnp.where(keep, inner_cols(k_out[at, :], q_head), -jnp.inf)
            highest = jnp.max(near, axis=0, keepdims=True)
            if j:
                far = inner_cols(k_out[: j * block, :], q_head)
                highest = jnp.maximum(highest, jnp.max(far, axis=0, keepdims=True))
                far = jnp.exp(far - highest)
            near = jnp.exp(near - highest)
            total = jnp.sum(near, axis=0, keepdims=True)
            if j:
                total = total + jnp.sum(far, axis=0, keepdims=True)
            logsum[0, 0, h : h + 1, at] = highest + jnp.log(total)
            share = 1.0 / total
            out = dot(v_turned[:, at], (near * share).astype(LOW))
            if j:
                out = out + dot(v_turned[:, : j * block], (far * share).astype(LOW))
            parts.append(out[h * HEAD_DIM : (h + 1) * HEAD_DIM])
        mixed[at, :] = jnp.concatenate(parts, 0).T.astype(LOW)


def attend_back_kernel(n_swap, query, key, value, grad, logsum, cosine, sine, *refs):
    mine_parts, refs = refs[:n_swap], refs[n_swap:]
    made, refs = refs[0], refs[1:]
    other_parts, refs = refs[:n_swap], refs[n_swap:]
    (k_sum, v_sum, q_out, k_out, v_out, out_sems), refs = refs[:6], refs[6:]
    length, lanes = query.shape
    if n_swap:
        beside = here()[2]
        wires = Wires(*refs)
        swaps = [
            wires.copy(source, target, i, beside)
            for i, (source, target) in enumerate(zip(mine_parts, other_parts))
        ]
        here_first = (pl.program_id(0) == 0) & (pl.program_id(1) == 0)
        here_last = (pl.program_id(0) == pl.num_programs(0) - 1) & (
            pl.program_id(1) == pl.num_programs(1) - 1
        )

        @pl.when(here_first)
        def _():
            greet([(beside, None)], 1)
            for copy in swaps:
                copy.start()

    block = min(256, length)
    k_sum[...] = jnp.zeros_like(k_sum)
    v_sum[...] = jnp.zeros_like(v_sum)
    k_turned = key[...].astype(jnp.float32).T.astype(LOW)
    head = lax.broadcasted_iota(jnp.int32, (block, lanes), 1) // HEAD_DIM
    keep = lax.broadcasted_iota(jnp.int32, (block, block), 0) <= lax.broadcasted_iota(
        jnp.int32, (block, block), 1
    )
    scale = HEAD_DIM ** (-0.5)

    def rotate_back(values, at):
        rows = values.shape[0]
        lane = lax.broadcasted_iota(jnp.int32, (rows, lanes), 1)
        first = lax.rem(lane, HEAD_DIM) < HEAD_DIM // 2
        return (values * cosine[at, :] - swap_halves(values, first) * sine[at, :]).astype(LOW)

    for j in range(length // block):
        at = slice(j * block, (j + 1) * block)
        before = slice(0, j * block)
        q_block = query[at, :].astype(jnp.float32) * scale
        g_block = grad[at, :].astype(jnp.float32)
        parts = []
        for h in range(lanes // HEAD_DIM):
            q_head = jnp.where(head == h, q_block, 0.0).astype(LOW)
            g_head = jnp.where(head == h, g_block, 0.0).astype(LOW)
            level = logsum[0, 0, h : h + 1, at]
            near = jnp.exp(jnp.where(keep, inner_cols(key[at, :], q_head), -jnp.inf) - level)
            d_near = inner_cols(value[at, :], g_head)
            inner = jnp.sum(near * d_near, axis=0, keepdims=True)
            if j:
                far = jnp.exp(inner_cols(key[before, :], q_head) - level)
                d_far = inner_cols(value[before, :], g_head)
                inner = inner + jnp.sum(far * d_far, axis=0, keepdims=True)
                v_sum[before, :] += dot(far.astype(LOW), g_head)
                s_far = (far * (d_far - inner)).astype(LOW)
                k_sum[before, :] += dot(s_far, q_head)
            v_sum[at, :] += dot(near.astype(LOW), g_head)
            s_near = (near * (d_near - inner)).astype(LOW)
            k_sum[at, :] += dot(s_near, q_head)
            out = dot(k_turned[:, at], s_near)
            if j:
                out = out + dot(k_turned[:, before], s_far)
            parts.append(out[h * HEAD_DIM : (h + 1) * HEAD_DIM])
        q_out[at, :] = rotate_back(jnp.concatenate(parts, 0).T * scale, at)
    k_out[...] = rotate_back(k_sum[...], slice(None))
    v_out[...] = v_sum[...].astype(LOW)
    rows_at = pl.ds(pl.multiple_of(pl.program_id(0) * length, length), length)
    columns = made.shape[1] // 3
    copies = [
        pltpu.make_async_copy(
            out,
            made.at[rows_at, pl.ds(pl.multiple_of(i * columns + pl.program_id(1) * lanes, lanes), lanes)],
            out_sems.at[i],
        )
        for i, out in enumerate((q_out, k_out, v_out))
    ]
    for copy in copies:
        copy.start()
    for copy in copies:
        copy.wait()
    if n_swap:

        @pl.when(here_last)
        def _():
            for copy in swaps:
                copy.wait()


def pair_tables(length):
    half = HEAD_DIM // 2
    freq = THETA ** (-(jnp.arange(half, dtype=jnp.float32) * 2.0 / HEAD_DIM))
    angle = jnp.arange(length, dtype=jnp.float32)[:, None] * freq[None, :]
    cosine, sine = jnp.cos(angle), jnp.sin(angle)
    return jnp.tile(cosine, (1, 4)), jnp.tile(jnp.concatenate([-sine, sine], 1), (1, 2))


def attend_pairs(projected, sequences):
    tokens, columns = projected.shape[0], projected.shape[1] // 3
    length, lanes = tokens // sequences, 2 * HEAD_DIM
    pairs = columns // lanes
    cosine, sine = pair_tables(length)

    def spec(offset):
        return pl.BlockSpec((length, lanes), lambda s, h: (s, offset + h))

    table = pl.BlockSpec((length, lanes), lambda s, h: (0, 0))
    level = pl.BlockSpec((1, 1, 2, length), lambda s, h: (s, h, 0, 0))
    shape = jax.ShapeDtypeStruct((tokens, columns), LOW)
    return pl.pallas_call(
        attend_kernel,
        grid=(sequences, pairs),
        in_specs=[spec(0), spec(pairs), spec(2 * pairs), table, table],
        out_specs=[spec(0)] * 4 + [level],
        out_shape=[shape] * 4 + [jax.ShapeDtypeStruct((sequences, pairs, 2, length), jnp.float32)],
        compiler_params=pltpu.CompilerParams(vmem_limit_bytes=VMEM_LIMIT),
        cost_estimate=pl.CostEstimate(
            flops=8 * tokens * length * columns, bytes_accessed=100_000_000, transcendentals=0
        ),
    )(projected, projected, projected, cosine, sine)


def attend_pairs_back(query, keys, values, grad_mixed, logsum, sequences, swap, collective_id):
    tokens, columns = query.shape
    length, lanes = tokens // sequences, 2 * HEAD_DIM
    pairs = columns // lanes
    cosine, sine = pair_tables(length)
    spec = pl.BlockSpec((length, lanes), lambda s, h: (s, h))
    table = pl.BlockSpec((length, lanes), lambda s, h: (0, 0))
    level = pl.BlockSpec((1, 1, 2, length), lambda s, h: (s, h, 0, 0))
    hbm = pl.BlockSpec(memory_space=pl.ANY)
    return pl.pallas_call(
        functools.partial(attend_back_kernel, len(swap)),
        grid=(sequences, pairs),
        in_specs=[spec] * 4 + [level, table, table] + [hbm] * len(swap),
        out_specs=[hbm] * (1 + len(swap)),
        out_shape=[jax.ShapeDtypeStruct((tokens, 3 * columns), LOW)] + [jax.ShapeDtypeStruct(m.shape, m.dtype) for m in swap],
        scratch_shapes=[pltpu.VMEM((length, lanes), jnp.float32)] * 2
        + [pltpu.VMEM((length, lanes), LOW)] * 3
        + [pltpu.SemaphoreType.DMA((4,))] * 3,
        compiler_params=pltpu.CompilerParams(
            collective_id=collective_id, has_side_effects=True, vmem_limit_bytes=VMEM_LIMIT
        ),
        cost_estimate=pl.CostEstimate(
            flops=20 * tokens * length * columns, bytes_accessed=60_000_000, transcendentals=0
        ),
    )(query, keys, values, grad_mixed, logsum, cosine, sine, *swap)


def lift_kernel(tokens, weights, activated, slope_up, gated):
    rows, width = activated.shape
    step = min(256, rows)
    for i in range(rows // step):
        at = slice(i * step, (i + 1) * step)
        left = tokens[at, :]
        both = dot(left, weights[...])
        gate, upward = both[:, :width], both[:, width:]
        sigmoid = 1.0 / (1.0 + jnp.exp(-gate))
        passed = gate * sigmoid
        activated[at, :] = (passed * upward).astype(LOW)
        gated[at, :] = passed.astype(LOW)
        slope_up[at, :] = (upward * (sigmoid + passed * (1.0 - sigmoid))).astype(LOW)


def lift(tokens, weights):
    count, width = tokens.shape
    units = weights.shape[1] // 2
    tile, rows = units // 2, min(512, count)
    out = pl.BlockSpec((rows, tile), lambda j, i: (i, j))
    shape = jax.ShapeDtypeStruct((count, units), LOW)
    return pl.pallas_call(
        lift_kernel,
        grid=(2, count // rows),
        in_specs=[
            pl.BlockSpec((rows, width), lambda j, i: (i, 0)),
            pl.BlockSpec((width, 2 * tile), lambda j, i: (0, j)),
        ],
        out_specs=[out] * 3,
        out_shape=[shape] * 3,
        compiler_params=pltpu.CompilerParams(vmem_limit_bytes=VMEM_LIMIT),
        cost_estimate=pl.CostEstimate(
            flops=4 * count * width * units, bytes_accessed=30_000_000, transcendentals=0
        ),
    )(tokens, weights)


def lift_back_rows(weights, grads, slope_up, gated, lifted):
    units = slope_up.shape[1]
    tile = units // 2
    for j in range(2):
        here_units = slice(j * tile, (j + 1) * tile)
        grad = inner_cols(grads[...], weights[here_units, :])
        start = 2 * j * tile
        lifted[:, start : start + tile] = (grad * slope_up[:, here_units].astype(jnp.float32)).astype(LOW)
        lifted[:, start + tile : start + 2 * tile] = (
            grad * gated[:, here_units].astype(jnp.float32)
        ).astype(LOW)


def lift_back_work(stage, weights, extra, made):
    grads, slope_up, gated, tokens = extra
    lifted, grad_weights = made
    count, units = slope_up.shape
    width = tokens.shape[1]
    if stage < 2:
        rows = count // 4
        first = stage * (count // 2)
        at = pl.ds(first, count // 2)
        pltpu.emit_pipeline(
            functools.partial(lift_back_rows, weights),
            grid=(2,),
            in_specs=[
                pl.BlockSpec((rows, width), lambda i: (i, 0)),
                pl.BlockSpec((rows, units), lambda i: (i, 0)),
                pl.BlockSpec((rows, units), lambda i: (i, 0)),
            ],
            out_specs=[pl.BlockSpec((rows, 2 * units), lambda i: (i, 0))],
        )(grads.at[at], slope_up.at[at], gated.at[at], lifted.at[at])

    def inner(left, right, out):
        out[...] = inner_rows(left[...], right[...]).astype(LOW)

    if stage == 1:
        part, tile = width // 2, units // 2
        pltpu.emit_pipeline(
            inner,
            grid=(2, 4),
            in_specs=[
                pl.BlockSpec((count, part), lambda i, j: (0, i)),
                pl.BlockSpec((count, tile), lambda i, j: (0, j)),
            ],
            out_specs=[pl.BlockSpec((part, tile), lambda i, j: (i, j))],
        )(tokens, lifted, grad_weights)


def lift_back_plain(grads, weights, slope_up, gated):
    grad = inner_cols(grads, weights)
    up, through = (grad * f.astype(jnp.float32) for f in (slope_up, gated))
    return pair_units(up, through).astype(LOW)


def attend_plain(projected, sequences):
    tokens, columns = projected.shape[0], projected.shape[1] // 3
    length = tokens // sequences
    shape = (sequences, length, columns // HEAD_DIM, HEAD_DIM)
    cosine, sine = rotation_tables(length)
    query = turn(projected[:, :columns].reshape(shape), cosine, sine).astype(LOW)
    keys = turn(projected[:, columns : 2 * columns].reshape(shape), cosine, sine).astype(LOW)
    values = projected[:, 2 * columns :].reshape(shape).astype(LOW)
    mixed, logsum = attend(query, keys, values)
    flat = (tokens, columns)
    return mixed.reshape(flat), query.reshape(flat), keys.reshape(flat), values.reshape(flat), logsum


def attend_plain_back(query, keys, values, grad_mixed, logsum, sequences, swap, collective_id):
    tokens, columns = query.shape
    length = tokens // sequences
    shape = (sequences, length, columns // HEAD_DIM, HEAD_DIM)
    cosine, sine = rotation_tables(length)
    grad_query, grad_keys, grad_values = attend_back(
        *(a.reshape(shape) for a in (query, keys, values, grad_mixed)), logsum
    )
    grads = (turn_back(grad_query, cosine, sine), turn_back(grad_keys, cosine, sine), grad_values)
    grads = jnp.concatenate([g.reshape(tokens, columns).astype(LOW) for g in grads], 1)
    return [grads] + [dp_other(m) for m in swap]


def body(
    hidden_in, w_query, w_key, w_value, w_out, w_gate, w_up, w_down, norm_attn, norm_ffn, grad_out
):
    rows, cols, parts = lax.axis_size("row"), lax.axis_size("col"), lax.axis_size("dp")
    own_kernels = (parts, rows, cols) == (2, 4, 4)
    plane, enter, spread = (
        (plane_call, enter_call, spread_call) if own_kernels else (plain_call, enter_plain, spread_plain)
    )
    count, width = hidden_in.shape[0] // rows, hidden_in.shape[1] * rows
    full_rows = jax.ShapeDtypeStruct((count, width), jnp.float32)
    gain_rows = jax.ShapeDtypeStruct((8, width), jnp.float32)

    local_gains = jnp.pad(jnp.stack([norm_attn, norm_ffn]), ((0, 6), (0, 0)))
    own_attn = [my_part(w, 1) for w in (w_query, w_key, w_value)] + [stack(my_part(w_out, 0))]
    w_attn = lax.all_gather(jnp.concatenate(own_attn, 1), "row", axis=0, tiled=True)
    normed_one, held, grad_here, gains = enter(hidden_in, grad_out, local_gains, 1)
    own_ffn = pair_units(my_part(w_gate, 1), my_part(w_up, 1))
    w_ffn = lax.all_gather(own_ffn, "row", axis=0, tiled=True)
    own_back, normed_one = after(my_part(w_down, 0), normed_one)
    if own_kernels:
        ahead, back = [pass_on(own_back, 1, 0)], [pass_on(own_back, -1, 0)]
    else:
        w_back = lax.all_gather(own_back, "row", axis=0, tiled=True)

    columns = w_attn.shape[1] // 4
    projected = dot(normed_one, w_attn[:, : 3 * columns])
    paired = columns % (2 * HEAD_DIM) == 0
    mixed, query, keys, values, logsum = (attend_pairs if paired else attend_plain)(projected, parts)
    normed_two, middle = plane(
        "sum", "gather", SecondNorm, mixed, [held, gains], [full_rows], 2, w_attn, "stacked"
    )

    if own_kernels:
        ahead[0], back[0], normed_two = after(ahead[0], back[0], normed_two)
        ahead.append(pass_on(ahead[0], 1, 1))
        back.append(pass_on(back[0], -1, 1))
    grad_here, normed_two = after(grad_here, normed_two)
    grad_wide = spread(grad_here, 7)
    if own_kernels:
        ahead[1], back[1], grad_wide = after(ahead[1], back[1], grad_wide)
        ahead.append(pass_on(ahead[1], 1, 2))
        back.append(pass_on(back[1], -1, 2))
        w_back = [own_back, *ahead, *back]
    grad_wide, w_ffn = after(grad_wide, w_ffn)
    w_proj, w_ffn = after(unstack(w_attn[:, 3 * columns :], columns), w_ffn)
    activated, slope_up, gated = lift(normed_two, w_ffn)
    part_down = inner_rows(activated, grad_wide).astype(LOW)
    part_down, w_back = after(part_down, w_back)
    mine_down = row_sum(part_down, 1)
    low = functools.partial(jax.ShapeDtypeStruct, dtype=LOW)
    out_rows, grad_lifted, part_ffn = plane(
        "sum",
        "stay",
        Add,
        activated,
        [middle],
        [],
        3,
        w_back,
        "blocks" if own_kernels else "stacked",
        beside_work=lift_back_work,
        extra=[grad_wide, slope_up, gated, normed_two],
        made=[low((normed_two.shape[0], w_ffn.shape[1])), low((width, w_ffn.shape[1]))],
    )
    mine_ffn = row_sum(part_ffn, 0)
    grad_branch, grad_middle, gain_two, layer_out = plane(
        "sum",
        "gather",
        BackSecond,
        grad_lifted,
        [middle, grad_here, gains],
        [full_rows, gain_rows],
        4,
        w_ffn,
        "turned",
        ship=[out_rows],
    )
    grad_branch, mine_down = after(grad_branch, mine_down)
    grad_mixed = inner_cols(grad_branch, w_proj).astype(LOW)
    part_out, grad_mixed = after(inner_rows(mixed, grad_branch).astype(LOW), grad_mixed)
    grad_projected, other_down = (attend_pairs_back if paired else attend_plain_back)(
        query, keys, values, grad_mixed, logsum, parts, [mine_down], 5
    )
    part_attn = inner_rows(normed_one, grad_projected).astype(LOW)
    grad_in, gain_grads, _, other_ffn, grad_wq, grad_wk, grad_wv, grad_attn_out = plane(
        "sum",
        "homes",
        BackFirst,
        grad_projected,
        [held, grad_middle, gains, gain_two],
        [jax.ShapeDtypeStruct((8, norm_attn.shape[0]), jnp.float32), gain_rows],
        6,
        w_attn,
        "turned",
        totals=True,
        swap=[mine_ffn],
        line=[part_attn, part_out],
        line_axes=(0, 1),
        line_pieces=(3, 1),
    )
    grad_down = join_wide(mine_down, other_down)
    grad_gate, grad_up = join_tall(mine_ffn, other_ffn, [(0, 2), (1, 3)])
    return (
        layer_out,
        grad_in,
        grad_wq,
        grad_wk,
        grad_wv,
        grad_attn_out,
        grad_gate,
        grad_up,
        grad_down,
        gain_grads[0],
        gain_grads[1],
    )


def solution(mesh):
    tokens = P(("dp", "col"), "row")
    tall = P("row", "col")
    wide = P("col", "row")
    gain = P("row")
    return jax.shard_map(
        body,
        mesh=mesh,
        in_specs=(tokens, tall, tall, tall, wide, tall, tall, wide, gain, gain, tokens),
        out_specs=(tokens, tokens, tall, tall, tall, wide, tall, tall, wide, gain, gain),
        check_vma=False,
    )
```

```python
import functools

import jax
import jax.numpy as jnp
from jax import lax
from jax.experimental import pallas as pl
from jax.experimental.pallas import tpu as pltpu
from jax.sharding import PartitionSpec as P

HEAD_DIM = 64
EPSILON = 1e-05
THETA = 130000.0
GROUP = ("dp", "col")
LOW = jnp.bfloat16


def dot(left, right):
    return jnp.dot(left, right, preferred_element_type=jnp.float32)


def inner_rows(left, right):
    return lax.dot_general(
        left, right, (((0,), (0,)), ((), ())), preferred_element_type=jnp.float32
    )


def inner_cols(left, right):
    return lax.dot_general(
        left, right, (((1,), (1,)), ((), ())), preferred_element_type=jnp.float32
    )


def seat_pairs():
    rows, cols = lax.axis_size("row"), lax.axis_size("col")
    per = cols // rows
    return [
        (r * cols + c, (c // per) * cols + (c % per) * rows + r)
        for r in range(rows)
        for c in range(cols)
    ]


def to_group(block):
    whole = lax.all_to_all(block, "row", split_axis=0, concat_axis=1, tiled=True)
    return lax.ppermute(whole, ("row", "col"), seat_pairs())


def from_group(block):
    back = lax.ppermute(block, ("row", "col"), [(b, a) for a, b in seat_pairs()])
    return lax.all_to_all(back, "row", split_axis=1, concat_axis=0, tiled=True)


def group_gather(shard):
    return lax.all_gather(shard, GROUP, axis=0, tiled=True)


def group_scatter(partial):
    return lax.psum_scatter(
        partial.astype(LOW), GROUP, scatter_dimension=0, tiled=True
    ).astype(jnp.float32)


def my_part(block, axis):
    size = block.shape[axis] // lax.axis_size("dp")
    return lax.dynamic_slice_in_dim(block, lax.axis_index("dp") * size, size, axis)


def halves(block):
    middle = block.shape[1] // 2
    return [block[:, :middle], block[:, middle:]]


def pair_units(gate, upward):
    (g, h), (u, v) = halves(gate), halves(upward)
    return jnp.concatenate([g, u, h, v], 1)


def stack(block):
    units = block.shape[0]
    return jnp.concatenate([block[:, i : i + units] for i in range(0, block.shape[1], units)], 0)


def unstack(blocks, units):
    cut = blocks.reshape(-1, units, blocks.shape[1])
    return cut.transpose(1, 0, 2).reshape(units, -1)


def after(*values):
    return lax.optimization_barrier(values)


def pass_on(block, way, first):
    rows = lax.axis_size("row")
    pairs = [(i, i + 1) for i in range(first, rows - 1)]
    if way < 0:
        pairs = [(rows - 1 - i, rows - 1 - j) for i, j in pairs]
    return lax.ppermute(block, "row", pairs)


def dp_other(mine):
    if lax.axis_size("dp") == 2:
        return lax.ppermute(mine, "dp", [(0, 1), (1, 0)])
    return lax.all_gather(mine, "dp", axis=0)


def dp_parts(mine, other):
    if lax.axis_size("dp") != 2:
        return list(other)
    lower = lax.axis_index("dp") == 0
    return [jnp.where(lower, mine, other), jnp.where(lower, other, mine)]


def row_sum(part, axis):
    return lax.psum_scatter(part, "row", scatter_dimension=axis, tiled=True)


def join_tall(mine, other, pieces):
    width = mine.shape[1] // sum(map(len, pieces))
    cuts = [slice(i * width, (i + 1) * width) for i in range(mine.shape[1] // width)]
    cut = [dp_parts(mine[:, at], other[..., at]) for at in cuts]
    return [
        jnp.concatenate([cut[i][d] for d in range(len(cut[0])) for i in piece], 1).astype(jnp.float32)
        for piece in pieces
    ]


def join_wide(mine, other):
    return jnp.concatenate(dp_parts(mine, other), 0).astype(jnp.float32)


def rms_scale(values):
    return lax.rsqrt(jnp.mean(values * values, axis=1, keepdims=True) + EPSILON)


def norm_back(values, scale, weighted):
    inner = jnp.mean(weighted * values, axis=1, keepdims=True)
    return scale * weighted - values * (scale * scale * scale * inner)


def rotation_tables(length):
    half = HEAD_DIM // 2
    freq = THETA ** (-(jnp.arange(half, dtype=jnp.float32) * 2.0 / HEAD_DIM))
    angle = jnp.arange(length, dtype=jnp.float32)[:, None] * freq[None, :]
    cosine = jnp.concatenate([jnp.cos(angle), jnp.cos(angle)], 1)[None, :, None, :]
    sine = jnp.concatenate([jnp.sin(angle), jnp.sin(angle)], 1)[None, :, None, :]
    return (cosine, sine)


def turn(values, cosine, sine):
    half = values.shape[-1] // 2
    turned = jnp.concatenate([-values[..., half:], values[..., :half]], -1)
    return values * cosine + turned * sine


def turn_back(grads, cosine, sine):
    half = grads.shape[-1] // 2
    moved = grads * sine
    return grads * cosine + jnp.concatenate([moved[..., half:], -moved[..., :half]], -1)


def masked_scores(query, keys):
    scores = jnp.einsum(
        "sqhd,skhd->shqk", query, keys, preferred_element_type=jnp.float32
    ) * HEAD_DIM ** (-0.5)
    length = query.shape[1]
    allowed = jnp.arange(length)[:, None] >= jnp.arange(length)[None, :]
    return jnp.where(allowed[None, None], scores, -jnp.inf)


def attend(query, keys, values):
    scores = masked_scores(query, keys)
    highest = jnp.max(scores, axis=-1, keepdims=True)
    expo = jnp.exp(scores - highest)
    total = jnp.sum(expo, axis=-1, keepdims=True)
    low_probs = (expo / total).astype(LOW)
    mixed = jnp.einsum(
        "shqk,skhd->sqhd", low_probs, values, preferred_element_type=jnp.float32
    ).astype(LOW)
    return mixed, highest + jnp.log(total)


def attend_back(query, keys, values, grad_mixed, logsum):
    scale = HEAD_DIM ** (-0.5)
    probs = jnp.exp(masked_scores(query, keys) - logsum)
    low_probs = probs.astype(LOW)
    dprobs = jnp.einsum("sqhd,skhd->shqk", grad_mixed, values, preferred_element_type=jnp.float32)
    grad_values = jnp.einsum(
        "shqk,sqhd->skhd", low_probs, grad_mixed, preferred_element_type=jnp.float32
    )
    low_scores = (probs * (dprobs - jnp.sum(probs * dprobs, axis=-1, keepdims=True))).astype(LOW)
    grad_query = (
        jnp.einsum("shqk,skhd->sqhd", low_scores, keys, preferred_element_type=jnp.float32) * scale
    )
    grad_keys = (
        jnp.einsum("shqk,sqhd->skhd", low_scores, query, preferred_element_type=jnp.float32) * scale
    )
    return grad_query, grad_keys, grad_values


MESH = pl.DeviceIdType.MESH
STEP = 16
VMEM_LIMIT = 56 * 1024 * 1024


class Wires:
    def __init__(self, send, recv):
        self.send, self.recv, self.used, self.sent = send, recv, 0, []

    def slots(self, count):
        first = self.used
        self.used += count
        return first

    def copy(self, source, target, slot, device, landing=None):
        return pltpu.make_async_remote_copy(
            src_ref=source,
            dst_ref=target,
            send_sem=self.send.at[slot],
            recv_sem=self.recv.at[slot if landing is None else landing],
            device_id=device,
            device_id_type=MESH,
        )

    def start(self, source, target, slot, device):
        copy = self.copy(source, target, slot, device)
        copy.start()
        self.sent.append(copy)
        return copy

    def finish(self):
        for copy in self.sent:
            copy.wait_send()


def here():
    x, r, c = lax.axis_index("dp"), lax.axis_index("row"), lax.axis_index("col")
    mate = (x, r, c + 1 - 2 * lax.rem(c, 2))
    beside = (1 - x, r, c)
    above = (x, r, lax.rem(c + 2, 4))
    return (x, r, c), mate, beside, above


def seat_of(x, r, c, rows, cols, piece):
    per = cols // rows
    return (x, lax.div(c, per), lax.rem(c, per) * rows + piece)


def home_of(x, r, c, rows, cols, source):
    per = cols // rows
    return (x, source, r * per + lax.div(c, rows))


def greet(devices, count):
    barrier = pltpu.get_barrier_semaphore()
    for device, remote in devices:
        if remote is None:
            pl.semaphore_signal(barrier, inc=1, device_id=device, device_id_type=MESH)
        else:

            @pl.when(remote)
            def _():
                pl.semaphore_signal(barrier, inc=1, device_id=device, device_id_type=MESH)

    pl.semaphore_wait(barrier, count)


COLUMNS = 1024
SWAPS = (2, 4)
DISTANCES = (0, -1, -2, -3, 1, 2, 3)


def weight_block(source, held, i, form, depth, size):
    if form == "turned":
        at = pl.ds(pl.multiple_of(i * size, size), size)
        return source.at[at, :depth], held.at[at, :]
    return (
        source.at[pl.ds(pl.multiple_of(i * depth, depth), depth), source.shape[1] - size :],
        held.at[:, pl.ds(pl.multiple_of(i * size, size), size)],
    )


def product_into(target, left, held, form, arrive=None):
    width = target.shape[1]
    size = min(COLUMNS, width)

    @pl.loop(0, width // size)
    def _(i):
        if arrive is not None:
            arrive(i, size)
        at = pl.ds(pl.multiple_of(i * size, size), size)
        if form == "turned":
            value = inner_cols(left[...], held[at, :])
        else:
            value = dot(left[...], held[:, at])
        target[:, at] = value.astype(LOW)


class PlaneGather:
    def __init__(self, wires, shard, main, sems, cols):
        (x, _, c), self.mate, self.beside, self.above = here()
        self.wires, self.shard, self.main, self.sems = wires, shard, main, sems
        half = shard.shape[0] // 2
        self.halves = [pl.ds(0, half), pl.ds(half, half)]
        self.spot = x * cols + c
        self.beside_spot, self.above_spot = self.beside[0] * cols + c, x * cols + self.above[2]
        self.corner_spot = self.beside[0] * cols + self.above[2]
        self.kept, self.to_mate, self.from_beside, self.from_above = [], [], [], []

    def start(self, i):
        part, target = self.shard.at[self.halves[i]], self.main.at[self.spot, self.halves[i]]
        self.kept.append(pltpu.make_async_copy(part, target, self.sems.at[i]))
        self.kept[-1].start()
        slot = self.wires.slots(3)
        self.from_beside.append(self.wires.start(part, target, slot, self.beside))
        self.from_above.append(self.wires.start(part, target, slot + 1, self.above))
        self.to_mate.append(self.wires.start(part, target, slot + 2, self.mate))

    def finish(self):
        slot = self.wires.slots(5)
        start, main = self.wires.start, self.main
        self.from_beside[0].wait_recv()
        part = main.at[self.beside_spot, self.halves[0]]
        corner_low = start(part, part, slot, self.above)
        self.from_above[0].wait_recv()
        self.from_above[1].wait_recv()
        part = main.at[self.above_spot, self.halves[1]]
        corner_high = start(part, part, slot + 1, self.beside)
        part = main.at[self.above_spot]
        self.to_mate.append(start(part, part, slot + 2, self.mate))
        self.from_beside[1].wait_recv()
        part = main.at[self.beside_spot]
        self.to_mate.append(start(part, part, slot + 3, self.mate))
        corner_low.wait_recv()
        corner_high.wait_recv()
        part = main.at[self.corner_spot]
        self.to_mate.append(start(part, part, slot + 4, self.mate))
        for copy in self.to_mate:
            copy.wait_recv()
        for copy in self.kept:
            copy.wait()


class Homing:
    def __init__(self, wires, shard, main, sem, rows, cols):
        x, r, c = here()[0]
        self.wires, self.shard, self.main, self.sem, self.rows = wires, shard, main, sem, rows
        self.seats = [seat_of(x, r, c, rows, cols, p) for p in range(rows)]
        self.homes = [home_of(x, r, c, rows, cols, s) for s in range(rows)]
        self.me, self.place = (x, r, c), lax.rem(c, rows)
        self.count, self.block = shard.shape[0], shard.shape[1] // rows

    def away(self, device):
        return jnp.logical_not(jnp.logical_and(device[1] == self.me[1], device[2] == self.me[2]))

    def sends(self):
        mine = pl.ds(pl.multiple_of(self.place * self.count, self.count), self.count)
        for s, home in enumerate(self.homes):
            part = self.shard.at[:, pl.ds(s * self.block, self.block)]
            there = self.wires.copy(part, self.main.at[mine], self.slot + s, home, self.slot + self.place)
            yield self.away(home), there, part, self.main.at[mine]

    def start(self):
        self.slot = self.wires.slots(self.rows)
        for remote, there, part, target in self.sends():
            pl.when(remote)(there.start)
            pl.when(jnp.logical_not(remote))(pltpu.make_async_copy(part, target, self.sem).start)

    def finish(self):
        for p, seat in enumerate(self.seats):
            part = self.main.at[pl.ds(p * self.count, self.count)]
            remote = self.away(seat)
            pl.when(remote)(self.wires.copy(part, part, self.slot + p, seat).wait_recv)
            pl.when(jnp.logical_not(remote))(pltpu.make_async_copy(part, part, self.sem).wait)
        for remote, there, _, _ in self.sends():
            pl.when(remote)(there.wait_send)


class LineSum:
    def __init__(self, wires, part, axis, columns, out, scratch, sems, rows):
        x, r, c = here()[0]
        self.wires, self.out, self.axis, self.rows, self.x, self.r = wires, out, axis, rows, x, r
        self.boxes, self.own, self.other = scratch[:2], scratch[2], scratch[3]
        self.devices = [(x, lax.rem(r + 1, rows), c), (x, lax.rem(r + rows - 1, rows), c)]
        self.beside = (1 - x, r, c)
        self.slot = wires.slots(2 * (rows - 1) + 1)
        size = part.shape[axis] // rows
        blocks = [pl.ds(k * size, size) for k in range(rows)]
        self.loads = [
            pltpu.make_async_copy(
                part.at[at, columns] if axis == 0 else part.at[:, at], self.own.at[k], sems.at[k]
            )
            for k, at in enumerate(blocks)
        ]
        for load in self.loads:
            load.start()

    def greeted(self):
        return [(self.devices[0], self.r < self.rows - 1), (self.devices[1], self.r > 0)]

    def blocks(self, step):
        return [lax.rem(2 * self.rows - step + self.r, self.rows), lax.rem(self.rows + self.r + step, self.rows)]

    def copies(self, step):
        return [
            self.wires.copy(self.own.at[s], box.at[step - 1], self.slot + 2 * (step - 1) + i, device)
            for i, (s, box, device) in enumerate(zip(self.blocks(step), self.boxes, self.devices))
        ]

    def sends(self, step):
        r, rows = self.r, self.rows
        return [(r < step) & (r < rows - 1), (r > rows - 1 - step) & (r > 0)]

    def arrivals(self, step):
        r, rows = self.r, self.rows
        return [(r > 0) & (r <= step), (r < rows - 1) & (r >= rows - 1 - step)]

    def chunk(self):
        rows, width = self.other.shape
        return min(rows, STEP * max(1, 2048 // width))

    def gain(self, step, blocks):
        copies, size = self.copies(step), self.chunk()
        for there, copy, s, box in zip(self.arrivals(step), copies, blocks, self.boxes):

            @pl.when(there)
            def _():
                copy.wait_recv()

                @pl.loop(0, self.other.shape[0] // size)
                def _(i):
                    at = pl.ds(pl.multiple_of(i * size, size), size)
                    total = self.own[s, at, :].astype(jnp.float32)
                    self.own[s, at, :] = (total + box[step - 1, at, :].astype(jnp.float32)).astype(LOW)

    def advance(self, step):
        if step == 1:
            for load in self.loads:
                load.wait()
        else:
            self.gain(step - 1, self.blocks(step))
        for there, copy in zip(self.sends(step), self.copies(step)):
            pl.when(there)(copy.start)

    def complete(self):
        self.gain(self.rows - 1, [self.r, self.r])

    def end(self):
        self.share = self.wires.start(self.own.at[self.r], self.other, self.slot + 2 * self.rows - 2, self.beside)
        self.write(lambda at: self.own[self.r, at, :], self.x)

    def finish(self):
        self.share.wait_recv()
        self.write(lambda at: self.other[at, :], 1 - self.x)
        for step in range(1, self.rows):
            for there, copy in zip(self.sends(step), self.copies(step)):
                pl.when(there)(copy.wait_send)

    def write(self, share, place):
        rows, width = self.other.shape
        size = self.chunk()

        @pl.loop(0, rows // size)
        def _(k):
            at = pl.multiple_of(k * size, size)
            value = share(pl.ds(at, size)).astype(jnp.float32)
            if self.axis == 0:
                self.out[pl.ds(at, size), pl.ds(pl.multiple_of(place * width, width), width)] = value
            else:
                self.out[pl.ds(pl.multiple_of(place * rows + at, size), size), :] = value


def plane_kernel(rows, cols, entry, leave, mid, counts, beside_work, line_axes, totals, form, *refs):
    n_blocks, n_small, n_out, n_swap, n_extra, n_made, n_ship, n_lines = counts
    refs = list(refs)
    big = refs.pop(0)
    blocks = [refs.pop(0) for _ in range(n_blocks)]
    weights = blocks[0]
    small = [refs.pop(0) for _ in range(n_small)]
    mine_parts = [refs.pop(0) for _ in range(n_swap)]
    extra = [refs.pop(0) for _ in range(n_extra)]
    leaving = [refs.pop(0) for _ in range(n_ship)]
    line_parts = [refs.pop(0) for _ in line_axes]
    main = refs.pop(0)
    outs = [refs.pop(0) for _ in range(n_out)]
    other_parts = [refs.pop(0) for _ in range(n_swap)]
    made = [refs.pop(0) for _ in range(n_made)]
    landing = [refs.pop(0) for _ in range(n_ship)]
    line_outs = [refs.pop(0) for _ in range(sum(n_lines))]
    shard, send, recv, local = (refs.pop(0) for _ in range(4))
    if totals:
        total, inbox, line_inbox = (refs.pop() for _ in range(3))
    line_scratch = [[refs.pop(8) for _ in range(4)] for _ in line_outs]
    wires = Wires(send, recv)
    me, mate, beside, above = here()
    x, r, c = me
    count, width = shard.shape
    half = count // 2
    low_half, high_half = pl.ds(0, half), pl.ds(half, half)
    homing = None
    if leave == "homes":
        homing = Homing(wires, shard, main, local.at[20], rows, cols)
    elif n_ship:
        homing = Homing(wires, leaving[0], landing[0], local.at[22], rows, cols)
    if leave == "gather":
        gather = PlaneGather(wires, shard, main, local.at[pl.ds(20, 2)], cols)
    greeted = []
    expected = 0
    if homing is not None:
        stays = (lax.div(c, cols // rows) == r) & (lax.rem(c, cols // rows) * rows + lax.rem(c, rows) == c)
        greeted += [(s, homing.away(s)) for s in homing.seats]
        expected = expected + rows - jnp.where(stays, 1, 0).astype(jnp.int32)
    lines = []
    for part, axis, pieces in zip(line_parts, line_axes, n_lines):
        for k in range(pieces):
            i, size = len(lines), part.shape[1] // pieces
            sems = local.at[pl.ds(24 + rows * i, rows)]
            columns = slice(k * size, (k + 1) * size)
            lines.append(LineSum(wires, part, axis, columns, line_outs[i], line_scratch[i], sems, rows))
    for line in lines[:1]:
        greeted += line.greeted()
        expected = expected + sum(jnp.where(there, 1, 0).astype(jnp.int32) for _, there in line.greeted())
    if totals:
        others = [(x, lax.rem(r + k, rows), c) for k in range(1, rows)]
        greeted += [(o, None) for o in others]
        expected = expected + rows - 1
    greeted += [(mate, None), (beside, None), (above, None)]
    swaps = []

    def send_swaps(first, last):
        for source, target in zip(mine_parts, other_parts):
            size = source.shape[0] // 4
            if first == last:
                return
            part = pl.ds(first * size, (last - first) * size)
            swaps.append(wires.start(source.at[part], target.at[part], wires.slots(1), beside))

    if entry == "sum":
        depth = big.shape[2]
        if form == "blocks":
            block_width = weights.shape[1]
        else:
            block_width = min(COLUMNS, width) if form == "turned" else width * depth // weights.shape[0]

        def fetch(i, source=weights):
            if form == "blocks":
                ends = source, refs[1].at[:, pl.ds(pl.multiple_of(i * block_width, block_width), block_width)]
            else:
                ends = weight_block(source, refs[1], i, form, depth, block_width)
            return pltpu.make_async_copy(*ends, local.at[4 + i])

        def arrive(i, size):
            for k in range(size // block_width):
                fetch(i * (size // block_width) + k).wait()

        @pl.loop(0, width // block_width)
        def _(i):
            if form == "blocks":
                for distance, block in zip(DISTANCES, blocks):
                    pl.when(i == r + distance)(fetch(i, block).start)
            else:
                fetch(i).start()

        chips = [(1 - x, above[2]), (1 - x, c), (x, above[2]), (x, c)]
        loads = [
            pltpu.make_async_copy(big.at[(tx * cols + tc) // 2], refs[0].at[k], local.at[k])
            for k, (tx, tc) in enumerate(chips)
        ]
        for load in loads:
            load.start()
    greet(greeted, expected + 3)
    if n_ship:
        homing.start()
    for line in lines:
        line.advance(1)

    if entry == "sum":
        factors, held_weights, both, mated, beside_pass, above_pass, beside_in, above_in = refs
        first = wires.slots(4)
        handed = []
        core = lax.rem(c, 2)
        own_start = pl.multiple_of(core * count, count)
        given_rows = pl.ds(pl.multiple_of((1 - core) * count, count), count)

        def own_rows(start, size):
            return pl.ds(pl.multiple_of(own_start + start, size), size)

        def supply(k, arrive=None):
            loads[k].wait()
            product_into(both.at[k], factors.at[k], held_weights, form, arrive)
            handed.append(wires.start(both.at[k, given_rows], mated.at[k], first + k, mate))

        def add(k, more, start, size):
            @pl.loop(0, size // STEP)
            def _(i):
                at = own_rows(start + i * STEP, STEP)
                to = pl.ds(pl.multiple_of(start + i * STEP, STEP), STEP)
                both[k, at, :] = (
                    both[k, at, :].astype(jnp.float32) + more(to).astype(jnp.float32)
                ).astype(LOW)

        def merge(k):
            handed[k].wait_recv()
            add(k, lambda at: mated[k, at, :], 0, count)

        own_low, own_high = own_rows(0, half), own_rows(half, half)
        if lines:
            send_swaps(0, SWAPS[0])
            slot = wires.slots(6)
            supply(0, arrive)
            handed[0].wait_recv()
            passes = []
            for k, rows_out in enumerate((own_low, own_high)):
                add(0, lambda at: mated[0, at, :], k * half, half)
                to = above_pass.at[pl.ds(k * half, half)]
                passes.append(wires.start(both.at[0, rows_out], to, slot + k, above))
            supply(1)
            merge(1)
            supply(2)
            merge(2)
            above_low = wires.start(both.at[2, own_low], above_in.at[low_half], slot + 2, above)
            above_high = wires.start(both.at[2, own_high], above_in.at[high_half], slot + 3, above)
            supply(3)
            passes[0].wait_recv()
            add(1, lambda at: above_pass[at, :], 0, half)
            beside_low = wires.start(both.at[1, own_low], beside_in.at[low_half], slot + 4, beside)
            for line in lines:
                line.advance(2)
            passes[1].wait_recv()
            add(1, lambda at: above_pass[at, :], half, half)
            beside_high = wires.start(both.at[1, own_high], beside_in.at[high_half], slot + 5, beside)
            send_swaps(SWAPS[0], SWAPS[1])
            groups = [lines[: len(lines) // 2], lines[len(lines) // 2 :]]
            for line in groups[0]:
                line.advance(3)
        else:
            slot = wires.slots(6)
            supply(0, arrive)
            handed[0].wait_recv()
            add(0, lambda at: mated[0, at, :], 0, half)
            pass_beside = wires.start(both.at[0, own_low], beside_pass, slot, beside)
            add(0, lambda at: mated[0, at, :], half, half)
            pass_above = wires.start(both.at[0, own_high], above_pass, slot + 1, above)
            supply(1)
            merge(1)
            beside_low = wires.start(both.at[1, own_low], beside_in.at[low_half], slot + 2, beside)
            supply(2)
            merge(2)
            pass_beside.wait_recv()
            add(2, lambda at: beside_pass[at, :], 0, half)
            above_low = wires.start(both.at[2, own_low], above_in.at[low_half], slot + 3, above)
            above_high = wires.start(both.at[2, own_high], above_in.at[high_half], slot + 4, above)
            supply(3)
            if beside_work is not None:
                beside_work(0, held_weights, extra, made)
            pass_above.wait_recv()
            add(1, lambda at: above_pass[pl.ds(pl.multiple_of(at.start - half, STEP), STEP), :], half, half)
            beside_high = wires.start(both.at[1, own_high], beside_in.at[high_half], slot + 5, beside)
        if beside_work is not None:
            beside_work(1, held_weights, extra, made)
        handed[3].wait_recv()

        def value(at):
            near = both[3, own_rows(at.start, STEP), :].astype(jnp.float32)
            near = near + mated[3, at, :].astype(jnp.float32)
            return near + (beside_in[at, :].astype(jnp.float32) + above_in[at, :].astype(jnp.float32))

    mid.start(outs)
    for k in range(2):
        if entry == "sum":
            (beside_low, beside_high)[k].wait_recv()
            (above_low, above_high)[k].wait_recv()

        @pl.loop(k * (half // STEP), (k + 1) * (half // STEP))
        def _(i):
            at = pl.ds(pl.multiple_of(i * STEP, STEP), STEP)
            shard[at, :] = mid.rows(at, value(at), small, outs).astype(LOW)

        if leave == "gather":
            gather.start(k)

    if leave == "gather":
        gather.finish()
    elif leave == "homes":
        if not lines:
            homing.start()
    else:
        keep = pltpu.make_async_copy(shard, main, local.at[20])
        keep.start()
    if leave == "stay":
        keep.wait()
    if not lines:
        send_swaps(0, 4)
    if totals and not lines:
        gain_sums(wires, me, (mate, beside, above), others, rows, small[-1], outs, total, inbox, line_inbox)
    for k, group in enumerate(groups if lines else ()):
        for line in group:
            line.complete()
        if k == 0:
            for line in groups[1]:
                line.advance(rows - 1)
            gain_sums(wires, me, (mate, beside, above), others, rows, small[-1], outs, total, inbox, line_inbox)
        else:
            homing.start()
        for line in group:
            line.end()
        if k == 1:
            send_swaps(SWAPS[1], 4)
    for line in lines:
        line.finish()
    if homing is not None:
        homing.finish()
    if n_swap:
        for copy in swaps:
            copy.wait_recv()
    wires.finish()


def enter_kernel(
    rows, cols, hidden_in, grad_out, gains_in, normed, held, grad_here, gains,
    shard, seated, grad_seated, hidden_relay, grad_relay, landing, send, recv, local,
):
    wires = Wires(send, recv)
    me, mate, beside, above = here()
    x, r, c = me
    count, width = seated.shape
    block = width // rows
    side = 2 * lax.div(c, 2)
    far = 2 - side
    ways = [(x, c, side), (x, c, side + 1), (x, above[2], side), (x, above[2], side + 1)]
    via = side + lax.rem(r, 2)
    sources = [(x, s, via) for s in range(rows)]
    others = [(x, lax.rem(r + k, rows), c) for k in range(1, rows)]

    def away(device):
        return jnp.logical_not(jnp.logical_and(device[1] == r, device[2] == c))

    kept = jnp.where(lax.rem(c, 2) == lax.rem(r, 2), 1, 0).astype(jnp.int32)
    greeted = [(s, away(s)) for s in sources] + [(o, None) for o in others]
    greeted += [(above, None), (mate, None), (beside, None)]
    greet(greeted, 2 * rows + 2 - kept)

    mine = pl.ds(pl.multiple_of(r * block, block), block)
    slot = wires.slots(rows - 1)
    spread = [wires.start(gains_in, landing.at[r], slot + k, other) for k, other in enumerate(others)]

    class Seating:
        def __init__(self, source, target, relay, sem):
            self.source, self.target, self.relay, self.sem = source, target, relay, sem
            self.slot, self.hop = wires.slots(rows), wires.slots(1)

        def pieces(self):
            near = pl.multiple_of(side * count, count)
            return [
                self.source.at[pl.ds(near, count)],
                self.source.at[pl.ds(near + count, count)],
                self.relay.at[pl.ds(0, count)],
                self.relay.at[pl.ds(count, count)],
            ]

        def cross(self):
            across = self.source.at[pl.ds(pl.multiple_of(far * count, count), 2 * count)]
            self.crossing = wires.start(across, self.relay, self.hop, above)

        def go(self, which):
            for i in which:
                piece, seat = self.pieces()[i], ways[i]
                there = wires.copy(piece, self.target.at[:, mine], self.slot + i, seat, self.slot + r)
                stay = pltpu.make_async_copy(piece, self.target.at[:, mine], self.sem)
                pl.when(away(seat))(there.start)
                pl.when(jnp.logical_not(away(seat)))(stay.start)

        def arrive(self):
            for s, source in enumerate(sources):
                part = self.target.at[:, pl.ds(s * block, block)]
                arrived = wires.copy(part, part, self.slot + s, source)
                stay = pltpu.make_async_copy(part, part, self.sem)
                pl.when(away(source))(arrived.wait_recv)
                pl.when(jnp.logical_not(away(source)))(stay.wait)

        def sent(self):
            for i, piece in enumerate(self.pieces()):
                there = wires.copy(piece, self.target.at[:, mine], self.slot + i, ways[i])
                pl.when(away(ways[i]))(there.wait_send)

    hidden = Seating(hidden_in, seated, hidden_relay, local.at[0])
    grad = Seating(grad_out, grad_seated, grad_relay, local.at[1])
    hidden.cross()
    hidden.go((0, 1))
    grad.cross()
    hidden.crossing.wait_recv()
    hidden.go((2, 3))
    for copy in spread:
        copy.wait_recv()
    landing[r] = gains_in[...]
    for s in range(rows):
        gains[:, s * block : (s + 1) * block] = landing[s]
    hidden.arrive()
    keep = pltpu.make_async_copy(seated, held, local.at[2])
    keep.start()

    gather = PlaneGather(wires, shard, normed, local.at[pl.ds(4, 2)], cols)
    for k in range(2):

        @pl.loop(k * (count // STEP // 2), (k + 1) * (count // STEP // 2))
        def _(i):
            at = pl.ds(pl.multiple_of(i * STEP, STEP), STEP)
            value = seated[at, :].astype(jnp.float32)
            shard[at, :] = (value * rms_scale(value) * gains[0:1, :]).astype(LOW)

        gather.start(k)
    gather.finish()
    grad.go((0, 1))
    grad.crossing.wait_recv()
    grad.go((2, 3))
    grad.arrive()
    keep_grad = pltpu.make_async_copy(grad_seated, grad_here, local.at[3])
    keep_grad.start()
    hidden.sent()
    grad.sent()
    keep.wait()
    keep_grad.wait()
    wires.finish()


def enter_call(hidden_in, grad_out, gains, collective_id):
    rows, cols, parts = lax.axis_size("row"), lax.axis_size("col"), lax.axis_size("dp")
    count, width = hidden_in.shape[0] // rows, hidden_in.shape[1] * rows
    block = width // rows
    vmem = pl.BlockSpec(memory_space=pltpu.VMEM)
    hbm = pl.BlockSpec(memory_space=pl.ANY)
    shape = jax.ShapeDtypeStruct((count, width), LOW)
    tile = pltpu.VMEM((count, width), LOW)
    relay = pltpu.VMEM((2 * count, block), LOW)
    whole = jax.ShapeDtypeStruct((parts * cols, count, width), LOW)
    normed, held, grad_here, gains = pl.pallas_call(
        functools.partial(enter_kernel, rows, cols),
        out_shape=[whole, shape, shape, jax.ShapeDtypeStruct((8, width), jnp.float32)],
        in_specs=[hbm, hbm, vmem],
        out_specs=[hbm, hbm, hbm, vmem],
        scratch_shapes=[tile, tile, tile, relay, relay, pltpu.VMEM((rows, 8, block), jnp.float32)]
        + [pltpu.SemaphoreType.DMA((48,))] * 2
        + [pltpu.SemaphoreType.DMA((8,))],
        compiler_params=pltpu.CompilerParams(
            collective_id=collective_id, has_side_effects=True, vmem_limit_bytes=VMEM_LIMIT
        ),
        cost_estimate=pl.CostEstimate(flops=0, bytes_accessed=20_000_000, transcendentals=0),
    )(hidden_in, grad_out, gains)
    flat = (parts * cols * count, width)
    return normed.reshape(flat), held, grad_here, gains


def spread_kernel(cols, shard, main, send, recv, local):
    wires = Wires(send, recv)
    greet([(device, None) for device in here()[1:]], 3)
    gather = PlaneGather(wires, shard, main, local, cols)
    gather.start(0)
    gather.start(1)
    gather.finish()
    wires.finish()


def spread_call(shard, collective_id):
    cols, parts = lax.axis_size("col"), lax.axis_size("dp")
    hbm = pl.BlockSpec(memory_space=pl.ANY)
    main = pl.pallas_call(
        functools.partial(spread_kernel, cols),
        out_shape=jax.ShapeDtypeStruct((parts * cols, *shard.shape), LOW),
        in_specs=[pl.BlockSpec(memory_space=pltpu.VMEM)],
        out_specs=hbm,
        scratch_shapes=[pltpu.SemaphoreType.DMA((16,))] * 2 + [pltpu.SemaphoreType.DMA((2,))],
        compiler_params=pltpu.CompilerParams(
            collective_id=collective_id, has_side_effects=True, vmem_limit_bytes=VMEM_LIMIT
        ),
        cost_estimate=pl.CostEstimate(flops=0, bytes_accessed=20_000_000, transcendentals=0),
    )(shard)
    return main.reshape(-1, shard.shape[1])


def spread_plain(shard, collective_id):
    return group_gather(shard)


def enter_plain(hidden_in, grad_out, gains, collective_id):
    gains = lax.all_gather(gains, "row", axis=1, tiled=True)
    held = to_group(hidden_in)
    value = held.astype(jnp.float32)
    normed = group_gather((value * rms_scale(value) * gains[0:1]).astype(LOW))
    return normed, held, to_group(grad_out), gains


def gain_sums(wires, me, partners, others, rows, gain_two, outs, total, inbox, line_inbox):
    x, r, c = me
    block = total.shape[1] // rows
    total[0:1, :] = jnp.sum(outs[1][...], axis=0, keepdims=True)
    total[1:2, :] = jnp.sum(gain_two[...], axis=0, keepdims=True)
    total[2:, :] = jnp.zeros_like(total[2:, :])
    first = wires.slots(len(partners))
    for k, partner in enumerate(partners):
        copy = wires.copy(total, inbox.at[k], first + k, partner)
        copy.start()
        copy.wait()
        total[...] += inbox[k]
    first = wires.slots(len(others))
    copies = []
    for k, (_, row, _) in enumerate(others):
        part = total.at[:, pl.ds(pl.multiple_of(row * block, block), block)]
        copies.append(wires.start(part, line_inbox.at[r], first + k, others[k]))
    line_inbox[r] = total[:, pl.ds(pl.multiple_of(r * block, block), block)]
    for copy in copies:
        copy.wait_recv()
    outs[0][...] = sum(line_inbox[k] for k in range(rows))


def plane_call(
    entry, leave, mid, big, small, outs, collective_id, weights=None, form=None, totals=False, swap=(),
    beside_work=None, extra=(), made=(), ship=(), line=(), line_axes=(), line_pieces=(),
):
    rows, cols, parts = lax.axis_size("row"), lax.axis_size("col"), lax.axis_size("dp")
    count, width = big.shape[0] // (parts * cols), small[0].shape[1]
    depth = big.shape[1]
    big = big.reshape(parts * cols // 2, 2 * count, depth)
    gathered = leave == "gather"
    shape = {"gather": (parts * cols, count, width), "homes": (rows * count, width // rows), "stay": (count, width)}[leave]
    landed = [jax.ShapeDtypeStruct((rows * a.shape[0], a.shape[1] // rows), a.dtype) for a in ship]
    plain = len(swap) + len(made) + len(ship)
    vmem = pl.BlockSpec(memory_space=pltpu.VMEM)
    hbm = pl.BlockSpec(memory_space=pl.ANY)
    tile = pltpu.VMEM((count, width), LOW)
    whole, part = pltpu.VMEM((4, count, width), LOW), pltpu.VMEM((count // 2, width), LOW)
    scratch = [tile, pltpu.SemaphoreType.DMA((64,)), pltpu.SemaphoreType.DMA((64,)), pltpu.SemaphoreType.DMA((40,))]
    scratch += [
        pltpu.VMEM(big.shape, LOW),
        pltpu.VMEM((width, depth) if form == "turned" else (depth, width), LOW),
        pltpu.VMEM((4, 2 * count, width), LOW),
    ]
    scratch += [whole, part, tile if line else part, tile, tile]
    line_outs = []
    for array, axis, pieces in zip(line, line_axes, line_pieces):
        block = [n // rows if i == axis else n for i, n in enumerate(array.shape)]
        block[1] //= pieces
        scratch += ([pltpu.VMEM((n, *block), LOW) for n in (rows - 1, rows - 1, rows)] + [pltpu.VMEM(tuple(block), LOW)]) * pieces
        block[1 - axis] *= parts
        line_outs += [jax.ShapeDtypeStruct(tuple(block), jnp.float32)] * pieces
    if totals:
        scratch += [
            pltpu.VMEM((rows, 8, width // rows), jnp.float32),
            pltpu.VMEM((3, 8, width), jnp.float32),
            pltpu.VMEM((8, width), jnp.float32),
        ]
    blocks = weights if form == "blocks" else [weights]
    counts = (len(blocks), len(small), len(outs), len(swap), len(extra), len(made), len(ship), tuple(line_pieces))
    main, *others = pl.pallas_call(
        functools.partial(plane_kernel, rows, cols, entry, leave, mid, counts, beside_work, line_axes, totals, form),
        out_shape=[jax.ShapeDtypeStruct(shape, LOW)]
        + list(outs)
        + [jax.ShapeDtypeStruct(m.shape, m.dtype) for m in (*swap, *made, *landed, *line_outs)],
        in_specs=[hbm] * (1 + len(blocks)) + [vmem] * len(small) + [hbm] * (len(swap) + len(extra) + len(ship) + len(line)),
        out_specs=[hbm] + [vmem] * len(outs) + [hbm] * plain + [vmem] * len(line_outs),
        scratch_shapes=scratch,
        compiler_params=pltpu.CompilerParams(
            collective_id=collective_id, has_side_effects=True, vmem_limit_bytes=VMEM_LIMIT
        ),
        cost_estimate=pl.CostEstimate(flops=0, bytes_accessed=20_000_000, transcendentals=0),
    )(big, *blocks, *small, *swap, *extra, *ship, *line)
    if gathered:
        main = main.reshape(parts * cols * count, width)
    return [main, *others]


def fold(values):
    return values.reshape(values.shape[0] // 8, 8, values.shape[1]).sum(0)


class Mid:
    @staticmethod
    def start(outs):
        pass


class SecondNorm(Mid):
    @staticmethod
    def rows(at, value, small, outs):
        held, gains = small
        middle = held[at, :].astype(jnp.float32) + value
        outs[0][at, :] = middle
        return middle * rms_scale(middle) * gains[1:2, :]


class Add(Mid):
    @staticmethod
    def rows(at, value, small, outs):
        return small[0][at, :] + value


class BackSecond(Mid):
    @staticmethod
    def start(outs):
        outs[1][...] = jnp.zeros_like(outs[1])

    @staticmethod
    def rows(at, value, small, outs):
        middle, grad_out, gains = small
        middle = middle[at, :]
        scale = rms_scale(middle)
        outs[1][...] += fold(value * middle * scale)
        grad = grad_out[at, :].astype(jnp.float32) + norm_back(
            middle, scale, value * gains[1:2, :]
        )
        outs[0][at, :] = grad
        return grad


class BackFirst(Mid):
    @staticmethod
    def start(outs):
        outs[1][...] = jnp.zeros_like(outs[1])

    @staticmethod
    def rows(at, value, small, outs):
        held, grad_middle, gains = small[:3]
        inputs = held[at, :].astype(jnp.float32)
        scale = rms_scale(inputs)
        outs[1][...] += fold(value * inputs * scale)
        return grad_middle[at, :] + norm_back(inputs, scale, value * gains[0:1, :])


def plain_call(
    entry, leave, mid, big, small, outs, collective_id, weights=None, form=None, totals=False, swap=(),
    beside_work=None, extra=(), made=(), ship=(), line=(), line_axes=(), line_pieces=(),
):
    refs = [Holder(a) for a in small]
    given = [Holder(jnp.zeros(o.shape, o.dtype)) for o in outs]
    depth, width = big.shape[1], small[0].shape[1]
    if form == "turned":
        product = inner_cols(big, weights[:, :depth])
    else:
        block = width * depth // weights.shape[0]
        whole = unstack(weights[:, weights.shape[1] - block :], depth)
        product = dot(big, whole)
    mid.start(given)
    shard = mid.rows(slice(None), group_scatter(product), refs, given).astype(LOW)
    main = {"gather": group_gather, "homes": from_group, "stay": lambda a: a}[leave](shard)
    if totals:
        sums = jnp.stack([given[1].value.sum(0), small[-1].sum(0)])
        sums = jnp.pad(lax.psum(sums, ("dp", "row", "col")), ((0, 6), (0, 0)))
        part = outs[0].shape[1]
        given[0].value = lax.dynamic_slice_in_dim(sums, lax.axis_index("row") * part, part, 1)
    others = [dp_other(m) for m in swap]
    if beside_work is not None:
        grads, slope_up, gated, tokens = extra
        lifted = lift_back_plain(grads, whole, slope_up, gated)
        others += [lifted, inner_rows(tokens, lifted).astype(LOW)]
    others += [from_group(a) for a in ship]
    for array, axis, pieces in zip(line, line_axes, line_pieces):
        mine = row_sum(array, axis)
        other = dp_other(mine)
        others += join_tall(mine, other, [(i,) for i in range(pieces)]) if axis == 0 else [join_wide(mine, other)]
    return [main] + [g.value for g in given] + others


class Holder:
    def __init__(self, value):
        self.value, self.dtype, self.shape = value, value.dtype, value.shape

    def __getitem__(self, at):
        return self.value[at]

    def __setitem__(self, at, value):
        self.value = self.value.at[at].set(value)


def swap_halves(values, first):
    lanes = values.shape[1]
    half = HEAD_DIM // 2
    return jnp.where(first, pltpu.roll(values, lanes - half, 1), pltpu.roll(values, half, 1))


def attend_kernel(query, key, value, cosine, sine, mixed, q_out, k_out, v_out, logsum):
    length, lanes = query.shape
    block = min(256, length)
    lane = lax.broadcasted_iota(jnp.int32, (length, lanes), 1)
    first = lax.rem(lane, HEAD_DIM) < HEAD_DIM // 2
    cos, sin = cosine[...], sine[...]

    def rotate(values):
        return (values * cos + swap_halves(values, first) * sin).astype(LOW)

    q_out[...] = rotate(query[...])
    k_out[...] = rotate(key[...])
    low_values = value[...].astype(LOW)
    v_out[...] = low_values
    v_turned = low_values.astype(jnp.float32).T.astype(LOW)
    head = lax.broadcasted_iota(jnp.int32, (block, lanes), 1) // HEAD_DIM
    keep = lax.broadcasted_iota(jnp.int32, (block, block), 0) <= lax.broadcasted_iota(
        jnp.int32, (block, block), 1
    )
    for j in range(length // block):
        at = slice(j * block, (j + 1) * block)
        q_block = q_out[at, :].astype(jnp.float32) * HEAD_DIM ** (-0.5)
        parts = []
        for h in range(lanes // HEAD_DIM):
            q_head = jnp.where(head == h, q_block, 0.0).astype(LOW)
            near = jnp.where(keep, inner_cols(k_out[at, :], q_head), -jnp.inf)
            highest = jnp.max(near, axis=0, keepdims=True)
            if j:
                far = inner_cols(k_out[: j * block, :], q_head)
                highest = jnp.maximum(highest, jnp.max(far, axis=0, keepdims=True))
                far = jnp.exp(far - highest)
            near = jnp.exp(near - highest)
            total = jnp.sum(near, axis=0, keepdims=True)
            if j:
                total = total + jnp.sum(far, axis=0, keepdims=True)
            logsum[0, 0, h : h + 1, at] = highest + jnp.log(total)
            share = 1.0 / total
            out = dot(v_turned[:, at], (near * share).astype(LOW))
            if j:
                out = out + dot(v_turned[:, : j * block], (far * share).astype(LOW))
            parts.append(out[h * HEAD_DIM : (h + 1) * HEAD_DIM])
        mixed[at, :] = jnp.concatenate(parts, 0).T.astype(LOW)


def attend_back_kernel(n_swap, query, key, value, grad, logsum, cosine, sine, *refs):
    mine_parts, refs = refs[:n_swap], refs[n_swap:]
    made, refs = refs[0], refs[1:]
    other_parts, refs = refs[:n_swap], refs[n_swap:]
    (k_sum, v_sum, q_out, k_out, v_out, out_sems), refs = refs[:6], refs[6:]
    length, lanes = query.shape
    if n_swap:
        beside = here()[2]
        wires = Wires(*refs)
        swaps = [
            wires.copy(source, target, i, beside)
            for i, (source, target) in enumerate(zip(mine_parts, other_parts))
        ]
        here_first = (pl.program_id(0) == 0) & (pl.program_id(1) == 0)
        here_last = (pl.program_id(0) == pl.num_programs(0) - 1) & (
            pl.program_id(1) == pl.num_programs(1) - 1
        )

        @pl.when(here_first)
        def _():
            greet([(beside, None)], 1)
            for copy in swaps:
                copy.start()

    block = min(256, length)
    k_sum[...] = jnp.zeros_like(k_sum)
    v_sum[...] = jnp.zeros_like(v_sum)
    k_turned = key[...].astype(jnp.float32).T.astype(LOW)
    head = lax.broadcasted_iota(jnp.int32, (block, lanes), 1) // HEAD_DIM
    keep = lax.broadcasted_iota(jnp.int32, (block, block), 0) <= lax.broadcasted_iota(
        jnp.int32, (block, block), 1
    )
    scale = HEAD_DIM ** (-0.5)

    def rotate_back(values, at):
        rows = values.shape[0]
        lane = lax.broadcasted_iota(jnp.int32, (rows, lanes), 1)
        first = lax.rem(lane, HEAD_DIM) < HEAD_DIM // 2
        return (values * cosine[at, :] - swap_halves(values, first) * sine[at, :]).astype(LOW)

    for j in range(length // block):
        at = slice(j * block, (j + 1) * block)
        before = slice(0, j * block)
        q_block = query[at, :].astype(jnp.float32) * scale
        g_block = grad[at, :].astype(jnp.float32)
        parts = []
        for h in range(lanes // HEAD_DIM):
            q_head = jnp.where(head == h, q_block, 0.0).astype(LOW)
            g_head = jnp.where(head == h, g_block, 0.0).astype(LOW)
            level = logsum[0, 0, h : h + 1, at]
            near = jnp.exp(jnp.where(keep, inner_cols(key[at, :], q_head), -jnp.inf) - level)
            d_near = inner_cols(value[at, :], g_head)
            inner = jnp.sum(near * d_near, axis=0, keepdims=True)
            if j:
                far = jnp.exp(inner_cols(key[before, :], q_head) - level)
                d_far = inner_cols(value[before, :], g_head)
                inner = inner + jnp.sum(far * d_far, axis=0, keepdims=True)
                v_sum[before, :] += dot(far.astype(LOW), g_head)
                s_far = (far * (d_far - inner)).astype(LOW)
                k_sum[before, :] += dot(s_far, q_head)
            v_sum[at, :] += dot(near.astype(LOW), g_head)
            s_near = (near * (d_near - inner)).astype(LOW)
            k_sum[at, :] += dot(s_near, q_head)
            out = dot(k_turned[:, at], s_near)
            if j:
                out = out + dot(k_turned[:, before], s_far)
            parts.append(out[h * HEAD_DIM : (h + 1) * HEAD_DIM])
        q_out[at, :] = rotate_back(jnp.concatenate(parts, 0).T * scale, at)
    k_out[...] = rotate_back(k_sum[...], slice(None))
    v_out[...] = v_sum[...].astype(LOW)
    rows_at = pl.ds(pl.multiple_of(pl.program_id(0) * length, length), length)
    columns = made.shape[1] // 3
    copies = [
        pltpu.make_async_copy(
            out,
            made.at[rows_at, pl.ds(pl.multiple_of(i * columns + pl.program_id(1) * lanes, lanes), lanes)],
            out_sems.at[i],
        )
        for i, out in enumerate((q_out, k_out, v_out))
    ]
    for copy in copies:
        copy.start()
    for copy in copies:
        copy.wait()
    if n_swap:

        @pl.when(here_last)
        def _():
            for copy in swaps:
                copy.wait()


def pair_tables(length):
    half = HEAD_DIM // 2
    freq = THETA ** (-(jnp.arange(half, dtype=jnp.float32) * 2.0 / HEAD_DIM))
    angle = jnp.arange(length, dtype=jnp.float32)[:, None] * freq[None, :]
    cosine, sine = jnp.cos(angle), jnp.sin(angle)
    return jnp.tile(cosine, (1, 4)), jnp.tile(jnp.concatenate([-sine, sine], 1), (1, 2))


def attend_pairs(projected, sequences):
    tokens, columns = projected.shape[0], projected.shape[1] // 3
    length, lanes = tokens // sequences, 2 * HEAD_DIM
    pairs = columns // lanes
    cosine, sine = pair_tables(length)

    def spec(offset):
        return pl.BlockSpec((length, lanes), lambda s, h: (s, offset + h))

    table = pl.BlockSpec((length, lanes), lambda s, h: (0, 0))
    level = pl.BlockSpec((1, 1, 2, length), lambda s, h: (s, h, 0, 0))
    shape = jax.ShapeDtypeStruct((tokens, columns), LOW)
    return pl.pallas_call(
        attend_kernel,
        grid=(sequences, pairs),
        in_specs=[spec(0), spec(pairs), spec(2 * pairs), table, table],
        out_specs=[spec(0)] * 4 + [level],
        out_shape=[shape] * 4 + [jax.ShapeDtypeStruct((sequences, pairs, 2, length), jnp.float32)],
        compiler_params=pltpu.CompilerParams(vmem_limit_bytes=VMEM_LIMIT),
        cost_estimate=pl.CostEstimate(
            flops=8 * tokens * length * columns, bytes_accessed=100_000_000, transcendentals=0
        ),
    )(projected, projected, projected, cosine, sine)


def attend_pairs_back(query, keys, values, grad_mixed, logsum, sequences, swap, collective_id):
    tokens, columns = query.shape
    length, lanes = tokens // sequences, 2 * HEAD_DIM
    pairs = columns // lanes
    cosine, sine = pair_tables(length)
    spec = pl.BlockSpec((length, lanes), lambda s, h: (s, h))
    table = pl.BlockSpec((length, lanes), lambda s, h: (0, 0))
    level = pl.BlockSpec((1, 1, 2, length), lambda s, h: (s, h, 0, 0))
    hbm = pl.BlockSpec(memory_space=pl.ANY)
    return pl.pallas_call(
        functools.partial(attend_back_kernel, len(swap)),
        grid=(sequences, pairs),
        in_specs=[spec] * 4 + [level, table, table] + [hbm] * len(swap),
        out_specs=[hbm] * (1 + len(swap)),
        out_shape=[jax.ShapeDtypeStruct((tokens, 3 * columns), LOW)] + [jax.ShapeDtypeStruct(m.shape, m.dtype) for m in swap],
        scratch_shapes=[pltpu.VMEM((length, lanes), jnp.float32)] * 2
        + [pltpu.VMEM((length, lanes), LOW)] * 3
        + [pltpu.SemaphoreType.DMA((4,))] * 3,
        compiler_params=pltpu.CompilerParams(
            collective_id=collective_id, has_side_effects=True, vmem_limit_bytes=VMEM_LIMIT
        ),
        cost_estimate=pl.CostEstimate(
            flops=20 * tokens * length * columns, bytes_accessed=60_000_000, transcendentals=0
        ),
    )(query, keys, values, grad_mixed, logsum, cosine, sine, *swap)


def lift_kernel(tokens, weights, activated, slope_up, gated):
    rows, width = activated.shape
    step = min(512, rows)
    for i in range(rows // step):
        at = slice(i * step, (i + 1) * step)
        left = tokens[at, :]
        both = dot(left, weights[...])
        gate, upward = both[:, :width], both[:, width:]
        sigmoid = 1.0 / (1.0 + jnp.exp(-gate))
        passed = gate * sigmoid
        activated[at, :] = (passed * upward).astype(LOW)
        gated[at, :] = passed.astype(LOW)
        slope_up[at, :] = (upward * (sigmoid + passed * (1.0 - sigmoid))).astype(LOW)


def lift(tokens, weights):
    count, width = tokens.shape
    units = weights.shape[1] // 2
    tile, rows = units // 2, min(512, count)
    out = pl.BlockSpec((rows, tile), lambda j, i: (i, j))
    shape = jax.ShapeDtypeStruct((count, units), LOW)
    return pl.pallas_call(
        lift_kernel,
        grid=(2, count // rows),
        in_specs=[
            pl.BlockSpec((rows, width), lambda j, i: (i, 0)),
            pl.BlockSpec((width, 2 * tile), lambda j, i: (0, j)),
        ],
        out_specs=[out] * 3,
        out_shape=[shape] * 3,
        compiler_params=pltpu.CompilerParams(vmem_limit_bytes=VMEM_LIMIT),
        cost_estimate=pl.CostEstimate(
            flops=4 * count * width * units, bytes_accessed=30_000_000, transcendentals=0
        ),
    )(tokens, weights)


def lift_back_rows(weights, grads, slope_up, gated, lifted):
    units = slope_up.shape[1]
    tile = units // 2
    for j in range(2):
        here_units = slice(j * tile, (j + 1) * tile)
        grad = inner_cols(grads[...], weights[here_units, :])
        start = 2 * j * tile
        lifted[:, start : start + tile] = (grad * slope_up[:, here_units].astype(jnp.float32)).astype(LOW)
        lifted[:, start + tile : start + 2 * tile] = (
            grad * gated[:, here_units].astype(jnp.float32)
        ).astype(LOW)


def lift_back_work(stage, weights, extra, made):
    grads, slope_up, gated, tokens = extra
    lifted, grad_weights = made
    count, units = slope_up.shape
    width = tokens.shape[1]
    if stage < 2:
        rows = count // 4
        first = stage * (count // 2)
        at = pl.ds(first, count // 2)
        pltpu.emit_pipeline(
            functools.partial(lift_back_rows, weights),
            grid=(2,),
            in_specs=[
                pl.BlockSpec((rows, width), lambda i: (i, 0)),
                pl.BlockSpec((rows, units), lambda i: (i, 0)),
                pl.BlockSpec((rows, units), lambda i: (i, 0)),
            ],
            out_specs=[pl.BlockSpec((rows, 2 * units), lambda i: (i, 0))],
        )(grads.at[at], slope_up.at[at], gated.at[at], lifted.at[at])

    def inner(left, right, out):
        out[...] = inner_rows(left[...], right[...]).astype(LOW)

    if stage == 1:
        part, tile = width // 2, units // 2
        pltpu.emit_pipeline(
            inner,
            grid=(2, 4),
            in_specs=[
                pl.BlockSpec((count, part), lambda i, j: (0, i)),
                pl.BlockSpec((count, tile), lambda i, j: (0, j)),
            ],
            out_specs=[pl.BlockSpec((part, tile), lambda i, j: (i, j))],
        )(tokens, lifted, grad_weights)


def lift_back_plain(grads, weights, slope_up, gated):
    grad = inner_cols(grads, weights)
    up, through = (grad * f.astype(jnp.float32) for f in (slope_up, gated))
    return pair_units(up, through).astype(LOW)


def attend_plain(projected, sequences):
    tokens, columns = projected.shape[0], projected.shape[1] // 3
    length = tokens // sequences
    shape = (sequences, length, columns // HEAD_DIM, HEAD_DIM)
    cosine, sine = rotation_tables(length)
    query = turn(projected[:, :columns].reshape(shape), cosine, sine).astype(LOW)
    keys = turn(projected[:, columns : 2 * columns].reshape(shape), cosine, sine).astype(LOW)
    values = projected[:, 2 * columns :].reshape(shape).astype(LOW)
    mixed, logsum = attend(query, keys, values)
    flat = (tokens, columns)
    return mixed.reshape(flat), query.reshape(flat), keys.reshape(flat), values.reshape(flat), logsum


def attend_plain_back(query, keys, values, grad_mixed, logsum, sequences, swap, collective_id):
    tokens, columns = query.shape
    length = tokens // sequences
    shape = (sequences, length, columns // HEAD_DIM, HEAD_DIM)
    cosine, sine = rotation_tables(length)
    grad_query, grad_keys, grad_values = attend_back(
        *(a.reshape(shape) for a in (query, keys, values, grad_mixed)), logsum
    )
    grads = (turn_back(grad_query, cosine, sine), turn_back(grad_keys, cosine, sine), grad_values)
    grads = jnp.concatenate([g.reshape(tokens, columns).astype(LOW) for g in grads], 1)
    return [grads] + [dp_other(m) for m in swap]


def body(
    hidden_in, w_query, w_key, w_value, w_out, w_gate, w_up, w_down, norm_attn, norm_ffn, grad_out
):
    rows, cols, parts = lax.axis_size("row"), lax.axis_size("col"), lax.axis_size("dp")
    own_kernels = (parts, rows, cols) == (2, 4, 4)
    plane, enter, spread = (
        (plane_call, enter_call, spread_call) if own_kernels else (plain_call, enter_plain, spread_plain)
    )
    count, width = hidden_in.shape[0] // rows, hidden_in.shape[1] * rows
    full_rows = jax.ShapeDtypeStruct((count, width), jnp.float32)
    gain_rows = jax.ShapeDtypeStruct((8, width), jnp.float32)

    local_gains = jnp.pad(jnp.stack([norm_attn, norm_ffn]), ((0, 6), (0, 0)))
    own_attn = [my_part(w, 1) for w in (w_query, w_key, w_value)] + [stack(my_part(w_out, 0))]
    w_attn = lax.all_gather(jnp.concatenate(own_attn, 1), "row", axis=0, tiled=True)
    normed_one, held, grad_here, gains = enter(hidden_in, grad_out, local_gains, 1)
    own_ffn = pair_units(my_part(w_gate, 1), my_part(w_up, 1))
    w_ffn = lax.all_gather(own_ffn, "row", axis=0, tiled=True)
    own_back, normed_one = after(my_part(w_down, 0), normed_one)
    if own_kernels:
        ahead, back = [pass_on(own_back, 1, 0)], [pass_on(own_back, -1, 0)]
    else:
        w_back = lax.all_gather(own_back, "row", axis=0, tiled=True)

    columns = w_attn.shape[1] // 4
    projected = dot(normed_one, w_attn[:, : 3 * columns])
    paired = columns % (2 * HEAD_DIM) == 0
    mixed, query, keys, values, logsum = (attend_pairs if paired else attend_plain)(projected, parts)
    normed_two, middle = plane(
        "sum", "gather", SecondNorm, mixed, [held, gains], [full_rows], 2, w_attn, "stacked"
    )

    if own_kernels:
        ahead[0], back[0], normed_two = after(ahead[0], back[0], normed_two)
        ahead.append(pass_on(ahead[0], 1, 1))
        back.append(pass_on(back[0], -1, 1))
    grad_here, normed_two = after(grad_here, normed_two)
    grad_wide = spread(grad_here, 7)
    if own_kernels:
        ahead[1], back[1], grad_wide = after(ahead[1], back[1], grad_wide)
        ahead.append(pass_on(ahead[1], 1, 2))
        back.append(pass_on(back[1], -1, 2))
        w_back = [own_back, *ahead, *back]
    grad_wide, w_ffn = after(grad_wide, w_ffn)
    w_proj, w_ffn = after(unstack(w_attn[:, 3 * columns :], columns), w_ffn)
    activated, slope_up, gated = lift(normed_two, w_ffn)
    part_down = inner_rows(activated, grad_wide).astype(LOW)
    part_down, w_back = after(part_down, w_back)
    mine_down = row_sum(part_down, 1)
    low = functools.partial(jax.ShapeDtypeStruct, dtype=LOW)
    out_rows, grad_lifted, part_ffn = plane(
        "sum",
        "stay",
        Add,
        activated,
        [middle],
        [],
        3,
        w_back,
        "blocks" if own_kernels else "stacked",
        beside_work=lift_back_work,
        extra=[grad_wide, slope_up, gated, normed_two],
        made=[low((normed_two.shape[0], w_ffn.shape[1])), low((width, w_ffn.shape[1]))],
    )
    mine_ffn = row_sum(part_ffn, 0)
    grad_branch, grad_middle, gain_two, layer_out = plane(
        "sum",
        "gather",
        BackSecond,
        grad_lifted,
        [middle, grad_here, gains],
        [full_rows, gain_rows],
        4,
        w_ffn,
        "turned",
        ship=[out_rows],
    )
    grad_branch, mine_down = after(grad_branch, mine_down)
    grad_mixed = inner_cols(grad_branch, w_proj).astype(LOW)
    part_out, grad_mixed = after(inner_rows(mixed, grad_branch).astype(LOW), grad_mixed)
    grad_projected, other_down = (attend_pairs_back if paired else attend_plain_back)(
        query, keys, values, grad_mixed, logsum, parts, [mine_down], 5
    )
    part_attn = inner_rows(normed_one, grad_projected).astype(LOW)
    grad_in, gain_grads, _, other_ffn, grad_wq, grad_wk, grad_wv, grad_attn_out = plane(
        "sum",
        "homes",
        BackFirst,
        grad_projected,
        [held, grad_middle, gains, gain_two],
        [jax.ShapeDtypeStruct((8, norm_attn.shape[0]), jnp.float32), gain_rows],
        6,
        w_attn,
        "turned",
        totals=True,
        swap=[mine_ffn],
        line=[part_attn, part_out],
        line_axes=(0, 1),
        line_pieces=(3, 1),
    )
    grad_down = join_wide(mine_down, other_down)
    grad_gate, grad_up = join_tall(mine_ffn, other_ffn, [(0, 2), (1, 3)])
    return (
        layer_out,
        grad_in,
        grad_wq,
        grad_wk,
        grad_wv,
        grad_attn_out,
        grad_gate,
        grad_up,
        grad_down,
        gain_grads[0],
        gain_grads[1],
    )


def solution(mesh):
    tokens = P(("dp", "col"), "row")
    tall = P("row", "col")
    wide = P("col", "row")
    gain = P("row")
    return jax.shard_map(
        body,
        mesh=mesh,
        in_specs=(tokens, tall, tall, tall, wide, tall, tall, wide, gain, gain, tokens),
        out_specs=(tokens, tokens, tall, tall, tall, wide, tall, tall, wide, gain, gain),
        check_vma=False,
    )
```
